128 devices in a mesh: ctx: 8 (over x_hi, y), fsdp: 16 (over x_lo, z, core).
Axes of the slice: x: 4 (x_hi: 2, x_lo: 2; x = x_hi * 2 + x_lo), y: 4, z: 4, core: 2. Of those that a mesh axis runs over, the one named last changes fastest.
Arguments:
- tokens: bfloat16 [16, 1024, 1024], P('fsdp', 'ctx'), may hold values from -6 to 6
- d_out: bfloat16 [16, 1024, 1024], P('fsdp', 'ctx'), may hold values from -6 to 6
- block_ids: int32 [16, 16], P('fsdp'), may hold values from 0 to 15, as said below
- w_qkv: float32 [1024, 4096], P('fsdp'), may hold values from -0.1875 to 0.1875
- w_out: float32 [2048, 1024], P('fsdp'), may hold values from -2 to 2
- w_gate_up: float32 [1024, 6144], P('fsdp'), may hold values from -0.1875 to 0.1875
- w_down: float32 [3072, 1024], P('fsdp'), may hold values from -0.21875 to 0.21875
- gains: float32 [2304], P('fsdp'), may hold values from 0.5 to 1.5
- moment_qkv: float32 [1024, 4096], P('fsdp'), may hold values from -64 to 64
- moment_out: float32 [2048, 1024], P('fsdp'), may hold values from -7 to 7
- moment_gate_up: float32 [1024, 6144], P('fsdp'), may hold values from -56 to 56
- moment_down: float32 [3072, 1024], P('fsdp'), may hold values from -48 to 48
- moment_gains: float32 [2304], P('fsdp'), may hold values from -128 to 128
- square_qkv: float32 [1024, 4096], P('fsdp'), may hold values from 245.76 to 3276.8
- square_out: float32 [2048, 1024], P('fsdp'), may hold values from 3.2 to 44.8
- square_gate_up: float32 [1024, 6144], P('fsdp'), may hold values from 212.992 to 2785.28
- square_down: float32 [3072, 1024], P('fsdp'), may hold values from 180.224 to 2293.76
- square_gains: float32 [2304], P('fsdp'), may hold values from 1146.88 to 14745.6
Outputs:
- out_tokens: bfloat16 [16, 1024, 1024], P('fsdp', 'ctx')
- d_tokens: bfloat16 [16, 1024, 1024], P('fsdp', 'ctx')
- updated_qkv: float32 [1024, 4096], P('fsdp')
- updated_out: float32 [2048, 1024], P('fsdp')
- updated_gate_up: float32 [1024, 6144], P('fsdp')
- updated_down: float32 [3072, 1024], P('fsdp')
- updated_gains: float32 [2304], P('fsdp')
- next_moment_qkv: float32 [1024, 4096], P('fsdp')
- next_moment_out: float32 [2048, 1024], P('fsdp')
- next_moment_gate_up: float32 [1024, 6144], P('fsdp')
- next_moment_down: float32 [3072, 1024], P('fsdp')
- next_moment_gains: float32 [2304], P('fsdp')
- next_square_qkv: float32 [1024, 4096], P('fsdp')
- next_square_out: float32 [2048, 1024], P('fsdp')
- next_square_gate_up: float32 [1024, 6144], P('fsdp')
- next_square_down: float32 [3072, 1024], P('fsdp')
- next_square_gains: float32 [2304], P('fsdp')
The draws below stay inside these ranges and needn't reach their ends.
Inputs may be any that keep to these rules, and one draw needn't show every extreme that they name: `block_ids`: in each sequence, the two stored blocks of index 2 r and 2 r + 1 are the blocks c and 15 - c for some c, in either order; every block of a sequence is stored once.
All inputs are finite; a program needn't handle non-finite values.
Results may differ from the reference program's by a relative error of at most 0.033.
Values may be sent and summed in bfloat16 or wider, within the bound.
A program may use at most 192 MiB of HBM per device.

```python
import math
import jax
import jax.numpy as jnp
from jax import lax

D = 1024
QUERY_HEADS = 16
KEY_VALUE_HEADS = 8
HEAD_SIZE = 128
FF = 3072
BLOCK = 64
STEP = 10
QKV = 4096
GAINS = 2304
LENGTH = 1024
SEQS = 16
TOKENS = 16384
OUT_FAN = 8
N_CTX = 8


def draw_block_ids(key, part):
    key = jax.random.fold_in(key, 7)
    order_key, flip_key = jax.random.split(key)
    seq_keys = jax.random.split(order_key, SEQS)
    early = jax.vmap(lambda single: jax.random.permutation(single, N_CTX))(seq_keys).astype(jnp.int32)
    late = 2 * N_CTX - 1 - early
    flips = jax.random.randint(flip_key, (SEQS, N_CTX), 0, 2).astype(jnp.int32)
    first = jnp.where(flips == 1, late, early)
    second = jnp.where(flips == 1, early, late)
    return jnp.stack([first, second], axis=-1).reshape(SEQS, 2 * N_CTX).astype(jnp.int32)


def steps_of(key, extent, shards, smallest, top_value):
    def one(dim, blocks):
        heights = jax.random.uniform(jax.random.fold_in(jax.random.fold_in(key, 6), dim), (blocks,), jnp.float32, smallest / len(shards), top_value / len(shards))
        return jnp.repeat(jnp.exp(heights), extent[dim] // blocks).reshape((-1,) + (1,) * (len(extent) - dim - 1))

    loudness = one(*shards[0])
    for cut in shards[1:]:
        loudness = loudness * one(*cut)
    return loudness


def centred(key, dims, scale, bound, pieces=(), kind=jnp.bfloat16):
    entries = jax.random.normal(key, dims, jnp.float32) * scale
    if len(pieces) > 0:
        entries = steps_of(key, dims, pieces, -0.22, 0.18) * entries
    return jnp.clip(entries, min=-bound, max=bound).astype(kind)


def setup_inputs(seed: int = 0) -> dict:
    seeds = jax.random.split(jax.random.key(seed), 19)
    return {
        "tokens": centred(seeds[0], (SEQS, LENGTH, D), 1.0, 6.0, ((0, 16), (1, 8))),
        "d_out": centred(seeds[1], (SEQS, LENGTH, D), 1.0, 6.0, ((0, 16), (1, 8))),
        "block_ids": draw_block_ids(jax.random.fold_in(seeds[18], 71), 0),
        "w_qkv": centred(seeds[3], (D, QKV), D ** -0.5, 0.1875, ((0, 16),), jnp.float32),
        "w_out": centred(seeds[4], (QUERY_HEADS * HEAD_SIZE, D), OUT_FAN ** -0.5, 2.0, ((0, 16),), jnp.float32),
        "w_gate_up": centred(seeds[5], (D, 2 * FF), D ** -0.5, 0.1875, ((0, 16),), jnp.float32),
        "w_down": centred(seeds[6], (FF, D), (FF // 4) ** -0.5, 0.21875, ((0, 16),), jnp.float32),
        "gains": jnp.clip(1.0 + 0.1 * jax.random.normal(seeds[7], (GAINS,), jnp.float32), 0.5, 1.5),
        "moment_qkv": centred(seeds[8], (D, QKV), (0.08 * TOKENS ** 0.5), 64.0, ((0, 16),), jnp.float32),
        "moment_out": centred(seeds[9], (QUERY_HEADS * HEAD_SIZE, D), (0.14 * (OUT_FAN * TOKENS // (QUERY_HEADS * HEAD_SIZE)) ** 0.5), 7.0, ((0, 16),), jnp.float32),
        "moment_gate_up": centred(seeds[10], (D, 2 * FF), (0.07 * TOKENS ** 0.5), 56.0, ((0, 16),), jnp.float32),
        "moment_down": centred(seeds[11], (FF, D), (0.066 * TOKENS ** 0.5), 48.0, ((0, 16),), jnp.float32),
        "moment_gains": centred(seeds[12], (GAINS,), (0.16 * TOKENS ** 0.5), 128.0, ((0, 16),), jnp.float32),
        "square_qkv": jnp.clip(jnp.exp(math.log(3276.8) - 2.5902672 * jax.random.uniform(seeds[13], (D, QKV), jnp.float32) ** steps_of(seeds[13], (D, QKV), ((0, 16),), -0.2, 0.2)), 245.76, 3276.8),
        "square_out": jnp.clip(jnp.exp(math.log(44.8) - 2.6390573 * jax.random.uniform(seeds[14], (QUERY_HEADS * HEAD_SIZE, D), jnp.float32) ** steps_of(seeds[14], (QUERY_HEADS * HEAD_SIZE, D), ((0, 16),), -0.2, 0.2)), 3.2, 44.8),
        "square_gate_up": jnp.clip(jnp.exp(math.log(2785.28) - 2.5708491 * jax.random.uniform(seeds[15], (D, 2 * FF), jnp.float32) ** steps_of(seeds[15], (D, 2 * FF), ((0, 16),), -0.2, 0.2)), 212.992, 2785.28),
        "square_down": jnp.clip(jnp.exp(math.log(2293.76) - 2.5437472 * jax.random.uniform(seeds[16], (FF, D), jnp.float32) ** steps_of(seeds[16], (FF, D), ((0, 16),), -0.2, 0.2)), 180.224, 2293.76),
        "square_gains": jnp.clip(jnp.exp(math.log(14745.6) - 2.5538995 * jax.random.uniform(seeds[17], (GAINS,), jnp.float32) ** steps_of(seeds[17], (GAINS,), ((0, 16),), -0.2, 0.2)), 1146.88, 14745.6),
    }


@jax.custom_vjp
def low(v):
    return lax.optimization_barrier(v.astype(jnp.bfloat16)).astype(jnp.float32)

@jax.custom_vjp
def low_back(v):
    return v

def low_keep(v):
    return (low(v), None)

def low_pass(kept, grad):
    return (grad,)

def back_keep(v):
    return (v, None)

def back_low(kept, grad):
    return (low(grad),)
low.defvjp(low_keep, low_pass)
low_back.defvjp(back_keep, back_low)
norm_eps = 1e-06
rope_base = 1000000.0
causal_masked_score = -1e+30
beta_first = 0.9
beta_second = 0.95
adam_eps = 1e-08
decay_rate = 0.1

def norm_rows(value):
    return value * lax.rsqrt(lax.optimization_barrier(jnp.mean(value * value, axis=-1, keepdims=True)) + norm_eps)

def rope_tables(positions):
    half = HEAD_SIZE // 2
    freqs = rope_base ** (-(jnp.arange(half, dtype=jnp.float32) * (2.0 / HEAD_SIZE)))
    angles = positions.astype(jnp.float32)[:, None] * freqs[None, :]
    cosine_table = jnp.cos(angles)
    sine_table = jnp.sin(angles)
    return (jnp.concatenate([cosine_table, cosine_table], axis=-1), jnp.concatenate([sine_table, sine_table], axis=-1))

def rotate(value, cosine_table, sine_table):
    half = value.shape[-1] // 2
    turned = jnp.concatenate([-value[..., half:], value[..., :half]], axis=-1)
    return value * cosine_table[:, None, :] + turned * sine_table[:, None, :]

def attend(query_rows, local_keys, local_values, positions):
    sequence_length = query_rows.shape[0]
    current_block = math.gcd(sequence_length, 512)
    softmax_scale = 1.0 / math.sqrt(HEAD_SIZE)
    grouped_queries = query_rows.reshape(sequence_length // current_block, current_block, KEY_VALUE_HEADS, QUERY_HEADS // KEY_VALUE_HEADS, HEAD_SIZE)
    spots = positions.reshape(sequence_length // current_block, current_block)

    def one_block(item):
        part, spot = item
        scores = jnp.einsum('qhgd,khd->hgqk', part, local_keys, precision=lax.Precision.HIGHEST) * softmax_scale
        scores = low_back(scores)
        allowed = positions[None, :] <= spot[:, None]
        scores = jnp.where(allowed, scores, causal_masked_score)
        top = lax.optimization_barrier(jnp.max(scores, axis=-1, keepdims=True))
        powers = jnp.where(allowed, jnp.exp(scores - top), 0.0)
        weights = low(powers / lax.optimization_barrier(jnp.sum(powers, axis=-1, keepdims=True)))
        return jnp.einsum('hgqk,khd->qhgd', weights, local_values, precision=lax.Precision.HIGHEST)
    result = lax.map(jax.checkpoint(one_block), (grouped_queries, spots))
    return result.reshape(sequence_length, QUERY_HEADS * HEAD_SIZE)

def layer(inputs, qkv_weight, out_weight, gate_up_weight, down_weight, gain_all, positions):
    sequence_length = inputs.shape[0]
    gain_one = gain_all[:D]
    gain_two = gain_all[D:2 * D]
    gain_query = gain_all[2 * D:2 * D + HEAD_SIZE]
    key_norm_gain = gain_all[2 * D + HEAD_SIZE:]
    cosine_table, sine_table = rope_tables(positions)
    normed_one = low(norm_rows(inputs) * gain_one)
    projected_rows = low_back(jnp.dot(normed_one, qkv_weight, precision=lax.Precision.HIGHEST))
    query_raw = projected_rows[:, :QUERY_HEADS * HEAD_SIZE].reshape(sequence_length, QUERY_HEADS, HEAD_SIZE)
    unrotated_key = projected_rows[:, QUERY_HEADS * HEAD_SIZE:(QUERY_HEADS + KEY_VALUE_HEADS) * HEAD_SIZE].reshape(sequence_length, KEY_VALUE_HEADS, HEAD_SIZE)
    unprojected_value = projected_rows[:, (QUERY_HEADS + KEY_VALUE_HEADS) * HEAD_SIZE:].reshape(sequence_length, KEY_VALUE_HEADS, HEAD_SIZE)
    rotated_query = low(rotate(norm_rows(query_raw) * gain_query, cosine_table, sine_table))
    rotated_key = low(rotate(norm_rows(unrotated_key) * key_norm_gain, cosine_table, sine_table))
    value_low = low(unprojected_value)
    attention_output = attend(rotated_query, rotated_key, value_low, positions)
    attention_output = low_back(low(attention_output))
    branch = low_back(jnp.dot(attention_output, out_weight, precision=lax.Precision.HIGHEST))
    middle = inputs + branch
    normed_two = low(norm_rows(middle) * gain_two)
    gate_up = low_back(jnp.dot(normed_two, gate_up_weight, precision=lax.Precision.HIGHEST))
    hidden = low(jax.nn.silu(gate_up[:, :FF]) * gate_up[:, FF:])
    return middle + jnp.dot(hidden, down_weight, precision=lax.Precision.HIGHEST)

def adam_update(weight, moment, square, grad, rate, decay):
    moment_new = beta_first * moment + (1.0 - beta_first) * grad
    square_new = beta_second * square + (1.0 - beta_second) * grad * grad
    fix_first = 1.0 - beta_first ** STEP
    fix_second = 1.0 - beta_second ** STEP
    step = moment_new / fix_first / (jnp.sqrt(square_new / fix_second) + adam_eps)
    return (weight - rate * (step + decay * weight), moment_new, square_new)

def reference(tokens, d_out, block_ids, w_qkv, w_out, w_gate_up, w_down, gains, moment_qkv, moment_out, moment_gate_up, moment_down, moment_gains, square_qkv, square_out, square_gate_up, square_down, square_gains):
    masters = (w_qkv, w_out, w_gate_up, w_down, gains)
    rounded = tuple((low(weight) for weight in masters))
    row_index = jnp.arange(LENGTH, dtype=jnp.int32)

    def one_sequence(carry, item):
        inputs, cotangent, order = item
        positions = order[row_index // BLOCK] * BLOCK + row_index % BLOCK

        def forward(local_values, qkv_weight, out_weight, gate_up_weight, down_weight, gain_all):
            return layer(local_values, qkv_weight, out_weight, gate_up_weight, down_weight, gain_all, positions)
        result, pull = jax.vjp(forward, inputs.astype(jnp.float32), *rounded)
        grads = pull(cotangent.astype(jnp.float32))
        carry = tuple((total + grad for total, grad in zip(carry, grads[1:])))
        return (carry, (result.astype(jnp.bfloat16), grads[0].astype(jnp.bfloat16)))
    start = tuple((jnp.zeros(weight.shape, jnp.float32) for weight in masters))
    totals, outputs = lax.scan(one_sequence, start, (tokens, d_out, block_ids))
    out_tokens, d_tokens = outputs
    moments = (moment_qkv, moment_out, moment_gate_up, moment_down, moment_gains)
    squares = (square_qkv, square_out, square_gate_up, square_down, square_gains)
    rates = (0.03, 0.3, 0.03, 0.03, 0.5)
    decays = (decay_rate, decay_rate, decay_rate, decay_rate, 0.0)
    updates = [adam_update(masters[i], moments[i], squares[i], totals[i], rates[i], decays[i]) for i in range(5)]
    return (out_tokens, d_tokens, updates[0][0], updates[1][0], updates[2][0], updates[3][0], updates[4][0], updates[0][1], updates[1][1], updates[2][1], updates[3][1], updates[4][1], updates[0][2], updates[1][2], updates[2][2], updates[3][2], updates[4][2])
```

```python
import math
import types

import jax
import jax.numpy as jnp
import numpy as np
from jax import lax
from jax.experimental import pallas as pl
from jax.experimental.pallas import tpu as pltpu
from jax.sharding import PartitionSpec as P

D = 1024
HEAD = 128
STEP = 10
BLOCK = 64
norm_eps = 1e-06
rope_base = 1000000.0
beta_first = 0.9
beta_second = 0.95
adam_eps = 1e-08
decay_rate = 0.1
SCALE = 1.0 / math.sqrt(HEAD)

f32 = jnp.float32
bf16 = jnp.bfloat16
MESH = pl.DeviceIdType.MESH

INPUTS = dict(
    tok=False, dyt=False, pos_in=False, gain_in=False, freq=False, wqkv_f=True, wo_f=False, wgu_f=True, wd_f=False
)
OUTPUTS = dict(
    out_tok=((128, D), bf16),
    dtok=((128, D), bf16),
    g_qkv=((64, 4096), bf16),
    g_out=((128, D), bf16),
    g_gu=((64, 6144), bf16),
    g_dn=((192, D), bf16),
    g_gain=((24, 128), f32),
)
BUFFERS = dict(
    x_all=((4, 2, 128, D), bf16),
    dy_all=((4, 2, 128, D), bf16),
    n2_all=((4, 2, 128, D), bf16),
    n1_all=((4, 256, D), bf16),
    wq_f=((2, 64, 512), f32),
    wgu_fs=((2, 64, 768), f32),
    wq_send=((2, 64, 512), bf16),
    wgu_send=((2, 64, 768), bf16),
    wo_own=((128, D), bf16),
    wd_own=((192, D), bf16),
    wq=((16, 64, 512), bf16),
    wgu=((16, 64, 768), bf16),
    wo=((256, D), bf16),
    wd=((384, D), bf16),
    gain_recv=((16, 24, 128), f32),
    pos=((2, 8, D), f32),
    posk=((2, D, 1), f32),
    cos_t=((4, 256, HEAD), f32),
    sin_t=((4, 256, HEAD), f32),
    qkraw=((4, 256, 384), f32),
    q_s=((2, 512, 256), bf16),
    kv=((2, D, 256), bf16),
    o_t=((2, 256, 512), f32),
    ob_t=((2, 256, 512), bf16),
    lse=((2, 2, 1, 512), f32),
    pa=((4, 2, 128, D), bf16),
    pb=((4, 2, 128, D), bf16),
    ca=((4, 128, D), bf16),
    cb=((4, 128, D), bf16),
    ra=((3, 128, D), bf16),
    rb=((3, 128, D), bf16),
    h1=((128, D), f32),
    dh1=((128, D), f32),
    hid_all=((4, 256, 384), bf16),
    dgu_all=((4, 256, 768), bf16),
    do_t=((2, 256, 512), bf16),
    delta=((2, 2, 1, 512), f32),
    dkv=((2, D, 256), f32),
    dkv_send=((2, 512, 256), bf16),
    dkv_recv=((2, 512, 256), bf16),
    dqkv=((4, 256, 512), bf16),
    gq=((D, 512), bf16),
    ggu=((D, 768), bf16),
    go=((256, D), bf16),
    gd=((384, D), bf16),
    rq=((16, 64, 512), bf16),
    rgu=((16, 64, 768), bf16),
    ro=((16, 32, 512), bf16),
    rd=((16, 48, 512), bf16),
    sq=((64, 512), bf16),
    sgu=((64, 768), bf16),
    so=((32, 512), bf16),
    sd=((48, 512), bf16),
    fq=((8, 64, 512), bf16),
    fgu=((8, 64, 768), bf16),
    fo=((128, D), bf16),
    fd=((192, D), bf16),
    dg=((24, 128), f32),
    dg_r1=((8, 24, 128), f32),
    dg_s=((24, 128), f32),
    dg_r2=((16, 24, 128), f32),
)
SEMAPHORES = dict(
    ld=16,
    s_x=7,
    r_x=7,
    s_dy=7,
    r_dy=7,
    s_n2=7,
    r_n2=7,
    s_dob=7,
    r_dob=7,
    s_pos=1,
    r_pos=1,
    s_gain=16,
    r_gain=16,
    s_wq=16,
    r_wq=16,
    s_wgu=16,
    r_wgu=16,
    s_wo=4,
    r_wo=1,
    s_wd=4,
    r_wd=1,
    s_wo2=8,
    r_wo2=8,
    s_wd2=8,
    r_wd2=8,
    s_kv=8,
    r_kv=8,
    s_c=16,
    r_c=16,
    s_r=12,
    r_r=12,
    s_dkv=2,
    r_dkv=2,
    s_gq=16,
    r_gq=16,
    s_ggu=16,
    r_ggu=16,
    s_go=16,
    r_go=16,
    s_gd=16,
    r_gd=16,
    s_fq=8,
    r_fq=8,
    s_fgu=8,
    r_fgu=8,
    s_fo=8,
    r_fo=8,
    s_fd=8,
    r_fd=8,
    s_dg1=8,
    r_dg1=8,
    s_dg2=16,
    r_dg2=16,
)


def dot(a, b):
    return jnp.dot(a, b, preferred_element_type=f32)


def dot_nt(a, b):
    return lax.dot_general(a, b, (((1,), (1,)), ((), ())), preferred_element_type=f32)


def dot_tn(a, b):
    return lax.dot_general(a, b, (((0,), (0,)), ((), ())), preferred_element_type=f32)


def to_row(g, first, count):
    return jnp.concatenate([g[first + i : first + i + 1, :] for i in range(count)], axis=1)


def layer_kernel(*refs):
    names = [*INPUTS, *OUTPUTS, *BUFFERS, *SEMAPHORES]
    r = types.SimpleNamespace(**dict(zip(names, refs, strict=True)))

    c = lax.axis_index("ctx")
    f = lax.axis_index("fsdp")
    xh, y = lax.div(c, 4), lax.rem(c, 4)
    xl, z, k = lax.div(f, 8), lax.rem(lax.div(f, 2), 4), lax.rem(f, 2)
    x = 2 * xh + xl
    part = 4 * xl + z
    t = 2 * y + k
    other = 1 - k

    def place(xh_, xl_, y_, z_, k_):
        return (xh_ * 4 + y_, xl_ * 8 + z_ * 2 + k_)

    partner = place(xh, xl, y, z, other)

    def around(value, step):
        return lax.rem(value + step, 4)

    def copy(src, dst, ss, rs, device):
        return pltpu.make_async_remote_copy(
            src_ref=src, dst_ref=dst, send_sem=ss, recv_sem=rs,
            device_id=device, device_id_type=MESH,
        )

    def send(src, dst, ss, rs, device):
        copy(src, dst, ss, rs, device).start()

    def got(ref, rs):
        copy(ref, ref, rs, rs, partner).wait_recv()

    def sent(ref, ss):
        copy(ref, ref, ss, ss, partner).wait_send()

    loads = []

    def load(src, dst):
        one = pltpu.make_async_copy(src, dst, r.ld.at[len(loads)])
        one.start()
        loads.append(one)

    for i in range(2):
        ti = 2 * y + i
        load(r.wqkv_f.at[:, pl.ds(pl.multiple_of(256 * ti, 256), 256)], r.wq_f.at[i, :, pl.ds(0, 256)])
        load(r.wqkv_f.at[:, pl.ds(pl.multiple_of(2048 + 128 * ti, 128), 128)], r.wq_f.at[i, :, pl.ds(256, 128)])
        load(r.wqkv_f.at[:, pl.ds(pl.multiple_of(3072 + 128 * ti, 128), 128)], r.wq_f.at[i, :, pl.ds(384, 128)])
    for i in range(2):
        ti = 2 * y + i
        load(r.wgu_f.at[:, pl.ds(pl.multiple_of(384 * ti, 128), 384)], r.wgu_fs.at[i, :, pl.ds(0, 384)])
        load(r.wgu_f.at[:, pl.ds(pl.multiple_of(3072 + 384 * ti, 128), 384)], r.wgu_fs.at[i, :, pl.ds(384, 384)])

    barrier = pltpu.get_barrier_semaphore()
    me = c * 16 + f

    def greet(i, carry):
        there = lax.rem(me + i, 128)
        pl.semaphore_signal(
            barrier, inc=1, device_id=(lax.div(there, 16), lax.rem(there, 16)), device_id_type=MESH
        )
        return carry

    lax.fori_loop(1, 128, greet, 0)
    pl.semaphore_wait(barrier, 127)

    def gather_start(src, whole, ss, rs):
        for d in (1, 3, 2):
            send(src, whole.at[y, k], ss.at[d - 1], rs.at[d - 1], place(xh, xl, around(y, d), z, k))
        send(src, whole.at[y, k], ss.at[3], rs.at[3], partner)

    def gather_forward(whole, ss, rs, d):
        yy = around(y, 4 - d)
        got(whole.at[yy, k], rs.at[d - 1])
        send(whole.at[yy, k], whole.at[yy, k], ss.at[3 + d], rs.at[3 + d], partner)

    def gather_own(whole, rs):
        got(whole.at[y, other], rs.at[3])

    def gather_pair(whole, rs, d):
        got(whole.at[around(y, 4 - d), other], rs.at[3 + d])

    def gather_end(whole, ss):
        for i in range(7):
            sent(whole.at[y, k], ss.at[i])

    def plane(i, sign):
        dxl, dz, dk = lax.div(i, 8), lax.rem(lax.div(i, 2), 4), lax.rem(i, 2)
        return lax.rem(xl + dxl, 2), lax.rem(z + 4 + sign * dz, 4), lax.rem(k + dk, 2)

    def plane_send(src_of, dst, ss, rs):
        def one(i, carry):
            xl_, z_, k_ = plane(i, 1)
            send(src_of(k_), dst.at[f], ss.at[i], rs.at[i], place(xh, xl_, y, z_, k_))
            return carry

        lax.fori_loop(1, 16, one, 0)

    def plane_got(dst, rs):
        def one(i, carry):
            xl_, z_, k_ = plane(i, -1)
            got(dst.at[xl_ * 8 + z_ * 2 + k_], rs.at[i])
            return carry

        lax.fori_loop(1, 16, one, 0)

    def loop_sent(ref, ss, first, last):
        def one(i, carry):
            sent(ref, ss.at[i])
            return carry

        lax.fori_loop(first, last, one, 0)

    gather_start(r.tok, r.x_all, r.s_x, r.r_x)
    send(r.pos_in, r.pos.at[k], r.s_pos.at[0], r.r_pos.at[0], partner)
    plane_send(lambda k_: r.gain_in, r.gain_recv, r.s_gain, r.r_gain)
    for one in loads[:6]:
        one.wait()
    r.wq_send[...] = r.wq_f[...].astype(bf16)
    plane_send(lambda k_: r.wq_send.at[k_], r.wq, r.s_wq, r.r_wq)
    r.x_all[y, k] = r.tok[...]
    r.dy_all[y, k] = r.dyt[...]
    r.wq[f] = r.wq_send[k]
    r.gain_recv[f] = r.gain_in[...]
    r.pos[k] = r.pos_in[...]
    gather_start(r.dyt, r.dy_all, r.s_dy, r.r_dy)

    r.wo_own[...] = r.wo_f[...].astype(bf16)
    r.wd_own[...] = r.wd_f[...].astype(bf16)
    is_source = lax.div(part, 2) == y
    to_core = lax.rem(part, 2)
    for i in range(4):
        piece = 4 * k + i
        here = (xl == k) & (z == i) & (to_core == k)

        @pl.when(is_source & jnp.logical_not(here))
        def _():
            there = place(xh, k, y, i, to_core)
            send(r.wo_own.at[pl.ds(32 * i, 32)], r.wo.at[pl.ds(pl.multiple_of(32 * piece, 32), 32)], r.s_wo.at[i], r.r_wo.at[0], there)
            send(r.wd_own.at[pl.ds(48 * i, 48)], r.wd.at[pl.ds(pl.multiple_of(48 * piece, 16), 48)], r.s_wd.at[i], r.r_wd.at[0], there)

        @pl.when(is_source & here)
        def _():
            r.wo[pl.ds(pl.multiple_of(32 * piece, 32), 32), :] = r.wo_own[32 * i : 32 * i + 32, :]
            r.wd[pl.ds(pl.multiple_of(48 * piece, 16), 48), :] = r.wd_own[48 * i : 48 * i + 48, :]

    def wo_rows(q):
        return r.wo.at[pl.ds(pl.multiple_of(32 * q, 32), 32)]

    def wd_rows(q):
        return r.wd.at[pl.ds(pl.multiple_of(48 * q, 16), 48)]

    for one in loads[6:]:
        one.wait()
    r.wgu_send[...] = r.wgu_fs[...].astype(bf16)
    r.wgu[f] = r.wgu_send[k]

    got(r.pos.at[other], r.r_pos.at[0])
    steps = lax.broadcasted_iota(jnp.int32, (BLOCK, 1), 0).astype(f32)
    for s in range(2):
        for b in range(16):
            r.posk[s, b * BLOCK : (b + 1) * BLOCK, :] = r.pos[s, 0:1, b * BLOCK : b * BLOCK + 1] + steps
    freq = r.freq[0:1, :]
    sign = r.freq[1:2, :]
    for yy in range(4):
        for s in range(2):
            rows = r.posk[s, pl.ds(pl.multiple_of(512 * xh + 128 * yy, 128), 128), :]
            angle = rows * freq
            r.cos_t[yy, s * 128 : (s + 1) * 128, :] = jnp.cos(angle)
            r.sin_t[yy, s * 128 : (s + 1) * 128, :] = jnp.sin(angle) * sign
    plane_got(r.gain_recv, r.r_gain)
    gains = jnp.sum(r.gain_recv[...], axis=0)
    g1 = to_row(gains, 0, 8)
    g2 = to_row(gains, 8, 8)
    gq = gains[16:17, :]
    gk = gains[17:18, :]
    plane_got(r.wq, r.r_wq)

    def rotated(u, cos, sin):
        return u * cos + pltpu.roll(u, 64, 1) * sin

    def unrotated(u, cos, sin):
        return u * cos - pltpu.roll(u, 64, 1) * sin

    def inverse_rms(u):
        return lax.rsqrt(jnp.mean(u * u, axis=-1, keepdims=True) + norm_eps)

    kv_partner = place(1 - xh, xl, y, z, k)

    def kv_rows(s, yy):
        return r.kv.at[s, pl.ds(pl.multiple_of(512 * xh + 128 * yy, 128), 128)]

    def project(yy):
        rows = r.x_all[yy].reshape(256, D).astype(f32)
        n1 = (rows * inverse_rms(rows) * g1).astype(bf16)
        r.n1_all[yy] = n1
        qkv = dot(n1, r.wq[...].reshape(D, 512))
        r.qkraw[yy] = qkv[:, :384]
        cos, sin = r.cos_t[yy], r.sin_t[yy]
        for h in range(3):
            u = qkv[:, h * HEAD : (h + 1) * HEAD]
            u = rotated(u * inverse_rms(u) * (gq if h < 2 else gk), cos, sin).astype(bf16)
            for s in range(2):
                if h < 2:
                    r.q_s[s, pl.ds(pl.multiple_of(128 * yy, 128), 128), h * HEAD : (h + 1) * HEAD] = u[s * 128 : (s + 1) * 128]
                else:
                    r.kv[s, pl.ds(pl.multiple_of(512 * xh + 128 * yy, 128), 128), 0:HEAD] = u[s * 128 : (s + 1) * 128]
        v = qkv[:, 384:].astype(bf16)
        for s in range(2):
            r.kv[s, pl.ds(pl.multiple_of(512 * xh + 128 * yy, 128), 128), HEAD : 2 * HEAD] = v[s * 128 : (s + 1) * 128]
            send(kv_rows(s, yy), kv_rows(s, yy), r.s_kv.at[2 * yy + s], r.r_kv.at[2 * yy + s], kv_partner)

    gather_own(r.x_all, r.r_x)
    project(y)
    for d in (1, 3, 2):
        gather_forward(r.x_all, r.s_x, r.r_x, d)
        gather_pair(r.x_all, r.r_x, d)
        project(around(y, 4 - d))
    plane_send(lambda k_: r.wgu_send.at[k_], r.wgu, r.s_wgu, r.r_wgu)

    own_piece = (2 * y + k == part) & (xl == k)

    @pl.when(jnp.logical_not(own_piece))
    def _():
        got(wo_rows(part), r.r_wo.at[0])
        got(wd_rows(part), r.r_wd.at[0])

    for i in range(1, 8):
        there = place(xh, lax.rem(xl + i // 4, 2), y, around(z, i % 4), k)
        send(wo_rows(part), wo_rows(part), r.s_wo2.at[i], r.r_wo2.at[i], there)
    for i in range(1, 8):
        there = place(xh, lax.rem(xl + i // 4, 2), y, around(z, i % 4), k)
        send(wd_rows(part), wd_rows(part), r.s_wd2.at[i], r.r_wd2.at[i], there)

    for d in (1, 3, 2):
        gather_forward(r.dy_all, r.s_dy, r.r_dy, d)

    for yy in range(4):
        for s in range(2):
            got(r.kv.at[s, pl.ds(pl.multiple_of(512 * (1 - xh) + 128 * yy, 128), 128)], r.r_kv.at[2 * yy + s])

    gather_end(r.x_all, r.s_x)

    def allowed(s, qc):
        row = r.pos[s, 0:1, pl.ds(pl.multiple_of(512 * xh + 256 * qc, 256), 256)]
        return r.posk[s] <= row

    def lanes(qc):
        return pl.ds(pl.multiple_of(256 * qc, 256), 256)

    def attend(i, carry):
        s, qc = lax.div(i, 2), lax.rem(i, 2)
        ok = allowed(s, qc)
        for h in range(2):
            q = r.q_s[s, pl.ds(pl.multiple_of(256 * qc, 256), 256), h * HEAD : (h + 1) * HEAD]
            scores = jnp.where(ok, dot_nt(r.kv[s, :, 0:HEAD], q) * SCALE, -1e30)
            top = jnp.max(scores, axis=0, keepdims=True)
            p = jnp.exp(scores - top)
            total = jnp.sum(p, axis=0, keepdims=True)
            o = dot_tn(r.kv[s, :, HEAD : 2 * HEAD], p.astype(bf16)) / total
            r.o_t[s, h * HEAD : (h + 1) * HEAD, lanes(qc)] = o
            r.ob_t[s, h * HEAD : (h + 1) * HEAD, lanes(qc)] = o.astype(bf16)
            r.lse[s, h, :, lanes(qc)] = top + jnp.log(total)
        return carry

    lax.fori_loop(0, 4, attend, 0)

    def reduce_first(use, p, cc, yy):
        send(p.at[yy, other], cc.at[yy], r.s_c.at[4 * use + yy], r.r_c.at[4 * use + yy], partner)

    def reduce_second(use, p, cc, rr, d):
        yy = around(y, d)
        got(cc.at[yy], r.r_c.at[4 * use + yy])
        p[yy, k] = (p[yy, k].astype(f32) + cc[yy].astype(f32)).astype(bf16)
        send(p.at[yy, k], rr.at[d - 1], r.s_r.at[3 * use + d - 1], r.r_r.at[3 * use + d - 1], place(xh, xl, yy, z, k))

    def reduce_third(use, p, cc, rr):
        got(cc.at[y], r.r_c.at[4 * use + y])
        total = p[y, k].astype(f32) + cc[y].astype(f32)
        for d in (1, 3, 2):
            got(rr.at[d - 1], r.r_r.at[3 * use + d - 1])
            total = total + rr[d - 1].astype(f32)
        return total

    def reduce_end(use, p):
        for yy in range(4):
            sent(p.at[yy, other], r.s_c.at[4 * use + yy])
        for d in range(3):
            sent(p.at[y, k], r.s_r.at[3 * use + d])

    for i in range(1, 8):
        q = 4 * lax.rem(xl + i // 4, 2) + around(z, 4 - i % 4)
        got(wo_rows(q), r.r_wo2.at[i])

    def out_partial(yy):
        for s in range(2):
            o = r.ob_t[s, :, pl.ds(pl.multiple_of(128 * yy, 128), 128)]
            r.pa[yy, s] = dot_tn(o, r.wo[...]).astype(bf16)

    for d in (2, 1, 3, 0):
        yy = around(y, d)
        out_partial(yy)
        reduce_first(0, r.pa, r.ca, yy)
    for d in (2, 1, 3):
        reduce_second(0, r.pa, r.ca, r.ra, d)
    h1 = r.tok[...].astype(f32) + reduce_third(0, r.pa, r.ca, r.ra)
    r.h1[...] = h1
    r.n2_all[y, k] = (h1 * inverse_rms(h1) * g2).astype(bf16)
    gather_start(r.n2_all.at[y, k], r.n2_all, r.s_n2, r.r_n2)

    gather_own(r.dy_all, r.r_dy)
    for d in (1, 3, 2):
        gather_pair(r.dy_all, r.r_dy, d)
    plane_got(r.wgu, r.r_wgu)
    for i in range(1, 8):
        q = 4 * lax.rem(xl + i // 4, 2) + around(z, 4 - i % 4)
        got(wd_rows(q), r.r_wd2.at[i])

    def feed(yy):
        n2 = r.n2_all[yy].reshape(256, D)
        ab = dot(n2, r.wgu[...].reshape(D, 768))
        a, b = ab[:, :384], ab[:, 384:]
        sig = jax.nn.sigmoid(a)
        silu = a * sig
        r.hid_all[yy] = (silu * b).astype(bf16)
        dhid = dot_nt(r.dy_all[yy].reshape(256, D), r.wd[...])
        r.dgu_all[yy, :, 0:384] = (dhid * b * sig * (1.0 + a * (1.0 - sig))).astype(bf16)
        r.dgu_all[yy, :, 384:768] = (dhid * silu).astype(bf16)
        dn2 = dot_nt(r.dgu_all[yy], r.wgu[...].reshape(D, 768))
        r.pb[yy] = dn2.astype(bf16).reshape(2, 128, D)
        reduce_first(1, r.pb, r.cb, yy)

    gather_own(r.n2_all, r.r_n2)
    feed(y)
    for d in (1, 3, 2):
        gather_forward(r.n2_all, r.s_n2, r.r_n2, d)
        gather_pair(r.n2_all, r.r_n2, d)
        feed(around(y, 4 - d))
    for d in (2, 1, 3):
        reduce_second(1, r.pb, r.cb, r.rb, d)

    def cross(i, sign):
        dx, dz = lax.div(i, 4), lax.rem(i, 4)
        x_, z_ = lax.rem(x + 4 + sign * dx, 4), lax.rem(z + 4 + sign * dz, 4)
        return lax.div(x_, 2), lax.rem(x_, 2), z_

    def cross_send(piece_of, dst, ss, rs):
        def one(i, carry):
            h_, l_, z_ = cross(i, 1)
            send(piece_of(h_, 4 * l_ + z_), dst.at[i], ss.at[i], rs.at[i], place(h_, l_, y, z_, k))
            return carry

        lax.fori_loop(1, 16, one, 0)

    def cross_sum(own, dst, rs):
        def one(i, total):
            got(dst.at[i], rs.at[i])
            return total + dst[i].astype(f32)

        return lax.fori_loop(1, 16, one, own.astype(f32))

    def piece_rows(whole, height):
        def of(h_, p_):
            return whole.at[pl.ds(pl.multiple_of(2 * height * p_ + height * h_, height), height)]

        return of

    def piece_block(whole, height):
        def of(h_, p_):
            return whole.at[pl.ds(pl.multiple_of(height * p_, 16), height), pl.ds(pl.multiple_of(512 * h_, 512), 512)]

        return of

    gq_piece, ggu_piece = piece_rows(r.gq, 64), piece_rows(r.ggu, 64)
    go_piece, gd_piece = piece_block(r.go, 32), piece_block(r.gd, 48)

    def weight_gradient(left, right, out):
        tiles = out.shape[1] // 256

        def one(i, carry):
            cols = pl.ds(pl.multiple_of(256 * i, 256), 256)
            out[:, cols] = dot_tn(left(), right(cols)).astype(bf16)
            return carry

        lax.fori_loop(0, tiles, one, 0)

    weight_gradient(
        lambda: r.hid_all[...].reshape(D, 384),
        lambda cols: r.dy_all[:, :, :, cols].reshape(D, 256),
        r.gd,
    )
    cross_send(gd_piece, r.rd, r.s_gd, r.r_gd)
    weight_gradient(
        lambda: r.n2_all[...].reshape(D, D),
        lambda cols: r.dgu_all[:, :, cols].reshape(D, 256),
        r.ggu,
    )
    cross_send(ggu_piece, r.rgu, r.s_ggu, r.r_ggu)

    dn2 = reduce_third(1, r.pb, r.cb, r.rb)
    h1 = r.h1[...]
    r2 = inverse_rms(h1)
    weighted = dn2 * g2
    dh1 = r.dyt[...].astype(f32) + r2 * weighted - h1 * (r2 * r2 * r2) * jnp.mean(weighted * h1, axis=-1, keepdims=True)
    r.dh1[...] = dh1
    r.dg[...] = jnp.zeros((24, 128), f32)
    dg2 = jnp.sum(dn2 * h1 * r2, axis=0, keepdims=True)
    for i in range(8):
        r.dg[8 + i : 9 + i, :] = dg2[:, 128 * i : 128 * (i + 1)]
    r.x_all[y, k] = dh1.astype(bf16)
    gather_start(r.x_all.at[y, k], r.x_all, r.s_dob, r.r_dob)

    def attention_grad(yy):
        do = dot_nt(r.wo[...], r.x_all[yy].reshape(256, D)).astype(bf16)
        cols = pl.ds(pl.multiple_of(128 * yy, 128), 128)
        for s in range(2):
            part_s = do[:, s * 128 : (s + 1) * 128]
            r.do_t[s, :, cols] = part_s
            prod = part_s.astype(f32) * r.o_t[s, :, cols]
            for h in range(2):
                r.delta[s, h, :, cols] = jnp.sum(prod[h * HEAD : (h + 1) * HEAD], axis=0, keepdims=True)

    gather_own(r.x_all, r.r_dob)
    attention_grad(y)
    for d in (1, 3, 2):
        gather_forward(r.x_all, r.s_dob, r.r_dob, d)
        gather_pair(r.x_all, r.r_dob, d)
        attention_grad(around(y, 4 - d))

    def norm_back(value, gain, grad):
        inverse = inverse_rms(value)
        w = grad * gain
        back = inverse * w - value * (inverse * inverse * inverse) * jnp.mean(w * value, axis=-1, keepdims=True)
        return back, jnp.sum(grad * value * inverse, axis=0, keepdims=True)

    r.dkv[...] = jnp.zeros((2, D, 256), f32)
    for s in range(2):

        def attend_back(qc, carry, s=s):
            ok = allowed(s, qc)
            keys, values = r.kv[s, :, 0:HEAD], r.kv[s, :, HEAD : 2 * HEAD]
            two = pl.ds(2 * qc, 2)
            cos = r.cos_t[two, s * 128 : (s + 1) * 128, :].reshape(256, HEAD)
            sin = r.sin_t[two, s * 128 : (s + 1) * 128, :].reshape(256, HEAD)
            for h in range(2):
                head = slice(h * HEAD, (h + 1) * HEAD)
                q = r.q_s[s, pl.ds(pl.multiple_of(256 * qc, 256), 256), head]
                do = r.do_t[s, head, lanes(qc)]
                scores = dot_nt(keys, q) * SCALE
                p = jnp.where(ok, jnp.exp(scores - r.lse[s, h, :, lanes(qc)]), 0.0)
                ds = (p * (dot(values, do) - r.delta[s, h, :, lanes(qc)])).astype(bf16)
                r.dkv[s, :, HEAD : 2 * HEAD] += dot_nt(p.astype(bf16), do)
                r.dkv[s, :, 0:HEAD] += dot(ds, q) * SCALE
                dq = (dot_tn(keys, ds) * SCALE).T
                raw = r.qkraw[two, s * 128 : (s + 1) * 128, head].reshape(256, HEAD)
                back, gain_grad = norm_back(raw, gq, unrotated(dq, cos, sin))
                r.dqkv[two, s * 128 : (s + 1) * 128, head] = back.astype(bf16).reshape(2, 128, HEAD)
                r.dg[16:17, :] += gain_grad
            return carry

        lax.fori_loop(0, 2, attend_back, 0)
        r.dkv_send[s] = r.dkv[s, pl.ds(pl.multiple_of(512 * (1 - xh), 512), 512), :].astype(bf16)
        send(r.dkv_send.at[s], r.dkv_recv.at[s], r.s_dkv.at[s], r.r_dkv.at[s], kv_partner)

    reduce_end(0, r.pa)

    def down_partial(i, carry):
        r.pa[i] = dot(r.hid_all[i], r.wd[...]).astype(bf16).reshape(2, 128, D)
        return carry

    lax.fori_loop(0, 4, down_partial, 0)
    for d in (2, 1, 3, 0):
        reduce_first(2, r.pa, r.ca, around(y, d))
    for d in (2, 1, 3):
        reduce_second(2, r.pa, r.ca, r.ra, d)

    def out_gradient(i, carry):
        cols = pl.ds(pl.multiple_of(256 * i, 256), 256)
        total = dot(r.ob_t[0], r.x_all[:, 0, :, cols].reshape(512, 256))
        total = total + dot(r.ob_t[1], r.x_all[:, 1, :, cols].reshape(512, 256))
        r.go[:, cols] = total.astype(bf16)
        return carry

    lax.fori_loop(0, 4, out_gradient, 0)
    cross_send(go_piece, r.ro, r.s_go, r.r_go)

    def spread_rows(total, hold, final, ss, rs):
        hold[...] = total.astype(bf16)

        def one(i, carry):
            there = place(lax.rem(xh + lax.div(i, 4), 2), xl, lax.rem(y + i, 4), z, xh)

            @pl.when((i > 0) | (k != xh))
            def _():
                send(hold, final.at[t], ss.at[i], rs.at[t], there)

            return carry

        lax.fori_loop(0, 8, one, 0)

        @pl.when(k == xh)
        def _():
            final[t] = hold[...]

    def spread_rows_sent(hold, ss):
        def one(i, carry):
            @pl.when((i > 0) | (k != xh))
            def _():
                sent(hold, ss.at[i])

            return carry

        lax.fori_loop(0, 8, one, 0)

    def spread_rows_got(final, rs):
        def one(i, carry):
            @pl.when((i != t) | (k != xh))
            def _():
                got(final.at[i], rs.at[i])

            return carry

        lax.fori_loop(0, 8, one, 0)

    home = (xl == lax.div(t, 4)) & (z == lax.rem(t, 4)) & (k == xl)

    def spread_block(total, hold, final, height, ss, rs):
        hold[...] = total.astype(bf16)
        rows = pl.ds(pl.multiple_of(height * z, 16), height)
        cols = pl.ds(pl.multiple_of(512 * xh, 512), 512)

        def one(i, carry):
            there = place(lax.rem(xh + lax.div(i, 4), 2), lax.div(t, 4), lax.rem(y + i, 4), lax.rem(t, 4), xl)

            @pl.when((i > 0) | jnp.logical_not(home))
            def _():
                send(hold, final.at[rows, cols], ss.at[i], rs.at[4 * xh + z], there)

            return carry

        lax.fori_loop(0, 8, one, 0)

        @pl.when(home)
        def _():
            final[rows, cols] = hold[...]

    def spread_block_sent(hold, ss):
        def one(i, carry):
            @pl.when((i > 0) | jnp.logical_not(home))
            def _():
                sent(hold, ss.at[i])

            return carry

        lax.fori_loop(0, 8, one, 0)

    def spread_block_got(final, height, rs):
        def one(i, carry):
            @pl.when((i != 4 * xh + z) | jnp.logical_not(home))
            def _():
                rows = pl.ds(pl.multiple_of(height * lax.rem(i, 4), 16), height)
                cols = pl.ds(pl.multiple_of(512 * lax.div(i, 4), 512), 512)
                got(final.at[rows, cols], rs.at[i])

            return carry

        lax.fori_loop(0, 8, one, 0)

    spread_block(cross_sum(gd_piece(xh, part)[...], r.rd, r.r_gd), r.sd, r.fd, 48, r.s_fd, r.r_fd)
    spread_rows(cross_sum(ggu_piece(xh, part)[...], r.rgu, r.r_ggu), r.sgu, r.fgu, r.s_fgu, r.r_fgu)

    for s in range(2):
        got(r.dkv_recv.at[s], r.r_dkv.at[s])
    reduce_end(1, r.pb)

    def key_back(yy, carry):
        rows = pl.ds(pl.multiple_of(512 * xh + 128 * yy, 128), 128)
        local = pl.ds(pl.multiple_of(128 * yy, 128), 128)
        grads = [r.dkv[s, rows, :] + r.dkv_recv[s, local, :].astype(f32) for s in range(2)]
        both = jnp.concatenate(grads, axis=0)
        du = unrotated(both[:, 0:HEAD], r.cos_t[yy], r.sin_t[yy])
        back, gain_grad = norm_back(r.qkraw[yy, :, 256:384], gk, du)
        r.dqkv[yy, :, 256:384] = back.astype(bf16)
        r.dqkv[yy, :, 384:512] = both[:, HEAD : 2 * HEAD].astype(bf16)
        r.dg[17:18, :] += gain_grad
        return carry

    lax.fori_loop(0, 4, key_back, 0)

    def project_back(yy):
        dn1 = dot_nt(r.dqkv[yy], r.wq[...].reshape(D, 512))
        r.pb[yy] = dn1.astype(bf16).reshape(2, 128, D)
        reduce_first(3, r.pb, r.cb, yy)

    for d in (2, 1, 3, 0):
        project_back(around(y, d))
    weight_gradient(
        lambda: r.n1_all[...].reshape(D, D),
        lambda cols: r.dqkv[:, :, cols].reshape(D, 256),
        r.gq,
    )
    cross_send(gq_piece, r.rq, r.s_gq, r.r_gq)
    for d in (2, 1, 3):
        reduce_second(3, r.pb, r.cb, r.rb, d)

    out_tokens = r.h1[...] + reduce_third(2, r.pa, r.ca, r.ra)
    r.out_tok[...] = out_tokens.astype(bf16)
    spread_block(cross_sum(go_piece(xh, part)[...], r.ro, r.r_go), r.so, r.fo, 32, r.s_fo, r.r_fo)

    dn1 = reduce_third(3, r.pb, r.cb, r.rb)
    rows = r.tok[...].astype(f32)
    back, dg1 = norm_back(rows, g1, dn1)
    r.dtok[...] = (r.dh1[...] + back).astype(bf16)
    for i in range(8):
        r.dg[i : i + 1, :] = dg1[:, 128 * i : 128 * (i + 1)]
    for i in range(1, 8):
        there = place(xh, xl, around(y, i // 2), z, lax.rem(k + i, 2))
        send(r.dg, r.dg_r1.at[i], r.s_dg1.at[i], r.r_dg1.at[i], there)
    spread_rows(cross_sum(gq_piece(xh, part)[...], r.rq, r.r_gq), r.sq, r.fq, r.s_fq, r.r_fq)
    total = r.dg[...]
    for i in range(1, 8):
        got(r.dg_r1.at[i], r.r_dg1.at[i])
        total = total + r.dg_r1[i]
    r.dg_s[...] = total
    cross_send(lambda h_, p_: r.dg_s, r.dg_r2, r.s_dg2, r.r_dg2)

    spread_block_got(r.fd, 48, r.r_fd)
    r.g_dn[...] = r.fd[...]
    spread_rows_got(r.fgu, r.r_fgu)
    for i in range(8):
        r.g_gu[:, 384 * i : 384 * (i + 1)] = r.fgu[i, :, 0:384]
        r.g_gu[:, 3072 + 384 * i : 3072 + 384 * (i + 1)] = r.fgu[i, :, 384:768]
    spread_block_got(r.fo, 32, r.r_fo)
    r.g_out[...] = r.fo[...]
    r.g_gain[...] = cross_sum(r.dg_s[...], r.dg_r2, r.r_dg2)
    spread_rows_got(r.fq, r.r_fq)
    for i in range(8):
        r.g_qkv[:, 256 * i : 256 * (i + 1)] = r.fq[i, :, 0:256]
        r.g_qkv[:, 2048 + 128 * i : 2048 + 128 * (i + 1)] = r.fq[i, :, 256:384]
        r.g_qkv[:, 3072 + 128 * i : 3072 + 128 * (i + 1)] = r.fq[i, :, 384:512]

    for whole, ss in ((r.dy_all, r.s_dy), (r.n2_all, r.s_n2), (r.x_all, r.s_dob)):
        gather_end(whole, ss)
    sent(r.pos_in, r.s_pos.at[0])
    loop_sent(r.gain_in, r.s_gain, 1, 16)
    loop_sent(r.wq_send.at[0], r.s_wq, 1, 16)
    loop_sent(r.wgu_send.at[0], r.s_wgu, 1, 16)
    for i in range(4):
        here = (xl == k) & (z == i) & (to_core == k)

        @pl.when(is_source & jnp.logical_not(here))
        def _():
            sent(r.wo_own.at[pl.ds(32 * i, 32)], r.s_wo.at[i])
            sent(r.wd_own.at[pl.ds(48 * i, 48)], r.s_wd.at[i])

    loop_sent(wo_rows(part), r.s_wo2, 1, 8)
    loop_sent(wd_rows(part), r.s_wd2, 1, 8)
    loop_sent(r.kv.at[0, pl.ds(0, 128)], r.s_kv, 0, 8)
    reduce_end(2, r.pa)
    reduce_end(3, r.pb)
    for s in range(2):
        sent(r.dkv_send.at[s], r.s_dkv.at[s])
    loop_sent(gq_piece(xh, part), r.s_gq, 1, 16)
    loop_sent(ggu_piece(xh, part), r.s_ggu, 1, 16)
    loop_sent(go_piece(xh, part), r.s_go, 1, 16)
    loop_sent(gd_piece(xh, part), r.s_gd, 1, 16)
    spread_rows_sent(r.sq, r.s_fq)
    spread_rows_sent(r.sgu, r.s_fgu)
    spread_block_sent(r.so, r.s_fo)
    spread_block_sent(r.sd, r.s_fd)
    loop_sent(r.dg, r.s_dg1, 1, 8)
    loop_sent(r.dg_s, r.s_dg2, 1, 16)


def layer(*args):
    vmem = pl.BlockSpec(memory_space=pltpu.VMEM)
    hbm = pl.BlockSpec(memory_space=pl.ANY)
    specs = [hbm if far else vmem for far in INPUTS.values()]
    return pl.pallas_call(
        layer_kernel,
        out_shape=[jax.ShapeDtypeStruct(shape, kind) for shape, kind in OUTPUTS.values()],
        in_specs=specs,
        out_specs=[vmem] * len(OUTPUTS),
        scratch_shapes=[pltpu.VMEM(shape, kind) for shape, kind in BUFFERS.values()]
        + [pltpu.SemaphoreType.DMA((count,)) for count in SEMAPHORES.values()],
        compiler_params=pltpu.CompilerParams(
            collective_id=0, has_side_effects=True, vmem_limit_bytes=62 << 20
        ),
        name="layer",
    )(*args)


def adam_update(weight, moment, square, grad, rate, decay):
    moment_new = beta_first * moment + (1.0 - beta_first) * grad
    square_new = beta_second * square + (1.0 - beta_second) * grad * grad
    fix_first = 1.0 - beta_first**STEP
    fix_second = 1.0 - beta_second**STEP
    step = moment_new / fix_first / (jnp.sqrt(square_new / fix_second) + adam_eps)
    return (weight - rate * (step + decay * weight), moment_new, square_new)


def on_device(
    tokens, d_out, block_ids,
    w_qkv, w_out, w_gate_up, w_down, gains,
    moment_qkv, moment_out, moment_gate_up, moment_down, moment_gains,
    square_qkv, square_out, square_gate_up, square_down, square_gains,
):
    f = lax.axis_index("fsdp")
    starts = block_ids[0].astype(f32) * BLOCK
    positions = (starts[:, None] + jnp.arange(BLOCK, dtype=f32)[None, :]).reshape(1, D)
    positions = jnp.broadcast_to(positions, (8, D))
    gain_rows = lax.dynamic_update_slice(
        jnp.zeros((24 * 128,), f32), gains.astype(bf16).astype(f32), (f * 144,)
    ).reshape(24, 128)
    half = rope_base ** (-(np.arange(64, dtype=np.float32) * np.float32(2.0 / HEAD)))
    table = np.zeros((8, 128), np.float32)
    table[0] = np.concatenate([half, half])
    table[1] = np.concatenate([-np.ones(64), np.ones(64)])
    out_tok, dtok, g_qkv, g_out, g_gu, g_dn, g_gain = layer(
        tokens[0], d_out[0], positions, gain_rows, jnp.asarray(table), w_qkv, w_out, w_gate_up, w_down
    )
    grad_gains = lax.dynamic_slice(g_gain.reshape(24 * 128), (f * 144,), (144,))
    grads = (g_qkv, g_out, g_gu, g_dn, grad_gains)
    masters = (w_qkv, w_out, w_gate_up, w_down, gains)
    moments = (moment_qkv, moment_out, moment_gate_up, moment_down, moment_gains)
    squares = (square_qkv, square_out, square_gate_up, square_down, square_gains)
    rates = (0.03, 0.3, 0.03, 0.03, 0.5)
    decays = (decay_rate, decay_rate, decay_rate, decay_rate, 0.0)
    updates = [
        adam_update(masters[i], moments[i], squares[i], grads[i].astype(f32), rates[i], decays[i])
        for i in range(5)
    ]
    return (
        out_tok[None],
        dtok[None],
        *(u[0] for u in updates),
        *(u[1] for u in updates),
        *(u[2] for u in updates),
    )


def solution(mesh):
    rows, flat = P("fsdp", None), P("fsdp")
    tokens = P("fsdp", "ctx", None)
    state = (rows, rows, rows, rows, flat)
    return jax.shard_map(
        on_device,
        mesh=mesh,
        in_specs=(tokens, tokens, rows) + state * 3,
        out_specs=(tokens, tokens) + state * 3,
        check_vma=False,
    )
```

```python
import math
import types

import jax
import jax.numpy as jnp
import numpy as np
from jax import lax
from jax.experimental import pallas as pl
from jax.experimental.pallas import tpu as pltpu
from jax.sharding import PartitionSpec as P

D = 1024
HEAD = 128
STEP = 10
BLOCK = 64
norm_eps = 1e-06
rope_base = 1000000.0
beta_first = 0.9
beta_second = 0.95
adam_eps = 1e-08
decay_rate = 0.1
SCALE = 1.0 / math.sqrt(HEAD)

f32 = jnp.float32
bf16 = jnp.bfloat16
MESH = pl.DeviceIdType.MESH

INPUTS = dict(
    tok=False, dyt=False, pos_in=False, gain_in=False, freq=False, wqkv_f=True, wo_f=False, wgu_f=True, wd_f=False
)
OUTPUTS = dict(
    out_tok=((128, D), bf16),
    dtok=((128, D), bf16),
    g_qkv=((64, 4096), bf16),
    g_out=((128, D), bf16),
    g_gu=((64, 6144), bf16),
    g_dn=((192, D), bf16),
    g_gain=((24, 128), f32),
)
BUFFERS = dict(
    x_all=((4, 2, 128, D), bf16),
    dy_all=((4, 2, 128, D), bf16),
    n2_all=((4, 2, 128, D), bf16),
    n1_all=((4, 256, D), bf16),
    wq_f=((2, 64, 512), f32),
    wgu_fs=((2, 64, 768), f32),
    wq_send=((2, 64, 512), bf16),
    wgu_send=((2, 64, 768), bf16),
    wo_own=((128, D), bf16),
    wd_own=((192, D), bf16),
    wq=((16, 64, 512), bf16),
    wgu=((16, 64, 768), bf16),
    wo=((256, D), bf16),
    wd=((384, D), bf16),
    gain_recv=((16, 24, 128), f32),
    pos=((2, 8, D), f32),
    posk=((2, D, 1), f32),
    cos_t=((4, 256, HEAD), f32),
    sin_t=((4, 256, HEAD), f32),
    qkraw=((4, 256, 384), f32),
    q_s=((2, 2, 256, 256), bf16),
    kv=((2, D, 256), bf16),
    o_t=((2, 256, 512), f32),
    ob_t=((2, 256, 512), bf16),
    lse=((2, 2, 1, 512), f32),
    pa=((4, 2, 128, D), bf16),
    pb=((4, 2, 128, D), bf16),
    ca=((4, 128, D), bf16),
    cb=((4, 128, D), bf16),
    ra=((3, 128, D), bf16),
    rb=((3, 128, D), bf16),
    h1=((128, D), f32),
    dh1=((128, D), f32),
    hid_all=((4, 2, 128, 384), bf16),
    dgu_all=((4, 2, 128, 768), bf16),
    do_t=((2, 256, 512), bf16),
    delta=((2, 2, 1, 512), f32),
    dkv=((2, D, 256), f32),
    dkv_send=((2, 512, 256), bf16),
    dkv_recv=((2, 512, 256), bf16),
    dqkv=((4, 256, 512), bf16),
    gqa=((D, 256), bf16),
    gqb=((D, 256), bf16),
    wdot=((D, HEAD), f32),
    ggu=((D, 768), bf16),
    go=((256, D), bf16),
    gd=((384, D), bf16),
    rqa=((16, 64, 256), bf16),
    rqb=((16, 64, 256), bf16),
    rgu=((16, 64, 768), bf16),
    ro=((16, 32, 512), bf16),
    rd=((16, 48, 512), bf16),
    sqa=((64, 256), bf16),
    sqb=((64, 256), bf16),
    sgu=((64, 768), bf16),
    so=((32, 512), bf16),
    sd=((48, 512), bf16),
    fqa=((8, 64, 256), bf16),
    fqb=((8, 64, 256), bf16),
    fgu=((8, 64, 768), bf16),
    fo=((128, D), bf16),
    fd=((192, D), bf16),
    dg=((24, 128), f32),
    dg_r1=((8, 24, 128), f32),
    dg_s=((24, 128), f32),
    dg_r2=((16, 24, 128), f32),
)
SEMAPHORES = dict(
    ld=16,
    s_x=7, r_x=7,
    s_dy=7, r_dy=7,
    s_n2=14, r_n2=14,
    s_dob=14, r_dob=14,
    s_pos=1, r_pos=1,
    s_gain=12, r_gain=12,
    s_wq=12, r_wq=12,
    s_wgu=12, r_wgu=12,
    s_wo=4, r_wo=1, s_wd=4, r_wd=1,
    s_wo2=8, r_wo2=8, s_wd2=8, r_wd2=8,
    s_kv=8, r_kv=8,
    s_c=32, r_c=32,
    s_r=24, r_r=24,
    s_dkv=2, r_dkv=2,
    s_gqa=16, r_gqa=16,
    s_gqb=16, r_gqb=16,
    s_ggu=16, r_ggu=16,
    s_go=16, r_go=16,
    s_gd=16, r_gd=16,
    s_fqa=8, r_fqa=8,
    s_fqb=8, r_fqb=8,
    s_fgu=8, r_fgu=8,
    s_fo=8, r_fo=8,
    s_fd=8, r_fd=8,
    s_dg1=8, r_dg1=8,
    s_dg2=16, r_dg2=16,
)


def dot(a, b):
    return jnp.dot(a, b, preferred_element_type=f32)


def dot_nt(a, b):
    return lax.dot_general(a, b, (((1,), (1,)), ((), ())), preferred_element_type=f32)


def dot_tn(a, b):
    return lax.dot_general(a, b, (((0,), (0,)), ((), ())), preferred_element_type=f32)


def to_row(g, first, count):
    return jnp.concatenate([g[first + i : first + i + 1, :] for i in range(count)], axis=1)


def layer_kernel(*refs):
    names = [*INPUTS, *OUTPUTS, *BUFFERS, *SEMAPHORES]
    r = types.SimpleNamespace(**dict(zip(names, refs, strict=True)))

    c = lax.axis_index("ctx")
    f = lax.axis_index("fsdp")
    xh, y = lax.div(c, 4), lax.rem(c, 4)
    xl, z, k = lax.div(f, 8), lax.rem(lax.div(f, 2), 4), lax.rem(f, 2)
    x = 2 * xh + xl
    part = 4 * xl + z
    t = 2 * y + k
    other = 1 - k

    def place(xh_, xl_, y_, z_, k_):
        return (xh_ * 4 + y_, xl_ * 8 + z_ * 2 + k_)

    partner = place(xh, xl, y, z, other)

    def around(value, step):
        return lax.rem(value + step, 4)

    def copy(src, dst, ss, rs, device):
        return pltpu.make_async_remote_copy(
            src_ref=src, dst_ref=dst, send_sem=ss, recv_sem=rs,
            device_id=device, device_id_type=MESH,
        )

    def send(src, dst, ss, rs, device):
        copy(src, dst, ss, rs, device).start()

    def got(ref, rs):
        copy(ref, ref, rs, rs, partner).wait_recv()

    def sent(ref, ss):
        copy(ref, ref, ss, ss, partner).wait_send()

    loads = []

    def load(src, dst):
        one = pltpu.make_async_copy(src, dst, r.ld.at[len(loads)])
        one.start()
        loads.append(one)

    for i in range(2):
        ti = 2 * y + i
        load(r.wqkv_f.at[:, pl.ds(pl.multiple_of(256 * ti, 256), 256)], r.wq_f.at[i, :, pl.ds(0, 256)])
        load(r.wqkv_f.at[:, pl.ds(pl.multiple_of(2048 + 128 * ti, 128), 128)], r.wq_f.at[i, :, pl.ds(256, 128)])
        load(r.wqkv_f.at[:, pl.ds(pl.multiple_of(3072 + 128 * ti, 128), 128)], r.wq_f.at[i, :, pl.ds(384, 128)])
    for i in range(2):
        ti = 2 * y + i
        load(r.wgu_f.at[:, pl.ds(pl.multiple_of(384 * ti, 128), 384)], r.wgu_fs.at[i, :, pl.ds(0, 384)])
        load(r.wgu_f.at[:, pl.ds(pl.multiple_of(3072 + 384 * ti, 128), 384)], r.wgu_fs.at[i, :, pl.ds(384, 384)])

    barrier = pltpu.get_barrier_semaphore()

    def greet(device):
        pl.semaphore_signal(barrier, inc=1, device_id=device, device_id_type=MESH)

    def greet_groups(i, carry):
        a, b, d = lax.div(i, 8), lax.rem(lax.div(i, 2), 4), lax.rem(i, 2)
        core = lax.rem(k + d, 2)
        greet(place(lax.rem(xh + a, 2), xl, around(y, b), z, core))
        greet(place(xh, lax.rem(xl + a, 2), y, around(z, b), core))
        x_ = lax.rem(x + lax.div(i, 4), 4)
        greet(place(lax.div(x_, 2), lax.rem(x_, 2), y, around(z, lax.rem(i, 4)), k))
        return carry

    home = (xl == lax.div(t, 4)) & (z == lax.rem(t, 4)) & (k == xl)

    def greet_senders(i, carry):
        @pl.when(jnp.logical_not(home & (lax.div(i, 4) == xh) & (lax.rem(i, 4) == z)))
        def _():
            greet(place(lax.div(i, 4), k, lax.div(part, 2), lax.rem(i, 4), lax.rem(part, 2)))

        return carry

    lax.fori_loop(1, 16, greet_groups, 0)
    lax.fori_loop(0, 8, greet_senders, 0)
    pl.semaphore_wait(barrier, 53 - home.astype(jnp.int32))

    def rows_of(half):
        return pl.ds(0, 128) if half is None else pl.ds(64 * half, 64)

    def gather_start(src, whole, ss, rs, half=None):
        rows, o = rows_of(half), 7 * (half or 0)
        for d in (1, 3, 2):
            send(src.at[rows], whole.at[y, k, rows], ss.at[o + d - 1], rs.at[o + d - 1], place(xh, xl, around(y, d), z, k))
        send(src.at[rows], whole.at[y, k, rows], ss.at[o + 3], rs.at[o + 3], partner)

    def gather_forward(whole, ss, rs, d, half=None):
        rows, o = rows_of(half), 7 * (half or 0)
        block = whole.at[around(y, 4 - d), k, rows]
        got(block, rs.at[o + d - 1])
        send(block, block, ss.at[o + 3 + d], rs.at[o + 3 + d], partner)

    def gather_own(whole, rs, half=None):
        got(whole.at[y, other, rows_of(half)], rs.at[7 * (half or 0) + 3])

    def gather_pair(whole, rs, d, half=None):
        got(whole.at[around(y, 4 - d), other, rows_of(half)], rs.at[7 * (half or 0) + 3 + d])

    def gather_end(whole, ss, half=None):
        for i in range(7):
            sent(whole.at[y, k, rows_of(half)], ss.at[7 * (half or 0) + i])

    def chip_slots(whole, l_, zz):
        return whole.at[pl.ds(8 * l_ + 2 * zz, 2)]

    def z_send(src_of, whole, ss, rs):
        for i in range(1, 8):
            core = lax.rem(k + i, 2)
            send(src_of(core), whole.at[f], ss.at[i], rs.at[i], place(xh, xl, y, around(z, i // 2), core))

    def z_got(whole, rs, dz):
        for dk in range(2):
            if dz + dk > 0:
                got(whole.at[8 * xl + 2 * around(z, 4 - dz) + lax.rem(k + dk, 2)], rs.at[2 * dz + dk])

    def beside(dz):
        x_ = around(x, 1 if dz < 2 else 3)
        return place(lax.div(x_, 2), lax.rem(x_, 2), y, z, k)

    def x_send(whole, ss, rs, dz):
        block = chip_slots(whole, xl, around(z, 4 - dz))
        send(block, block, ss.at[8 + dz], rs.at[8 + dz], beside(dz))

    def x_got(whole, rs, dz):
        got(chip_slots(whole, 1 - xl, around(z, 4 - dz)), rs.at[8 + dz])

    def rows_sent(whole, ss):
        for i in range(1, 8):
            sent(whole.at[f], ss.at[i])
        for dz in range(4):
            sent(chip_slots(whole, xl, around(z, 4 - dz)), ss.at[8 + dz])

    def loop_sent(ref, ss, first, last):
        def one(i, carry):
            sent(ref, ss.at[i])
            return carry

        lax.fori_loop(first, last, one, 0)

    gather_start(r.tok, r.x_all, r.s_x, r.r_x)
    send(r.pos_in, r.pos.at[k], r.s_pos.at[0], r.r_pos.at[0], partner)
    for one in loads[:6]:
        one.wait()
    r.wq_send[...] = r.wq_f[...].astype(bf16)
    z_send(lambda k_: r.wq_send.at[k_], r.wq, r.s_wq, r.r_wq)
    z_send(lambda k_: r.gain_in, r.gain_recv, r.s_gain, r.r_gain)
    r.wq[f] = r.wq_send[k]
    r.gain_recv[f] = r.gain_in[...]

    r.wo_own[...] = r.wo_f[...].astype(bf16)
    r.wd_own[...] = r.wd_f[...].astype(bf16)
    is_source = lax.div(part, 2) == y
    to_core = lax.rem(part, 2)
    for i in range(4):
        piece = 4 * k + i
        here = (xl == k) & (z == i) & (to_core == k)

        @pl.when(is_source & jnp.logical_not(here))
        def _():
            there = place(xh, k, y, i, to_core)
            send(r.wo_own.at[pl.ds(32 * i, 32)], r.wo.at[pl.ds(pl.multiple_of(32 * piece, 32), 32)], r.s_wo.at[i], r.r_wo.at[0], there)
            send(r.wd_own.at[pl.ds(48 * i, 48)], r.wd.at[pl.ds(pl.multiple_of(48 * piece, 16), 48)], r.s_wd.at[i], r.r_wd.at[0], there)

        @pl.when(is_source & here)
        def _():
            r.wo[pl.ds(pl.multiple_of(32 * piece, 32), 32), :] = r.wo_own[32 * i : 32 * i + 32, :]
            r.wd[pl.ds(pl.multiple_of(48 * piece, 16), 48), :] = r.wd_own[48 * i : 48 * i + 48, :]

    def wo_rows(q):
        return r.wo.at[pl.ds(pl.multiple_of(32 * q, 32), 32)]

    def wd_rows(q):
        return r.wd.at[pl.ds(pl.multiple_of(48 * q, 16), 48)]

    r.x_all[y, k] = r.tok[...]
    r.dy_all[y, k] = r.dyt[...]
    r.pos[k] = r.pos_in[...]
    for one in loads[6:]:
        one.wait()
    r.wgu_send[...] = r.wgu_fs[...].astype(bf16)
    r.wgu[f] = r.wgu_send[k]

    got(r.pos.at[other], r.r_pos.at[0])
    steps = lax.broadcasted_iota(jnp.int32, (BLOCK, 1), 0).astype(f32)
    for s in range(2):
        for b in range(16):
            r.posk[s, b * BLOCK : (b + 1) * BLOCK, :] = r.pos[s, 0:1, b * BLOCK : b * BLOCK + 1] + steps
    freq = r.freq[0:1, :]
    sign = r.freq[1:2, :]

    def tables(yy, carry):
        for s in range(2):
            rows = r.posk[s, pl.ds(pl.multiple_of(512 * xh + 128 * yy, 128), 128), :]
            angle = rows * freq
            r.cos_t[yy, s * 128 : (s + 1) * 128, :] = jnp.cos(angle)
            r.sin_t[yy, s * 128 : (s + 1) * 128, :] = jnp.sin(angle) * sign
        return carry

    lax.fori_loop(0, 4, tables, 0)

    for dz in (0, 1, 3, 2):
        z_got(r.gain_recv, r.r_gain, dz)
        x_send(r.gain_recv, r.s_gain, r.r_gain, dz)
        z_got(r.wq, r.r_wq, dz)
        x_send(r.wq, r.s_wq, r.r_wq, dz)
    z_send(lambda k_: r.wgu_send.at[k_], r.wgu, r.s_wgu, r.r_wgu)
    gather_start(r.dyt, r.dy_all, r.s_dy, r.r_dy)
    own_piece = (2 * y + k == part) & (xl == k)

    @pl.when(jnp.logical_not(own_piece))
    def _():
        got(wo_rows(part), r.r_wo.at[0])
        got(wd_rows(part), r.r_wd.at[0])

    for dz in range(1, 4):
        there = place(xh, xl, y, around(z, dz), k)
        send(wo_rows(part), wo_rows(part), r.s_wo2.at[dz], r.r_wo2.at[dz], there)
        send(wd_rows(part), wd_rows(part), r.s_wd2.at[dz], r.r_wd2.at[dz], there)

    def piece_of(l_, dz):
        return 4 * l_ + around(z, 4 - dz)

    for dz in range(4):
        x_got(r.gain_recv, r.r_gain, dz)
    gains = jnp.sum(r.gain_recv[...], axis=0)
    g1 = to_row(gains, 0, 8)
    g2 = to_row(gains, 8, 8)
    gq = gains[16:17, :]
    gk = gains[17:18, :]

    def rotated(u, cos, sin):
        return u * cos + pltpu.roll(u, 64, 1) * sin

    def unrotated(u, cos, sin):
        return u * cos - pltpu.roll(u, 64, 1) * sin

    def inverse_rms(u):
        return lax.rsqrt(jnp.mean(u * u, axis=-1, keepdims=True) + norm_eps)

    kv_partner = place(1 - xh, xl, y, z, k)

    def kv_rows(s, hh, yy):
        return r.kv.at[s, pl.ds(pl.multiple_of(512 * hh + 128 * yy, 128), 128)]

    def project(d):
        yy = around(y, 4 - d)
        rows = r.x_all[yy].reshape(256, D).astype(f32)
        n1 = (rows * inverse_rms(rows) * g1).astype(bf16)
        r.n1_all[yy] = n1
        qkv = dot(n1, r.wq[...].reshape(D, 512))
        r.qkraw[yy] = qkv[:, :384]
        cos, sin = r.cos_t[yy], r.sin_t[yy]
        local = pl.ds(pl.multiple_of(512 * xh + 128 * yy, 128), 128)
        u = qkv[:, 256:384]
        u = rotated(u * inverse_rms(u) * gk, cos, sin).astype(bf16)
        v = qkv[:, 384:].astype(bf16)
        for s in range(2):
            r.kv[s, local, 0:HEAD] = u[s * 128 : (s + 1) * 128]
            r.kv[s, local, HEAD : 2 * HEAD] = v[s * 128 : (s + 1) * 128]
            send(kv_rows(s, xh, yy), kv_rows(s, xh, yy), r.s_kv.at[2 * d + s], r.r_kv.at[2 * d + s], kv_partner)
        for h in range(2):
            u = qkv[:, h * HEAD : (h + 1) * HEAD]
            u = rotated(u * inverse_rms(u) * gq, cos, sin).astype(bf16)
            for s in range(2):
                for half in range(2):
                    first = s * 128 + half * 64
                    r.q_s[s, half, pl.ds(pl.multiple_of(64 * yy, 64), 64), h * HEAD : (h + 1) * HEAD] = u[first : first + 64]

    gather_own(r.x_all, r.r_x)
    for d in (1, 3):
        gather_forward(r.x_all, r.s_x, r.r_x, d)
    for dz in range(4):
        x_got(r.wq, r.r_wq, dz)
    project(0)
    gather_pair(r.x_all, r.r_x, 1)
    project(1)
    gather_forward(r.x_all, r.s_x, r.r_x, 2)
    gather_pair(r.x_all, r.r_x, 3)
    project(3)
    gather_pair(r.x_all, r.r_x, 2)
    project(2)
    gather_end(r.x_all, r.s_x)

    for dz in range(4):
        if dz > 0:
            got(wo_rows(piece_of(xl, dz)), r.r_wo2.at[dz])
        block = wo_rows(piece_of(xl, dz))
        send(block, block, r.s_wo2.at[4 + dz], r.r_wo2.at[4 + dz], beside(dz))
    for dz in range(4):
        z_got(r.wgu, r.r_wgu, dz)
        x_send(r.wgu, r.s_wgu, r.r_wgu, dz)
    for dz in range(4):
        if dz > 0:
            got(wd_rows(piece_of(xl, dz)), r.r_wd2.at[dz])
        block = wd_rows(piece_of(xl, dz))
        send(block, block, r.s_wd2.at[4 + dz], r.r_wd2.at[4 + dz], beside(dz))
    for d in (1, 3, 2):
        gather_forward(r.dy_all, r.s_dy, r.r_dy, d)

    for d in (0, 1, 3, 2):
        for s in range(2):
            got(kv_rows(s, 1 - xh, around(y, 4 - d)), r.r_kv.at[2 * d + s])

    def lanes(half):
        return pl.ds(pl.multiple_of(256 * half, 256), 256)

    def allowed(s, half):
        return r.posk[s] <= r.pos[s, 1:2, lanes(half)]

    def attend(half):
        def one(s, carry):
            ok = allowed(s, half)
            for h in range(2):
                q = r.q_s[s, half, :, h * HEAD : (h + 1) * HEAD]
                scores = jnp.where(ok, dot_nt(r.kv[s, :, 0:HEAD], q) * SCALE, -1e30)
                top = jnp.max(scores, axis=0, keepdims=True)
                p = jnp.exp(scores - top)
                total = jnp.sum(p, axis=0, keepdims=True)
                o = dot_tn(r.kv[s, :, HEAD : 2 * HEAD], p.astype(bf16)) / total
                r.o_t[s, h * HEAD : (h + 1) * HEAD, lanes(half)] = o
                r.ob_t[s, h * HEAD : (h + 1) * HEAD, lanes(half)] = o.astype(bf16)
                r.lse[s, h, :, lanes(half)] = top + jnp.log(total)
            return carry

        lax.fori_loop(0, 2, one, 0)

    def reduce_first(use, p, cc, d, half=None):
        yy, rows, i = around(y, d), rows_of(half), 8 * use + 4 * (half or 0) + d
        send(p.at[yy, other, rows], cc.at[yy, rows], r.s_c.at[i], r.r_c.at[i], partner)

    def both_cores(use, p, cc, d, half):
        yy, rows, i = around(y, d), rows_of(half), 8 * use + 4 * (half or 0) + d
        got(cc.at[yy, rows], r.r_c.at[i])
        return p[yy, k, rows, :].astype(f32) + cc[yy, rows, :].astype(f32)

    def reduce_second(use, p, cc, rr, d, half=None):
        yy, rows, i = around(y, d), rows_of(half), 6 * use + 3 * (half or 0) + d - 1
        p[yy, k, rows, :] = both_cores(use, p, cc, d, half).astype(bf16)
        send(p.at[yy, k, rows], rr.at[d - 1, rows], r.s_r.at[i], r.r_r.at[i], place(xh, xl, yy, z, k))

    def reduce_third(use, p, cc, rr, half=None):
        rows = rows_of(half)
        total = both_cores(use, p, cc, 0, half)
        for d in (1, 3, 2):
            got(rr.at[d - 1, rows], r.r_r.at[6 * use + 3 * (half or 0) + d - 1])
            total = total + rr[d - 1, rows, :].astype(f32)
        return total

    def reduce_end(use, p, half=None):
        rows = rows_of(half)
        for d in range(4):
            sent(p.at[y, other, rows], r.s_c.at[8 * use + 4 * (half or 0) + d])
        for d in range(3):
            sent(p.at[y, k, rows], r.s_r.at[6 * use + 3 * (half or 0) + d])

    def out_partial(half):
        for s in range(2):
            o = r.ob_t[s, :, lanes(half)]
            r.pa[:, s, rows_of(half), :] = dot_tn(o, r.wo[...]).astype(bf16).reshape(4, 64, D)
        for d in (2, 1, 3, 0):
            reduce_first(0, r.pa, r.ca, d, half)

    attend(0)
    for dz in range(4):
        got(wo_rows(piece_of(1 - xl, dz)), r.r_wo2.at[4 + dz])
    out_partial(0)
    attend(1)
    for d in (2, 1, 3):
        reduce_second(0, r.pa, r.ca, r.ra, d, 0)
    out_partial(1)
    for d in (2, 1, 3):
        reduce_second(0, r.pa, r.ca, r.ra, d, 1)
    for half in range(2):
        rows = rows_of(half)
        h1 = r.tok[rows, :].astype(f32) + reduce_third(0, r.pa, r.ca, r.ra, half)
        r.h1[rows, :] = h1
        r.n2_all[y, k, rows, :] = (h1 * inverse_rms(h1) * g2).astype(bf16)
        gather_start(r.n2_all.at[y, k], r.n2_all, r.s_n2, r.r_n2, half)

    gather_own(r.dy_all, r.r_dy)
    for d in (1, 3, 2):
        gather_pair(r.dy_all, r.r_dy, d)
    for dz in range(4):
        x_got(r.wgu, r.r_wgu, dz)
        got(wd_rows(piece_of(1 - xl, dz)), r.r_wd2.at[4 + dz])

    def two_blocks(whole, ds, half):
        blocks = [whole[around(y, d), :, rows_of(half), :].reshape(128, whole.shape[-1]) for d in ds]
        return jnp.concatenate(blocks, axis=0)

    def put_blocks(whole, ds, half, cols, value):
        for i, d in enumerate(ds):
            block = value[128 * i : 128 * (i + 1)].reshape(2, 64, value.shape[-1])
            whole[around(y, d), :, rows_of(half), cols] = block

    def feed(ds, half):
        n2 = two_blocks(r.n2_all, ds, half)
        ab = dot(n2, r.wgu[...].reshape(D, 768))
        a, b = ab[:, :384], ab[:, 384:]
        sig = jax.nn.sigmoid(a)
        silu = a * sig
        put_blocks(r.hid_all, ds, half, slice(None), (silu * b).astype(bf16))
        dhid = dot_nt(two_blocks(r.dy_all, ds, half), r.wd[...])
        da = (dhid * b * sig * (1.0 + a * (1.0 - sig))).astype(bf16)
        db = (dhid * silu).astype(bf16)
        put_blocks(r.dgu_all, ds, half, slice(0, 384), da)
        put_blocks(r.dgu_all, ds, half, slice(384, 768), db)
        dn2 = dot_nt(jnp.concatenate([da, db], axis=1), r.wgu[...].reshape(D, 768))
        put_blocks(r.pb, ds, half, slice(None), dn2.astype(bf16))
        for d in ds:
            reduce_first(1, r.pb, r.cb, d, half)

    for half in range(2):
        gather_own(r.n2_all, r.r_n2, half)
        for d in (1, 3):
            gather_forward(r.n2_all, r.s_n2, r.r_n2, d, half)
        gather_pair(r.n2_all, r.r_n2, 1, half)
        feed((0, 3), half)
        gather_forward(r.n2_all, r.s_n2, r.r_n2, 2, half)
        gather_pair(r.n2_all, r.r_n2, 3, half)
        gather_pair(r.n2_all, r.r_n2, 2, half)
        feed((2, 1), half)
        for d in (3, 2, 1):
            reduce_second(1, r.pb, r.cb, r.rb, d, half)

    def cross(i, sign):
        dx, dz = lax.div(i, 4), lax.rem(i, 4)
        x_, z_ = lax.rem(x + 4 + sign * dx, 4), lax.rem(z + 4 + sign * dz, 4)
        return lax.div(x_, 2), lax.rem(x_, 2), z_

    def cross_send(piece_of, dst, ss, rs):
        def one(i, carry):
            h_, l_, z_ = cross(i, 1)
            send(piece_of(h_, 4 * l_ + z_), dst.at[i], ss.at[i], rs.at[i], place(h_, l_, y, z_, k))
            return carry

        lax.fori_loop(1, 16, one, 0)

    def cross_sum(own, dst, rs):
        def one(i, total):
            got(dst.at[i], rs.at[i])
            return total + dst[i].astype(f32)

        return lax.fori_loop(1, 16, one, own.astype(f32))

    def piece_rows(whole, height):
        def of(h_, p_):
            return whole.at[pl.ds(pl.multiple_of(2 * height * p_ + height * h_, height), height)]

        return of

    def piece_block(whole, height):
        def of(h_, p_):
            return whole.at[pl.ds(pl.multiple_of(height * p_, 16), height), pl.ds(pl.multiple_of(512 * h_, 512), 512)]

        return of

    gqa_piece, gqb_piece, ggu_piece = piece_rows(r.gqa, 64), piece_rows(r.gqb, 64), piece_rows(r.ggu, 64)
    go_piece, gd_piece = piece_block(r.go, 32), piece_block(r.gd, 48)

    def weight_gradient(left, right, out):
        def one(i, carry):
            cols = pl.ds(pl.multiple_of(256 * i, 256), 256)
            out[:, cols] = dot_tn(left(), right(cols)).astype(bf16)
            return carry

        lax.fori_loop(0, out.shape[1] // 256, one, 0)

    r.dg[...] = jnp.zeros((24, 128), f32)

    def middle_back(half):
        rows = rows_of(half)
        dn2 = reduce_third(1, r.pb, r.cb, r.rb, half)
        h1 = r.h1[rows, :]
        r2 = inverse_rms(h1)
        weighted = dn2 * g2
        back = r2 * weighted - h1 * (r2 * r2 * r2) * jnp.mean(weighted * h1, axis=-1, keepdims=True)
        dh1 = r.dyt[rows, :].astype(f32) + back
        r.dh1[rows, :] = dh1
        dg2 = jnp.sum(dn2 * h1 * r2, axis=0, keepdims=True)
        for i in range(8):
            r.dg[8 + i : 9 + i, :] += dg2[:, 128 * i : 128 * (i + 1)]
        r.x_all[y, k, rows, :] = dh1.astype(bf16)
        gather_start(r.x_all.at[y, k], r.x_all, r.s_dob, r.r_dob, half)

    weight_gradient(
        lambda: r.hid_all[...].reshape(D, 384),
        lambda cols: r.dy_all[:, :, :, cols].reshape(D, 256),
        r.gd,
    )
    cross_send(gd_piece, r.rd, r.s_gd, r.r_gd)
    middle_back(0)
    weight_gradient(
        lambda: r.n2_all[...].reshape(D, D),
        lambda cols: r.dgu_all[:, :, :, cols].reshape(D, 256),
        r.ggu,
    )
    middle_back(1)
    cross_send(ggu_piece, r.rgu, r.s_ggu, r.r_ggu)

    def norm_back(value, gain, grad):
        inverse = inverse_rms(value)
        w = grad * gain
        back = inverse * w - value * (inverse * inverse * inverse) * jnp.mean(w * value, axis=-1, keepdims=True)
        return back, jnp.sum(grad * value * inverse, axis=0, keepdims=True)

    def attend_back(half, s):
        rows = rows_of(half)
        do_s = dot_nt(r.wo[...], r.x_all[:, s, rows, :].reshape(256, D)).astype(bf16)
        prod = do_s.astype(f32) * r.o_t[s, :, lanes(half)]
        r.do_t[s, :, lanes(half)] = do_s
        ok = allowed(s, half)
        keys, values = r.kv[s, :, 0:HEAD], r.kv[s, :, HEAD : 2 * HEAD]
        mine = pl.ds(s * 128 + 64 * half, 64)
        cos = r.cos_t[:, mine, :].reshape(256, HEAD)
        sin = r.sin_t[:, mine, :].reshape(256, HEAD)
        for h in range(2):
            head = slice(h * HEAD, (h + 1) * HEAD)
            q = r.q_s[s, half, :, head]
            do = r.do_t[s, head, lanes(half)]
            delta = jnp.sum(prod[head], axis=0, keepdims=True)
            scores = dot_nt(keys, q) * SCALE
            p = jnp.where(ok, jnp.exp(scores - r.lse[s, h, :, lanes(half)]), 0.0)
            ds = (p * (dot(values, do) - delta)).astype(bf16)
            dv = dot_nt(p.astype(bf16), do)
            dk = dot(ds, q) * SCALE
            if half == 0 and h == 0:
                r.dkv[s, :, HEAD : 2 * HEAD] = dv
                r.dkv[s, :, 0:HEAD] = dk
            else:
                r.dkv[s, :, HEAD : 2 * HEAD] += dv
                r.dkv[s, :, 0:HEAD] += dk
            dq = (dot_tn(keys, ds) * SCALE).T
            raw = r.qkraw[:, mine, head].reshape(256, HEAD)
            back, gain_grad = norm_back(raw, gq, unrotated(dq, cos, sin))
            r.dqkv[:, mine, head] = back.astype(bf16).reshape(4, 64, HEAD)
            r.dg[16:17, :] += gain_grad

    def gather_rest(half):
        gather_own(r.x_all, r.r_dob, half)
        for d in (1, 3, 2):
            gather_forward(r.x_all, r.s_dob, r.r_dob, d, half)
        for d in (1, 3, 2):
            gather_pair(r.x_all, r.r_dob, d, half)

    for half in range(2):
        reduce_end(0, r.pa, half)

    def down_partial(i, carry):
        hid = r.hid_all[i].reshape(256, 384)
        r.pa[i] = dot(hid, r.wd[...]).astype(bf16).reshape(2, 128, D)
        return carry

    lax.fori_loop(0, 4, down_partial, 0)
    for d in (2, 1, 3, 0):
        reduce_first(2, r.pa, r.ca, d)
    gather_rest(0)
    for s in range(2):
        attend_back(0, s)
    gather_rest(1)
    for d in (2, 1, 3):
        reduce_second(2, r.pa, r.ca, r.ra, d)
    for s in range(2):
        attend_back(1, s)
        r.dkv_send[s] = r.dkv[s, pl.ds(pl.multiple_of(512 * (1 - xh), 512), 512), :].astype(bf16)
        send(r.dkv_send.at[s], r.dkv_recv.at[s], r.s_dkv.at[s], r.r_dkv.at[s], kv_partner)

    def qkv_gradient(first, out):
        grad = dot_tn(r.n1_all[...].reshape(D, D), r.dqkv[:, :, first : first + 256].reshape(D, 256))
        out[...] = grad.astype(bf16)
        prod = grad * r.wq[:, :, first : first + 256].reshape(D, 256).astype(f32)
        return prod[:, 0:128] + prod[:, 128:256]

    r.wdot[...] = qkv_gradient(0, r.gqa)
    cross_send(gqa_piece, r.rqa, r.s_gqa, r.r_gqa)

    def out_gradient(i, carry):
        cols = pl.ds(pl.multiple_of(256 * i, 256), 256)
        total = jnp.zeros((256, 256), f32)
        for s in range(2):
            for half in range(2):
                rows = r.x_all[:, s, rows_of(half), cols].reshape(256, 256)
                total = total + dot(r.ob_t[s, :, lanes(half)], rows)
        r.go[:, cols] = total.astype(bf16)
        return carry

    lax.fori_loop(0, 4, out_gradient, 0)
    cross_send(go_piece, r.ro, r.s_go, r.r_go)

    def spread_rows(total, hold, final, ss, rs):
        hold[...] = total.astype(bf16)

        def one(i, carry):
            there = place(lax.rem(xh + lax.div(i, 4), 2), xl, lax.rem(y + i, 4), z, xh)

            @pl.when((i > 0) | (k != xh))
            def _():
                send(hold, final.at[t], ss.at[i], rs.at[t], there)

            return carry

        lax.fori_loop(0, 8, one, 0)

        @pl.when(k == xh)
        def _():
            final[t] = hold[...]

    def spread_rows_sent(hold, ss):
        def one(i, carry):
            @pl.when((i > 0) | (k != xh))
            def _():
                sent(hold, ss.at[i])

            return carry

        lax.fori_loop(0, 8, one, 0)

    def spread_rows_got(final, rs):
        def one(i, carry):
            @pl.when((i != t) | (k != xh))
            def _():
                got(final.at[i], rs.at[i])

            return carry

        lax.fori_loop(0, 8, one, 0)

    def spread_block(total, hold, final, height, ss, rs):
        hold[...] = total.astype(bf16)
        rows = pl.ds(pl.multiple_of(height * z, 16), height)
        cols = pl.ds(pl.multiple_of(512 * xh, 512), 512)

        def one(i, carry):
            there = place(lax.rem(xh + lax.div(i, 4), 2), lax.div(t, 4), lax.rem(y + i, 4), lax.rem(t, 4), xl)

            @pl.when((i > 0) | jnp.logical_not(home))
            def _():
                send(hold, final.at[rows, cols], ss.at[i], rs.at[4 * xh + z], there)

            return carry

        lax.fori_loop(0, 8, one, 0)

        @pl.when(home)
        def _():
            final[rows, cols] = hold[...]

    def spread_block_sent(hold, ss):
        def one(i, carry):
            @pl.when((i > 0) | jnp.logical_not(home))
            def _():
                sent(hold, ss.at[i])

            return carry

        lax.fori_loop(0, 8, one, 0)

    def spread_block_got(final, height, rs):
        def one(i, carry):
            @pl.when((i != 4 * xh + z) | jnp.logical_not(home))
            def _():
                rows = pl.ds(pl.multiple_of(height * lax.rem(i, 4), 16), height)
                cols = pl.ds(pl.multiple_of(512 * lax.div(i, 4), 512), 512)
                got(final.at[rows, cols], rs.at[i])

            return carry

        lax.fori_loop(0, 8, one, 0)

    spread_block(cross_sum(gd_piece(xh, part)[...], r.rd, r.r_gd), r.sd, r.fd, 48, r.s_fd, r.r_fd)
    spread_rows(cross_sum(ggu_piece(xh, part)[...], r.rgu, r.r_ggu), r.sgu, r.fgu, r.s_fgu, r.r_fgu)

    for half in range(2):
        reduce_end(1, r.pb, half)
    for s in range(2):
        got(r.dkv_recv.at[s], r.r_dkv.at[s])

    def key_back(yy, carry):
        rows = pl.ds(pl.multiple_of(512 * xh + 128 * yy, 128), 128)
        local = pl.ds(pl.multiple_of(128 * yy, 128), 128)
        grads = [r.dkv[s, rows, :] + r.dkv_recv[s, local, :].astype(f32) for s in range(2)]
        both = jnp.concatenate(grads, axis=0)
        du = unrotated(both[:, 0:HEAD], r.cos_t[yy], r.sin_t[yy])
        back, gain_grad = norm_back(r.qkraw[yy, :, 256:384], gk, du)
        r.dqkv[yy, :, 256:384] = back.astype(bf16)
        r.dqkv[yy, :, 384:512] = both[:, HEAD : 2 * HEAD].astype(bf16)
        r.dg[17:18, :] += gain_grad
        return carry

    lax.fori_loop(0, 4, key_back, 0)
    for d in (2, 1, 3, 0):
        yy = around(y, d)
        dn1 = dot_nt(r.dqkv[yy], r.wq[...].reshape(D, 512))
        r.pb[yy] = dn1.astype(bf16).reshape(2, 128, D)
        reduce_first(3, r.pb, r.cb, d)
    wdot = r.wdot[...] + qkv_gradient(256, r.gqb)
    cross_send(gqb_piece, r.rqb, r.s_gqb, r.r_gqb)
    for d in (2, 1, 3):
        reduce_second(3, r.pb, r.cb, r.rb, d)
    dg1 = jnp.sum(wdot.T, axis=0, keepdims=True) / g1
    for i in range(8):
        r.dg[i : i + 1, :] = dg1[:, 128 * i : 128 * (i + 1)]
    for i in range(1, 8):
        there = place(xh, xl, around(y, i // 2), z, lax.rem(k + i, 2))
        send(r.dg, r.dg_r1.at[i], r.s_dg1.at[i], r.r_dg1.at[i], there)

    spread_rows(cross_sum(gqa_piece(xh, part)[...], r.rqa, r.r_gqa), r.sqa, r.fqa, r.s_fqa, r.r_fqa)
    spread_block(cross_sum(go_piece(xh, part)[...], r.ro, r.r_go), r.so, r.fo, 32, r.s_fo, r.r_fo)
    out_tokens = r.h1[...] + reduce_third(2, r.pa, r.ca, r.ra)
    r.out_tok[...] = out_tokens.astype(bf16)
    total = r.dg[...]
    for i in range(1, 8):
        got(r.dg_r1.at[i], r.r_dg1.at[i])
        total = total + r.dg_r1[i]
    r.dg_s[...] = total
    cross_send(lambda h_, p_: r.dg_s, r.dg_r2, r.s_dg2, r.r_dg2)
    spread_rows(cross_sum(gqb_piece(xh, part)[...], r.rqb, r.r_gqb), r.sqb, r.fqb, r.s_fqb, r.r_fqb)

    dn1 = reduce_third(3, r.pb, r.cb, r.rb)
    rows = r.tok[...].astype(f32)
    back, unused = norm_back(rows, g1, dn1)
    r.dtok[...] = (r.dh1[...] + back).astype(bf16)

    spread_block_got(r.fd, 48, r.r_fd)
    r.g_dn[...] = r.fd[...]
    spread_rows_got(r.fgu, r.r_fgu)
    for i in range(8):
        r.g_gu[:, 384 * i : 384 * (i + 1)] = r.fgu[i, :, 0:384]
        r.g_gu[:, 3072 + 384 * i : 3072 + 384 * (i + 1)] = r.fgu[i, :, 384:768]
    spread_block_got(r.fo, 32, r.r_fo)
    r.g_out[...] = r.fo[...]
    spread_rows_got(r.fqa, r.r_fqa)
    for i in range(8):
        r.g_qkv[:, 256 * i : 256 * (i + 1)] = r.fqa[i]
    r.g_gain[...] = cross_sum(r.dg_s[...], r.dg_r2, r.r_dg2)
    spread_rows_got(r.fqb, r.r_fqb)
    for i in range(8):
        r.g_qkv[:, 2048 + 128 * i : 2048 + 128 * (i + 1)] = r.fqb[i, :, 0:128]
        r.g_qkv[:, 3072 + 128 * i : 3072 + 128 * (i + 1)] = r.fqb[i, :, 128:256]

    gather_end(r.dy_all, r.s_dy)
    for half in range(2):
        gather_end(r.n2_all, r.s_n2, half)
        gather_end(r.x_all, r.s_dob, half)
    sent(r.pos_in, r.s_pos.at[0])
    for whole, ss in ((r.gain_recv, r.s_gain), (r.wq, r.s_wq), (r.wgu, r.s_wgu)):
        rows_sent(whole, ss)
    for i in range(4):
        here = (xl == k) & (z == i) & (to_core == k)

        @pl.when(is_source & jnp.logical_not(here))
        def _():
            sent(r.wo_own.at[pl.ds(32 * i, 32)], r.s_wo.at[i])
            sent(r.wd_own.at[pl.ds(48 * i, 48)], r.s_wd.at[i])

    loop_sent(wo_rows(part), r.s_wo2, 1, 8)
    loop_sent(wd_rows(part), r.s_wd2, 1, 8)
    loop_sent(r.kv.at[0, pl.ds(0, 128)], r.s_kv, 0, 8)
    reduce_end(2, r.pa)
    reduce_end(3, r.pb)
    for s in range(2):
        sent(r.dkv_send.at[s], r.s_dkv.at[s])
    loop_sent(gqa_piece(xh, part), r.s_gqa, 1, 16)
    loop_sent(gqb_piece(xh, part), r.s_gqb, 1, 16)
    loop_sent(ggu_piece(xh, part), r.s_ggu, 1, 16)
    loop_sent(go_piece(xh, part), r.s_go, 1, 16)
    loop_sent(gd_piece(xh, part), r.s_gd, 1, 16)
    spread_rows_sent(r.sqa, r.s_fqa)
    spread_rows_sent(r.sqb, r.s_fqb)
    spread_rows_sent(r.sgu, r.s_fgu)
    spread_block_sent(r.so, r.s_fo)
    spread_block_sent(r.sd, r.s_fd)
    loop_sent(r.dg, r.s_dg1, 1, 8)
    loop_sent(r.dg_s, r.s_dg2, 1, 16)


def layer(*args):
    vmem = pl.BlockSpec(memory_space=pltpu.VMEM)
    hbm = pl.BlockSpec(memory_space=pl.ANY)
    specs = [hbm if far else vmem for far in INPUTS.values()]
    return pl.pallas_call(
        layer_kernel,
        out_shape=[jax.ShapeDtypeStruct(shape, kind) for shape, kind in OUTPUTS.values()],
        in_specs=specs,
        out_specs=[vmem] * len(OUTPUTS),
        scratch_shapes=[pltpu.VMEM(shape, kind) for shape, kind in BUFFERS.values()]
        + [pltpu.SemaphoreType.DMA((count,)) for count in SEMAPHORES.values()],
        compiler_params=pltpu.CompilerParams(
            collective_id=0, has_side_effects=True, vmem_limit_bytes=62 << 20
        ),
        name="layer",
    )(*args)


def adam_update(weight, moment, square, grad, rate, decay):
    moment_new = beta_first * moment + (1.0 - beta_first) * grad
    square_new = beta_second * square + (1.0 - beta_second) * grad * grad
    fix_first = 1.0 - beta_first**STEP
    fix_second = 1.0 - beta_second**STEP
    step = moment_new / fix_first / (jnp.sqrt(square_new / fix_second) + adam_eps)
    return (weight - rate * (step + decay * weight), moment_new, square_new)


def on_device(
    tokens, d_out, block_ids,
    w_qkv, w_out, w_gate_up, w_down, gains,
    moment_qkv, moment_out, moment_gate_up, moment_down, moment_gains,
    square_qkv, square_out, square_gate_up, square_down, square_gains,
):
    f = lax.axis_index("fsdp")
    starts = block_ids[0].astype(f32) * BLOCK
    spots = starts[:, None] + jnp.arange(BLOCK, dtype=f32)[None, :]
    mine = lax.dynamic_slice(spots, (8 * lax.div(lax.axis_index("ctx"), 4), 0), (8, BLOCK))
    mine = mine.reshape(4, 2, BLOCK).transpose(1, 0, 2).reshape(1, 512)
    positions = jnp.concatenate([spots.reshape(1, D), jnp.tile(mine, (7, 2))], axis=0)
    gain_rows = lax.dynamic_update_slice(
        jnp.zeros((24 * 128,), f32), gains.astype(bf16).astype(f32), (f * 144,)
    ).reshape(24, 128)
    half = rope_base ** (-(np.arange(64, dtype=np.float32) * np.float32(2.0 / HEAD)))
    table = np.zeros((8, 128), np.float32)
    table[0] = np.concatenate([half, half])
    table[1] = np.concatenate([-np.ones(64), np.ones(64)])
    out_tok, dtok, g_qkv, g_out, g_gu, g_dn, g_gain = layer(
        tokens[0], d_out[0], positions, gain_rows, jnp.asarray(table), w_qkv, w_out, w_gate_up, w_down
    )
    grad_gains = lax.dynamic_slice(g_gain.reshape(24 * 128), (f * 144,), (144,))
    grads = (g_qkv, g_out, g_gu, g_dn, grad_gains)
    masters = (w_qkv, w_out, w_gate_up, w_down, gains)
    moments = (moment_qkv, moment_out, moment_gate_up, moment_down, moment_gains)
    squares = (square_qkv, square_out, square_gate_up, square_down, square_gains)
    rates = (0.03, 0.3, 0.03, 0.03, 0.5)
    decays = (decay_rate, decay_rate, decay_rate, decay_rate, 0.0)
    updates = [
        adam_update(masters[i], moments[i], squares[i], grads[i].astype(f32), rates[i], decays[i])
        for i in range(5)
    ]
    return (
        out_tok[None],
        dtok[None],
        *(u[0] for u in updates),
        *(u[1] for u in updates),
        *(u[2] for u in updates),
    )


def solution(mesh):
    rows, flat = P("fsdp", None), P("fsdp")
    tokens = P("fsdp", "ctx", None)
    state = (rows, rows, rows, rows, flat)
    return jax.shard_map(
        on_device,
        mesh=mesh,
        in_specs=(tokens, tokens, rows) + state * 3,
        out_specs=(tokens, tokens) + state * 3,
        check_vma=False,
    )
```

```python
import math
import types

import jax
import jax.numpy as jnp
import numpy as np
from jax import lax
from jax.experimental import pallas as pl
from jax.experimental.pallas import tpu as pltpu
from jax.sharding import PartitionSpec as P

D = 1024
HEAD = 128
STEP = 10
BLOCK = 64
norm_eps = 1e-06
rope_base = 1000000.0
beta_first = 0.9
beta_second = 0.95
adam_eps = 1e-08
decay_rate = 0.1
SCALE = 1.0 / math.sqrt(HEAD)

f32 = jnp.float32
bf16 = jnp.bfloat16
MESH = pl.DeviceIdType.MESH

INPUTS = dict(
    tok=False, dyt=False, pos_in=False, gain_in=False, freq=False, wqkv_f=True, wo_f=False, wgu_f=True, wd_f=False
)
OUTPUTS = dict(
    out_tok=((128, D), bf16),
    dtok=((128, D), bf16),
    g_qkv=((64, 4096), bf16),
    g_out=((128, D), bf16),
    g_gu=((64, 6144), bf16),
    g_dn=((192, D), bf16),
    g_gain=((24, 128), f32),
)
BUFFERS = dict(
    x_all=((4, 2, 128, D), bf16),
    dy_all=((4, 2, 128, D), bf16),
    n2_all=((4, 2, 128, D), bf16),
    n1_all=((4, 256, D), bf16),
    wq_f=((2, 64, 512), f32),
    wgu_fs=((2, 64, 768), f32),
    wq_send=((2, 64, 512), bf16),
    wgu_send=((2, 64, 768), bf16),
    wo_own=((128, D), bf16),
    wd_own=((192, D), bf16),
    wq=((16, 64, 512), bf16),
    wgu=((16, 64, 768), bf16),
    wo=((256, D), bf16),
    wd=((384, D), bf16),
    gain_recv=((16, 24, 128), f32),
    pos=((2, 8, D), f32),
    posk=((2, D, 1), f32),
    cos_t=((4, 256, HEAD), f32),
    sin_t=((4, 256, HEAD), f32),
    qkraw=((4, 256, 384), f32),
    q_s=((2, 2, 256, 256), bf16),
    kv=((2, D, 256), bf16),
    o_t=((2, 256, 512), f32),
    ob_t=((2, 256, 512), bf16),
    lse=((2, 2, 1, 512), f32),
    pa=((4, 2, 128, D), bf16),
    pb=((4, 2, 128, D), bf16),
    ca=((4, 128, D), bf16),
    cb=((4, 128, D), bf16),
    ra=((3, 128, D), bf16),
    rb=((3, 128, D), bf16),
    h1=((128, D), f32),
    dh1=((128, D), f32),
    hid_all=((4, 2, 128, 384), bf16),
    dgu_all=((4, 2, 128, 768), bf16),
    do_t=((2, 256, 512), bf16),
    delta=((2, 2, 1, 512), f32),
    dkv=((2, D, 256), f32),
    dkv_send=((2, 512, 256), bf16),
    dkv_recv=((2, 512, 256), bf16),
    dqkv=((4, 256, 512), bf16),
    gqa=((D, 256), bf16),
    gqb=((D, 256), bf16),
    wdot=((D, HEAD), f32),
    ggu=((D, 768), bf16),
    go=((256, D), bf16),
    gd=((384, D), bf16),
    zqa=((3, 2, 128, 256), bf16),
    zqb=((3, 2, 128, 256), bf16),
    zgu=((3, 2, 128, 768), bf16),
    zo=((3, 2, 32, D), bf16),
    zd=((3, 2, 48, D), bf16),
    sqa=((2, 128, 256), bf16),
    sqb=((2, 128, 256), bf16),
    sgu=((2, 128, 768), bf16),
    so=((2, 32, D), bf16),
    sd=((2, 48, D), bf16),
    xqa=((3, 64, 256), bf16),
    xqb=((3, 64, 256), bf16),
    xgu=((3, 64, 768), bf16),
    xo=((3, 32, 512), bf16),
    xd=((3, 48, 512), bf16),
    hqa=((2, 64, 256), bf16),
    hqb=((2, 64, 256), bf16),
    hgu=((2, 64, 768), bf16),
    ho=((32, D), bf16),
    hd=((48, D), bf16),
    fqa=((8, 64, 256), bf16),
    fqb=((8, 64, 256), bf16),
    fgu=((8, 64, 768), bf16),
    fo=((128, D), bf16),
    fd=((192, D), bf16),
    dg=((24, 128), f32),
    dg_r1=((8, 24, 128), f32),
    dg_s=((2, 24, 128), f32),
    dg_r2=((6, 24, 128), f32),
)
SEMAPHORES = dict(
    ld=16,
    s_x=8, r_x=8,
    s_dy=8, r_dy=8,
    s_n2=16, r_n2=16,
    s_dob=16, r_dob=16,
    s_pos=1, r_pos=1,
    s_gain=12, r_gain=12,
    s_wq=12, r_wq=12,
    s_wgu=12, r_wgu=12,
    s_wo=4, r_wo=1, s_wd=4, r_wd=1,
    s_wo2=8, r_wo2=8, s_wd2=8, r_wd2=8,
    s_kv=8, r_kv=8,
    s_c=32, r_c=32,
    s_r=24, r_r=24,
    s_dkv=2, r_dkv=2,
    s_gqa=9, r_gqa=9,
    s_gqb=9, r_gqb=9,
    s_ggu=9, r_ggu=9,
    s_go=9, r_go=9,
    s_gd=9, r_gd=9,
    s_fqa=9, r_fqa=9,
    s_fqb=9, r_fqb=9,
    s_fgu=9, r_fgu=9,
    s_fo=5, r_fo=5,
    s_fd=5, r_fd=5,
    s_dg1=8, r_dg1=8,
    s_dg2=6, r_dg2=6,
)


def dot(a, b):
    return jnp.dot(a, b, preferred_element_type=f32)


def dot_nt(a, b):
    return lax.dot_general(a, b, (((1,), (1,)), ((), ())), preferred_element_type=f32)


def dot_tn(a, b):
    return lax.dot_general(a, b, (((0,), (0,)), ((), ())), preferred_element_type=f32)


def to_row(g, first, count):
    return jnp.concatenate([g[first + i : first + i + 1, :] for i in range(count)], axis=1)


def layer_kernel(*refs):
    names = [*INPUTS, *OUTPUTS, *BUFFERS, *SEMAPHORES]
    r = types.SimpleNamespace(**dict(zip(names, refs, strict=True)))

    c = lax.axis_index("ctx")
    f = lax.axis_index("fsdp")
    xh, y = lax.div(c, 4), lax.rem(c, 4)
    xl, z, k = lax.div(f, 8), lax.rem(lax.div(f, 2), 4), lax.rem(f, 2)
    x = 2 * xh + xl
    part = 4 * xl + z
    t = 2 * y + k
    other = 1 - k

    def place(xh_, xl_, y_, z_, k_):
        return (xh_ * 4 + y_, xl_ * 8 + z_ * 2 + k_)

    partner = place(xh, xl, y, z, other)

    def around(value, step):
        return lax.rem(value + step, 4)

    def copy(src, dst, ss, rs, device):
        return pltpu.make_async_remote_copy(
            src_ref=src, dst_ref=dst, send_sem=ss, recv_sem=rs,
            device_id=device, device_id_type=MESH,
        )

    def send(src, dst, ss, rs, device):
        copy(src, dst, ss, rs, device).start()

    def got(ref, rs):
        copy(ref, ref, rs, rs, partner).wait_recv()

    def sent(ref, ss):
        copy(ref, ref, ss, ss, partner).wait_send()

    loads = []

    def load(src, dst):
        one = pltpu.make_async_copy(src, dst, r.ld.at[len(loads)])
        one.start()
        loads.append(one)

    for i in range(2):
        ti = 2 * y + i
        load(r.wqkv_f.at[:, pl.ds(pl.multiple_of(256 * ti, 256), 256)], r.wq_f.at[i, :, pl.ds(0, 256)])
        load(r.wqkv_f.at[:, pl.ds(pl.multiple_of(2048 + 128 * ti, 128), 128)], r.wq_f.at[i, :, pl.ds(256, 128)])
        load(r.wqkv_f.at[:, pl.ds(pl.multiple_of(3072 + 128 * ti, 128), 128)], r.wq_f.at[i, :, pl.ds(384, 128)])
    for i in range(2):
        ti = 2 * y + i
        load(r.wgu_f.at[:, pl.ds(pl.multiple_of(384 * ti, 128), 384)], r.wgu_fs.at[i, :, pl.ds(0, 384)])
        load(r.wgu_f.at[:, pl.ds(pl.multiple_of(3072 + 384 * ti, 128), 384)], r.wgu_fs.at[i, :, pl.ds(384, 384)])

    barrier = pltpu.get_barrier_semaphore()

    def greet(device):
        pl.semaphore_signal(barrier, inc=1, device_id=device, device_id_type=MESH)

    def greet_plane(i, carry):
        greet(place(xh, lax.rem(xl + lax.div(i, 8), 2), y, around(z, lax.rem(lax.div(i, 2), 4)), lax.rem(k + i, 2)))
        return carry

    home = (xl == lax.div(t, 4)) & (z == lax.rem(t, 4)) & (k == xl)

    def greet_senders(i, carry):
        @pl.when(jnp.logical_not(home & (i == z)))
        def _():
            greet(place(xh, k, lax.div(part, 2), i, lax.rem(part, 2)))

        return carry

    def along_x(d):
        x_ = around(x, d)
        return place(lax.div(x_, 2), lax.rem(x_, 2), y, z, k)

    for i in range(1, 8):
        greet(place(xh, xl, around(y, i // 2), z, lax.rem(k + i, 2)))
    lax.fori_loop(1, 16, greet_plane, 0)
    for d in range(1, 4):
        greet(along_x(d))
    lax.fori_loop(0, 4, greet_senders, 0)

    for one in loads:
        one.wait()
    r.wq_send[...] = r.wq_f[...].astype(bf16)
    r.wgu_send[...] = r.wgu_fs[...].astype(bf16)
    r.wo_own[...] = r.wo_f[...].astype(bf16)
    r.wd_own[...] = r.wd_f[...].astype(bf16)
    r.wq[f] = r.wq_send[k]
    r.wgu[f] = r.wgu_send[k]
    r.gain_recv[f] = r.gain_in[...]
    r.x_all[y, k] = r.tok[...]
    r.dy_all[y, k] = r.dyt[...]
    r.pos[k] = r.pos_in[...]
    r.dg[...] = jnp.zeros((24, 128), f32)
    pl.semaphore_wait(barrier, 29 - home.astype(jnp.int32))

    def rows_of(half):
        return pl.ds(0, 128) if half is None else pl.ds(64 * half, 64)

    def far_part(half, which):
        size = 64 if half is None else 32
        return pl.ds((0 if half is None else 64 * half) + size * which, size)

    def gather_start(src, whole, ss, rs, half=None):
        rows, o = rows_of(half), 8 * (half or 0)
        for d in (1, 3):
            send(src.at[rows], whole.at[y, k, rows], ss.at[o + d - 1], rs.at[o + d - 1], place(xh, xl, around(y, d), z, k))
        send(src.at[rows], whole.at[y, k, rows], ss.at[o + 3], rs.at[o + 3], partner)

    def gather_forward(whole, ss, rs, d, half=None):
        rows, o = rows_of(half), 8 * (half or 0)
        block = whole.at[around(y, 4 - d), k, rows]
        if d == 2:
            for which in range(2):
                got(whole.at[around(y, 2), k, far_part(half, which)], rs.at[o + (1, 7)[which]])
        else:
            got(block, rs.at[o + d - 1])
            which = 0 if d == 1 else 1
            part_of = whole.at[around(y, 4 - d), k, far_part(half, which)]
            i = o + (1, 7)[which]
            send(part_of, part_of, ss.at[i], rs.at[i], place(xh, xl, around(y, d), z, k))
        send(block, block, ss.at[o + 3 + d], rs.at[o + 3 + d], partner)

    def gather_own(whole, rs, half=None):
        got(whole.at[y, other, rows_of(half)], rs.at[8 * (half or 0) + 3])

    def gather_pair(whole, rs, d, half=None):
        got(whole.at[around(y, 4 - d), other, rows_of(half)], rs.at[8 * (half or 0) + 3 + d])

    def gather_end(whole, ss, half=None):
        o = 8 * (half or 0)
        for i in (0, 2, 3, 4, 5, 6):
            sent(whole.at[y, k, rows_of(half)], ss.at[o + i])
        for i in (1, 7):
            sent(whole.at[y, k, far_part(half, 0)], ss.at[o + i])

    def chip_slots(whole, l_, zz):
        return whole.at[pl.ds(8 * l_ + 2 * zz, 2)]

    def z_send(src_of, whole, ss, rs):
        for i in range(1, 8):
            core = lax.rem(k + i, 2)
            send(src_of(core), whole.at[f], ss.at[i], rs.at[i], place(xh, xl, y, around(z, i // 2), core))

    def z_got(whole, rs, dz):
        for dk in range(2):
            if dz + dk > 0:
                got(whole.at[8 * xl + 2 * around(z, 4 - dz) + lax.rem(k + dk, 2)], rs.at[2 * dz + dk])

    def beside(dz):
        return along_x(1 if dz < 2 else 3)

    def x_send(whole, ss, rs, dz):
        block = chip_slots(whole, xl, around(z, 4 - dz))
        send(block, block, ss.at[8 + dz], rs.at[8 + dz], beside(dz))

    def x_got(whole, rs, dz):
        got(chip_slots(whole, 1 - xl, around(z, 4 - dz)), rs.at[8 + dz])

    def rows_sent(whole, ss):
        for i in range(1, 8):
            sent(whole.at[f], ss.at[i])
        for dz in range(4):
            sent(chip_slots(whole, xl, around(z, 4 - dz)), ss.at[8 + dz])

    def loop_sent(ref, ss, first, last):
        def one(i, carry):
            sent(ref, ss.at[i])
            return carry

        lax.fori_loop(first, last, one, 0)

    gather_start(r.tok, r.x_all, r.s_x, r.r_x)
    z_send(lambda k_: r.wq_send.at[k_], r.wq, r.s_wq, r.r_wq)
    send(r.pos_in, r.pos.at[k], r.s_pos.at[0], r.r_pos.at[0], partner)
    z_send(lambda k_: r.gain_in, r.gain_recv, r.s_gain, r.r_gain)

    is_source = lax.div(part, 2) == y
    to_core = lax.rem(part, 2)
    for i in range(4):
        piece = 4 * k + i
        here = (xl == k) & (z == i) & (to_core == k)

        @pl.when(is_source & jnp.logical_not(here))
        def _():
            there = place(xh, k, y, i, to_core)
            send(r.wo_own.at[pl.ds(32 * i, 32)], r.wo.at[pl.ds(pl.multiple_of(32 * piece, 32), 32)], r.s_wo.at[i], r.r_wo.at[0], there)
            send(r.wd_own.at[pl.ds(48 * i, 48)], r.wd.at[pl.ds(pl.multiple_of(48 * piece, 16), 48)], r.s_wd.at[i], r.r_wd.at[0], there)

        @pl.when(is_source & here)
        def _():
            r.wo[pl.ds(pl.multiple_of(32 * piece, 32), 32), :] = r.wo_own[32 * i : 32 * i + 32, :]
            r.wd[pl.ds(pl.multiple_of(48 * piece, 16), 48), :] = r.wd_own[48 * i : 48 * i + 48, :]

    def wo_rows(q):
        return r.wo.at[pl.ds(pl.multiple_of(32 * q, 32), 32)]

    def wd_rows(q):
        return r.wd.at[pl.ds(pl.multiple_of(48 * q, 16), 48)]

    z_got(r.wq, r.r_wq, 0)
    x_send(r.wq, r.s_wq, r.r_wq, 0)

    got(r.pos.at[other], r.r_pos.at[0])
    steps = lax.broadcasted_iota(jnp.int32, (BLOCK, 1), 0).astype(f32)
    for s in range(2):
        for b in range(16):
            r.posk[s, b * BLOCK : (b + 1) * BLOCK, :] = r.pos[s, 0:1, b * BLOCK : b * BLOCK + 1] + steps
    freq = r.freq[0:1, :]
    sign = r.freq[1:2, :]

    def tables(yy, carry):
        for s in range(2):
            rows = r.posk[s, pl.ds(pl.multiple_of(512 * xh + 128 * yy, 128), 128), :]
            angle = rows * freq
            r.cos_t[yy, s * 128 : (s + 1) * 128, :] = jnp.cos(angle)
            r.sin_t[yy, s * 128 : (s + 1) * 128, :] = jnp.sin(angle) * sign
        return carry

    lax.fori_loop(0, 2, tables, 0)

    for dz in (1, 3):
        z_got(r.wq, r.r_wq, dz)
        x_send(r.wq, r.s_wq, r.r_wq, dz)
    for d in (1, 3):
        gather_forward(r.x_all, r.s_x, r.r_x, d)
    lax.fori_loop(2, 4, tables, 0)
    z_got(r.wq, r.r_wq, 2)
    x_send(r.wq, r.s_wq, r.r_wq, 2)
    for dz in range(4):
        z_got(r.gain_recv, r.r_gain, dz)
        x_send(r.gain_recv, r.s_gain, r.r_gain, dz)
    z_send(lambda k_: r.wgu_send.at[k_], r.wgu, r.s_wgu, r.r_wgu)
    gather_start(r.dyt, r.dy_all, r.s_dy, r.r_dy)
    own_piece = (2 * y + k == part) & (xl == k)

    @pl.when(jnp.logical_not(own_piece))
    def _():
        got(wo_rows(part), r.r_wo.at[0])
        got(wd_rows(part), r.r_wd.at[0])

    for dz in range(1, 4):
        there = place(xh, xl, y, around(z, dz), k)
        send(wo_rows(part), wo_rows(part), r.s_wo2.at[dz], r.r_wo2.at[dz], there)
        send(wd_rows(part), wd_rows(part), r.s_wd2.at[dz], r.r_wd2.at[dz], there)

    def piece_of(l_, dz):
        return 4 * l_ + around(z, 4 - dz)

    for dz in range(4):
        x_got(r.gain_recv, r.r_gain, dz)
    gains = jnp.sum(r.gain_recv[...], axis=0)
    g1 = to_row(gains, 0, 8)
    g2 = to_row(gains, 8, 8)
    gq = gains[16:17, :]
    gk = gains[17:18, :]

    def rotated(u, cos, sin):
        return u * cos + pltpu.roll(u, 64, 1) * sin

    def unrotated(u, cos, sin):
        return u * cos - pltpu.roll(u, 64, 1) * sin

    def inverse_rms(u):
        return lax.rsqrt(jnp.mean(u * u, axis=-1, keepdims=True) + norm_eps)

    kv_partner = place(1 - xh, xl, y, z, k)

    def kv_rows(s, hh, yy):
        return r.kv.at[s, pl.ds(pl.multiple_of(512 * hh + 128 * yy, 128), 128)]

    def project(d):
        yy = around(y, 4 - d)
        rows = r.x_all[yy].reshape(256, D).astype(f32)
        n1 = (rows * inverse_rms(rows) * g1).astype(bf16)
        r.n1_all[yy] = n1
        qkv = dot(n1, r.wq[...].reshape(D, 512))
        r.qkraw[yy] = qkv[:, :384]
        cos, sin = r.cos_t[yy], r.sin_t[yy]
        local = pl.ds(pl.multiple_of(512 * xh + 128 * yy, 128), 128)
        u = qkv[:, 256:384]
        u = rotated(u * inverse_rms(u) * gk, cos, sin).astype(bf16)
        v = qkv[:, 384:].astype(bf16)
        for s in range(2):
            r.kv[s, local, 0:HEAD] = u[s * 128 : (s + 1) * 128]
            r.kv[s, local, HEAD : 2 * HEAD] = v[s * 128 : (s + 1) * 128]
            send(kv_rows(s, xh, yy), kv_rows(s, xh, yy), r.s_kv.at[2 * d + s], r.r_kv.at[2 * d + s], kv_partner)
        for h in range(2):
            u = qkv[:, h * HEAD : (h + 1) * HEAD]
            u = rotated(u * inverse_rms(u) * gq, cos, sin).astype(bf16)
            for s in range(2):
                for half in range(2):
                    first = s * 128 + half * 64
                    r.q_s[s, half, pl.ds(pl.multiple_of(64 * yy, 64), 64), h * HEAD : (h + 1) * HEAD] = u[first : first + 64]

    gather_own(r.x_all, r.r_x)
    for dz in range(4):
        x_got(r.wq, r.r_wq, dz)
    project(0)
    gather_pair(r.x_all, r.r_x, 1)
    project(1)
    gather_forward(r.x_all, r.s_x, r.r_x, 2)
    gather_pair(r.x_all, r.r_x, 3)
    project(3)
    gather_pair(r.x_all, r.r_x, 2)
    project(2)
    gather_end(r.x_all, r.s_x)

    for dz in range(4):
        if dz > 0:
            got(wo_rows(piece_of(xl, dz)), r.r_wo2.at[dz])
        block = wo_rows(piece_of(xl, dz))
        send(block, block, r.s_wo2.at[4 + dz], r.r_wo2.at[4 + dz], beside(dz))
    for dz in range(4):
        z_got(r.wgu, r.r_wgu, dz)
        x_send(r.wgu, r.s_wgu, r.r_wgu, dz)
    for dz in range(4):
        if dz > 0:
            got(wd_rows(piece_of(xl, dz)), r.r_wd2.at[dz])
        block = wd_rows(piece_of(xl, dz))
        send(block, block, r.s_wd2.at[4 + dz], r.r_wd2.at[4 + dz], beside(dz))
    for d in (1, 3, 2):
        gather_forward(r.dy_all, r.s_dy, r.r_dy, d)

    for d in (0, 1, 3, 2):
        for s in range(2):
            got(kv_rows(s, 1 - xh, around(y, 4 - d)), r.r_kv.at[2 * d + s])

    def lanes(half):
        return pl.ds(pl.multiple_of(256 * half, 256), 256)

    def allowed(s, half):
        return r.posk[s] <= r.pos[s, 1:2, lanes(half)]

    def attend(half):
        def one(s, carry):
            ok = allowed(s, half)
            for h in range(2):
                q = r.q_s[s, half, :, h * HEAD : (h + 1) * HEAD]
                scores = jnp.where(ok, dot_nt(r.kv[s, :, 0:HEAD], q) * SCALE, -1e30)
                top = jnp.max(scores, axis=0, keepdims=True)
                p = jnp.exp(scores - top)
                total = jnp.sum(p, axis=0, keepdims=True)
                o = dot_tn(r.kv[s, :, HEAD : 2 * HEAD], p.astype(bf16)) / total
                r.o_t[s, h * HEAD : (h + 1) * HEAD, lanes(half)] = o
                r.ob_t[s, h * HEAD : (h + 1) * HEAD, lanes(half)] = o.astype(bf16)
                r.lse[s, h, :, lanes(half)] = top + jnp.log(total)
            return carry

        lax.fori_loop(0, 2, one, 0)

    def reduce_first(use, p, cc, d, half=None):
        yy, rows, i = around(y, d), rows_of(half), 8 * use + 4 * (half or 0) + d
        send(p.at[yy, other, rows], cc.at[yy, rows], r.s_c.at[i], r.r_c.at[i], partner)

    def both_cores(use, p, cc, d, half):
        yy, rows, i = around(y, d), rows_of(half), 8 * use + 4 * (half or 0) + d
        got(cc.at[yy, rows], r.r_c.at[i])
        return p[yy, k, rows, :].astype(f32) + cc[yy, rows, :].astype(f32)

    def reduce_second(use, p, cc, rr, d, half=None):
        yy, rows, i = around(y, d), rows_of(half), 6 * use + 3 * (half or 0) + d - 1
        p[yy, k, rows, :] = both_cores(use, p, cc, d, half).astype(bf16)
        send(p.at[yy, k, rows], rr.at[d - 1, rows], r.s_r.at[i], r.r_r.at[i], place(xh, xl, yy, z, k))

    def reduce_third(use, p, cc, rr, half=None):
        rows = rows_of(half)
        total = both_cores(use, p, cc, 0, half)
        for d in (1, 3, 2):
            got(rr.at[d - 1, rows], r.r_r.at[6 * use + 3 * (half or 0) + d - 1])
            total = total + rr[d - 1, rows, :].astype(f32)
        return total

    def reduce_end(use, p, half=None):
        rows = rows_of(half)
        for d in range(4):
            sent(p.at[y, other, rows], r.s_c.at[8 * use + 4 * (half or 0) + d])
        for d in range(3):
            sent(p.at[y, k, rows], r.s_r.at[6 * use + 3 * (half or 0) + d])

    def out_partial(half):
        for s in range(2):
            o = r.ob_t[s, :, lanes(half)]
            r.pa[:, s, rows_of(half), :] = dot_tn(o, r.wo[...]).astype(bf16).reshape(4, 64, D)
        for d in (2, 1, 3, 0):
            reduce_first(0, r.pa, r.ca, d, half)

    attend(0)
    for dz in range(4):
        got(wo_rows(piece_of(1 - xl, dz)), r.r_wo2.at[4 + dz])
    out_partial(0)
    attend(1)
    for d in (2, 1, 3):
        reduce_second(0, r.pa, r.ca, r.ra, d, 0)
    out_partial(1)
    for d in (2, 1, 3):
        reduce_second(0, r.pa, r.ca, r.ra, d, 1)
    for half in range(2):
        rows = rows_of(half)
        h1 = r.tok[rows, :].astype(f32) + reduce_third(0, r.pa, r.ca, r.ra, half)
        r.h1[rows, :] = h1
        r.n2_all[y, k, rows, :] = (h1 * inverse_rms(h1) * g2).astype(bf16)
        gather_start(r.n2_all.at[y, k], r.n2_all, r.s_n2, r.r_n2, half)

    gather_own(r.dy_all, r.r_dy)
    for d in (1, 3, 2):
        gather_pair(r.dy_all, r.r_dy, d)
    for dz in range(4):
        x_got(r.wgu, r.r_wgu, dz)
        got(wd_rows(piece_of(1 - xl, dz)), r.r_wd2.at[4 + dz])

    def two_blocks(whole, ds, half):
        blocks = [whole[around(y, d), :, rows_of(half), :].reshape(128, whole.shape[-1]) for d in ds]
        return jnp.concatenate(blocks, axis=0)

    def put_blocks(whole, ds, half, cols, value):
        for i, d in enumerate(ds):
            block = value[128 * i : 128 * (i + 1)].reshape(2, 64, value.shape[-1])
            whole[around(y, d), :, rows_of(half), cols] = block

    def feed(ds, half):
        n2 = two_blocks(r.n2_all, ds, half)
        ab = dot(n2, r.wgu[...].reshape(D, 768))
        a, b = ab[:, :384], ab[:, 384:]
        sig = jax.nn.sigmoid(a)
        silu = a * sig
        put_blocks(r.hid_all, ds, half, slice(None), (silu * b).astype(bf16))
        dhid = dot_nt(two_blocks(r.dy_all, ds, half), r.wd[...])
        da = (dhid * b * sig * (1.0 + a * (1.0 - sig))).astype(bf16)
        db = (dhid * silu).astype(bf16)
        put_blocks(r.dgu_all, ds, half, slice(0, 384), da)
        put_blocks(r.dgu_all, ds, half, slice(384, 768), db)
        dn2 = dot_nt(jnp.concatenate([da, db], axis=1), r.wgu[...].reshape(D, 768))
        put_blocks(r.pb, ds, half, slice(None), dn2.astype(bf16))
        for d in ds:
            reduce_first(1, r.pb, r.cb, d, half)

    def near_forward(whole, ss, rs, half):
        for d in (1, 3):
            gather_forward(whole, ss, rs, d, half)

    near_forward(r.n2_all, r.s_n2, r.r_n2, 0)
    for half in range(2):
        gather_own(r.n2_all, r.r_n2, half)
        gather_pair(r.n2_all, r.r_n2, 1, half)
        feed((0, 3), half)
        gather_forward(r.n2_all, r.s_n2, r.r_n2, 2, half)
        if half == 0:
            near_forward(r.n2_all, r.s_n2, r.r_n2, 1)
        gather_pair(r.n2_all, r.r_n2, 3, half)
        gather_pair(r.n2_all, r.r_n2, 2, half)
        feed((2, 1), half)
        for d in (3, 2, 1):
            reduce_second(1, r.pb, r.cb, r.rb, d, half)

    def rows_at(whole, height):
        return lambda l_, z_: whole.at[pl.ds(pl.multiple_of(height * (4 * l_ + z_), 16), height)]

    def cross_z(piece, dst, ss, rs):
        for dz in (1, 3, 2):
            zz = around(z, dz)
            for l_ in range(2):
                i = 2 * (dz - 1) + l_
                send(piece(l_, zz), dst.at[dz - 1, l_], ss.at[i], rs.at[i], place(xh, xl, y, zz, k))

    def row_half(ref, h_):
        return ref.at[pl.ds(pl.multiple_of(64 * h_, 64), 64)]

    def column_half(ref, h_):
        return ref.at[:, pl.ds(pl.multiple_of(512 * h_, 512), 512)]

    def cross_x(piece, zrecv, sums, xrecv, half_of, ss, rs):
        for l_ in range(2):
            total = piece(l_, z)[...].astype(f32)
            for dz in range(1, 4):
                got(zrecv.at[dz - 1, l_], rs.at[2 * (dz - 1) + l_])
                total = total + zrecv[dz - 1, l_].astype(f32)
            sums[l_] = total.astype(bf16)
        for dx in (1, 3, 2):
            x_ = around(x, dx)
            block = half_of(sums.at[lax.rem(x_, 2)], lax.div(x_, 2))
            send(block, xrecv.at[dx - 1], ss.at[5 + dx], rs.at[5 + dx], along_x(dx))

    def cross_total(sums, xrecv, half_of, rs):
        total = half_of(sums.at[xl], xh)[...].astype(f32)
        for dx in (1, 3, 2):
            got(xrecv.at[dx - 1], rs.at[5 + dx])
            total = total + xrecv[dx - 1].astype(f32)
        return total

    def cross_sent(zrecv, xrecv, ss):
        for i in range(6):
            sent(zrecv.at[0, 0], ss.at[i])
        for i in range(3):
            sent(xrecv.at[0], ss.at[6 + i])

    gqa_piece, gqb_piece, ggu_piece = rows_at(r.gqa, 128), rows_at(r.gqb, 128), rows_at(r.ggu, 128)
    go_piece, gd_piece = rows_at(r.go, 32), rows_at(r.gd, 48)

    def weight_gradient(left, right, out):
        def one(i, carry):
            cols = pl.ds(pl.multiple_of(256 * i, 256), 256)
            out[:, cols] = dot_tn(left(), right(cols)).astype(bf16)
            return carry

        lax.fori_loop(0, out.shape[1] // 256, one, 0)

    def middle_back(half):
        rows = rows_of(half)
        dn2 = reduce_third(1, r.pb, r.cb, r.rb, half)
        h1 = r.h1[rows, :]
        r2 = inverse_rms(h1)
        weighted = dn2 * g2
        back = r2 * weighted - h1 * (r2 * r2 * r2) * jnp.mean(weighted * h1, axis=-1, keepdims=True)
        dh1 = r.dyt[rows, :].astype(f32) + back
        r.dh1[rows, :] = dh1
        dg2 = jnp.sum(dn2 * h1 * r2, axis=0, keepdims=True)
        for i in range(8):
            r.dg[8 + i : 9 + i, :] += dg2[:, 128 * i : 128 * (i + 1)]
        r.x_all[y, k, rows, :] = dh1.astype(bf16)
        gather_start(r.x_all.at[y, k], r.x_all, r.s_dob, r.r_dob, half)

    weight_gradient(
        lambda: r.hid_all[...].reshape(D, 384),
        lambda cols: r.dy_all[:, :, :, cols].reshape(D, 256),
        r.gd,
    )
    cross_z(gd_piece, r.zd, r.s_gd, r.r_gd)
    middle_back(0)
    weight_gradient(
        lambda: r.n2_all[...].reshape(D, D),
        lambda cols: r.dgu_all[:, :, :, cols].reshape(D, 256),
        r.ggu,
    )
    middle_back(1)
    cross_z(ggu_piece, r.zgu, r.s_ggu, r.r_ggu)

    def norm_back(value, gain, grad):
        inverse = inverse_rms(value)
        w = grad * gain
        back = inverse * w - value * (inverse * inverse * inverse) * jnp.mean(w * value, axis=-1, keepdims=True)
        return back, jnp.sum(grad * value * inverse, axis=0, keepdims=True)

    def attend_back(half, s):
        rows = rows_of(half)
        do_s = dot_nt(r.wo[...], r.x_all[:, s, rows, :].reshape(256, D)).astype(bf16)
        prod = do_s.astype(f32) * r.o_t[s, :, lanes(half)]
        r.do_t[s, :, lanes(half)] = do_s
        ok = allowed(s, half)
        keys, values = r.kv[s, :, 0:HEAD], r.kv[s, :, HEAD : 2 * HEAD]
        mine = pl.ds(s * 128 + 64 * half, 64)
        cos = r.cos_t[:, mine, :].reshape(256, HEAD)
        sin = r.sin_t[:, mine, :].reshape(256, HEAD)
        for h in range(2):
            head = slice(h * HEAD, (h + 1) * HEAD)
            q = r.q_s[s, half, :, head]
            do = r.do_t[s, head, lanes(half)]
            delta = jnp.sum(prod[head], axis=0, keepdims=True)
            scores = dot_nt(keys, q) * SCALE
            p = jnp.where(ok, jnp.exp(scores - r.lse[s, h, :, lanes(half)]), 0.0)
            ds = (p * (dot(values, do) - delta)).astype(bf16)
            dv = dot_nt(p.astype(bf16), do)
            dk = dot(ds, q) * SCALE
            if half == 0 and h == 0:
                r.dkv[s, :, HEAD : 2 * HEAD] = dv
                r.dkv[s, :, 0:HEAD] = dk
            else:
                r.dkv[s, :, HEAD : 2 * HEAD] += dv
                r.dkv[s, :, 0:HEAD] += dk
            dq = (dot_tn(keys, ds) * SCALE).T
            raw = r.qkraw[:, mine, head].reshape(256, HEAD)
            back, gain_grad = norm_back(raw, gq, unrotated(dq, cos, sin))
            r.dqkv[:, mine, head] = back.astype(bf16).reshape(4, 64, HEAD)
            r.dg[16:17, :] += gain_grad

    def gather_rest(half):
        gather_forward(r.x_all, r.s_dob, r.r_dob, 2, half)
        gather_own(r.x_all, r.r_dob, half)
        for d in (1, 3, 2):
            gather_pair(r.x_all, r.r_dob, d, half)

    for half in range(2):
        reduce_end(0, r.pa, half)

    def down_partial(i, carry):
        hid = r.hid_all[i].reshape(256, 384)
        r.pa[i] = dot(hid, r.wd[...]).astype(bf16).reshape(2, 128, D)
        return carry

    lax.fori_loop(0, 4, down_partial, 0)
    for d in (2, 1, 3, 0):
        reduce_first(2, r.pa, r.ca, d)
    near_forward(r.x_all, r.s_dob, r.r_dob, 0)
    gather_rest(0)
    attend_back(0, 0)
    near_forward(r.x_all, r.s_dob, r.r_dob, 1)
    attend_back(0, 1)
    gather_rest(1)
    for d in (2, 1, 3):
        reduce_second(2, r.pa, r.ca, r.ra, d)
    cross_x(gd_piece, r.zd, r.sd, r.xd, column_half, r.s_gd, r.r_gd)
    for s in range(2):
        attend_back(1, s)
        r.dkv_send[s] = r.dkv[s, pl.ds(pl.multiple_of(512 * (1 - xh), 512), 512), :].astype(bf16)
        send(r.dkv_send.at[s], r.dkv_recv.at[s], r.s_dkv.at[s], r.r_dkv.at[s], kv_partner)

    def qkv_gradient(first, out):
        grad = dot_tn(r.n1_all[...].reshape(D, D), r.dqkv[:, :, first : first + 256].reshape(D, 256))
        out[...] = grad.astype(bf16)
        prod = grad * r.wq[:, :, first : first + 256].reshape(D, 256).astype(f32)
        return prod[:, 0:128] + prod[:, 128:256]

    r.wdot[...] = qkv_gradient(0, r.gqa)
    cross_z(gqa_piece, r.zqa, r.s_gqa, r.r_gqa)

    def out_gradient(i, carry):
        cols = pl.ds(pl.multiple_of(256 * i, 256), 256)
        total = jnp.zeros((256, 256), f32)
        for s in range(2):
            for half in range(2):
                rows = r.x_all[:, s, rows_of(half), cols].reshape(256, 256)
                total = total + dot(r.ob_t[s, :, lanes(half)], rows)
        r.go[:, cols] = total.astype(bf16)
        return carry

    lax.fori_loop(0, 4, out_gradient, 0)
    cross_z(go_piece, r.zo, r.s_go, r.r_go)

    other_half = place(1 - xh, xl, y, z, k)

    def rows_exchange(total, hold, ss, rs):
        hold[xh] = total.astype(bf16)
        send(hold.at[xh], hold.at[xh], ss.at[8], rs.at[8], other_half)

    def rows_spread(hold, final, ss, rs):
        for which in range(2):
            h = xh if which == 0 else 1 - xh
            if which == 1:
                got(hold.at[h], rs.at[8])
            for i in (2, 1, 3):
                send(hold.at[h], final.at[t], ss.at[4 * which + i], rs.at[t], place(xh, xl, around(y, i), z, h))

            @pl.when(k != h)
            def _():
                send(hold.at[h], final.at[t], ss.at[4 * which], rs.at[t], partner)

            @pl.when(k == h)
            def _():
                final[t] = hold[h]

    def rows_spread_sent(hold, ss):
        sent(hold.at[0], ss.at[8])
        for which in range(2):
            h = xh if which == 0 else 1 - xh
            for i in range(1, 4):
                sent(hold.at[0], ss.at[4 * which + i])

            @pl.when(k != h)
            def _():
                sent(hold.at[0], ss.at[4 * which])

    def rows_spread_got(final, rs):
        def one(i, carry):
            @pl.when(i != t)
            def _():
                got(final.at[i], rs.at[i])

            return carry

        lax.fori_loop(0, 8, one, 0)

    def block_exchange(total, hold, ss, rs):
        column_half(hold, xh)[...] = total.astype(bf16)
        send(column_half(hold, xh), column_half(hold, xh), ss.at[4], rs.at[4], other_half)

    def block_spread(hold, final, height, ss, rs):
        got(column_half(hold, 1 - xh), rs.at[4])
        rows = pl.ds(pl.multiple_of(height * z, 16), height)

        def to(i):
            there = place(xh, lax.div(t, 4), around(y, i), lax.rem(t, 4), xl)
            send(hold, final.at[rows], ss.at[i], rs.at[z], there)

        for i in (2, 1, 3):
            to(i)

        @pl.when(jnp.logical_not(home))
        def _():
            to(0)

        @pl.when(home)
        def _():
            final[rows, :] = hold[...]

    def block_spread_sent(hold, ss):
        sent(column_half(hold, 0), ss.at[4])
        for i in range(1, 4):
            sent(hold, ss.at[i])

        @pl.when(jnp.logical_not(home))
        def _():
            sent(hold, ss.at[0])

    def block_spread_got(final, height, rs):
        def one(i, carry):
            @pl.when((i != z) | jnp.logical_not(home))
            def _():
                got(final.at[pl.ds(pl.multiple_of(height * i, 16), height)], rs.at[i])

            return carry

        lax.fori_loop(0, 4, one, 0)

    cross_x(ggu_piece, r.zgu, r.sgu, r.xgu, row_half, r.s_ggu, r.r_ggu)
    block_exchange(cross_total(r.sd, r.xd, column_half, r.r_gd), r.hd, r.s_fd, r.r_fd)
    rows_exchange(cross_total(r.sgu, r.xgu, row_half, r.r_ggu), r.hgu, r.s_fgu, r.r_fgu)
    block_spread(r.hd, r.fd, 48, r.s_fd, r.r_fd)
    rows_spread(r.hgu, r.fgu, r.s_fgu, r.r_fgu)
    cross_x(gqa_piece, r.zqa, r.sqa, r.xqa, row_half, r.s_gqa, r.r_gqa)
    cross_x(go_piece, r.zo, r.so, r.xo, column_half, r.s_go, r.r_go)
    out_tokens = r.h1[...] + reduce_third(2, r.pa, r.ca, r.ra)
    r.out_tok[...] = out_tokens.astype(bf16)

    for half in range(2):
        reduce_end(1, r.pb, half)
    for s in range(2):
        got(r.dkv_recv.at[s], r.r_dkv.at[s])

    def key_back(yy, carry):
        rows = pl.ds(pl.multiple_of(512 * xh + 128 * yy, 128), 128)
        local = pl.ds(pl.multiple_of(128 * yy, 128), 128)
        grads = [r.dkv[s, rows, :] + r.dkv_recv[s, local, :].astype(f32) for s in range(2)]
        both = jnp.concatenate(grads, axis=0)
        du = unrotated(both[:, 0:HEAD], r.cos_t[yy], r.sin_t[yy])
        back, gain_grad = norm_back(r.qkraw[yy, :, 256:384], gk, du)
        r.dqkv[yy, :, 256:384] = back.astype(bf16)
        r.dqkv[yy, :, 384:512] = both[:, HEAD : 2 * HEAD].astype(bf16)
        r.dg[17:18, :] += gain_grad
        return carry

    lax.fori_loop(0, 4, key_back, 0)
    for d in (2, 1, 3, 0):
        yy = around(y, d)
        dn1 = dot_nt(r.dqkv[yy], r.wq[...].reshape(D, 512))
        r.pb[yy] = dn1.astype(bf16).reshape(2, 128, D)
        reduce_first(3, r.pb, r.cb, d)
    wdot = r.wdot[...] + qkv_gradient(256, r.gqb)
    cross_z(gqb_piece, r.zqb, r.s_gqb, r.r_gqb)
    for d in (2, 1, 3):
        reduce_second(3, r.pb, r.cb, r.rb, d)
    dg1 = jnp.sum(wdot.T, axis=0, keepdims=True) / g1
    for i in range(8):
        r.dg[i : i + 1, :] = dg1[:, 128 * i : 128 * (i + 1)]
    for i in range(1, 8):
        there = place(xh, xl, around(y, i // 2), z, lax.rem(k + i, 2))
        send(r.dg, r.dg_r1.at[i], r.s_dg1.at[i], r.r_dg1.at[i], there)

    rows_exchange(cross_total(r.sqa, r.xqa, row_half, r.r_gqa), r.hqa, r.s_fqa, r.r_fqa)
    block_exchange(cross_total(r.so, r.xo, column_half, r.r_go), r.ho, r.s_fo, r.r_fo)
    total = r.dg[...]
    for i in range(1, 8):
        got(r.dg_r1.at[i], r.r_dg1.at[i])
        total = total + r.dg_r1[i]
    r.dg_s[0] = total
    for dz in range(1, 4):
        send(r.dg_s.at[0], r.dg_r2.at[dz - 1], r.s_dg2.at[dz - 1], r.r_dg2.at[dz - 1], place(xh, xl, y, around(z, dz), k))
    rows_spread(r.hqa, r.fqa, r.s_fqa, r.r_fqa)
    block_spread(r.ho, r.fo, 32, r.s_fo, r.r_fo)
    cross_x(gqb_piece, r.zqb, r.sqb, r.xqb, row_half, r.s_gqb, r.r_gqb)
    for dz in range(1, 4):
        got(r.dg_r2.at[dz - 1], r.r_dg2.at[dz - 1])
        total = total + r.dg_r2[dz - 1]
    r.dg_s[1] = total
    for dx in range(1, 4):
        send(r.dg_s.at[1], r.dg_r2.at[2 + dx], r.s_dg2.at[2 + dx], r.r_dg2.at[2 + dx], along_x(dx))
    rows_exchange(cross_total(r.sqb, r.xqb, row_half, r.r_gqb), r.hqb, r.s_fqb, r.r_fqb)

    dn1 = reduce_third(3, r.pb, r.cb, r.rb)
    rows = r.tok[...].astype(f32)
    back, unused = norm_back(rows, g1, dn1)
    r.dtok[...] = (r.dh1[...] + back).astype(bf16)
    rows_spread(r.hqb, r.fqb, r.s_fqb, r.r_fqb)

    block_spread_got(r.fd, 48, r.r_fd)
    r.g_dn[...] = r.fd[...]
    rows_spread_got(r.fgu, r.r_fgu)
    for i in range(8):
        r.g_gu[:, 384 * i : 384 * (i + 1)] = r.fgu[i, :, 0:384]
        r.g_gu[:, 3072 + 384 * i : 3072 + 384 * (i + 1)] = r.fgu[i, :, 384:768]
    block_spread_got(r.fo, 32, r.r_fo)
    r.g_out[...] = r.fo[...]
    rows_spread_got(r.fqa, r.r_fqa)
    for i in range(8):
        r.g_qkv[:, 256 * i : 256 * (i + 1)] = r.fqa[i]
    for dx in range(1, 4):
        got(r.dg_r2.at[2 + dx], r.r_dg2.at[2 + dx])
        total = total + r.dg_r2[2 + dx]
    r.g_gain[...] = total
    rows_spread_got(r.fqb, r.r_fqb)
    for i in range(8):
        r.g_qkv[:, 2048 + 128 * i : 2048 + 128 * (i + 1)] = r.fqb[i, :, 0:128]
        r.g_qkv[:, 3072 + 128 * i : 3072 + 128 * (i + 1)] = r.fqb[i, :, 128:256]

    gather_end(r.dy_all, r.s_dy)
    for half in range(2):
        gather_end(r.n2_all, r.s_n2, half)
        gather_end(r.x_all, r.s_dob, half)
    sent(r.pos_in, r.s_pos.at[0])
    for whole, ss in ((r.gain_recv, r.s_gain), (r.wq, r.s_wq), (r.wgu, r.s_wgu)):
        rows_sent(whole, ss)
    for i in range(4):
        here = (xl == k) & (z == i) & (to_core == k)

        @pl.when(is_source & jnp.logical_not(here))
        def _():
            sent(r.wo_own.at[pl.ds(32 * i, 32)], r.s_wo.at[i])
            sent(r.wd_own.at[pl.ds(48 * i, 48)], r.s_wd.at[i])

    loop_sent(wo_rows(part), r.s_wo2, 1, 8)
    loop_sent(wd_rows(part), r.s_wd2, 1, 8)
    loop_sent(r.kv.at[0, pl.ds(0, 128)], r.s_kv, 0, 8)
    reduce_end(2, r.pa)
    reduce_end(3, r.pb)
    for s in range(2):
        sent(r.dkv_send.at[s], r.s_dkv.at[s])
    cross_sent(r.zqa, r.xqa, r.s_gqa)
    cross_sent(r.zqb, r.xqb, r.s_gqb)
    cross_sent(r.zgu, r.xgu, r.s_ggu)
    cross_sent(r.zo, r.xo, r.s_go)
    cross_sent(r.zd, r.xd, r.s_gd)
    for hold, ss in ((r.hqa, r.s_fqa), (r.hqb, r.s_fqb), (r.hgu, r.s_fgu)):
        rows_spread_sent(hold, ss)
    block_spread_sent(r.ho, r.s_fo)
    block_spread_sent(r.hd, r.s_fd)
    loop_sent(r.dg, r.s_dg1, 1, 8)
    loop_sent(r.dg_s.at[0], r.s_dg2, 0, 6)


def layer(*args):
    vmem = pl.BlockSpec(memory_space=pltpu.VMEM)
    hbm = pl.BlockSpec(memory_space=pl.ANY)
    specs = [hbm if far else vmem for far in INPUTS.values()]
    return pl.pallas_call(
        layer_kernel,
        out_shape=[jax.ShapeDtypeStruct(shape, kind) for shape, kind in OUTPUTS.values()],
        in_specs=specs,
        out_specs=[vmem] * len(OUTPUTS),
        scratch_shapes=[pltpu.VMEM(shape, kind) for shape, kind in BUFFERS.values()]
        + [pltpu.SemaphoreType.DMA((count,)) for count in SEMAPHORES.values()],
        compiler_params=pltpu.CompilerParams(
            collective_id=0, has_side_effects=True, vmem_limit_bytes=62 << 20
        ),
        name="layer",
    )(*args)


def adam_update(weight, moment, square, grad, rate, decay):
    moment_new = beta_first * moment + (1.0 - beta_first) * grad
    square_new = beta_second * square + (1.0 - beta_second) * grad * grad
    fix_first = 1.0 - beta_first**STEP
    fix_second = 1.0 - beta_second**STEP
    step = moment_new / fix_first / (jnp.sqrt(square_new / fix_second) + adam_eps)
    return (weight - rate * (step + decay * weight), moment_new, square_new)


def on_device(
    tokens, d_out, block_ids,
    w_qkv, w_out, w_gate_up, w_down, gains,
    moment_qkv, moment_out, moment_gate_up, moment_down, moment_gains,
    square_qkv, square_out, square_gate_up, square_down, square_gains,
):
    f = lax.axis_index("fsdp")
    starts = block_ids[0].astype(f32) * BLOCK
    spots = starts[:, None] + jnp.arange(BLOCK, dtype=f32)[None, :]
    mine = lax.dynamic_slice(spots, (8 * lax.div(lax.axis_index("ctx"), 4), 0), (8, BLOCK))
    mine = mine.reshape(4, 2, BLOCK).transpose(1, 0, 2).reshape(1, 512)
    positions = jnp.concatenate([spots.reshape(1, D), jnp.tile(mine, (7, 2))], axis=0)
    gain_rows = lax.dynamic_update_slice(
        jnp.zeros((24 * 128,), f32), gains.astype(bf16).astype(f32), (f * 144,)
    ).reshape(24, 128)
    half = rope_base ** (-(np.arange(64, dtype=np.float32) * np.float32(2.0 / HEAD)))
    table = np.zeros((8, 128), np.float32)
    table[0] = np.concatenate([half, half])
    table[1] = np.concatenate([-np.ones(64), np.ones(64)])
    out_tok, dtok, g_qkv, g_out, g_gu, g_dn, g_gain = layer(
        tokens[0], d_out[0], positions, gain_rows, jnp.asarray(table), w_qkv, w_out, w_gate_up, w_down
    )
    grad_gains = lax.dynamic_slice(g_gain.reshape(24 * 128), (f * 144,), (144,))
    grads = (g_qkv, g_out, g_gu, g_dn, grad_gains)
    masters = (w_qkv, w_out, w_gate_up, w_down, gains)
    moments = (moment_qkv, moment_out, moment_gate_up, moment_down, moment_gains)
    squares = (square_qkv, square_out, square_gate_up, square_down, square_gains)
    rates = (0.03, 0.3, 0.03, 0.03, 0.5)
    decays = (decay_rate, decay_rate, decay_rate, decay_rate, 0.0)
    updates = [
        adam_update(masters[i], moments[i], squares[i], grads[i].astype(f32), rates[i], decays[i])
        for i in range(5)
    ]
    return (
        out_tok[None],
        dtok[None],
        *(u[0] for u in updates),
        *(u[1] for u in updates),
        *(u[2] for u in updates),
    )


def solution(mesh):
    rows, flat = P("fsdp", None), P("fsdp")
    tokens = P("fsdp", "ctx", None)
    state = (rows, rows, rows, rows, flat)
    return jax.shard_map(
        on_device,
        mesh=mesh,
        in_specs=(tokens, tokens, rows) + state * 3,
        out_specs=(tokens, tokens) + state * 3,
        check_vma=False,
    )
```

```python
import math
import types

import jax
import jax.numpy as jnp
import numpy as np
from jax import lax
from jax.experimental import pallas as pl
from jax.experimental.pallas import tpu as pltpu
from jax.sharding import PartitionSpec as P

D = 1024
HEAD = 128
STEP = 10
BLOCK = 64
norm_eps = 1e-06
rope_base = 1000000.0
beta_first = 0.9
beta_second = 0.95
adam_eps = 1e-08
decay_rate = 0.1
SCALE = 1.0 / math.sqrt(HEAD)

f32 = jnp.float32
bf16 = jnp.bfloat16
MESH = pl.DeviceIdType.MESH

INPUTS = dict(
    tok=False, dyt=False, pos_in=False, gain_in=False, freq=False, wqkv_f=True, wo_f=False, wgu_f=True, wd_f=False
)
OUTPUTS = dict(
    out_tok=((128, D), bf16),
    dtok=((128, D), bf16),
    g_qkv=((64, 4096), bf16),
    g_out=((128, D), bf16),
    g_gu=((64, 6144), bf16),
    g_dn=((192, D), bf16),
    g_gain=((24, 128), f32),
)
BUFFERS = dict(
    x_all=((4, 2, 128, D), bf16),
    dy_all=((4, 2, 128, D), bf16),
    n2_all=((4, 2, 128, D), bf16),
    n1_all=((4, 256, D), bf16),
    wq_f=((2, 64, 512), f32),
    wgu_fs=((2, 64, 768), f32),
    wqq_send=((2, 64, 256), bf16),
    wkv_send=((2, 64, 256), bf16),
    wgu_send=((2, 64, 768), bf16),
    wo_own=((128, D), bf16),
    wd_own=((192, D), bf16),
    wqq=((16, 64, 256), bf16),
    wkv=((16, 64, 256), bf16),
    wgu=((16, 64, 768), bf16),
    wo=((256, D), bf16),
    wd=((384, D), bf16),
    gain_recv=((16, 24, 128), f32),
    pos=((2, 8, D), f32),
    posk=((2, D, 1), f32),
    cos_t=((4, 256, HEAD), f32),
    sin_t=((4, 256, HEAD), f32),
    qkraw=((4, 256, 384), f32),
    q_s=((2, 2, 256, 256), bf16),
    kv=((2, D, 256), bf16),
    o_t=((2, 256, 512), f32),
    ob_t=((2, 256, 512), bf16),
    lse=((2, 2, 1, 512), f32),
    pa=((4, 2, 128, D), bf16),
    pb=((4, 2, 128, D), bf16),
    ca=((4, 128, D), bf16),
    cb=((4, 128, D), bf16),
    ra=((3, 128, D), bf16),
    rb=((3, 128, D), bf16),
    h1=((128, D), f32),
    dh1=((128, D), f32),
    hid_all=((4, 2, 128, 384), bf16),
    dgu_all=((4, 2, 128, 768), bf16),
    do_t=((2, 256, 512), bf16),
    delta=((2, 2, 1, 512), f32),
    dkv=((2, D, 256), f32),
    dkv_send=((2, 512, 256), bf16),
    dkv_recv=((2, 512, 256), bf16),
    dqkv=((4, 256, 512), bf16),
    gqa=((D, 256), bf16),
    gqb=((D, 256), bf16),
    wdot=((D, HEAD), f32),
    ggu=((D, 768), bf16),
    go=((256, D), bf16),
    gd=((384, D), bf16),
    zqa=((3, 2, 128, 256), bf16),
    zgu=((3, 2, 128, 768), bf16),
    zo=((3, 2, 32, D), bf16),
    zd=((3, 48, 512), bf16),
    sqa=((2, 128, 256), bf16),
    sgu=((2, 128, 768), bf16),
    so=((2, 32, D), bf16),
    sd=((192, 512), bf16),
    xqa=((3, 64, 256), bf16),
    rqb=((16, 64, 256), bf16),
    xgu=((3, 64, 768), bf16),
    xo=((3, 32, 512), bf16),
    xd=((3, 192, 512), bf16),
    hqa=((2, 64, 256), bf16),
    hqb=((64, 256), bf16),
    hgu=((2, 64, 768), bf16),
    ho=((32, D), bf16),
    hd=((48, D), bf16),
    fqa=((8, 64, 256), bf16),
    fqb=((8, 64, 256), bf16),
    fgu=((8, 64, 768), bf16),
    fo=((128, D), bf16),
    fd=((192, D), bf16),
    dg=((24, 128), f32),
    dg_r1=((8, 24, 128), f32),
    dg_s=((2, 24, 128), f32),
    dg_r2=((6, 24, 128), f32),
)
SEMAPHORES = dict(
    ld=16,
    s_x=8, r_x=8,
    s_dy=8, r_dy=8,
    s_n2=16, r_n2=16,
    s_dob=16, r_dob=16,
    s_pos=1, r_pos=1,
    s_gain=12, r_gain=12,
    s_wqq=12, r_wqq=12,
    s_wkv=12, r_wkv=12,
    s_wgu=12, r_wgu=12,
    s_wo=4, r_wo=1, s_wd=4, r_wd=1,
    s_wo2=8, r_wo2=8, s_wd2=8, r_wd2=8,
    s_kv=8, r_kv=8,
    s_c=32, r_c=32,
    s_r=48, r_r=48,
    s_dkv=2, r_dkv=2,
    s_gqa=9, r_gqa=9,
    s_gqb=16, r_gqb=16,
    s_ggu=9, r_ggu=9,
    s_go=9, r_go=9,
    s_gd=6, r_gd=6,
    s_fqa=9, r_fqa=9,
    s_fqb=8, r_fqb=8,
    s_fgu=9, r_fgu=9,
    s_fo=5, r_fo=5,
    s_fd=5, r_fd=5,
    s_dg1=8, r_dg1=8,
    s_dg2=6, r_dg2=6,
)


def dot(a, b):
    return jnp.dot(a, b, preferred_element_type=f32)


def dot_nt(a, b):
    return lax.dot_general(a, b, (((1,), (1,)), ((), ())), preferred_element_type=f32)


def dot_tn(a, b):
    return lax.dot_general(a, b, (((0,), (0,)), ((), ())), preferred_element_type=f32)


def to_row(g, first, count):
    return jnp.concatenate([g[first + i : first + i + 1, :] for i in range(count)], axis=1)


def layer_kernel(*refs):
    names = [*INPUTS, *OUTPUTS, *BUFFERS, *SEMAPHORES]
    r = types.SimpleNamespace(**dict(zip(names, refs, strict=True)))

    c = lax.axis_index("ctx")
    f = lax.axis_index("fsdp")
    xh, y = lax.div(c, 4), lax.rem(c, 4)
    xl, z, k = lax.div(f, 8), lax.rem(lax.div(f, 2), 4), lax.rem(f, 2)
    x = 2 * xh + xl
    part = 4 * xl + z
    t = 2 * y + k
    other = 1 - k

    def place(xh_, xl_, y_, z_, k_):
        return (xh_ * 4 + y_, xl_ * 8 + z_ * 2 + k_)

    partner = place(xh, xl, y, z, other)

    def around(value, step):
        return lax.rem(value + step, 4)

    def copy(src, dst, ss, rs, device):
        return pltpu.make_async_remote_copy(
            src_ref=src, dst_ref=dst, send_sem=ss, recv_sem=rs,
            device_id=device, device_id_type=MESH,
        )

    def send(src, dst, ss, rs, device):
        copy(src, dst, ss, rs, device).start()

    def got(ref, rs):
        copy(ref, ref, rs, rs, partner).wait_recv()

    def sent(ref, ss):
        copy(ref, ref, ss, ss, partner).wait_send()

    loads = []

    def load(src, dst):
        one = pltpu.make_async_copy(src, dst, r.ld.at[len(loads)])
        one.start()
        loads.append(one)

    for i in range(2):
        ti = 2 * y + i
        load(r.wqkv_f.at[:, pl.ds(pl.multiple_of(256 * ti, 256), 256)], r.wq_f.at[i, :, pl.ds(0, 256)])
        load(r.wqkv_f.at[:, pl.ds(pl.multiple_of(2048 + 128 * ti, 128), 128)], r.wq_f.at[i, :, pl.ds(256, 128)])
        load(r.wqkv_f.at[:, pl.ds(pl.multiple_of(3072 + 128 * ti, 128), 128)], r.wq_f.at[i, :, pl.ds(384, 128)])
    for i in range(2):
        ti = 2 * y + i
        load(r.wgu_f.at[:, pl.ds(pl.multiple_of(384 * ti, 128), 384)], r.wgu_fs.at[i, :, pl.ds(0, 384)])
        load(r.wgu_f.at[:, pl.ds(pl.multiple_of(3072 + 384 * ti, 128), 384)], r.wgu_fs.at[i, :, pl.ds(384, 384)])

    barrier = pltpu.get_barrier_semaphore()

    def greet(device):
        pl.semaphore_signal(barrier, inc=1, device_id=device, device_id_type=MESH)

    def greet_groups(i, carry):
        a, b, core = lax.div(i, 8), lax.rem(lax.div(i, 2), 4), lax.rem(k + i, 2)
        greet(place(lax.rem(xh + a, 2), xl, around(y, b), z, core))
        greet(place(xh, lax.rem(xl + a, 2), y, around(z, b), core))
        x_ = around(x, lax.div(i, 4))
        greet(place(lax.div(x_, 2), lax.rem(x_, 2), y, around(z, lax.rem(i, 4)), k))
        return carry

    home = (xl == lax.div(t, 4)) & (z == lax.rem(t, 4)) & (k == xl)

    def greet_senders(i, carry):
        @pl.when(jnp.logical_not(home & (i == z)))
        def _():
            greet(place(xh, k, lax.div(part, 2), i, lax.rem(part, 2)))

        return carry

    def along_x(d):
        x_ = around(x, d)
        return place(lax.div(x_, 2), lax.rem(x_, 2), y, z, k)

    lax.fori_loop(1, 16, greet_groups, 0)
    lax.fori_loop(0, 4, greet_senders, 0)

    for one in loads:
        one.wait()
    r.wqq_send[...] = r.wq_f[:, :, 0:256].astype(bf16)
    r.wkv_send[...] = r.wq_f[:, :, 256:512].astype(bf16)
    r.wgu_send[...] = r.wgu_fs[...].astype(bf16)
    r.wo_own[...] = r.wo_f[...].astype(bf16)
    r.wd_own[...] = r.wd_f[...].astype(bf16)
    r.wqq[f] = r.wqq_send[k]
    r.wkv[f] = r.wkv_send[k]
    r.wgu[f] = r.wgu_send[k]
    r.gain_recv[f] = r.gain_in[...]
    r.x_all[y, k] = r.tok[...]
    r.dy_all[y, k] = r.dyt[...]
    r.pos[k] = r.pos_in[...]
    r.dg[...] = jnp.zeros((24, 128), f32)
    pl.semaphore_wait(barrier, 49 - home.astype(jnp.int32))

    def rows_of(half):
        return pl.ds(0, 128) if half is None else pl.ds(64 * half, 64)

    def far_part(half, which):
        size = 64 if half is None else 32
        return pl.ds((0 if half is None else 64 * half) + size * which, size)

    def gather_start(src, whole, ss, rs, half=None):
        rows, o = rows_of(half), 8 * (half or 0)
        for d in (1, 3):
            send(src.at[rows], whole.at[y, k, rows], ss.at[o + d - 1], rs.at[o + d - 1], place(xh, xl, around(y, d), z, k))
        send(src.at[rows], whole.at[y, k, rows], ss.at[o + 3], rs.at[o + 3], partner)

    def gather_forward(whole, ss, rs, d, half=None):
        rows, o = rows_of(half), 8 * (half or 0)
        block = whole.at[around(y, 4 - d), k, rows]
        if d == 2:
            for which in range(2):
                got(whole.at[around(y, 2), k, far_part(half, which)], rs.at[o + (1, 7)[which]])
        else:
            got(block, rs.at[o + d - 1])
            which = 0 if d == 1 else 1
            part_of = whole.at[around(y, 4 - d), k, far_part(half, which)]
            i = o + (1, 7)[which]
            send(part_of, part_of, ss.at[i], rs.at[i], place(xh, xl, around(y, d), z, k))
        send(block, block, ss.at[o + 3 + d], rs.at[o + 3 + d], partner)

    def gather_own(whole, rs, half=None):
        got(whole.at[y, other, rows_of(half)], rs.at[8 * (half or 0) + 3])

    def gather_pair(whole, rs, d, half=None):
        got(whole.at[around(y, 4 - d), other, rows_of(half)], rs.at[8 * (half or 0) + 3 + d])

    def gather_end(whole, ss, half=None):
        o = 8 * (half or 0)
        for i in (0, 2, 3, 4, 5, 6):
            sent(whole.at[y, k, rows_of(half)], ss.at[o + i])
        for i in (1, 7):
            sent(whole.at[y, k, far_part(half, 0)], ss.at[o + i])

    def chip_slots(whole, l_, zz):
        return whole.at[pl.ds(8 * l_ + 2 * zz, 2)]

    def z_send(src_of, whole, ss, rs):
        for i in range(1, 8):
            core = lax.rem(k + i, 2)
            send(src_of(core), whole.at[f], ss.at[i], rs.at[i], place(xh, xl, y, around(z, i // 2), core))

    def z_got(whole, rs, dz):
        for dk in range(2):
            if dz + dk > 0:
                got(whole.at[8 * xl + 2 * around(z, 4 - dz) + lax.rem(k + dk, 2)], rs.at[2 * dz + dk])

    def beside(dz):
        return along_x(1 if dz < 2 else 3)

    def x_send(whole, ss, rs, dz):
        block = chip_slots(whole, xl, around(z, 4 - dz))
        send(block, block, ss.at[8 + dz], rs.at[8 + dz], beside(dz))

    def x_got(whole, rs, dz):
        got(chip_slots(whole, 1 - xl, around(z, 4 - dz)), rs.at[8 + dz])

    def rows_sent(whole, ss):
        for i in range(1, 8):
            sent(whole.at[f], ss.at[i])
        for dz in range(4):
            sent(chip_slots(whole, xl, around(z, 4 - dz)), ss.at[8 + dz])

    def loop_sent(ref, ss, first, last):
        def one(i, carry):
            sent(ref, ss.at[i])
            return carry

        lax.fori_loop(first, last, one, 0)

    gather_start(r.tok, r.x_all, r.s_x, r.r_x)
    z_send(lambda k_: r.gain_in, r.gain_recv, r.s_gain, r.r_gain)
    z_send(lambda k_: r.wkv_send.at[k_], r.wkv, r.s_wkv, r.r_wkv)
    send(r.pos_in, r.pos.at[k], r.s_pos.at[0], r.r_pos.at[0], partner)
    z_send(lambda k_: r.wqq_send.at[k_], r.wqq, r.s_wqq, r.r_wqq)

    is_source = lax.div(part, 2) == y
    to_core = lax.rem(part, 2)
    for i in range(4):
        piece = 4 * k + i
        here = (xl == k) & (z == i) & (to_core == k)

        @pl.when(is_source & jnp.logical_not(here))
        def _():
            there = place(xh, k, y, i, to_core)
            send(r.wo_own.at[pl.ds(32 * i, 32)], r.wo.at[pl.ds(pl.multiple_of(32 * piece, 32), 32)], r.s_wo.at[i], r.r_wo.at[0], there)
            send(r.wd_own.at[pl.ds(48 * i, 48)], r.wd.at[pl.ds(pl.multiple_of(48 * piece, 16), 48)], r.s_wd.at[i], r.r_wd.at[0], there)

        @pl.when(is_source & here)
        def _():
            r.wo[pl.ds(pl.multiple_of(32 * piece, 32), 32), :] = r.wo_own[32 * i : 32 * i + 32, :]
            r.wd[pl.ds(pl.multiple_of(48 * piece, 16), 48), :] = r.wd_own[48 * i : 48 * i + 48, :]

    def wo_rows(q):
        return r.wo.at[pl.ds(pl.multiple_of(32 * q, 32), 32)]

    def wd_rows(q):
        return r.wd.at[pl.ds(pl.multiple_of(48 * q, 16), 48)]

    def pass_on(whole, ss, rs, dz):
        z_got(whole, rs, dz)
        x_send(whole, ss, rs, dz)

    pass_on(r.gain_recv, r.s_gain, r.r_gain, 0)
    pass_on(r.wkv, r.s_wkv, r.r_wkv, 0)

    got(r.pos.at[other], r.r_pos.at[0])
    steps = lax.broadcasted_iota(jnp.int32, (BLOCK, 1), 0).astype(f32)
    for s in range(2):
        for b in range(16):
            r.posk[s, b * BLOCK : (b + 1) * BLOCK, :] = r.pos[s, 0:1, b * BLOCK : b * BLOCK + 1] + steps
    freq = r.freq[0:1, :]
    sign = r.freq[1:2, :]

    def tables(yy, carry):
        for s in range(2):
            rows = r.posk[s, pl.ds(pl.multiple_of(512 * xh + 128 * yy, 128), 128), :]
            angle = rows * freq
            r.cos_t[yy, s * 128 : (s + 1) * 128, :] = jnp.cos(angle)
            r.sin_t[yy, s * 128 : (s + 1) * 128, :] = jnp.sin(angle) * sign
        return carry

    lax.fori_loop(0, 2, tables, 0)

    for dz in (1, 3):
        pass_on(r.gain_recv, r.s_gain, r.r_gain, dz)
        pass_on(r.wkv, r.s_wkv, r.r_wkv, dz)
    for d in (1, 3):
        gather_forward(r.x_all, r.s_x, r.r_x, d)
    lax.fori_loop(2, 4, tables, 0)
    pass_on(r.gain_recv, r.s_gain, r.r_gain, 2)
    pass_on(r.wkv, r.s_wkv, r.r_wkv, 2)
    for dz in (0, 1, 3, 2):
        pass_on(r.wqq, r.s_wqq, r.r_wqq, dz)
    z_send(lambda k_: r.wgu_send.at[k_], r.wgu, r.s_wgu, r.r_wgu)
    gather_start(r.dyt, r.dy_all, r.s_dy, r.r_dy)
    own_piece = (2 * y + k == part) & (xl == k)

    @pl.when(jnp.logical_not(own_piece))
    def _():
        got(wo_rows(part), r.r_wo.at[0])
        got(wd_rows(part), r.r_wd.at[0])

    for dz in range(1, 4):
        there = place(xh, xl, y, around(z, dz), k)
        send(wo_rows(part), wo_rows(part), r.s_wo2.at[dz], r.r_wo2.at[dz], there)
        send(wd_rows(part), wd_rows(part), r.s_wd2.at[dz], r.r_wd2.at[dz], there)

    def piece_of(l_, dz):
        return 4 * l_ + around(z, 4 - dz)

    for dz in range(4):
        x_got(r.gain_recv, r.r_gain, dz)
    gains = jnp.sum(r.gain_recv[...], axis=0)
    g1 = to_row(gains, 0, 8)
    g2 = to_row(gains, 8, 8)
    gq = gains[16:17, :]
    gk = gains[17:18, :]

    def rotated(u, cos, sin):
        return u * cos + pltpu.roll(u, 64, 1) * sin

    def unrotated(u, cos, sin):
        return u * cos - pltpu.roll(u, 64, 1) * sin

    def inverse_rms(u):
        return lax.rsqrt(jnp.mean(u * u, axis=-1, keepdims=True) + norm_eps)

    kv_partner = place(1 - xh, xl, y, z, k)

    def kv_rows(s, hh, yy):
        return r.kv.at[s, pl.ds(pl.multiple_of(512 * hh + 128 * yy, 128), 128)]

    def project_keys(d):
        yy = around(y, 4 - d)
        rows = r.x_all[yy].reshape(256, D).astype(f32)
        n1 = (rows * inverse_rms(rows) * g1).astype(bf16)
        r.n1_all[yy] = n1
        kv = dot(n1, r.wkv[...].reshape(D, 256))
        raw = kv[:, 0:HEAD]
        r.qkraw[yy, :, 256:384] = raw
        local = pl.ds(pl.multiple_of(512 * xh + 128 * yy, 128), 128)
        key = rotated(raw * inverse_rms(raw) * gk, r.cos_t[yy], r.sin_t[yy]).astype(bf16)
        value = kv[:, HEAD:].astype(bf16)
        for s in range(2):
            r.kv[s, local, 0:HEAD] = key[s * 128 : (s + 1) * 128]
            r.kv[s, local, HEAD : 2 * HEAD] = value[s * 128 : (s + 1) * 128]
            send(kv_rows(s, xh, yy), kv_rows(s, xh, yy), r.s_kv.at[2 * d + s], r.r_kv.at[2 * d + s], kv_partner)

    def project_queries(yy, carry):
        qs = dot(r.n1_all[yy], r.wqq[...].reshape(D, 256))
        r.qkraw[yy, :, 0:256] = qs
        for h in range(2):
            raw = qs[:, h * HEAD : (h + 1) * HEAD]
            query = rotated(raw * inverse_rms(raw) * gq, r.cos_t[yy], r.sin_t[yy]).astype(bf16)
            for s in range(2):
                for half in range(2):
                    first = s * 128 + half * 64
                    rows = pl.ds(pl.multiple_of(64 * yy, 64), 64)
                    r.q_s[s, half, rows, h * HEAD : (h + 1) * HEAD] = query[first : first + 64]
        return carry

    gather_own(r.x_all, r.r_x)
    for dz in range(4):
        x_got(r.wkv, r.r_wkv, dz)
    project_keys(0)
    gather_pair(r.x_all, r.r_x, 1)
    project_keys(1)
    gather_forward(r.x_all, r.s_x, r.r_x, 2)
    gather_pair(r.x_all, r.r_x, 3)
    project_keys(3)
    gather_pair(r.x_all, r.r_x, 2)
    project_keys(2)
    for dz in range(4):
        x_got(r.wqq, r.r_wqq, dz)
    lax.fori_loop(0, 4, project_queries, 0)
    gather_end(r.x_all, r.s_x)

    for dz in range(4):
        if dz > 0:
            got(wo_rows(piece_of(xl, dz)), r.r_wo2.at[dz])
        block = wo_rows(piece_of(xl, dz))
        send(block, block, r.s_wo2.at[4 + dz], r.r_wo2.at[4 + dz], beside(dz))
    for dz in range(4):
        z_got(r.wgu, r.r_wgu, dz)
        x_send(r.wgu, r.s_wgu, r.r_wgu, dz)
    for dz in range(4):
        if dz > 0:
            got(wd_rows(piece_of(xl, dz)), r.r_wd2.at[dz])
        block = wd_rows(piece_of(xl, dz))
        send(block, block, r.s_wd2.at[4 + dz], r.r_wd2.at[4 + dz], beside(dz))
    for d in (1, 3, 2):
        gather_forward(r.dy_all, r.s_dy, r.r_dy, d)

    for d in (0, 1, 3, 2):
        for s in range(2):
            got(kv_rows(s, 1 - xh, around(y, 4 - d)), r.r_kv.at[2 * d + s])

    def lanes(half):
        return pl.ds(pl.multiple_of(256 * half, 256), 256)

    def allowed(s, half):
        return r.posk[s] <= r.pos[s, 1:2, lanes(half)]

    def attend(s, half):
        ok = allowed(s, half)
        for h in range(2):
            q = r.q_s[s, half, :, h * HEAD : (h + 1) * HEAD]
            scores = jnp.where(ok, dot_nt(r.kv[s, :, 0:HEAD], q) * SCALE, -1e30)
            top = jnp.max(scores, axis=0, keepdims=True)
            p = jnp.exp(scores - top)
            total = jnp.sum(p, axis=0, keepdims=True)
            o = dot_tn(r.kv[s, :, HEAD : 2 * HEAD], p.astype(bf16)) / total
            r.o_t[s, h * HEAD : (h + 1) * HEAD, lanes(half)] = o
            r.ob_t[s, h * HEAD : (h + 1) * HEAD, lanes(half)] = o.astype(bf16)
            r.lse[s, h, :, lanes(half)] = top + jnp.log(total)

    def reduce_first(use, p, cc, d, half=None):
        yy, rows, i = around(y, d), rows_of(half), 8 * use + 4 * (half or 0) + d
        send(p.at[yy, other, rows], cc.at[yy, rows], r.s_c.at[i], r.r_c.at[i], partner)

    def both_cores(use, p, cc, d, half):
        yy, rows, i = around(y, d), rows_of(half), 8 * use + 4 * (half or 0) + d
        got(cc.at[yy, rows], r.r_c.at[i])
        return p[yy, k, rows, :].astype(f32) + cc[yy, rows, :].astype(f32)

    def reduce_far(use, p, cc, rr, half=None):
        rows, o = rows_of(half), 12 * use + 6 * (half or 0)
        yy = around(y, 2)
        p[yy, k, rows, :] = both_cores(use, p, cc, 2, half).astype(bf16)
        for which in range(2):
            rest = far_part(half, which)
            there = place(xh, xl, around(y, 1 + 2 * which), z, k)
            send(p.at[yy, k, rest], rr.at[2, rest], r.s_r.at[o + which], r.r_r.at[o + which], there)
        for which in range(2):
            yy = around(y, 1 + 2 * which)
            p[yy, k, rows, :] = both_cores(use, p, cc, 1 + 2 * which, half).astype(bf16)
            early, i = far_part(half, 1 - which), o + 2 + which
            send(p.at[yy, k, early], rr.at[which, early], r.s_r.at[i], r.r_r.at[i], place(xh, xl, yy, z, k))

    def reduce_near(use, p, rr, half=None):
        o = 12 * use + 6 * (half or 0)
        for which in range(2):
            yy = around(y, 1 + 2 * which)
            late, i = far_part(half, which), o + 4 + which
            got(rr.at[2, late], r.r_r.at[o + which])
            p[yy, k, late, :] = (p[yy, k, late, :].astype(f32) + rr[2, late, :].astype(f32)).astype(bf16)
            send(p.at[yy, k, late], rr.at[which, late], r.s_r.at[i], r.r_r.at[i], place(xh, xl, yy, z, k))

    def reduce_third(use, p, cc, rr, half=None):
        rows, o = rows_of(half), 12 * use + 6 * (half or 0)
        total = both_cores(use, p, cc, 0, half)
        for which in range(2):
            got(rr.at[which, far_part(half, 1 - which)], r.r_r.at[o + 2 + which])
            got(rr.at[which, far_part(half, which)], r.r_r.at[o + 4 + which])
            total = total + rr[which, rows, :].astype(f32)
        return total

    def reduce_end(use, p, half=None):
        for d in range(4):
            sent(p.at[y, other, rows_of(half)], r.s_c.at[8 * use + 4 * (half or 0) + d])
        for i in range(6):
            sent(p.at[y, k, far_part(half, 0)], r.s_r.at[12 * use + 6 * (half or 0) + i])

    def out_partial(half):
        for s in range(2):
            o = r.ob_t[s, :, lanes(half)]
            r.pa[:, s, rows_of(half), :] = dot_tn(o, r.wo[...]).astype(bf16).reshape(4, 64, D)
        for d in (2, 1, 3, 0):
            reduce_first(0, r.pa, r.ca, d, half)

    for s in range(2):
        attend(s, 0)
    for dz in range(4):
        got(wo_rows(piece_of(1 - xl, dz)), r.r_wo2.at[4 + dz])
    out_partial(0)
    attend(0, 1)
    reduce_far(0, r.pa, r.ca, r.ra, 0)
    attend(1, 1)
    out_partial(1)
    reduce_near(0, r.pa, r.ra, 0)
    reduce_far(0, r.pa, r.ca, r.ra, 1)

    def middle(half):
        rows = rows_of(half)
        h1 = r.tok[rows, :].astype(f32) + reduce_third(0, r.pa, r.ca, r.ra, half)
        r.h1[rows, :] = h1
        r.n2_all[y, k, rows, :] = (h1 * inverse_rms(h1) * g2).astype(bf16)
        gather_start(r.n2_all.at[y, k], r.n2_all, r.s_n2, r.r_n2, half)

    middle(0)
    reduce_near(0, r.pa, r.ra, 1)
    middle(1)

    gather_own(r.dy_all, r.r_dy)
    for d in (1, 3, 2):
        gather_pair(r.dy_all, r.r_dy, d)
    for dz in range(4):
        x_got(r.wgu, r.r_wgu, dz)
        got(wd_rows(piece_of(1 - xl, dz)), r.r_wd2.at[4 + dz])

    def two_blocks(whole, ds, half):
        blocks = [whole[around(y, d), :, rows_of(half), :].reshape(128, whole.shape[-1]) for d in ds]
        return jnp.concatenate(blocks, axis=0)

    def put_blocks(whole, ds, half, cols, value):
        for i, d in enumerate(ds):
            block = value[128 * i : 128 * (i + 1)].reshape(2, 64, value.shape[-1])
            whole[around(y, d), :, rows_of(half), cols] = block

    def feed(ds, half):
        n2 = two_blocks(r.n2_all, ds, half)
        ab = dot(n2, r.wgu[...].reshape(D, 768))
        a, b = ab[:, :384], ab[:, 384:]
        sig = jax.nn.sigmoid(a)
        silu = a * sig
        put_blocks(r.hid_all, ds, half, slice(None), (silu * b).astype(bf16))
        dhid = dot_nt(two_blocks(r.dy_all, ds, half), r.wd[...])
        da = (dhid * b * sig * (1.0 + a * (1.0 - sig))).astype(bf16)
        db = (dhid * silu).astype(bf16)
        put_blocks(r.dgu_all, ds, half, slice(0, 384), da)
        put_blocks(r.dgu_all, ds, half, slice(384, 768), db)
        dn2 = dot_nt(jnp.concatenate([da, db], axis=1), r.wgu[...].reshape(D, 768))
        put_blocks(r.pb, ds, half, slice(None), dn2.astype(bf16))
        for d in ds:
            reduce_first(1, r.pb, r.cb, d, half)

    def near_forward(whole, ss, rs, half):
        for d in (1, 3):
            gather_forward(whole, ss, rs, d, half)

    near_forward(r.n2_all, r.s_n2, r.r_n2, 0)
    for half in range(2):
        gather_own(r.n2_all, r.r_n2, half)
        gather_pair(r.n2_all, r.r_n2, 1, half)
        feed((0, 3), half)
        if half == 1:
            reduce_near(1, r.pb, r.rb, 0)
        gather_forward(r.n2_all, r.s_n2, r.r_n2, 2, half)
        if half == 0:
            near_forward(r.n2_all, r.s_n2, r.r_n2, 1)
        gather_pair(r.n2_all, r.r_n2, 3, half)
        gather_pair(r.n2_all, r.r_n2, 2, half)
        feed((2, 1), half)
        reduce_far(1, r.pb, r.cb, r.rb, half)

    def rows_at(whole, height):
        return lambda l_, z_: whole.at[pl.ds(pl.multiple_of(height * (4 * l_ + z_), 16), height)]

    def cross_z(piece, dst, ss, rs):
        for dz in (1, 3, 2):
            zz = around(z, dz)
            for l_ in range(2):
                i = 2 * (dz - 1) + l_
                send(piece(l_, zz), dst.at[dz - 1, l_], ss.at[i], rs.at[i], place(xh, xl, y, zz, k))

    def row_half(ref, h_):
        return ref.at[pl.ds(pl.multiple_of(64 * h_, 64), 64)]

    def column_half(ref, h_):
        return ref.at[:, pl.ds(pl.multiple_of(512 * h_, 512), 512)]

    def cross_x(piece, zrecv, sums, xrecv, half_of, ss, rs):
        for l_ in range(2):
            total = piece(l_, z)[...].astype(f32)
            for dz in range(1, 4):
                got(zrecv.at[dz - 1, l_], rs.at[2 * (dz - 1) + l_])
                total = total + zrecv[dz - 1, l_].astype(f32)
            sums[l_] = total.astype(bf16)
        for dx in (1, 3, 2):
            x_ = around(x, dx)
            block = half_of(sums.at[lax.rem(x_, 2)], lax.div(x_, 2))
            send(block, xrecv.at[dx - 1], ss.at[5 + dx], rs.at[5 + dx], along_x(dx))

    def cross_total(sums, xrecv, half_of, rs):
        total = half_of(sums.at[xl], xh)[...].astype(f32)
        for dx in (1, 3, 2):
            got(xrecv.at[dx - 1], rs.at[5 + dx])
            total = total + xrecv[dx - 1].astype(f32)
        return total

    def cross_x_first(whole, height, xrecv, ss, rs):
        for dx in (1, 3, 2):
            x_ = around(x, dx)
            rows = pl.ds(pl.multiple_of(4 * height * lax.rem(x_, 2), 16), 4 * height)
            block = column_half(whole.at[rows], lax.div(x_, 2))
            send(block, xrecv.at[dx - 1], ss.at[dx - 1], rs.at[dx - 1], along_x(dx))

    def cross_z_second(whole, height, xrecv, sums, zrecv, ss, rs):
        rows = pl.ds(pl.multiple_of(4 * height * xl, 16), 4 * height)
        total = column_half(whole.at[rows], xh)[...].astype(f32)
        for dx in (1, 3, 2):
            got(xrecv.at[dx - 1], rs.at[dx - 1])
            total = total + xrecv[dx - 1].astype(f32)
        sums[...] = total.astype(bf16)
        for dz in (1, 3, 2):
            zz = around(z, dz)
            block = sums.at[pl.ds(pl.multiple_of(height * zz, 16), height)]
            send(block, zrecv.at[dz - 1], ss.at[2 + dz], rs.at[2 + dz], place(xh, xl, y, zz, k))

    def cross_z_total(height, sums, zrecv, rs):
        total = sums[pl.ds(pl.multiple_of(height * z, 16), height), :].astype(f32)
        for dz in (1, 3, 2):
            got(zrecv.at[dz - 1], rs.at[2 + dz])
            total = total + zrecv[dz - 1].astype(f32)
        return total

    def cross_sent(zrecv, xrecv, ss):
        for i in range(6):
            sent(zrecv.at[0, 0], ss.at[i])
        for i in range(3):
            sent(xrecv.at[0], ss.at[6 + i])

    gqa_piece, ggu_piece = rows_at(r.gqa, 128), rows_at(r.ggu, 128)
    go_piece = rows_at(r.go, 32)

    def weight_gradient(left, right, out):
        def one(i, carry):
            cols = pl.ds(pl.multiple_of(256 * i, 256), 256)
            out[:, cols] = dot_tn(left(), right(cols)).astype(bf16)
            return carry

        lax.fori_loop(0, out.shape[1] // 256, one, 0)

    def middle_back(half):
        rows = rows_of(half)
        dn2 = reduce_third(1, r.pb, r.cb, r.rb, half)
        h1 = r.h1[rows, :]
        r2 = inverse_rms(h1)
        weighted = dn2 * g2
        back = r2 * weighted - h1 * (r2 * r2 * r2) * jnp.mean(weighted * h1, axis=-1, keepdims=True)
        dh1 = r.dyt[rows, :].astype(f32) + back
        r.dh1[rows, :] = dh1
        dg2 = jnp.sum(dn2 * h1 * r2, axis=0, keepdims=True)
        for i in range(8):
            r.dg[8 + i : 9 + i, :] += dg2[:, 128 * i : 128 * (i + 1)]
        r.x_all[y, k, rows, :] = dh1.astype(bf16)
        gather_start(r.x_all.at[y, k], r.x_all, r.s_dob, r.r_dob, half)

    weight_gradient(
        lambda: r.n2_all[...].reshape(D, D),
        lambda cols: r.dgu_all[:, :, :, cols].reshape(D, 256),
        r.ggu,
    )
    cross_z(ggu_piece, r.zgu, r.s_ggu, r.r_ggu)
    reduce_near(1, r.pb, r.rb, 1)
    middle_back(0)
    weight_gradient(
        lambda: r.hid_all[...].reshape(D, 384),
        lambda cols: r.dy_all[:, :, :, cols].reshape(D, 256),
        r.gd,
    )
    cross_x_first(r.gd, 48, r.xd, r.s_gd, r.r_gd)
    middle_back(1)

    def norm_back(value, gain, grad):
        inverse = inverse_rms(value)
        w = grad * gain
        back = inverse * w - value * (inverse * inverse * inverse) * jnp.mean(w * value, axis=-1, keepdims=True)
        return back, jnp.sum(grad * value * inverse, axis=0, keepdims=True)

    def attend_back(half, s):
        rows = rows_of(half)
        do_s = dot_nt(r.wo[...], r.x_all[:, s, rows, :].reshape(256, D)).astype(bf16)
        prod = do_s.astype(f32) * r.o_t[s, :, lanes(half)]
        r.do_t[s, :, lanes(half)] = do_s
        ok = allowed(s, half)
        keys, values = r.kv[s, :, 0:HEAD], r.kv[s, :, HEAD : 2 * HEAD]
        mine = pl.ds(s * 128 + 64 * half, 64)
        cos = r.cos_t[:, mine, :].reshape(256, HEAD)
        sin = r.sin_t[:, mine, :].reshape(256, HEAD)
        for h in range(2):
            head = slice(h * HEAD, (h + 1) * HEAD)
            q = r.q_s[s, half, :, head]
            do = r.do_t[s, head, lanes(half)]
            delta = jnp.sum(prod[head], axis=0, keepdims=True)
            scores = dot_nt(keys, q) * SCALE
            p = jnp.where(ok, jnp.exp(scores - r.lse[s, h, :, lanes(half)]), 0.0)
            ds = (p * (dot(values, do) - delta)).astype(bf16)
            dv = dot_nt(p.astype(bf16), do)
            dk = dot(ds, q) * SCALE
            if half == 0 and h == 0:
                r.dkv[s, :, HEAD : 2 * HEAD] = dv
                r.dkv[s, :, 0:HEAD] = dk
            else:
                r.dkv[s, :, HEAD : 2 * HEAD] += dv
                r.dkv[s, :, 0:HEAD] += dk
            dq = (dot_tn(keys, ds) * SCALE).T
            raw = r.qkraw[:, mine, head].reshape(256, HEAD)
            back, gain_grad = norm_back(raw, gq, unrotated(dq, cos, sin))
            r.dqkv[:, mine, head] = back.astype(bf16).reshape(4, 64, HEAD)
            r.dg[16:17, :] += gain_grad

    def gather_rest(half):
        gather_forward(r.x_all, r.s_dob, r.r_dob, 2, half)
        gather_own(r.x_all, r.r_dob, half)
        for d in (1, 3, 2):
            gather_pair(r.x_all, r.r_dob, d, half)

    for half in range(2):
        reduce_end(0, r.pa, half)

    def down_partial(i, carry):
        hid = r.hid_all[i].reshape(256, 384)
        r.pa[i] = dot(hid, r.wd[...]).astype(bf16).reshape(2, 128, D)
        return carry

    near_forward(r.x_all, r.s_dob, r.r_dob, 0)
    lax.fori_loop(0, 4, down_partial, 0)
    for d in (2, 1, 3, 0):
        reduce_first(2, r.pa, r.ca, d)
    gather_rest(0)
    attend_back(0, 0)
    near_forward(r.x_all, r.s_dob, r.r_dob, 1)
    attend_back(0, 1)
    reduce_far(2, r.pa, r.ca, r.ra)
    cross_z_second(r.gd, 48, r.xd, r.sd, r.zd, r.s_gd, r.r_gd)
    gather_rest(1)
    for s in range(2):
        attend_back(1, s)
        if s == 0:
            reduce_near(2, r.pa, r.ra)
        r.dkv_send[s] = r.dkv[s, pl.ds(pl.multiple_of(512 * (1 - xh), 512), 512), :].astype(bf16)
        send(r.dkv_send.at[s], r.dkv_recv.at[s], r.s_dkv.at[s], r.r_dkv.at[s], kv_partner)

    def qkv_gradient(first, out, weight):
        grad = dot_tn(r.n1_all[...].reshape(D, D), r.dqkv[:, :, first : first + 256].reshape(D, 256))
        out[...] = grad.astype(bf16)
        prod = grad * weight[...].reshape(D, 256).astype(f32)
        return prod[:, 0:128] + prod[:, 128:256]

    r.wdot[...] = qkv_gradient(0, r.gqa, r.wqq)
    cross_z(gqa_piece, r.zqa, r.s_gqa, r.r_gqa)

    def out_gradient(i, carry):
        cols = pl.ds(pl.multiple_of(256 * i, 256), 256)
        total = jnp.zeros((256, 256), f32)
        for s in range(2):
            for half in range(2):
                rows = r.x_all[:, s, rows_of(half), cols].reshape(256, 256)
                total = total + dot(r.ob_t[s, :, lanes(half)], rows)
        r.go[:, cols] = total.astype(bf16)
        return carry

    lax.fori_loop(0, 4, out_gradient, 0)
    cross_z(go_piece, r.zo, r.s_go, r.r_go)

    def cross(i, sign):
        dx, dz = lax.div(i, 4), lax.rem(i, 4)
        x_, z_ = lax.rem(x + 4 + sign * dx, 4), lax.rem(z + 4 + sign * dz, 4)
        return lax.div(x_, 2), lax.rem(x_, 2), z_

    def direct_piece(whole, h_, p_):
        return whole.at[pl.ds(pl.multiple_of(128 * p_ + 64 * h_, 64), 64)]

    def direct_send(whole, dst, ss, rs):
        def one(i, carry):
            h_, l_, z_ = cross(i, 1)
            send(direct_piece(whole, h_, 4 * l_ + z_), dst.at[i], ss.at[i], rs.at[i], place(h_, l_, y, z_, k))
            return carry

        lax.fori_loop(1, 16, one, 0)

    def direct_sum(whole, dst, rs):
        def one(i, total):
            got(dst.at[i], rs.at[i])
            return total + dst[i].astype(f32)

        return lax.fori_loop(1, 16, one, direct_piece(whole, xh, part)[...].astype(f32))

    def direct_spread(total, hold, final, ss, rs):
        hold[...] = total.astype(bf16)

        def one(i, carry):
            there = place(lax.rem(xh + lax.div(i, 4), 2), xl, lax.rem(y + i, 4), z, xh)

            @pl.when((i > 0) | (k != xh))
            def _():
                send(hold, final.at[t], ss.at[i], rs.at[t], there)

            return carry

        lax.fori_loop(0, 8, one, 0)

        @pl.when(k == xh)
        def _():
            final[t] = hold[...]

    def direct_spread_sent(hold, ss):
        def one(i, carry):
            @pl.when((i > 0) | (k != xh))
            def _():
                sent(hold, ss.at[i])

            return carry

        lax.fori_loop(0, 8, one, 0)

    def direct_spread_got(final, rs):
        def one(i, carry):
            @pl.when((i != t) | (k != xh))
            def _():
                got(final.at[i], rs.at[i])

            return carry

        lax.fori_loop(0, 8, one, 0)

    other_half = place(1 - xh, xl, y, z, k)

    def rows_exchange(total, hold, ss, rs):
        hold[xh] = total.astype(bf16)
        send(hold.at[xh], hold.at[xh], ss.at[8], rs.at[8], other_half)

    def rows_spread(hold, final, ss, rs):
        for which in range(2):
            h = xh if which == 0 else 1 - xh
            if which == 1:
                got(hold.at[h], rs.at[8])
            for i in (2, 1, 3):
                send(hold.at[h], final.at[t], ss.at[4 * which + i], rs.at[t], place(xh, xl, around(y, i), z, h))

            @pl.when(k != h)
            def _():
                send(hold.at[h], final.at[t], ss.at[4 * which], rs.at[t], partner)

            @pl.when(k == h)
            def _():
                final[t] = hold[h]

    def rows_spread_sent(hold, ss):
        sent(hold.at[0], ss.at[8])
        for which in range(2):
            h = xh if which == 0 else 1 - xh
            for i in range(1, 4):
                sent(hold.at[0], ss.at[4 * which + i])

            @pl.when(k != h)
            def _():
                sent(hold.at[0], ss.at[4 * which])

    def rows_spread_got(final, rs):
        def one(i, carry):
            @pl.when(i != t)
            def _():
                got(final.at[i], rs.at[i])

            return carry

        lax.fori_loop(0, 8, one, 0)

    def block_exchange(total, hold, ss, rs):
        column_half(hold, xh)[...] = total.astype(bf16)
        send(column_half(hold, xh), column_half(hold, xh), ss.at[4], rs.at[4], other_half)

    def block_spread(hold, final, height, ss, rs):
        got(column_half(hold, 1 - xh), rs.at[4])
        rows = pl.ds(pl.multiple_of(height * z, 16), height)

        def to(i):
            there = place(xh, lax.div(t, 4), around(y, i), lax.rem(t, 4), xl)
            send(hold, final.at[rows], ss.at[i], rs.at[z], there)

        for i in (2, 1, 3):
            to(i)

        @pl.when(jnp.logical_not(home))
        def _():
            to(0)

        @pl.when(home)
        def _():
            final[rows, :] = hold[...]

    def block_spread_sent(hold, ss):
        sent(column_half(hold, 0), ss.at[4])
        for i in range(1, 4):
            sent(hold, ss.at[i])

        @pl.when(jnp.logical_not(home))
        def _():
            sent(hold, ss.at[0])

    def block_spread_got(final, height, rs):
        def one(i, carry):
            @pl.when((i != z) | jnp.logical_not(home))
            def _():
                got(final.at[pl.ds(pl.multiple_of(height * i, 16), height)], rs.at[i])

            return carry

        lax.fori_loop(0, 4, one, 0)

    cross_x(ggu_piece, r.zgu, r.sgu, r.xgu, row_half, r.s_ggu, r.r_ggu)
    block_exchange(cross_z_total(48, r.sd, r.zd, r.r_gd), r.hd, r.s_fd, r.r_fd)
    r.out_tok[...] = (r.h1[...] + reduce_third(2, r.pa, r.ca, r.ra)).astype(bf16)
    block_spread(r.hd, r.fd, 48, r.s_fd, r.r_fd)
    rows_exchange(cross_total(r.sgu, r.xgu, row_half, r.r_ggu), r.hgu, r.s_fgu, r.r_fgu)

    for half in range(2):
        reduce_end(1, r.pb, half)
    for s in range(2):
        got(r.dkv_recv.at[s], r.r_dkv.at[s])

    def key_back(yy, carry):
        rows = pl.ds(pl.multiple_of(512 * xh + 128 * yy, 128), 128)
        local = pl.ds(pl.multiple_of(128 * yy, 128), 128)
        grads = [r.dkv[s, rows, :] + r.dkv_recv[s, local, :].astype(f32) for s in range(2)]
        both = jnp.concatenate(grads, axis=0)
        du = unrotated(both[:, 0:HEAD], r.cos_t[yy], r.sin_t[yy])
        back, gain_grad = norm_back(r.qkraw[yy, :, 256:384], gk, du)
        r.dqkv[yy, :, 256:384] = back.astype(bf16)
        r.dqkv[yy, :, 384:512] = both[:, HEAD : 2 * HEAD].astype(bf16)
        r.dg[17:18, :] += gain_grad
        return carry

    lax.fori_loop(0, 4, key_back, 0)
    wdot = r.wdot[...] + qkv_gradient(256, r.gqb, r.wkv)
    direct_send(r.gqb, r.rqb, r.s_gqb, r.r_gqb)
    dg1 = jnp.sum(wdot.T, axis=0, keepdims=True) / g1
    for i in range(8):
        r.dg[i : i + 1, :] = dg1[:, 128 * i : 128 * (i + 1)]
    for i in range(1, 8):
        there = place(xh, xl, around(y, i // 2), z, lax.rem(k + i, 2))
        send(r.dg, r.dg_r1.at[i], r.s_dg1.at[i], r.r_dg1.at[i], there)
    for d in (2, 1, 3, 0):
        yy = around(y, d)
        dn1 = dot_nt(r.dqkv[yy, :, 0:256], r.wqq[...].reshape(D, 256))
        dn1 = dn1 + dot_nt(r.dqkv[yy, :, 256:512], r.wkv[...].reshape(D, 256))
        r.pb[yy] = dn1.astype(bf16).reshape(2, 128, D)
        reduce_first(3, r.pb, r.cb, d)
    rows_spread(r.hgu, r.fgu, r.s_fgu, r.r_fgu)
    reduce_far(3, r.pb, r.cb, r.rb)
    cross_x(gqa_piece, r.zqa, r.sqa, r.xqa, row_half, r.s_gqa, r.r_gqa)
    cross_x(go_piece, r.zo, r.so, r.xo, column_half, r.s_go, r.r_go)
    total = r.dg[...]
    for i in range(1, 8):
        got(r.dg_r1.at[i], r.r_dg1.at[i])
        total = total + r.dg_r1[i]
    r.dg_s[0] = total
    for dz in range(1, 4):
        send(r.dg_s.at[0], r.dg_r2.at[dz - 1], r.s_dg2.at[dz - 1], r.r_dg2.at[dz - 1], place(xh, xl, y, around(z, dz), k))
    reduce_near(3, r.pb, r.rb)
    direct_spread(direct_sum(r.gqb, r.rqb, r.r_gqb), r.hqb, r.fqb, r.s_fqb, r.r_fqb)
    rows_exchange(cross_total(r.sqa, r.xqa, row_half, r.r_gqa), r.hqa, r.s_fqa, r.r_fqa)
    block_exchange(cross_total(r.so, r.xo, column_half, r.r_go), r.ho, r.s_fo, r.r_fo)
    for dz in range(1, 4):
        got(r.dg_r2.at[dz - 1], r.r_dg2.at[dz - 1])
        total = total + r.dg_r2[dz - 1]
    r.dg_s[1] = total
    for dx in range(1, 4):
        send(r.dg_s.at[1], r.dg_r2.at[2 + dx], r.s_dg2.at[2 + dx], r.r_dg2.at[2 + dx], along_x(dx))
    rows_spread(r.hqa, r.fqa, r.s_fqa, r.r_fqa)
    block_spread(r.ho, r.fo, 32, r.s_fo, r.r_fo)

    dn1 = reduce_third(3, r.pb, r.cb, r.rb)
    rows = r.tok[...].astype(f32)
    back, unused = norm_back(rows, g1, dn1)
    r.dtok[...] = (r.dh1[...] + back).astype(bf16)

    block_spread_got(r.fd, 48, r.r_fd)
    r.g_dn[...] = r.fd[...]
    rows_spread_got(r.fgu, r.r_fgu)
    for i in range(8):
        r.g_gu[:, 384 * i : 384 * (i + 1)] = r.fgu[i, :, 0:384]
        r.g_gu[:, 3072 + 384 * i : 3072 + 384 * (i + 1)] = r.fgu[i, :, 384:768]
    block_spread_got(r.fo, 32, r.r_fo)
    r.g_out[...] = r.fo[...]
    rows_spread_got(r.fqa, r.r_fqa)
    for i in range(8):
        r.g_qkv[:, 256 * i : 256 * (i + 1)] = r.fqa[i]
    for dx in range(1, 4):
        got(r.dg_r2.at[2 + dx], r.r_dg2.at[2 + dx])
        total = total + r.dg_r2[2 + dx]
    r.g_gain[...] = total
    direct_spread_got(r.fqb, r.r_fqb)
    for i in range(8):
        r.g_qkv[:, 2048 + 128 * i : 2048 + 128 * (i + 1)] = r.fqb[i, :, 0:128]
        r.g_qkv[:, 3072 + 128 * i : 3072 + 128 * (i + 1)] = r.fqb[i, :, 128:256]

    gather_end(r.dy_all, r.s_dy)
    for half in range(2):
        gather_end(r.n2_all, r.s_n2, half)
        gather_end(r.x_all, r.s_dob, half)
    sent(r.pos_in, r.s_pos.at[0])
    for whole, ss in ((r.gain_recv, r.s_gain), (r.wqq, r.s_wqq), (r.wkv, r.s_wkv), (r.wgu, r.s_wgu)):
        rows_sent(whole, ss)
    for i in range(4):
        here = (xl == k) & (z == i) & (to_core == k)

        @pl.when(is_source & jnp.logical_not(here))
        def _():
            sent(r.wo_own.at[pl.ds(32 * i, 32)], r.s_wo.at[i])
            sent(r.wd_own.at[pl.ds(48 * i, 48)], r.s_wd.at[i])

    loop_sent(wo_rows(part), r.s_wo2, 1, 8)
    loop_sent(wd_rows(part), r.s_wd2, 1, 8)
    loop_sent(r.kv.at[0, pl.ds(0, 128)], r.s_kv, 0, 8)
    reduce_end(2, r.pa)
    reduce_end(3, r.pb)
    for s in range(2):
        sent(r.dkv_send.at[s], r.s_dkv.at[s])
    cross_sent(r.zqa, r.xqa, r.s_gqa)
    loop_sent(direct_piece(r.gqb, xh, part), r.s_gqb, 1, 16)
    cross_sent(r.zgu, r.xgu, r.s_ggu)
    cross_sent(r.zo, r.xo, r.s_go)
    for i in range(3):
        sent(r.xd.at[0], r.s_gd.at[i])
        sent(r.zd.at[0], r.s_gd.at[3 + i])
    for hold, ss in ((r.hqa, r.s_fqa), (r.hgu, r.s_fgu)):
        rows_spread_sent(hold, ss)
    direct_spread_sent(r.hqb, r.s_fqb)
    block_spread_sent(r.ho, r.s_fo)
    block_spread_sent(r.hd, r.s_fd)
    loop_sent(r.dg, r.s_dg1, 1, 8)
    loop_sent(r.dg_s.at[0], r.s_dg2, 0, 6)


def layer(*args):
    vmem = pl.BlockSpec(memory_space=pltpu.VMEM)
    hbm = pl.BlockSpec(memory_space=pl.ANY)
    specs = [hbm if far else vmem for far in INPUTS.values()]
    return pl.pallas_call(
        layer_kernel,
        out_shape=[jax.ShapeDtypeStruct(shape, kind) for shape, kind in OUTPUTS.values()],
        in_specs=specs,
        out_specs=[vmem] * len(OUTPUTS),
        scratch_shapes=[pltpu.VMEM(shape, kind) for shape, kind in BUFFERS.values()]
        + [pltpu.SemaphoreType.DMA((count,)) for count in SEMAPHORES.values()],
        compiler_params=pltpu.CompilerParams(
            collective_id=0, has_side_effects=True, vmem_limit_bytes=62 << 20
        ),
        name="layer",
    )(*args)


def adam_update(weight, moment, square, grad, rate, decay):
    moment_new = beta_first * moment + (1.0 - beta_first) * grad
    square_new = beta_second * square + (1.0 - beta_second) * grad * grad
    fix_first = 1.0 - beta_first**STEP
    fix_second = 1.0 - beta_second**STEP
    step = moment_new / fix_first / (jnp.sqrt(square_new / fix_second) + adam_eps)
    return (weight - rate * (step + decay * weight), moment_new, square_new)


def on_device(
    tokens, d_out, block_ids,
    w_qkv, w_out, w_gate_up, w_down, gains,
    moment_qkv, moment_out, moment_gate_up, moment_down, moment_gains,
    square_qkv, square_out, square_gate_up, square_down, square_gains,
):
    f = lax.axis_index("fsdp")
    starts = block_ids[0].astype(f32) * BLOCK
    spots = starts[:, None] + jnp.arange(BLOCK, dtype=f32)[None, :]
    mine = lax.dynamic_slice(spots, (8 * lax.div(lax.axis_index("ctx"), 4), 0), (8, BLOCK))
    mine = mine.reshape(4, 2, BLOCK).transpose(1, 0, 2).reshape(1, 512)
    positions = jnp.concatenate([spots.reshape(1, D), jnp.tile(mine, (7, 2))], axis=0)
    gain_rows = lax.dynamic_update_slice(
        jnp.zeros((24 * 128,), f32), gains.astype(bf16).astype(f32), (f * 144,)
    ).reshape(24, 128)
    half = rope_base ** (-(np.arange(64, dtype=np.float32) * np.float32(2.0 / HEAD)))
    table = np.zeros((8, 128), np.float32)
    table[0] = np.concatenate([half, half])
    table[1] = np.concatenate([-np.ones(64), np.ones(64)])
    out_tok, dtok, g_qkv, g_out, g_gu, g_dn, g_gain = layer(
        tokens[0], d_out[0], positions, gain_rows, jnp.asarray(table), w_qkv, w_out, w_gate_up, w_down
    )
    grad_gains = lax.dynamic_slice(g_gain.reshape(24 * 128), (f * 144,), (144,))
    grads = (g_qkv, g_out, g_gu, g_dn, grad_gains)
    masters = (w_qkv, w_out, w_gate_up, w_down, gains)
    moments = (moment_qkv, moment_out, moment_gate_up, moment_down, moment_gains)
    squares = (square_qkv, square_out, square_gate_up, square_down, square_gains)
    rates = (0.03, 0.3, 0.03, 0.03, 0.5)
    decays = (decay_rate, decay_rate, decay_rate, decay_rate, 0.0)
    updates = [
        adam_update(masters[i], moments[i], squares[i], grads[i].astype(f32), rates[i], decays[i])
        for i in range(5)
    ]
    return (
        out_tok[None],
        dtok[None],
        *(u[0] for u in updates),
        *(u[1] for u in updates),
        *(u[2] for u in updates),
    )


def solution(mesh):
    rows, flat = P("fsdp", None), P("fsdp")
    tokens = P("fsdp", "ctx", None)
    state = (rows, rows, rows, rows, flat)
    return jax.shard_map(
        on_device,
        mesh=mesh,
        in_specs=(tokens, tokens, rows) + state * 3,
        out_specs=(tokens, tokens) + state * 3,
        check_vma=False,
    )
```

```python
import math
import types

import jax
import jax.numpy as jnp
import numpy as np
from jax import lax
from jax.experimental import pallas as pl
from jax.experimental.pallas import tpu as pltpu
from jax.sharding import PartitionSpec as P

D = 1024
HEAD = 128
STEP = 10
BLOCK = 64
norm_eps = 1e-06
rope_base = 1000000.0
beta_first = 0.9
beta_second = 0.95
adam_eps = 1e-08
decay_rate = 0.1
SCALE = 1.0 / math.sqrt(HEAD)

f32 = jnp.float32
bf16 = jnp.bfloat16
MESH = pl.DeviceIdType.MESH

INPUTS = dict(
    tok=False, dyt=False, pos_in=False, gain_in=False, freq=False, wqkv_f=True, wo_f=False, wgu_f=True, wd_f=False
)
OUTPUTS = dict(
    out_tok=((128, D), bf16),
    dtok=((128, D), bf16),
    g_qkv=((64, 4096), bf16),
    g_out=((128, D), bf16),
    g_gu=((64, 6144), bf16),
    g_dn=((192, D), bf16),
    g_gain=((24, 128), f32),
)
BUFFERS = dict(
    x_all=((4, 2, 128, D), bf16),
    dy_all=((4, 2, 128, D), bf16),
    n2_all=((4, 2, 128, D), bf16),
    n1_all=((4, 256, D), bf16),
    wq_f=((2, 64, 512), f32),
    wgu_fs=((2, 64, 768), f32),
    wqq_send=((2, 64, 256), bf16),
    wkv_send=((2, 64, 256), bf16),
    wgu_send=((2, 64, 768), bf16),
    wo_own=((128, D), bf16),
    wd_own=((192, D), bf16),
    wqq=((16, 64, 256), bf16),
    wkv=((16, 64, 256), bf16),
    wgu=((16, 64, 768), bf16),
    wo=((256, D), bf16),
    wd=((384, D), bf16),
    gain_recv=((16, 24, 128), f32),
    pos=((2, 8, D), f32),
    posk=((2, D, 1), f32),
    cos_t=((4, 256, HEAD), f32),
    sin_t=((4, 256, HEAD), f32),
    qkraw=((4, 256, 384), f32),
    q_s=((2, 2, 256, 256), bf16),
    kv=((2, D, 256), bf16),
    o_t=((2, 256, 512), f32),
    ob_t=((2, 256, 512), bf16),
    lse=((2, 2, 1, 512), f32),
    pa=((4, 2, 128, D), bf16),
    pb=((4, 2, 128, D), bf16),
    ca=((4, 128, D), bf16),
    cb=((4, 128, D), bf16),
    ra=((3, 128, D), bf16),
    rb=((3, 128, D), bf16),
    h1=((128, D), f32),
    dh1=((128, D), f32),
    hid_all=((4, 2, 128, 384), bf16),
    dgu_all=((4, 2, 128, 768), bf16),
    do_t=((2, 256, 512), bf16),
    delta=((2, 2, 1, 512), f32),
    dkv=((2, D, 256), f32),
    dkv_send=((2, 512, 256), bf16),
    dkv_recv=((2, 512, 256), bf16),
    dqkv=((4, 256, 512), bf16),
    gqa=((D, 256), bf16),
    gqb=((D, 256), bf16),
    wdot=((D, HEAD), f32),
    ggua=((8, 2, 64, 256), bf16),
    ggub=((D, 512), bf16),
    go=((256, D), bf16),
    gd=((384, D), bf16),
    zqa=((3, 2, 128, 256), bf16),
    zgua=((3, 64, 256), bf16),
    zgub=((3, 2, 128, 512), bf16),
    zo=((3, 2, 32, D), bf16),
    zd=((3, 48, 512), bf16),
    sqa=((2, 128, 256), bf16),
    sgua=((4, 64, 256), bf16),
    sgub=((2, 128, 512), bf16),
    so=((2, 32, D), bf16),
    sd=((192, 512), bf16),
    xqa=((3, 64, 256), bf16),
    rqb=((16, 64, 256), bf16),
    xgua=((3, 4, 64, 256), bf16),
    xgub=((3, 64, 512), bf16),
    xo=((3, 32, 512), bf16),
    xd=((3, 192, 512), bf16),
    hqa=((2, 64, 256), bf16),
    hqb=((64, 256), bf16),
    hgu=((2, 64, 768), bf16),
    ho=((32, D), bf16),
    hd=((48, D), bf16),
    fqa=((8, 64, 256), bf16),
    fqb=((8, 64, 256), bf16),
    fgu=((8, 64, 768), bf16),
    fo=((128, D), bf16),
    fd=((192, D), bf16),
    dg=((24, 128), f32),
    dg_r1=((8, 24, 128), f32),
    dg_s=((2, 24, 128), f32),
    dg_r2=((6, 24, 128), f32),
)
SEMAPHORES = dict(
    ld=16,
    s_x=8, r_x=8,
    s_dy=8, r_dy=8,
    s_n2=16, r_n2=16,
    s_dob=16, r_dob=16,
    s_pos=1, r_pos=1,
    s_gain=12, r_gain=12,
    s_wqq=12, r_wqq=12,
    s_wkv=12, r_wkv=12,
    s_wgu=12, r_wgu=12,
    s_wo=4, r_wo=1, s_wd=4, r_wd=1,
    s_wo2=8, r_wo2=8, s_wd2=8, r_wd2=8,
    s_kv=8, r_kv=8,
    s_c=32, r_c=32,
    s_r=48, r_r=48,
    s_dkv=2, r_dkv=2,
    s_gqa=9, r_gqa=9,
    s_gqb=16, r_gqb=16,
    s_ggua=6, r_ggua=6,
    s_ggub=9, r_ggub=9,
    s_go=9, r_go=9,
    s_gd=6, r_gd=6,
    s_fqa=9, r_fqa=9,
    s_fqb=8, r_fqb=8,
    s_fgu=9, r_fgu=9,
    s_fo=5, r_fo=5,
    s_fd=5, r_fd=5,
    s_dg1=8, r_dg1=8,
    s_dg2=6, r_dg2=6,
)


def dot(a, b):
    return jnp.dot(a, b, preferred_element_type=f32)


def dot_nt(a, b):
    return lax.dot_general(a, b, (((1,), (1,)), ((), ())), preferred_element_type=f32)


def dot_tn(a, b):
    return lax.dot_general(a, b, (((0,), (0,)), ((), ())), preferred_element_type=f32)


def to_row(g, first, count):
    return jnp.concatenate([g[first + i : first + i + 1, :] for i in range(count)], axis=1)


def layer_kernel(*refs):
    names = [*INPUTS, *OUTPUTS, *BUFFERS, *SEMAPHORES]
    r = types.SimpleNamespace(**dict(zip(names, refs, strict=True)))

    c = lax.axis_index("ctx")
    f = lax.axis_index("fsdp")
    xh, y = lax.div(c, 4), lax.rem(c, 4)
    xl, z, k = lax.div(f, 8), lax.rem(lax.div(f, 2), 4), lax.rem(f, 2)
    x = 2 * xh + xl
    part = 4 * xl + z
    t = 2 * y + k
    other = 1 - k

    def place(xh_, xl_, y_, z_, k_):
        return (xh_ * 4 + y_, xl_ * 8 + z_ * 2 + k_)

    partner = place(xh, xl, y, z, other)

    def around(value, step):
        return lax.rem(value + step, 4)

    def copy(src, dst, ss, rs, device):
        return pltpu.make_async_remote_copy(
            src_ref=src, dst_ref=dst, send_sem=ss, recv_sem=rs,
            device_id=device, device_id_type=MESH,
        )

    def send(src, dst, ss, rs, device):
        copy(src, dst, ss, rs, device).start()

    def got(ref, rs):
        copy(ref, ref, rs, rs, partner).wait_recv()

    def sent(ref, ss):
        copy(ref, ref, ss, ss, partner).wait_send()

    loads = []

    def load(src, dst):
        one = pltpu.make_async_copy(src, dst, r.ld.at[len(loads)])
        one.start()
        loads.append(one)

    for i in range(2):
        ti = 2 * y + i
        load(r.wqkv_f.at[:, pl.ds(pl.multiple_of(256 * ti, 256), 256)], r.wq_f.at[i, :, pl.ds(0, 256)])
        load(r.wqkv_f.at[:, pl.ds(pl.multiple_of(2048 + 128 * ti, 128), 128)], r.wq_f.at[i, :, pl.ds(256, 128)])
        load(r.wqkv_f.at[:, pl.ds(pl.multiple_of(3072 + 128 * ti, 128), 128)], r.wq_f.at[i, :, pl.ds(384, 128)])
    for i in range(2):
        ti = 2 * y + i
        load(r.wgu_f.at[:, pl.ds(pl.multiple_of(384 * ti, 128), 384)], r.wgu_fs.at[i, :, pl.ds(0, 384)])
        load(r.wgu_f.at[:, pl.ds(pl.multiple_of(3072 + 384 * ti, 128), 384)], r.wgu_fs.at[i, :, pl.ds(384, 384)])

    barrier = pltpu.get_barrier_semaphore()

    def greet(device):
        pl.semaphore_signal(barrier, inc=1, device_id=device, device_id_type=MESH)

    def greet_groups(i, carry):
        a, b, core = lax.div(i, 8), lax.rem(lax.div(i, 2), 4), lax.rem(k + i, 2)
        greet(place(lax.rem(xh + a, 2), xl, around(y, b), z, core))
        greet(place(xh, lax.rem(xl + a, 2), y, around(z, b), core))
        x_ = around(x, lax.div(i, 4))
        greet(place(lax.div(x_, 2), lax.rem(x_, 2), y, around(z, lax.rem(i, 4)), k))
        return carry

    home = (xl == lax.div(t, 4)) & (z == lax.rem(t, 4)) & (k == xl)

    def greet_senders(i, carry):
        @pl.when(jnp.logical_not(home & (i == z)))
        def _():
            greet(place(xh, k, lax.div(part, 2), i, lax.rem(part, 2)))

        return carry

    def along_x(d):
        x_ = around(x, d)
        return place(lax.div(x_, 2), lax.rem(x_, 2), y, z, k)

    lax.fori_loop(1, 16, greet_groups, 0)
    lax.fori_loop(0, 4, greet_senders, 0)

    for one in loads:
        one.wait()
    r.wqq_send[...] = r.wq_f[:, :, 0:256].astype(bf16)
    r.wkv_send[...] = r.wq_f[:, :, 256:512].astype(bf16)
    r.wgu_send[...] = r.wgu_fs[...].astype(bf16)
    r.wo_own[...] = r.wo_f[...].astype(bf16)
    r.wd_own[...] = r.wd_f[...].astype(bf16)
    r.wqq[f] = r.wqq_send[k]
    r.wkv[f] = r.wkv_send[k]
    r.wgu[f] = r.wgu_send[k]
    r.gain_recv[f] = r.gain_in[...]
    r.x_all[y, k] = r.tok[...]
    r.dy_all[y, k] = r.dyt[...]
    r.pos[k] = r.pos_in[...]
    r.dg[...] = jnp.zeros((24, 128), f32)
    pl.semaphore_wait(barrier, 49 - home.astype(jnp.int32))

    def rows_of(half):
        return pl.ds(0, 128) if half is None else pl.ds(64 * half, 64)

    def far_part(half, which):
        size = 64 if half is None else 32
        return pl.ds((0 if half is None else 64 * half) + size * which, size)

    def gather_start(src, whole, ss, rs, half=None):
        rows, o = rows_of(half), 8 * (half or 0)
        for d in (1, 3):
            send(src.at[rows], whole.at[y, k, rows], ss.at[o + d - 1], rs.at[o + d - 1], place(xh, xl, around(y, d), z, k))
        send(src.at[rows], whole.at[y, k, rows], ss.at[o + 3], rs.at[o + 3], partner)

    def gather_forward(whole, ss, rs, d, half=None):
        rows, o = rows_of(half), 8 * (half or 0)
        block = whole.at[around(y, 4 - d), k, rows]
        if d == 2:
            for which in range(2):
                got(whole.at[around(y, 2), k, far_part(half, which)], rs.at[o + (1, 7)[which]])
        else:
            got(block, rs.at[o + d - 1])
            which = 0 if d == 1 else 1
            part_of = whole.at[around(y, 4 - d), k, far_part(half, which)]
            i = o + (1, 7)[which]
            send(part_of, part_of, ss.at[i], rs.at[i], place(xh, xl, around(y, d), z, k))
        send(block, block, ss.at[o + 3 + d], rs.at[o + 3 + d], partner)

    def gather_own(whole, rs, half=None):
        got(whole.at[y, other, rows_of(half)], rs.at[8 * (half or 0) + 3])

    def gather_pair(whole, rs, d, half=None):
        got(whole.at[around(y, 4 - d), other, rows_of(half)], rs.at[8 * (half or 0) + 3 + d])

    def gather_end(whole, ss, half=None):
        o = 8 * (half or 0)
        for i in (0, 2, 3, 4, 5, 6):
            sent(whole.at[y, k, rows_of(half)], ss.at[o + i])
        for i in (1, 7):
            sent(whole.at[y, k, far_part(half, 0)], ss.at[o + i])

    def chip_slots(whole, l_, zz):
        return whole.at[pl.ds(8 * l_ + 2 * zz, 2)]

    def z_send(src_of, whole, ss, rs):
        for i in range(1, 8):
            core = lax.rem(k + i, 2)
            send(src_of(core), whole.at[f], ss.at[i], rs.at[i], place(xh, xl, y, around(z, i // 2), core))

    def z_got(whole, rs, dz):
        for dk in range(2):
            if dz + dk > 0:
                got(whole.at[8 * xl + 2 * around(z, 4 - dz) + lax.rem(k + dk, 2)], rs.at[2 * dz + dk])

    def beside(dz):
        return along_x(1 if dz < 2 else 3)

    def x_send(whole, ss, rs, dz):
        block = chip_slots(whole, xl, around(z, 4 - dz))
        send(block, block, ss.at[8 + dz], rs.at[8 + dz], beside(dz))

    def x_got(whole, rs, dz):
        got(chip_slots(whole, 1 - xl, around(z, 4 - dz)), rs.at[8 + dz])

    def rows_sent(whole, ss):
        for i in range(1, 8):
            sent(whole.at[f], ss.at[i])
        for dz in range(4):
            sent(chip_slots(whole, xl, around(z, 4 - dz)), ss.at[8 + dz])

    def loop_sent(ref, ss, first, last):
        def one(i, carry):
            sent(ref, ss.at[i])
            return carry

        lax.fori_loop(first, last, one, 0)

    gather_start(r.tok, r.x_all, r.s_x, r.r_x)
    z_send(lambda k_: r.gain_in, r.gain_recv, r.s_gain, r.r_gain)
    z_send(lambda k_: r.wkv_send.at[k_], r.wkv, r.s_wkv, r.r_wkv)
    send(r.pos_in, r.pos.at[k], r.s_pos.at[0], r.r_pos.at[0], partner)
    z_send(lambda k_: r.wqq_send.at[k_], r.wqq, r.s_wqq, r.r_wqq)

    is_source = lax.div(part, 2) == y
    to_core = lax.rem(part, 2)
    for i in range(4):
        piece = 4 * k + i
        here = (xl == k) & (z == i) & (to_core == k)

        @pl.when(is_source & jnp.logical_not(here))
        def _():
            there = place(xh, k, y, i, to_core)
            send(r.wo_own.at[pl.ds(32 * i, 32)], r.wo.at[pl.ds(pl.multiple_of(32 * piece, 32), 32)], r.s_wo.at[i], r.r_wo.at[0], there)
            send(r.wd_own.at[pl.ds(48 * i, 48)], r.wd.at[pl.ds(pl.multiple_of(48 * piece, 16), 48)], r.s_wd.at[i], r.r_wd.at[0], there)

        @pl.when(is_source & here)
        def _():
            r.wo[pl.ds(pl.multiple_of(32 * piece, 32), 32), :] = r.wo_own[32 * i : 32 * i + 32, :]
            r.wd[pl.ds(pl.multiple_of(48 * piece, 16), 48), :] = r.wd_own[48 * i : 48 * i + 48, :]

    def wo_rows(q):
        return r.wo.at[pl.ds(pl.multiple_of(32 * q, 32), 32)]

    def wd_rows(q):
        return r.wd.at[pl.ds(pl.multiple_of(48 * q, 16), 48)]

    def pass_on(whole, ss, rs, dz):
        z_got(whole, rs, dz)
        x_send(whole, ss, rs, dz)

    pass_on(r.gain_recv, r.s_gain, r.r_gain, 0)
    pass_on(r.wkv, r.s_wkv, r.r_wkv, 0)

    got(r.pos.at[other], r.r_pos.at[0])
    steps = lax.broadcasted_iota(jnp.int32, (BLOCK, 1), 0).astype(f32)
    for s in range(2):
        for b in range(16):
            r.posk[s, b * BLOCK : (b + 1) * BLOCK, :] = r.pos[s, 0:1, b * BLOCK : b * BLOCK + 1] + steps
    freq = r.freq[0:1, :]
    sign = r.freq[1:2, :]

    def tables(yy, carry):
        for s in range(2):
            rows = r.posk[s, pl.ds(pl.multiple_of(512 * xh + 128 * yy, 128), 128), :]
            angle = rows * freq
            r.cos_t[yy, s * 128 : (s + 1) * 128, :] = jnp.cos(angle)
            r.sin_t[yy, s * 128 : (s + 1) * 128, :] = jnp.sin(angle) * sign
        return carry

    lax.fori_loop(0, 2, tables, 0)

    for dz in (1, 3):
        pass_on(r.gain_recv, r.s_gain, r.r_gain, dz)
        pass_on(r.wkv, r.s_wkv, r.r_wkv, dz)
    for d in (1, 3):
        gather_forward(r.x_all, r.s_x, r.r_x, d)
    lax.fori_loop(2, 4, tables, 0)
    pass_on(r.gain_recv, r.s_gain, r.r_gain, 2)
    pass_on(r.wkv, r.s_wkv, r.r_wkv, 2)
    for dz in (0, 1, 3, 2):
        pass_on(r.wqq, r.s_wqq, r.r_wqq, dz)
    gather_start(r.dyt, r.dy_all, r.s_dy, r.r_dy)
    own_piece = (2 * y + k == part) & (xl == k)

    @pl.when(jnp.logical_not(own_piece))
    def _():
        got(wo_rows(part), r.r_wo.at[0])
        got(wd_rows(part), r.r_wd.at[0])

    for dz in range(1, 4):
        there = place(xh, xl, y, around(z, dz), k)
        send(wo_rows(part), wo_rows(part), r.s_wo2.at[dz], r.r_wo2.at[dz], there)
    z_send(lambda k_: r.wgu_send.at[k_], r.wgu, r.s_wgu, r.r_wgu)
    for dz in range(1, 4):
        there = place(xh, xl, y, around(z, dz), k)
        send(wd_rows(part), wd_rows(part), r.s_wd2.at[dz], r.r_wd2.at[dz], there)

    def piece_of(l_, dz):
        return 4 * l_ + around(z, 4 - dz)

    for dz in range(4):
        x_got(r.gain_recv, r.r_gain, dz)
    gains = jnp.sum(r.gain_recv[...], axis=0)
    g1 = to_row(gains, 0, 8)
    g2 = to_row(gains, 8, 8)
    gq = gains[16:17, :]
    gk = gains[17:18, :]

    def rotated(u, cos, sin):
        return u * cos + pltpu.roll(u, 64, 1) * sin

    def unrotated(u, cos, sin):
        return u * cos - pltpu.roll(u, 64, 1) * sin

    def inverse_rms(u):
        return lax.rsqrt(jnp.mean(u * u, axis=-1, keepdims=True) + norm_eps)

    kv_partner = place(1 - xh, xl, y, z, k)

    def kv_rows(s, hh, yy):
        return r.kv.at[s, pl.ds(pl.multiple_of(512 * hh + 128 * yy, 128), 128)]

    def project_keys(d):
        yy = around(y, 4 - d)
        rows = r.x_all[yy].reshape(256, D).astype(f32)
        n1 = (rows * inverse_rms(rows) * g1).astype(bf16)
        r.n1_all[yy] = n1
        kv = dot(n1, r.wkv[...].reshape(D, 256))
        raw = kv[:, 0:HEAD]
        r.qkraw[yy, :, 256:384] = raw
        local = pl.ds(pl.multiple_of(512 * xh + 128 * yy, 128), 128)
        key = rotated(raw * inverse_rms(raw) * gk, r.cos_t[yy], r.sin_t[yy]).astype(bf16)
        value = kv[:, HEAD:].astype(bf16)
        for s in range(2):
            r.kv[s, local, 0:HEAD] = key[s * 128 : (s + 1) * 128]
            r.kv[s, local, HEAD : 2 * HEAD] = value[s * 128 : (s + 1) * 128]
            send(kv_rows(s, xh, yy), kv_rows(s, xh, yy), r.s_kv.at[2 * d + s], r.r_kv.at[2 * d + s], kv_partner)

    def project_queries(yy, carry):
        qs = dot(r.n1_all[yy], r.wqq[...].reshape(D, 256))
        r.qkraw[yy, :, 0:256] = qs
        for h in range(2):
            raw = qs[:, h * HEAD : (h + 1) * HEAD]
            query = rotated(raw * inverse_rms(raw) * gq, r.cos_t[yy], r.sin_t[yy]).astype(bf16)
            for s in range(2):
                for half in range(2):
                    first = s * 128 + half * 64
                    rows = pl.ds(pl.multiple_of(64 * yy, 64), 64)
                    r.q_s[s, half, rows, h * HEAD : (h + 1) * HEAD] = query[first : first + 64]
        return carry

    gather_own(r.x_all, r.r_x)
    for dz in range(4):
        x_got(r.wkv, r.r_wkv, dz)
    project_keys(0)
    gather_pair(r.x_all, r.r_x, 1)
    project_keys(1)
    gather_forward(r.x_all, r.s_x, r.r_x, 2)
    gather_pair(r.x_all, r.r_x, 3)
    project_keys(3)
    gather_pair(r.x_all, r.r_x, 2)
    project_keys(2)
    for dz in range(4):
        x_got(r.wqq, r.r_wqq, dz)
    lax.fori_loop(0, 4, project_queries, 0)
    gather_end(r.x_all, r.s_x)

    for dz in range(4):
        if dz > 0:
            got(wo_rows(piece_of(xl, dz)), r.r_wo2.at[dz])
        block = wo_rows(piece_of(xl, dz))
        send(block, block, r.s_wo2.at[4 + dz], r.r_wo2.at[4 + dz], beside(dz))
    def rest_forward():
        for dz in range(4):
            pass_on(r.wgu, r.s_wgu, r.r_wgu, dz)
        for dz in range(4):
            if dz > 0:
                got(wd_rows(piece_of(xl, dz)), r.r_wd2.at[dz])
            block = wd_rows(piece_of(xl, dz))
            send(block, block, r.s_wd2.at[4 + dz], r.r_wd2.at[4 + dz], beside(dz))

    for d in (0, 1, 3, 2):
        for s in range(2):
            got(kv_rows(s, 1 - xh, around(y, 4 - d)), r.r_kv.at[2 * d + s])

    def lanes(half):
        return pl.ds(pl.multiple_of(256 * half, 256), 256)

    def allowed(s, half):
        return r.posk[s] <= r.pos[s, 1:2, lanes(half)]

    def attend(s, half):
        ok = allowed(s, half)
        for h in range(2):
            q = r.q_s[s, half, :, h * HEAD : (h + 1) * HEAD]
            scores = jnp.where(ok, dot_nt(r.kv[s, :, 0:HEAD], q) * SCALE, -1e30)
            top = jnp.max(scores, axis=0, keepdims=True)
            p = jnp.exp(scores - top)
            total = jnp.sum(p, axis=0, keepdims=True)
            o = dot_tn(r.kv[s, :, HEAD : 2 * HEAD], p.astype(bf16)) / total
            r.o_t[s, h * HEAD : (h + 1) * HEAD, lanes(half)] = o
            r.ob_t[s, h * HEAD : (h + 1) * HEAD, lanes(half)] = o.astype(bf16)
            r.lse[s, h, :, lanes(half)] = top + jnp.log(total)

    def reduce_first(use, p, cc, d, half=None):
        yy, rows, i = around(y, d), rows_of(half), 8 * use + 4 * (half or 0) + d
        send(p.at[yy, other, rows], cc.at[yy, rows], r.s_c.at[i], r.r_c.at[i], partner)

    def both_cores(use, p, cc, d, half):
        yy, rows, i = around(y, d), rows_of(half), 8 * use + 4 * (half or 0) + d
        got(cc.at[yy, rows], r.r_c.at[i])
        return p[yy, k, rows, :].astype(f32) + cc[yy, rows, :].astype(f32)

    def reduce_far(use, p, cc, rr, half=None):
        rows, o = rows_of(half), 12 * use + 6 * (half or 0)
        yy = around(y, 2)
        p[yy, k, rows, :] = both_cores(use, p, cc, 2, half).astype(bf16)
        for which in range(2):
            rest = far_part(half, which)
            there = place(xh, xl, around(y, 1 + 2 * which), z, k)
            send(p.at[yy, k, rest], rr.at[2, rest], r.s_r.at[o + which], r.r_r.at[o + which], there)
        for which in range(2):
            yy = around(y, 1 + 2 * which)
            p[yy, k, rows, :] = both_cores(use, p, cc, 1 + 2 * which, half).astype(bf16)
            early, i = far_part(half, 1 - which), o + 2 + which
            send(p.at[yy, k, early], rr.at[which, early], r.s_r.at[i], r.r_r.at[i], place(xh, xl, yy, z, k))

    def reduce_near(use, p, rr, half=None):
        o = 12 * use + 6 * (half or 0)
        for which in range(2):
            yy = around(y, 1 + 2 * which)
            late, i = far_part(half, which), o + 4 + which
            got(rr.at[2, late], r.r_r.at[o + which])
            p[yy, k, late, :] = (p[yy, k, late, :].astype(f32) + rr[2, late, :].astype(f32)).astype(bf16)
            send(p.at[yy, k, late], rr.at[which, late], r.s_r.at[i], r.r_r.at[i], place(xh, xl, yy, z, k))

    def reduce_third(use, p, cc, rr, half=None):
        rows, o = rows_of(half), 12 * use + 6 * (half or 0)
        total = both_cores(use, p, cc, 0, half)
        for which in range(2):
            got(rr.at[which, far_part(half, 1 - which)], r.r_r.at[o + 2 + which])
            got(rr.at[which, far_part(half, which)], r.r_r.at[o + 4 + which])
            total = total + rr[which, rows, :].astype(f32)
        return total

    def reduce_end(use, p, half=None):
        for d in range(4):
            sent(p.at[y, other, rows_of(half)], r.s_c.at[8 * use + 4 * (half or 0) + d])
        for i in range(6):
            sent(p.at[y, k, far_part(half, 0)], r.s_r.at[12 * use + 6 * (half or 0) + i])

    def out_partial(half):
        for s in range(2):
            o = r.ob_t[s, :, lanes(half)]
            r.pa[:, s, rows_of(half), :] = dot_tn(o, r.wo[...]).astype(bf16).reshape(4, 64, D)
        for d in (2, 1, 3, 0):
            reduce_first(0, r.pa, r.ca, d, half)

    attend(0, 0)
    rest_forward()
    attend(1, 0)
    for d in (1, 3):
        gather_forward(r.dy_all, r.s_dy, r.r_dy, d)
    for dz in range(4):
        got(wo_rows(piece_of(1 - xl, dz)), r.r_wo2.at[4 + dz])
    out_partial(0)
    attend(0, 1)
    reduce_far(0, r.pa, r.ca, r.ra, 0)
    gather_forward(r.dy_all, r.s_dy, r.r_dy, 2)
    attend(1, 1)
    out_partial(1)
    reduce_near(0, r.pa, r.ra, 0)
    reduce_far(0, r.pa, r.ca, r.ra, 1)

    def middle(half):
        rows = rows_of(half)
        h1 = r.tok[rows, :].astype(f32) + reduce_third(0, r.pa, r.ca, r.ra, half)
        r.h1[rows, :] = h1
        r.n2_all[y, k, rows, :] = (h1 * inverse_rms(h1) * g2).astype(bf16)
        gather_start(r.n2_all.at[y, k], r.n2_all, r.s_n2, r.r_n2, half)

    middle(0)
    reduce_near(0, r.pa, r.ra, 1)
    middle(1)

    gather_own(r.dy_all, r.r_dy)
    for d in (1, 3, 2):
        gather_pair(r.dy_all, r.r_dy, d)
    for dz in range(4):
        x_got(r.wgu, r.r_wgu, dz)
        got(wd_rows(piece_of(1 - xl, dz)), r.r_wd2.at[4 + dz])

    def two_blocks(whole, ds, half):
        blocks = [whole[around(y, d), :, rows_of(half), :].reshape(128, whole.shape[-1]) for d in ds]
        return jnp.concatenate(blocks, axis=0)

    def put_blocks(whole, ds, half, cols, value):
        for i, d in enumerate(ds):
            block = value[128 * i : 128 * (i + 1)].reshape(2, 64, value.shape[-1])
            whole[around(y, d), :, rows_of(half), cols] = block

    def feed(ds, half):
        n2 = two_blocks(r.n2_all, ds, half)
        ab = dot(n2, r.wgu[...].reshape(D, 768))
        a, b = ab[:, :384], ab[:, 384:]
        sig = jax.nn.sigmoid(a)
        silu = a * sig
        put_blocks(r.hid_all, ds, half, slice(None), (silu * b).astype(bf16))
        dhid = dot_nt(two_blocks(r.dy_all, ds, half), r.wd[...])
        da = (dhid * b * sig * (1.0 + a * (1.0 - sig))).astype(bf16)
        db = (dhid * silu).astype(bf16)
        put_blocks(r.dgu_all, ds, half, slice(0, 384), da)
        put_blocks(r.dgu_all, ds, half, slice(384, 768), db)
        dn2 = dot_nt(jnp.concatenate([da, db], axis=1), r.wgu[...].reshape(D, 768))
        put_blocks(r.pb, ds, half, slice(None), dn2.astype(bf16))
        for d in ds:
            reduce_first(1, r.pb, r.cb, d, half)

    def near_forward(whole, ss, rs, half):
        for d in (1, 3):
            gather_forward(whole, ss, rs, d, half)

    near_forward(r.n2_all, r.s_n2, r.r_n2, 0)
    for half in range(2):
        gather_own(r.n2_all, r.r_n2, half)
        gather_pair(r.n2_all, r.r_n2, 1, half)
        feed((0, 3), half)
        if half == 1:
            reduce_near(1, r.pb, r.rb, 0)
        gather_forward(r.n2_all, r.s_n2, r.r_n2, 2, half)
        if half == 0:
            near_forward(r.n2_all, r.s_n2, r.r_n2, 1)
        gather_pair(r.n2_all, r.r_n2, 3, half)
        gather_pair(r.n2_all, r.r_n2, 2, half)
        feed((2, 1), half)
        reduce_far(1, r.pb, r.cb, r.rb, half)

    def rows_at(whole, height):
        return lambda l_, z_: whole.at[pl.ds(pl.multiple_of(height * (4 * l_ + z_), 16), height)]

    def cross_z(piece, dst, ss, rs):
        for dz in (1, 3, 2):
            zz = around(z, dz)
            for l_ in range(2):
                i = 2 * (dz - 1) + l_
                send(piece(l_, zz), dst.at[dz - 1, l_], ss.at[i], rs.at[i], place(xh, xl, y, zz, k))

    def row_half(ref, h_):
        return ref.at[pl.ds(pl.multiple_of(64 * h_, 64), 64)]

    def column_half(ref, h_):
        return ref.at[:, pl.ds(pl.multiple_of(512 * h_, 512), 512)]

    def cross_x(piece, zrecv, sums, xrecv, half_of, ss, rs):
        for l_ in range(2):
            total = piece(l_, z)[...].astype(f32)
            for dz in range(1, 4):
                got(zrecv.at[dz - 1, l_], rs.at[2 * (dz - 1) + l_])
                total = total + zrecv[dz - 1, l_].astype(f32)
            sums[l_] = total.astype(bf16)
        for dx in (1, 3, 2):
            x_ = around(x, dx)
            block = half_of(sums.at[lax.rem(x_, 2)], lax.div(x_, 2))
            send(block, xrecv.at[dx - 1], ss.at[5 + dx], rs.at[5 + dx], along_x(dx))

    def cross_total(sums, xrecv, half_of, rs):
        total = half_of(sums.at[xl], xh)[...].astype(f32)
        for dx in (1, 3, 2):
            got(xrecv.at[dx - 1], rs.at[5 + dx])
            total = total + xrecv[dx - 1].astype(f32)
        return total

    def cross_x_first(whole, height, xrecv, ss, rs):
        for dx in (1, 3, 2):
            x_ = around(x, dx)
            rows = pl.ds(pl.multiple_of(4 * height * lax.rem(x_, 2), 16), 4 * height)
            block = column_half(whole.at[rows], lax.div(x_, 2))
            send(block, xrecv.at[dx - 1], ss.at[dx - 1], rs.at[dx - 1], along_x(dx))

    def cross_z_second(whole, height, xrecv, sums, zrecv, ss, rs):
        rows = pl.ds(pl.multiple_of(4 * height * xl, 16), 4 * height)
        total = column_half(whole.at[rows], xh)[...].astype(f32)
        for dx in (1, 3, 2):
            got(xrecv.at[dx - 1], rs.at[dx - 1])
            total = total + xrecv[dx - 1].astype(f32)
        sums[...] = total.astype(bf16)
        for dz in (1, 3, 2):
            zz = around(z, dz)
            block = sums.at[pl.ds(pl.multiple_of(height * zz, 16), height)]
            send(block, zrecv.at[dz - 1], ss.at[2 + dz], rs.at[2 + dz], place(xh, xl, y, zz, k))

    def cross_z_total(height, sums, zrecv, rs):
        total = sums[pl.ds(pl.multiple_of(height * z, 16), height), :].astype(f32)
        for dz in (1, 3, 2):
            got(zrecv.at[dz - 1], rs.at[2 + dz])
            total = total + zrecv[dz - 1].astype(f32)
        return total

    def rows_x_first():
        for dx in (1, 3, 2):
            x_ = around(x, dx)
            block = r.ggua.at[pl.ds(4 * lax.rem(x_, 2), 4), lax.div(x_, 2)]
            send(block, r.xgua.at[dx - 1], r.s_ggua.at[dx - 1], r.r_ggua.at[dx - 1], along_x(dx))

    def rows_z_second():
        total = r.ggua[pl.ds(4 * xl, 4), xh].astype(f32)
        for dx in (1, 3, 2):
            got(r.xgua.at[dx - 1], r.r_ggua.at[dx - 1])
            total = total + r.xgua[dx - 1].astype(f32)
        r.sgua[...] = total.astype(bf16)
        for dz in (1, 3, 2):
            zz = around(z, dz)
            send(r.sgua.at[zz], r.zgua.at[dz - 1], r.s_ggua.at[2 + dz], r.r_ggua.at[2 + dz], place(xh, xl, y, zz, k))

    def rows_z_total():
        total = r.sgua[z].astype(f32)
        for dz in (1, 3, 2):
            got(r.zgua.at[dz - 1], r.r_ggua.at[2 + dz])
            total = total + r.zgua[dz - 1].astype(f32)
        return total

    def cross_sent(zrecv, xrecv, ss):
        for i in range(6):
            sent(zrecv.at[0, 0], ss.at[i])
        for i in range(3):
            sent(xrecv.at[0], ss.at[6 + i])

    gqa_piece, ggub_piece = rows_at(r.gqa, 128), rows_at(r.ggub, 128)
    go_piece = rows_at(r.go, 32)

    def weight_gradient(left, right, out, first=0):
        def one(i, carry):
            cols = pl.ds(pl.multiple_of(256 * i, 256), 256)
            taken = pl.ds(pl.multiple_of(first + 256 * i, 256), 256)
            out[:, cols] = dot_tn(left(), right(taken)).astype(bf16)
            return carry

        lax.fori_loop(0, out.shape[1] // 256, one, 0)

    def middle_back(half):
        rows = rows_of(half)
        dn2 = reduce_third(1, r.pb, r.cb, r.rb, half)
        h1 = r.h1[rows, :]
        r2 = inverse_rms(h1)
        weighted = dn2 * g2
        back = r2 * weighted - h1 * (r2 * r2 * r2) * jnp.mean(weighted * h1, axis=-1, keepdims=True)
        dh1 = r.dyt[rows, :].astype(f32) + back
        r.dh1[rows, :] = dh1
        dg2 = jnp.sum(dn2 * h1 * r2, axis=0, keepdims=True)
        for i in range(8):
            r.dg[8 + i : 9 + i, :] += dg2[:, 128 * i : 128 * (i + 1)]
        r.x_all[y, k, rows, :] = dh1.astype(bf16)
        gather_start(r.x_all.at[y, k], r.x_all, r.s_dob, r.r_dob, half)

    ggua = dot_tn(r.n2_all[...].reshape(D, D), r.dgu_all[:, :, :, 0:256].reshape(D, 256))
    r.ggua[...] = ggua.astype(bf16).reshape(8, 2, 64, 256)
    rows_x_first()
    weight_gradient(
        lambda: r.n2_all[...].reshape(D, D),
        lambda cols: r.dgu_all[:, :, :, cols].reshape(D, 256),
        r.ggub,
        256,
    )
    cross_z(ggub_piece, r.zgub, r.s_ggub, r.r_ggub)
    reduce_near(1, r.pb, r.rb, 1)
    middle_back(0)
    weight_gradient(
        lambda: r.hid_all[...].reshape(D, 384),
        lambda cols: r.dy_all[:, :, :, cols].reshape(D, 256),
        r.gd,
    )
    cross_x_first(r.gd, 48, r.xd, r.s_gd, r.r_gd)
    middle_back(1)

    other_half = place(1 - xh, xl, y, z, k)

    def rows_exchange(total, hold, ss, rs):
        hold[xh] = total.astype(bf16)
        send(hold.at[xh], hold.at[xh], ss.at[8], rs.at[8], other_half)

    def rows_spread(hold, final, ss, rs):
        for which in range(2):
            h = xh if which == 0 else 1 - xh
            if which == 1:
                got(hold.at[h], rs.at[8])
            for i in (2, 1, 3):
                send(hold.at[h], final.at[t], ss.at[4 * which + i], rs.at[t], place(xh, xl, around(y, i), z, h))

            @pl.when(k != h)
            def _():
                send(hold.at[h], final.at[t], ss.at[4 * which], rs.at[t], partner)

            @pl.when(k == h)
            def _():
                final[t] = hold[h]

    def rows_spread_sent(hold, ss):
        sent(hold.at[0], ss.at[8])
        for which in range(2):
            h = xh if which == 0 else 1 - xh
            for i in range(1, 4):
                sent(hold.at[0], ss.at[4 * which + i])

            @pl.when(k != h)
            def _():
                sent(hold.at[0], ss.at[4 * which])

    def rows_spread_got(final, rs):
        def one(i, carry):
            @pl.when(i != t)
            def _():
                got(final.at[i], rs.at[i])

            return carry

        lax.fori_loop(0, 8, one, 0)

    def block_exchange(total, hold, ss, rs):
        column_half(hold, xh)[...] = total.astype(bf16)
        send(column_half(hold, xh), column_half(hold, xh), ss.at[4], rs.at[4], other_half)

    def block_spread(hold, final, height, ss, rs):
        got(column_half(hold, 1 - xh), rs.at[4])
        rows = pl.ds(pl.multiple_of(height * z, 16), height)

        def to(i):
            there = place(xh, lax.div(t, 4), around(y, i), lax.rem(t, 4), xl)
            send(hold, final.at[rows], ss.at[i], rs.at[z], there)

        for i in (2, 1, 3):
            to(i)

        @pl.when(jnp.logical_not(home))
        def _():
            to(0)

        @pl.when(home)
        def _():
            final[rows, :] = hold[...]

    def block_spread_sent(hold, ss):
        sent(column_half(hold, 0), ss.at[4])
        for i in range(1, 4):
            sent(hold, ss.at[i])

        @pl.when(jnp.logical_not(home))
        def _():
            sent(hold, ss.at[0])

    def block_spread_got(final, height, rs):
        def one(i, carry):
            @pl.when((i != z) | jnp.logical_not(home))
            def _():
                got(final.at[pl.ds(pl.multiple_of(height * i, 16), height)], rs.at[i])

            return carry

        lax.fori_loop(0, 4, one, 0)

    def norm_back(value, gain, grad):
        inverse = inverse_rms(value)
        w = grad * gain
        back = inverse * w - value * (inverse * inverse * inverse) * jnp.mean(w * value, axis=-1, keepdims=True)
        return back, jnp.sum(grad * value * inverse, axis=0, keepdims=True)

    def attend_back(half, s):
        rows = rows_of(half)
        do_s = dot_nt(r.wo[...], r.x_all[:, s, rows, :].reshape(256, D)).astype(bf16)
        prod = do_s.astype(f32) * r.o_t[s, :, lanes(half)]
        r.do_t[s, :, lanes(half)] = do_s
        ok = allowed(s, half)
        keys, values = r.kv[s, :, 0:HEAD], r.kv[s, :, HEAD : 2 * HEAD]
        mine = pl.ds(s * 128 + 64 * half, 64)
        cos = r.cos_t[:, mine, :].reshape(256, HEAD)
        sin = r.sin_t[:, mine, :].reshape(256, HEAD)
        for h in range(2):
            head = slice(h * HEAD, (h + 1) * HEAD)
            q = r.q_s[s, half, :, head]
            do = r.do_t[s, head, lanes(half)]
            delta = jnp.sum(prod[head], axis=0, keepdims=True)
            scores = dot_nt(keys, q) * SCALE
            p = jnp.where(ok, jnp.exp(scores - r.lse[s, h, :, lanes(half)]), 0.0)
            ds = (p * (dot(values, do) - delta)).astype(bf16)
            dv = dot_nt(p.astype(bf16), do)
            dk = dot(ds, q) * SCALE
            if half == 0 and h == 0:
                r.dkv[s, :, HEAD : 2 * HEAD] = dv
                r.dkv[s, :, 0:HEAD] = dk
            else:
                r.dkv[s, :, HEAD : 2 * HEAD] += dv
                r.dkv[s, :, 0:HEAD] += dk
            dq = (dot_tn(keys, ds) * SCALE).T
            raw = r.qkraw[:, mine, head].reshape(256, HEAD)
            back, gain_grad = norm_back(raw, gq, unrotated(dq, cos, sin))
            r.dqkv[:, mine, head] = back.astype(bf16).reshape(4, 64, HEAD)
            r.dg[16:17, :] += gain_grad

    def gather_rest(half):
        gather_forward(r.x_all, r.s_dob, r.r_dob, 2, half)
        gather_own(r.x_all, r.r_dob, half)
        for d in (1, 3, 2):
            gather_pair(r.x_all, r.r_dob, d, half)

    for half in range(2):
        reduce_end(0, r.pa, half)

    def down_partial(i, carry):
        hid = r.hid_all[i].reshape(256, 384)
        r.pa[i] = dot(hid, r.wd[...]).astype(bf16).reshape(2, 128, D)
        return carry

    near_forward(r.x_all, r.s_dob, r.r_dob, 0)
    lax.fori_loop(0, 4, down_partial, 0)
    for d in (2, 1, 3, 0):
        reduce_first(2, r.pa, r.ca, d)
    gather_rest(0)
    attend_back(0, 0)
    near_forward(r.x_all, r.s_dob, r.r_dob, 1)
    attend_back(0, 1)
    reduce_far(2, r.pa, r.ca, r.ra)
    rows_z_second()
    cross_x(ggub_piece, r.zgub, r.sgub, r.xgub, row_half, r.s_ggub, r.r_ggub)
    gather_rest(1)
    for s in range(2):
        attend_back(1, s)
        if s == 0:
            reduce_near(2, r.pa, r.ra)
            cross_z_second(r.gd, 48, r.xd, r.sd, r.zd, r.s_gd, r.r_gd)
        r.dkv_send[s] = r.dkv[s, pl.ds(pl.multiple_of(512 * (1 - xh), 512), 512), :].astype(bf16)
        send(r.dkv_send.at[s], r.dkv_recv.at[s], r.s_dkv.at[s], r.r_dkv.at[s], kv_partner)
        if s == 0:
            gu_total = jnp.concatenate([rows_z_total(), cross_total(r.sgub, r.xgub, row_half, r.r_ggub)], axis=1)
            rows_exchange(gu_total, r.hgu, r.s_fgu, r.r_fgu)

    def qkv_gradient(first, out, weight):
        grad = dot_tn(r.n1_all[...].reshape(D, D), r.dqkv[:, :, first : first + 256].reshape(D, 256))
        out[...] = grad.astype(bf16)
        prod = grad * weight[...].reshape(D, 256).astype(f32)
        return prod[:, 0:128] + prod[:, 128:256]

    r.wdot[...] = qkv_gradient(0, r.gqa, r.wqq)
    cross_z(gqa_piece, r.zqa, r.s_gqa, r.r_gqa)

    def out_gradient(i, carry):
        cols = pl.ds(pl.multiple_of(256 * i, 256), 256)
        total = jnp.zeros((256, 256), f32)
        for s in range(2):
            for half in range(2):
                rows = r.x_all[:, s, rows_of(half), cols].reshape(256, 256)
                total = total + dot(r.ob_t[s, :, lanes(half)], rows)
        r.go[:, cols] = total.astype(bf16)
        return carry

    lax.fori_loop(0, 4, out_gradient, 0)
    cross_z(go_piece, r.zo, r.s_go, r.r_go)

    def cross(i, sign):
        dx, dz = lax.div(i, 4), lax.rem(i, 4)
        x_, z_ = lax.rem(x + 4 + sign * dx, 4), lax.rem(z + 4 + sign * dz, 4)
        return lax.div(x_, 2), lax.rem(x_, 2), z_

    def direct_piece(whole, h_, p_):
        return whole.at[pl.ds(pl.multiple_of(128 * p_ + 64 * h_, 64), 64)]

    def direct_send(whole, dst, ss, rs):
        def one(i, carry):
            h_, l_, z_ = cross(i, 1)
            send(direct_piece(whole, h_, 4 * l_ + z_), dst.at[i], ss.at[i], rs.at[i], place(h_, l_, y, z_, k))
            return carry

        lax.fori_loop(1, 16, one, 0)

    def direct_sum(whole, dst, rs):
        def one(i, total):
            got(dst.at[i], rs.at[i])
            return total + dst[i].astype(f32)

        return lax.fori_loop(1, 16, one, direct_piece(whole, xh, part)[...].astype(f32))

    def direct_spread(total, hold, final, ss, rs):
        hold[...] = total.astype(bf16)

        def one(i, carry):
            there = place(lax.rem(xh + lax.div(i, 4), 2), xl, lax.rem(y + i, 4), z, xh)

            @pl.when((i > 0) | (k != xh))
            def _():
                send(hold, final.at[t], ss.at[i], rs.at[t], there)

            return carry

        lax.fori_loop(0, 8, one, 0)

        @pl.when(k == xh)
        def _():
            final[t] = hold[...]

    def direct_spread_sent(hold, ss):
        def one(i, carry):
            @pl.when((i > 0) | (k != xh))
            def _():
                sent(hold, ss.at[i])

            return carry

        lax.fori_loop(0, 8, one, 0)

    def direct_spread_got(final, rs):
        def one(i, carry):
            @pl.when((i != t) | (k != xh))
            def _():
                got(final.at[i], rs.at[i])

            return carry

        lax.fori_loop(0, 8, one, 0)

    block_exchange(cross_z_total(48, r.sd, r.zd, r.r_gd), r.hd, r.s_fd, r.r_fd)
    rows_spread(r.hgu, r.fgu, r.s_fgu, r.r_fgu)
    r.out_tok[...] = (r.h1[...] + reduce_third(2, r.pa, r.ca, r.ra)).astype(bf16)
    block_spread(r.hd, r.fd, 48, r.s_fd, r.r_fd)

    for half in range(2):
        reduce_end(1, r.pb, half)
    for s in range(2):
        got(r.dkv_recv.at[s], r.r_dkv.at[s])

    def key_back(yy, carry):
        rows = pl.ds(pl.multiple_of(512 * xh + 128 * yy, 128), 128)
        local = pl.ds(pl.multiple_of(128 * yy, 128), 128)
        grads = [r.dkv[s, rows, :] + r.dkv_recv[s, local, :].astype(f32) for s in range(2)]
        both = jnp.concatenate(grads, axis=0)
        du = unrotated(both[:, 0:HEAD], r.cos_t[yy], r.sin_t[yy])
        back, gain_grad = norm_back(r.qkraw[yy, :, 256:384], gk, du)
        r.dqkv[yy, :, 256:384] = back.astype(bf16)
        r.dqkv[yy, :, 384:512] = both[:, HEAD : 2 * HEAD].astype(bf16)
        r.dg[17:18, :] += gain_grad
        return carry

    lax.fori_loop(0, 4, key_back, 0)
    wdot = r.wdot[...] + qkv_gradient(256, r.gqb, r.wkv)
    direct_send(r.gqb, r.rqb, r.s_gqb, r.r_gqb)
    dg1 = jnp.sum(wdot.T, axis=0, keepdims=True) / g1
    for i in range(8):
        r.dg[i : i + 1, :] = dg1[:, 128 * i : 128 * (i + 1)]
    for i in range(1, 8):
        there = place(xh, xl, around(y, i // 2), z, lax.rem(k + i, 2))
        send(r.dg, r.dg_r1.at[i], r.s_dg1.at[i], r.r_dg1.at[i], there)
    for d in (2, 1, 3, 0):
        yy = around(y, d)
        dn1 = dot_nt(r.dqkv[yy, :, 0:256], r.wqq[...].reshape(D, 256))
        dn1 = dn1 + dot_nt(r.dqkv[yy, :, 256:512], r.wkv[...].reshape(D, 256))
        r.pb[yy] = dn1.astype(bf16).reshape(2, 128, D)
        reduce_first(3, r.pb, r.cb, d)
    reduce_far(3, r.pb, r.cb, r.rb)
    cross_x(gqa_piece, r.zqa, r.sqa, r.xqa, row_half, r.s_gqa, r.r_gqa)
    cross_x(go_piece, r.zo, r.so, r.xo, column_half, r.s_go, r.r_go)
    total = r.dg[...]
    for i in range(1, 8):
        got(r.dg_r1.at[i], r.r_dg1.at[i])
        total = total + r.dg_r1[i]
    r.dg_s[0] = total
    for dz in range(1, 4):
        send(r.dg_s.at[0], r.dg_r2.at[dz - 1], r.s_dg2.at[dz - 1], r.r_dg2.at[dz - 1], place(xh, xl, y, around(z, dz), k))
    reduce_near(3, r.pb, r.rb)
    direct_spread(direct_sum(r.gqb, r.rqb, r.r_gqb), r.hqb, r.fqb, r.s_fqb, r.r_fqb)
    rows_exchange(cross_total(r.sqa, r.xqa, row_half, r.r_gqa), r.hqa, r.s_fqa, r.r_fqa)
    block_exchange(cross_total(r.so, r.xo, column_half, r.r_go), r.ho, r.s_fo, r.r_fo)
    for dz in range(1, 4):
        got(r.dg_r2.at[dz - 1], r.r_dg2.at[dz - 1])
        total = total + r.dg_r2[dz - 1]
    r.dg_s[1] = total
    for dx in range(1, 4):
        send(r.dg_s.at[1], r.dg_r2.at[2 + dx], r.s_dg2.at[2 + dx], r.r_dg2.at[2 + dx], along_x(dx))
    rows_spread(r.hqa, r.fqa, r.s_fqa, r.r_fqa)
    block_spread(r.ho, r.fo, 32, r.s_fo, r.r_fo)

    dn1 = reduce_third(3, r.pb, r.cb, r.rb)
    rows = r.tok[...].astype(f32)
    back, unused = norm_back(rows, g1, dn1)
    r.dtok[...] = (r.dh1[...] + back).astype(bf16)

    block_spread_got(r.fd, 48, r.r_fd)
    r.g_dn[...] = r.fd[...]
    rows_spread_got(r.fgu, r.r_fgu)
    for i in range(8):
        r.g_gu[:, 384 * i : 384 * (i + 1)] = r.fgu[i, :, 0:384]
        r.g_gu[:, 3072 + 384 * i : 3072 + 384 * (i + 1)] = r.fgu[i, :, 384:768]
    block_spread_got(r.fo, 32, r.r_fo)
    r.g_out[...] = r.fo[...]
    rows_spread_got(r.fqa, r.r_fqa)
    for i in range(8):
        r.g_qkv[:, 256 * i : 256 * (i + 1)] = r.fqa[i]
    for dx in range(1, 4):
        got(r.dg_r2.at[2 + dx], r.r_dg2.at[2 + dx])
        total = total + r.dg_r2[2 + dx]
    r.g_gain[...] = total
    direct_spread_got(r.fqb, r.r_fqb)
    for i in range(8):
        r.g_qkv[:, 2048 + 128 * i : 2048 + 128 * (i + 1)] = r.fqb[i, :, 0:128]
        r.g_qkv[:, 3072 + 128 * i : 3072 + 128 * (i + 1)] = r.fqb[i, :, 128:256]

    gather_end(r.dy_all, r.s_dy)
    for half in range(2):
        gather_end(r.n2_all, r.s_n2, half)
        gather_end(r.x_all, r.s_dob, half)
    sent(r.pos_in, r.s_pos.at[0])
    for whole, ss in ((r.gain_recv, r.s_gain), (r.wqq, r.s_wqq), (r.wkv, r.s_wkv), (r.wgu, r.s_wgu)):
        rows_sent(whole, ss)
    for i in range(4):
        here = (xl == k) & (z == i) & (to_core == k)

        @pl.when(is_source & jnp.logical_not(here))
        def _():
            sent(r.wo_own.at[pl.ds(32 * i, 32)], r.s_wo.at[i])
            sent(r.wd_own.at[pl.ds(48 * i, 48)], r.s_wd.at[i])

    loop_sent(wo_rows(part), r.s_wo2, 1, 8)
    loop_sent(wd_rows(part), r.s_wd2, 1, 8)
    loop_sent(r.kv.at[0, pl.ds(0, 128)], r.s_kv, 0, 8)
    reduce_end(2, r.pa)
    reduce_end(3, r.pb)
    for s in range(2):
        sent(r.dkv_send.at[s], r.s_dkv.at[s])
    cross_sent(r.zqa, r.xqa, r.s_gqa)
    loop_sent(direct_piece(r.gqb, xh, part), r.s_gqb, 1, 16)
    cross_sent(r.zgub, r.xgub, r.s_ggub)
    for i in range(3):
        sent(r.xgua.at[0], r.s_ggua.at[i])
        sent(r.zgua.at[0], r.s_ggua.at[3 + i])
    cross_sent(r.zo, r.xo, r.s_go)
    for i in range(3):
        sent(r.xd.at[0], r.s_gd.at[i])
        sent(r.zd.at[0], r.s_gd.at[3 + i])
    for hold, ss in ((r.hqa, r.s_fqa), (r.hgu, r.s_fgu)):
        rows_spread_sent(hold, ss)
    direct_spread_sent(r.hqb, r.s_fqb)
    block_spread_sent(r.ho, r.s_fo)
    block_spread_sent(r.hd, r.s_fd)
    loop_sent(r.dg, r.s_dg1, 1, 8)
    loop_sent(r.dg_s.at[0], r.s_dg2, 0, 6)


def layer(*args):
    vmem = pl.BlockSpec(memory_space=pltpu.VMEM)
    hbm = pl.BlockSpec(memory_space=pl.ANY)
    specs = [hbm if far else vmem for far in INPUTS.values()]
    return pl.pallas_call(
        layer_kernel,
        out_shape=[jax.ShapeDtypeStruct(shape, kind) for shape, kind in OUTPUTS.values()],
        in_specs=specs,
        out_specs=[vmem] * len(OUTPUTS),
        scratch_shapes=[pltpu.VMEM(shape, kind) for shape, kind in BUFFERS.values()]
        + [pltpu.SemaphoreType.DMA((count,)) for count in SEMAPHORES.values()],
        compiler_params=pltpu.CompilerParams(
            collective_id=0, has_side_effects=True, vmem_limit_bytes=62 << 20
        ),
        name="layer",
    )(*args)


def adam_update(weight, moment, square, grad, rate, decay):
    moment_new = beta_first * moment + (1.0 - beta_first) * grad
    square_new = beta_second * square + (1.0 - beta_second) * grad * grad
    fix_first = 1.0 - beta_first**STEP
    fix_second = 1.0 - beta_second**STEP
    step = moment_new / fix_first / (jnp.sqrt(square_new / fix_second) + adam_eps)
    return (weight - rate * (step + decay * weight), moment_new, square_new)


def on_device(
    tokens, d_out, block_ids,
    w_qkv, w_out, w_gate_up, w_down, gains,
    moment_qkv, moment_out, moment_gate_up, moment_down, moment_gains,
    square_qkv, square_out, square_gate_up, square_down, square_gains,
):
    f = lax.axis_index("fsdp")
    starts = block_ids[0].astype(f32) * BLOCK
    spots = starts[:, None] + jnp.arange(BLOCK, dtype=f32)[None, :]
    mine = lax.dynamic_slice(spots, (8 * lax.div(lax.axis_index("ctx"), 4), 0), (8, BLOCK))
    mine = mine.reshape(4, 2, BLOCK).transpose(1, 0, 2).reshape(1, 512)
    positions = jnp.concatenate([spots.reshape(1, D), jnp.tile(mine, (7, 2))], axis=0)
    gain_rows = lax.dynamic_update_slice(
        jnp.zeros((24 * 128,), f32), gains.astype(bf16).astype(f32), (f * 144,)
    ).reshape(24, 128)
    half = rope_base ** (-(np.arange(64, dtype=np.float32) * np.float32(2.0 / HEAD)))
    table = np.zeros((8, 128), np.float32)
    table[0] = np.concatenate([half, half])
    table[1] = np.concatenate([-np.ones(64), np.ones(64)])
    out_tok, dtok, g_qkv, g_out, g_gu, g_dn, g_gain = layer(
        tokens[0], d_out[0], positions, gain_rows, jnp.asarray(table), w_qkv, w_out, w_gate_up, w_down
    )
    grad_gains = lax.dynamic_slice(g_gain.reshape(24 * 128), (f * 144,), (144,))
    grads = (g_qkv, g_out, g_gu, g_dn, grad_gains)
    masters = (w_qkv, w_out, w_gate_up, w_down, gains)
    moments = (moment_qkv, moment_out, moment_gate_up, moment_down, moment_gains)
    squares = (square_qkv, square_out, square_gate_up, square_down, square_gains)
    rates = (0.03, 0.3, 0.03, 0.03, 0.5)
    decays = (decay_rate, decay_rate, decay_rate, decay_rate, 0.0)
    updates = [
        adam_update(masters[i], moments[i], squares[i], grads[i].astype(f32), rates[i], decays[i])
        for i in range(5)
    ]
    return (
        out_tok[None],
        dtok[None],
        *(u[0] for u in updates),
        *(u[1] for u in updates),
        *(u[2] for u in updates),
    )


def solution(mesh):
    rows, flat = P("fsdp", None), P("fsdp")
    tokens = P("fsdp", "ctx", None)
    state = (rows, rows, rows, rows, flat)
    return jax.shard_map(
        on_device,
        mesh=mesh,
        in_specs=(tokens, tokens, rows) + state * 3,
        out_specs=(tokens, tokens) + state * 3,
        check_vma=False,
    )
```

```python
import math
import types

import jax
import jax.numpy as jnp
import numpy as np
from jax import lax
from jax.experimental import pallas as pl
from jax.experimental.pallas import tpu as pltpu
from jax.sharding import PartitionSpec as P

D = 1024
HEAD = 128
STEP = 10
BLOCK = 64
norm_eps = 1e-06
rope_base = 1000000.0
beta_first = 0.9
beta_second = 0.95
adam_eps = 1e-08
decay_rate = 0.1
SCALE = 1.0 / math.sqrt(HEAD)

f32 = jnp.float32
bf16 = jnp.bfloat16
MESH = pl.DeviceIdType.MESH

INPUTS = dict(
    tok=False, dyt=False, pos_in=False, gain_in=False, freq=False, wqkv_f=True, wo_f=False, wgu_f=True, wd_f=False
)
OUTPUTS = dict(
    out_tok=((128, D), bf16),
    dtok=((128, D), bf16),
    g_qkv=((64, 4096), bf16),
    g_out=((128, D), bf16),
    g_gu=((64, 6144), bf16),
    g_dn=((192, D), bf16),
    g_gain=((24, 128), f32),
)
BUFFERS = dict(
    x_all=((4, 2, 128, D), bf16),
    dy_all=((4, 2, 128, D), bf16),
    n2_all=((4, 2, 128, D), bf16),
    n1_all=((4, 256, D), bf16),
    xo_all=((4, 2, 128, D), bf16),
    n1o_all=((4, 256, D), bf16),
    cos_o=((4, 256, HEAD), f32),
    sin_o=((4, 256, HEAD), f32),
    kraw_o=((4, 256, HEAD), f32),
    wq_f=((2, 64, 512), f32),
    wgu_fs=((2, 64, 768), f32),
    wqq_send=((2, 64, 256), bf16),
    wkv_send=((2, 64, 256), bf16),
    wgu_send=((2, 64, 768), bf16),
    wo_own=((128, D), bf16),
    wd_own=((192, D), bf16),
    wqq=((16, 64, 256), bf16),
    wkv=((16, 64, 256), bf16),
    wgu=((16, 64, 768), bf16),
    wo=((256, D), bf16),
    wd=((384, D), bf16),
    gain_recv=((16, 24, 128), f32),
    pos=((2, 8, D), f32),
    posk=((2, D, 1), f32),
    cos_t=((4, 256, HEAD), f32),
    sin_t=((4, 256, HEAD), f32),
    qkraw=((4, 256, 384), f32),
    q_s=((2, 2, 256, 256), bf16),
    kv=((2, D, 256), bf16),
    o_t=((2, 256, 512), f32),
    ob_t=((2, 256, 512), bf16),
    lse=((2, 2, 1, 512), f32),
    pa=((4, 2, 128, D), bf16),
    pb=((4, 2, 128, D), bf16),
    ca=((4, 128, D), bf16),
    cb=((4, 128, D), bf16),
    ra=((3, 128, D), bf16),
    rb=((3, 128, D), bf16),
    h1=((128, D), f32),
    dh1=((128, D), f32),
    hid_all=((4, 2, 128, 384), bf16),
    dgu_all=((4, 2, 128, 768), bf16),
    do_t=((2, 256, 512), bf16),
    delta=((2, 2, 1, 512), f32),
    dkv=((2, D, 256), f32),
    dkv_o=((4, 256, 256), bf16),
    dkv_recv=((4, 256, 256), bf16),
    go_sum=((256, D), f32),
    dqkv=((4, 256, 512), bf16),
    gqa=((D, 256), bf16),
    gqb=((D, 256), bf16),
    ggua=((8, 2, 64, 256), bf16),
    ggub=((D, 512), bf16),
    go=((256, D), bf16),
    gd=((384, D), bf16),
    zqa=((3, 2, 128, 256), bf16),
    zqb=((3, 2, 128, 256), bf16),
    zgua=((3, 64, 256), bf16),
    zgub=((3, 2, 128, 512), bf16),
    zo=((3, 2, 32, D), bf16),
    zd=((3, 48, 512), bf16),
    sqa=((2, 128, 256), bf16),
    sqb=((2, 128, 256), bf16),
    sgua=((4, 64, 256), bf16),
    sgub=((2, 128, 512), bf16),
    so=((2, 32, D), bf16),
    sd=((192, 512), bf16),
    xqa=((3, 64, 256), bf16),
    xqb=((3, 64, 256), bf16),
    xgua=((3, 4, 64, 256), bf16),
    xgub=((3, 64, 512), bf16),
    xo=((3, 32, 512), bf16),
    xd=((3, 192, 512), bf16),
    hqa=((2, 64, 256), bf16),
    hqb=((64, 256), bf16),
    hgu=((2, 64, 768), bf16),
    ho=((32, D), bf16),
    hd=((48, D), bf16),
    yo=((3, 32, D), bf16),
    yd=((3, 48, D), bf16),
    fqa=((8, 64, 256), bf16),
    fqb=((8, 64, 256), bf16),
    fgu=((8, 64, 768), bf16),
    fo=((128, D), bf16),
    fd=((192, D), bf16),
    dg=((24, 128), f32),
    dg_r1=((8, 24, 128), f32),
    dg_s=((2, 24, 128), f32),
    dg_r2=((6, 24, 128), f32),
)
SEMAPHORES = dict(
    ld=16,
    s_x=8, r_x=8,
    s_dy=8, r_dy=8,
    s_n2=16, r_n2=16,
    s_dob=16, r_dob=16,
    s_pos=1, r_pos=1,
    s_gain=12, r_gain=12,
    s_wqq=12, r_wqq=12,
    s_wkv=12, r_wkv=12,
    s_wgu=12, r_wgu=12,
    s_wo=4, r_wo=1, s_wd=4, r_wd=1,
    s_wo2=8, r_wo2=8, s_wd2=8, r_wd2=8,
    s_xo=9, r_xo=9,
    s_c=32, r_c=32,
    s_r=48, r_r=48,
    s_dkv=2, r_dkv=2,
    s_gqa=9, r_gqa=9,
    s_gqb=9, r_gqb=9,
    s_ggua=6, r_ggua=6,
    s_ggub=9, r_ggub=9,
    s_go=9, r_go=9,
    s_gd=6, r_gd=6,
    s_fqa=9, r_fqa=9,
    s_fqb=8, r_fqb=8,
    s_fgu=9, r_fgu=9,
    s_fo=9, r_fo=9,
    s_fd=9, r_fd=9,
    s_dg1=8, r_dg1=8,
    s_dg2=6, r_dg2=6,
)


def dot(a, b):
    return jnp.dot(a, b, preferred_element_type=f32)


def dot_nt(a, b):
    return lax.dot_general(a, b, (((1,), (1,)), ((), ())), preferred_element_type=f32)


def dot_tn(a, b):
    return lax.dot_general(a, b, (((0,), (0,)), ((), ())), preferred_element_type=f32)


def to_row(g, first, count):
    return jnp.concatenate([g[first + i : first + i + 1, :] for i in range(count)], axis=1)


def layer_kernel(*refs):
    names = [*INPUTS, *OUTPUTS, *BUFFERS, *SEMAPHORES]
    r = types.SimpleNamespace(**dict(zip(names, refs, strict=True)))

    c = lax.axis_index("ctx")
    f = lax.axis_index("fsdp")
    xh, y = lax.div(c, 4), lax.rem(c, 4)
    xl, z, k = lax.div(f, 8), lax.rem(lax.div(f, 2), 4), lax.rem(f, 2)
    x = 2 * xh + xl
    part = 4 * xl + z
    t = 2 * y + k
    other = 1 - k

    def place(xh_, xl_, y_, z_, k_):
        return (xh_ * 4 + y_, xl_ * 8 + z_ * 2 + k_)

    partner = place(xh, xl, y, z, other)

    def around(value, step):
        return lax.rem(value + step, 4)

    def copy(src, dst, ss, rs, device):
        return pltpu.make_async_remote_copy(
            src_ref=src, dst_ref=dst, send_sem=ss, recv_sem=rs,
            device_id=device, device_id_type=MESH,
        )

    def send(src, dst, ss, rs, device):
        copy(src, dst, ss, rs, device).start()

    def got(ref, rs):
        copy(ref, ref, rs, rs, partner).wait_recv()

    def sent(ref, ss):
        copy(ref, ref, ss, ss, partner).wait_send()

    loads = []

    def load(src, dst):
        one = pltpu.make_async_copy(src, dst, r.ld.at[len(loads)])
        one.start()
        loads.append(one)

    for i in range(2):
        ti = 2 * y + i
        load(r.wqkv_f.at[:, pl.ds(pl.multiple_of(256 * ti, 256), 256)], r.wq_f.at[i, :, pl.ds(0, 256)])
        load(r.wqkv_f.at[:, pl.ds(pl.multiple_of(2048 + 128 * ti, 128), 128)], r.wq_f.at[i, :, pl.ds(256, 128)])
        load(r.wqkv_f.at[:, pl.ds(pl.multiple_of(3072 + 128 * ti, 128), 128)], r.wq_f.at[i, :, pl.ds(384, 128)])
    for i in range(2):
        ti = 2 * y + i
        load(r.wgu_f.at[:, pl.ds(pl.multiple_of(384 * ti, 128), 384)], r.wgu_fs.at[i, :, pl.ds(0, 384)])
        load(r.wgu_f.at[:, pl.ds(pl.multiple_of(3072 + 384 * ti, 128), 384)], r.wgu_fs.at[i, :, pl.ds(384, 384)])

    barrier = pltpu.get_barrier_semaphore()

    def greet(device):
        pl.semaphore_signal(barrier, inc=1, device_id=device, device_id_type=MESH)

    def greet_plane(i, carry):
        greet(place(xh, lax.rem(xl + lax.div(i, 8), 2), y, around(z, lax.rem(lax.div(i, 2), 4)), lax.rem(k + i, 2)))
        return carry

    def along_x(d):
        x_ = around(x, d)
        return place(lax.div(x_, 2), lax.rem(x_, 2), y, z, k)

    for i in range(1, 8):
        greet(place(xh, xl, around(y, i // 2), z, lax.rem(k + i, 2)))
    for i in range(8):
        greet(place(1 - xh, xl, around(y, i // 2), z, lax.rem(k + i, 2)))
    lax.fori_loop(1, 16, greet_plane, 0)
    for d in range(1, 4):
        greet(along_x(d))

    for one in loads:
        one.wait()
    r.wqq_send[...] = r.wq_f[:, :, 0:256].astype(bf16)
    r.wkv_send[...] = r.wq_f[:, :, 256:512].astype(bf16)
    r.wgu_send[...] = r.wgu_fs[...].astype(bf16)
    r.wo_own[...] = r.wo_f[...].astype(bf16)
    r.wd_own[...] = r.wd_f[...].astype(bf16)
    r.wqq[f] = r.wqq_send[k]
    r.wkv[f] = r.wkv_send[k]
    r.wgu[f] = r.wgu_send[k]
    r.gain_recv[f] = r.gain_in[...]
    r.x_all[y, k] = r.tok[...]
    r.dy_all[y, k] = r.dyt[...]
    r.pos[k] = r.pos_in[...]
    r.dg[...] = jnp.zeros((24, 128), f32)
    pl.semaphore_wait(barrier, 33)

    def rows_of(half):
        return pl.ds(0, 128) if half is None else pl.ds(64 * half, 64)

    def far_part(half, which):
        size = 64 if half is None else 32
        return pl.ds((0 if half is None else 64 * half) + size * which, size)

    def gather_start(src, whole, ss, rs, half=None):
        rows, o = rows_of(half), 8 * (half or 0)
        for d in (1, 3):
            send(src.at[rows], whole.at[y, k, rows], ss.at[o + d - 1], rs.at[o + d - 1], place(xh, xl, around(y, d), z, k))
        send(src.at[rows], whole.at[y, k, rows], ss.at[o + 3], rs.at[o + 3], partner)

    def gather_forward(whole, ss, rs, d, half=None):
        rows, o = rows_of(half), 8 * (half or 0)
        block = whole.at[around(y, 4 - d), k, rows]
        if d == 2:
            for which in range(2):
                got(whole.at[around(y, 2), k, far_part(half, which)], rs.at[o + (1, 7)[which]])
        else:
            got(block, rs.at[o + d - 1])
            which = 0 if d == 1 else 1
            part_of = whole.at[around(y, 4 - d), k, far_part(half, which)]
            i = o + (1, 7)[which]
            send(part_of, part_of, ss.at[i], rs.at[i], place(xh, xl, around(y, d), z, k))
        send(block, block, ss.at[o + 3 + d], rs.at[o + 3 + d], partner)

    def gather_own(whole, rs, half=None):
        got(whole.at[y, other, rows_of(half)], rs.at[8 * (half or 0) + 3])

    def gather_pair(whole, rs, d, half=None):
        got(whole.at[around(y, 4 - d), other, rows_of(half)], rs.at[8 * (half or 0) + 3 + d])

    def gather_end(whole, ss, half=None):
        o = 8 * (half or 0)
        for i in (0, 2, 3, 4, 5, 6):
            sent(whole.at[y, k, rows_of(half)], ss.at[o + i])
        for i in (1, 7):
            sent(whole.at[y, k, far_part(half, 0)], ss.at[o + i])

    def chip_slots(whole, l_, zz):
        return whole.at[pl.ds(8 * l_ + 2 * zz, 2)]

    def z_send(src_of, whole, ss, rs):
        for i in range(1, 8):
            core = lax.rem(k + i, 2)
            send(src_of(core), whole.at[f], ss.at[i], rs.at[i], place(xh, xl, y, around(z, i // 2), core))

    def z_got(whole, rs, dz):
        for dk in range(2):
            if dz + dk > 0:
                got(whole.at[8 * xl + 2 * around(z, 4 - dz) + lax.rem(k + dk, 2)], rs.at[2 * dz + dk])

    def beside(dz):
        return along_x(1 if dz < 2 else 3)

    def x_send(whole, ss, rs, dz):
        block = chip_slots(whole, xl, around(z, 4 - dz))
        send(block, block, ss.at[8 + dz], rs.at[8 + dz], beside(dz))

    def x_got(whole, rs, dz):
        got(chip_slots(whole, 1 - xl, around(z, 4 - dz)), rs.at[8 + dz])

    def rows_sent(whole, ss):
        for i in range(1, 8):
            sent(whole.at[f], ss.at[i])
        for dz in range(4):
            sent(chip_slots(whole, xl, around(z, 4 - dz)), ss.at[8 + dz])

    def loop_sent(ref, ss, first, last):
        def one(i, carry):
            sent(ref, ss.at[i])
            return carry

        lax.fori_loop(first, last, one, 0)

    gather_start(r.tok, r.x_all, r.s_x, r.r_x)
    send(r.tok, r.xo_all.at[y, k], r.s_xo.at[8], r.r_xo.at[8], along_x(2))
    z_send(lambda k_: r.gain_in, r.gain_recv, r.s_gain, r.r_gain)
    z_send(lambda k_: r.wkv_send.at[k_], r.wkv, r.s_wkv, r.r_wkv)
    send(r.pos_in, r.pos.at[k], r.s_pos.at[0], r.r_pos.at[0], partner)
    z_send(lambda k_: r.wqq_send.at[k_], r.wqq, r.s_wqq, r.r_wqq)

    is_source = lax.div(part, 2) == y
    to_core = lax.rem(part, 2)
    for i in range(4):
        piece = 4 * k + i
        here = (xl == k) & (z == i) & (to_core == k)

        @pl.when(is_source & jnp.logical_not(here))
        def _():
            there = place(xh, k, y, i, to_core)
            send(r.wo_own.at[pl.ds(32 * i, 32)], r.wo.at[pl.ds(pl.multiple_of(32 * piece, 32), 32)], r.s_wo.at[i], r.r_wo.at[0], there)
            send(r.wd_own.at[pl.ds(48 * i, 48)], r.wd.at[pl.ds(pl.multiple_of(48 * piece, 16), 48)], r.s_wd.at[i], r.r_wd.at[0], there)

        @pl.when(is_source & here)
        def _():
            r.wo[pl.ds(pl.multiple_of(32 * piece, 32), 32), :] = r.wo_own[32 * i : 32 * i + 32, :]
            r.wd[pl.ds(pl.multiple_of(48 * piece, 16), 48), :] = r.wd_own[48 * i : 48 * i + 48, :]

    def wo_rows(q):
        return r.wo.at[pl.ds(pl.multiple_of(32 * q, 32), 32)]

    def wd_rows(q):
        return r.wd.at[pl.ds(pl.multiple_of(48 * q, 16), 48)]

    def pass_on(whole, ss, rs, dz):
        z_got(whole, rs, dz)
        x_send(whole, ss, rs, dz)

    pass_on(r.gain_recv, r.s_gain, r.r_gain, 0)
    pass_on(r.wkv, r.s_wkv, r.r_wkv, 0)

    got(r.pos.at[other], r.r_pos.at[0])
    steps = lax.broadcasted_iota(jnp.int32, (BLOCK, 1), 0).astype(f32)
    for s in range(2):
        for b in range(16):
            r.posk[s, b * BLOCK : (b + 1) * BLOCK, :] = r.pos[s, 0:1, b * BLOCK : b * BLOCK + 1] + steps
    freq = r.freq[0:1, :]
    sign = r.freq[1:2, :]

    def tables(i, carry):
        hh, yy = lax.rem(xh + lax.div(i, 4), 2), lax.rem(i, 4)
        for s in range(2):
            rows = r.posk[s, pl.ds(pl.multiple_of(512 * hh + 128 * yy, 128), 128), :]
            angle = rows * freq
            cos, sin = jnp.cos(angle), jnp.sin(angle) * sign

            @pl.when(i < 4)
            def _():
                r.cos_t[yy, s * 128 : (s + 1) * 128, :] = cos
                r.sin_t[yy, s * 128 : (s + 1) * 128, :] = sin

            @pl.when(i >= 4)
            def _():
                r.cos_o[yy, s * 128 : (s + 1) * 128, :] = cos
                r.sin_o[yy, s * 128 : (s + 1) * 128, :] = sin

        return carry

    lax.fori_loop(0, 2, tables, 0)

    for dz in (1, 3):
        pass_on(r.gain_recv, r.s_gain, r.r_gain, dz)
        pass_on(r.wkv, r.s_wkv, r.r_wkv, dz)
    for d in (1, 3):
        gather_forward(r.x_all, r.s_x, r.r_x, d)
    lax.fori_loop(2, 4, tables, 0)
    got(r.xo_all.at[y, k], r.r_xo.at[8])
    gather_start(r.xo_all.at[y, k], r.xo_all, r.s_xo, r.r_xo)
    pass_on(r.gain_recv, r.s_gain, r.r_gain, 2)
    pass_on(r.wkv, r.s_wkv, r.r_wkv, 2)
    lax.fori_loop(4, 8, tables, 0)
    for dz in (0, 1, 3, 2):
        pass_on(r.wqq, r.s_wqq, r.r_wqq, dz)
    gather_start(r.dyt, r.dy_all, r.s_dy, r.r_dy)
    own_piece = (2 * y + k == part) & (xl == k)

    @pl.when(jnp.logical_not(own_piece))
    def _():
        got(wo_rows(part), r.r_wo.at[0])
        got(wd_rows(part), r.r_wd.at[0])

    for dz in range(1, 4):
        there = place(xh, xl, y, around(z, dz), k)
        send(wo_rows(part), wo_rows(part), r.s_wo2.at[dz], r.r_wo2.at[dz], there)
    z_send(lambda k_: r.wgu_send.at[k_], r.wgu, r.s_wgu, r.r_wgu)
    for dz in range(1, 4):
        there = place(xh, xl, y, around(z, dz), k)
        send(wd_rows(part), wd_rows(part), r.s_wd2.at[dz], r.r_wd2.at[dz], there)

    def piece_of(l_, dz):
        return 4 * l_ + around(z, 4 - dz)

    for dz in range(4):
        x_got(r.gain_recv, r.r_gain, dz)
    gains = jnp.sum(r.gain_recv[...], axis=0)
    g1 = to_row(gains, 0, 8)
    g2 = to_row(gains, 8, 8)
    gq = gains[16:17, :]
    gk = gains[17:18, :]

    def rotated(u, cos, sin):
        return u * cos + pltpu.roll(u, 64, 1) * sin

    def unrotated(u, cos, sin):
        return u * cos - pltpu.roll(u, 64, 1) * sin

    def inverse_rms(u):
        return lax.rsqrt(jnp.mean(u * u, axis=-1, keepdims=True) + norm_eps)

    def project_keys(d, x_all, n1_all, raw_at, cos, sin, hh):
        yy = around(y, 4 - d)
        rows = x_all[yy].reshape(256, D).astype(f32)
        n1 = (rows * inverse_rms(rows) * g1).astype(bf16)
        n1_all[yy] = n1
        kv = dot(n1, r.wkv[...].reshape(D, 256))
        raw = kv[:, 0:HEAD]
        raw_at(yy)[...] = raw
        local = pl.ds(pl.multiple_of(512 * hh + 128 * yy, 128), 128)
        key = rotated(raw * inverse_rms(raw) * gk, cos[yy], sin[yy]).astype(bf16)
        value = kv[:, HEAD:].astype(bf16)
        for s in range(2):
            r.kv[s, local, 0:HEAD] = key[s * 128 : (s + 1) * 128]
            r.kv[s, local, HEAD : 2 * HEAD] = value[s * 128 : (s + 1) * 128]

    def project_mine(d):
        project_keys(d, r.x_all, r.n1_all, lambda yy: r.qkraw.at[yy, :, pl.ds(256, HEAD)], r.cos_t, r.sin_t, xh)

    def project_others(d):
        project_keys(d, r.xo_all, r.n1o_all, lambda yy: r.kraw_o.at[yy], r.cos_o, r.sin_o, 1 - xh)

    def project_queries(yy, carry):
        qs = dot(r.n1_all[yy], r.wqq[...].reshape(D, 256))
        r.qkraw[yy, :, 0:256] = qs
        for h in range(2):
            raw = qs[:, h * HEAD : (h + 1) * HEAD]
            query = rotated(raw * inverse_rms(raw) * gq, r.cos_t[yy], r.sin_t[yy]).astype(bf16)
            for s in range(2):
                for half in range(2):
                    first = s * 128 + half * 64
                    rows = pl.ds(pl.multiple_of(64 * yy, 64), 64)
                    r.q_s[s, half, rows, h * HEAD : (h + 1) * HEAD] = query[first : first + 64]
        return carry

    gather_own(r.x_all, r.r_x)
    for dz in range(4):
        x_got(r.wkv, r.r_wkv, dz)
    project_mine(0)
    gather_pair(r.x_all, r.r_x, 1)
    project_mine(1)
    gather_forward(r.x_all, r.s_x, r.r_x, 2)
    gather_pair(r.x_all, r.r_x, 3)
    project_mine(3)
    gather_pair(r.x_all, r.r_x, 2)
    project_mine(2)
    for d in (1, 3):
        gather_forward(r.xo_all, r.s_xo, r.r_xo, d)
    for dz in range(4):
        if dz > 0:
            got(wo_rows(piece_of(xl, dz)), r.r_wo2.at[dz])
        block = wo_rows(piece_of(xl, dz))
        send(block, block, r.s_wo2.at[4 + dz], r.r_wo2.at[4 + dz], beside(dz))
    for dz in range(4):
        x_got(r.wqq, r.r_wqq, dz)
    lax.fori_loop(0, 4, project_queries, 0)
    gather_own(r.xo_all, r.r_xo)
    project_others(0)
    gather_forward(r.xo_all, r.s_xo, r.r_xo, 2)
    gather_pair(r.xo_all, r.r_xo, 1)
    project_others(1)
    gather_pair(r.xo_all, r.r_xo, 3)
    project_others(3)
    gather_pair(r.xo_all, r.r_xo, 2)
    project_others(2)
    gather_end(r.x_all, r.s_x)

    def rest_forward():
        for dz in range(4):
            pass_on(r.wgu, r.s_wgu, r.r_wgu, dz)
        for dz in range(4):
            if dz > 0:
                got(wd_rows(piece_of(xl, dz)), r.r_wd2.at[dz])
            block = wd_rows(piece_of(xl, dz))
            send(block, block, r.s_wd2.at[4 + dz], r.r_wd2.at[4 + dz], beside(dz))

    def lanes(half):
        return pl.ds(pl.multiple_of(256 * half, 256), 256)

    def allowed(s, half):
        return r.posk[s] <= r.pos[s, 1:2, lanes(half)]

    def attend(s, half):
        ok = allowed(s, half)
        for h in range(2):
            q = r.q_s[s, half, :, h * HEAD : (h + 1) * HEAD]
            scores = jnp.where(ok, dot_nt(r.kv[s, :, 0:HEAD], q) * SCALE, -1e30)
            top = jnp.max(scores, axis=0, keepdims=True)
            p = jnp.exp(scores - top)
            total = jnp.sum(p, axis=0, keepdims=True)
            o = dot_tn(r.kv[s, :, HEAD : 2 * HEAD], p.astype(bf16)) / total
            r.o_t[s, h * HEAD : (h + 1) * HEAD, lanes(half)] = o
            r.ob_t[s, h * HEAD : (h + 1) * HEAD, lanes(half)] = o.astype(bf16)
            r.lse[s, h, :, lanes(half)] = top + jnp.log(total)

    def reduce_first(use, p, cc, d, half=None):
        yy, rows, i = around(y, d), rows_of(half), 8 * use + 4 * (half or 0) + d
        send(p.at[yy, other, rows], cc.at[yy, rows], r.s_c.at[i], r.r_c.at[i], partner)

    def both_cores(use, p, cc, d, half):
        yy, rows, i = around(y, d), rows_of(half), 8 * use + 4 * (half or 0) + d
        got(cc.at[yy, rows], r.r_c.at[i])
        return p[yy, k, rows, :].astype(f32) + cc[yy, rows, :].astype(f32)

    def reduce_far(use, p, cc, rr, half=None):
        rows, o = rows_of(half), 12 * use + 6 * (half or 0)
        yy = around(y, 2)
        p[yy, k, rows, :] = both_cores(use, p, cc, 2, half).astype(bf16)
        for which in range(2):
            rest = far_part(half, which)
            there = place(xh, xl, around(y, 1 + 2 * which), z, k)
            send(p.at[yy, k, rest], rr.at[2, rest], r.s_r.at[o + which], r.r_r.at[o + which], there)
        for which in range(2):
            yy = around(y, 1 + 2 * which)
            p[yy, k, rows, :] = both_cores(use, p, cc, 1 + 2 * which, half).astype(bf16)
            early, i = far_part(half, 1 - which), o + 2 + which
            send(p.at[yy, k, early], rr.at[which, early], r.s_r.at[i], r.r_r.at[i], place(xh, xl, yy, z, k))

    def reduce_near(use, p, rr, half=None):
        o = 12 * use + 6 * (half or 0)
        for which in range(2):
            yy = around(y, 1 + 2 * which)
            late, i = far_part(half, which), o + 4 + which
            got(rr.at[2, late], r.r_r.at[o + which])
            p[yy, k, late, :] = (p[yy, k, late, :].astype(f32) + rr[2, late, :].astype(f32)).astype(bf16)
            send(p.at[yy, k, late], rr.at[which, late], r.s_r.at[i], r.r_r.at[i], place(xh, xl, yy, z, k))

    def reduce_third(use, p, cc, rr, half=None):
        rows, o = rows_of(half), 12 * use + 6 * (half or 0)
        total = both_cores(use, p, cc, 0, half)
        for which in range(2):
            got(rr.at[which, far_part(half, 1 - which)], r.r_r.at[o + 2 + which])
            got(rr.at[which, far_part(half, which)], r.r_r.at[o + 4 + which])
            total = total + rr[which, rows, :].astype(f32)
        return total

    def reduce_end(use, p, half=None):
        for d in range(4):
            sent(p.at[y, other, rows_of(half)], r.s_c.at[8 * use + 4 * (half or 0) + d])
        for i in range(6):
            sent(p.at[y, k, far_part(half, 0)], r.s_r.at[12 * use + 6 * (half or 0) + i])

    def out_partial(half):
        for s in range(2):
            o = r.ob_t[s, :, lanes(half)]
            r.pa[:, s, rows_of(half), :] = dot_tn(o, r.wo[...]).astype(bf16).reshape(4, 64, D)
        for d in (2, 1, 3, 0):
            reduce_first(0, r.pa, r.ca, d, half)

    attend(0, 0)
    attend(1, 0)
    for dz in range(4):
        got(wo_rows(piece_of(1 - xl, dz)), r.r_wo2.at[4 + dz])
    out_partial(0)
    rest_forward()
    attend(0, 1)
    reduce_far(0, r.pa, r.ca, r.ra, 0)
    for d in (1, 3):
        gather_forward(r.dy_all, r.s_dy, r.r_dy, d)
    attend(1, 1)
    out_partial(1)
    reduce_near(0, r.pa, r.ra, 0)
    reduce_far(0, r.pa, r.ca, r.ra, 1)

    def middle(half):
        rows = rows_of(half)
        h1 = r.tok[rows, :].astype(f32) + reduce_third(0, r.pa, r.ca, r.ra, half)
        r.h1[rows, :] = h1
        r.n2_all[y, k, rows, :] = (h1 * inverse_rms(h1) * g2).astype(bf16)
        gather_start(r.n2_all.at[y, k], r.n2_all, r.s_n2, r.r_n2, half)

    middle(0)
    reduce_near(0, r.pa, r.ra, 1)
    middle(1)
    gather_forward(r.dy_all, r.s_dy, r.r_dy, 2)

    gather_own(r.dy_all, r.r_dy)
    for d in (1, 3, 2):
        gather_pair(r.dy_all, r.r_dy, d)
    for dz in range(4):
        x_got(r.wgu, r.r_wgu, dz)
        got(wd_rows(piece_of(1 - xl, dz)), r.r_wd2.at[4 + dz])

    def two_blocks(whole, ds, half):
        blocks = [whole[around(y, d), :, rows_of(half), :].reshape(128, whole.shape[-1]) for d in ds]
        return jnp.concatenate(blocks, axis=0)

    def put_blocks(whole, ds, half, cols, value):
        for i, d in enumerate(ds):
            block = value[128 * i : 128 * (i + 1)].reshape(2, 64, value.shape[-1])
            whole[around(y, d), :, rows_of(half), cols] = block

    def feed(ds, half):
        n2 = two_blocks(r.n2_all, ds, half)
        ab = dot(n2, r.wgu[...].reshape(D, 768))
        a, b = ab[:, :384], ab[:, 384:]
        sig = jax.nn.sigmoid(a)
        silu = a * sig
        put_blocks(r.hid_all, ds, half, slice(None), (silu * b).astype(bf16))
        dhid = dot_nt(two_blocks(r.dy_all, ds, half), r.wd[...])
        da = (dhid * b * sig * (1.0 + a * (1.0 - sig))).astype(bf16)
        db = (dhid * silu).astype(bf16)
        put_blocks(r.dgu_all, ds, half, slice(0, 384), da)
        put_blocks(r.dgu_all, ds, half, slice(384, 768), db)
        dn2 = dot_nt(jnp.concatenate([da, db], axis=1), r.wgu[...].reshape(D, 768))
        put_blocks(r.pb, ds, half, slice(None), dn2.astype(bf16))
        for d in ds:
            reduce_first(1, r.pb, r.cb, d, half)

    def near_forward(whole, ss, rs, half):
        for d in (1, 3):
            gather_forward(whole, ss, rs, d, half)

    near_forward(r.n2_all, r.s_n2, r.r_n2, 0)
    for half in range(2):
        gather_own(r.n2_all, r.r_n2, half)
        gather_pair(r.n2_all, r.r_n2, 1, half)
        feed((0, 3), half)
        if half == 1:
            reduce_near(1, r.pb, r.rb, 0)
        gather_forward(r.n2_all, r.s_n2, r.r_n2, 2, half)
        if half == 0:
            near_forward(r.n2_all, r.s_n2, r.r_n2, 1)
        gather_pair(r.n2_all, r.r_n2, 3, half)
        gather_pair(r.n2_all, r.r_n2, 2, half)
        feed((2, 1), half)
        reduce_far(1, r.pb, r.cb, r.rb, half)

    def rows_at(whole, height):
        return lambda l_, z_: whole.at[pl.ds(pl.multiple_of(height * (4 * l_ + z_), 16), height)]

    def cross_z(piece, dst, ss, rs):
        for dz in (1, 3, 2):
            zz = around(z, dz)
            for l_ in range(2):
                i = 2 * (dz - 1) + l_
                send(piece(l_, zz), dst.at[dz - 1, l_], ss.at[i], rs.at[i], place(xh, xl, y, zz, k))

    def row_half(ref, h_):
        return ref.at[pl.ds(pl.multiple_of(64 * h_, 64), 64)]

    def column_half(ref, h_):
        return ref.at[:, pl.ds(pl.multiple_of(512 * h_, 512), 512)]

    def cross_x(piece, zrecv, sums, xrecv, half_of, ss, rs):
        for l_ in range(2):
            total = piece(l_, z)[...].astype(f32)
            for dz in range(1, 4):
                got(zrecv.at[dz - 1, l_], rs.at[2 * (dz - 1) + l_])
                total = total + zrecv[dz - 1, l_].astype(f32)
            sums[l_] = total.astype(bf16)
        for dx in (1, 3, 2):
            x_ = around(x, dx)
            block = half_of(sums.at[lax.rem(x_, 2)], lax.div(x_, 2))
            send(block, xrecv.at[dx - 1], ss.at[5 + dx], rs.at[5 + dx], along_x(dx))

    def cross_total(sums, xrecv, half_of, rs):
        total = half_of(sums.at[xl], xh)[...].astype(f32)
        for dx in (1, 3, 2):
            got(xrecv.at[dx - 1], rs.at[5 + dx])
            total = total + xrecv[dx - 1].astype(f32)
        return total

    def cross_x_first(whole, height, xrecv, ss, rs):
        for dx in (1, 3, 2):
            x_ = around(x, dx)
            rows = pl.ds(pl.multiple_of(4 * height * lax.rem(x_, 2), 16), 4 * height)
            block = column_half(whole.at[rows], lax.div(x_, 2))
            send(block, xrecv.at[dx - 1], ss.at[dx - 1], rs.at[dx - 1], along_x(dx))

    def cross_z_second(whole, height, xrecv, sums, zrecv, ss, rs):
        rows = pl.ds(pl.multiple_of(4 * height * xl, 16), 4 * height)
        total = column_half(whole.at[rows], xh)[...].astype(f32)
        for dx in (1, 3, 2):
            got(xrecv.at[dx - 1], rs.at[dx - 1])
            total = total + xrecv[dx - 1].astype(f32)
        sums[...] = total.astype(bf16)
        for dz in (1, 3, 2):
            zz = around(z, dz)
            block = sums.at[pl.ds(pl.multiple_of(height * zz, 16), height)]
            send(block, zrecv.at[dz - 1], ss.at[2 + dz], rs.at[2 + dz], place(xh, xl, y, zz, k))

    def cross_z_total(height, sums, zrecv, rs):
        total = sums[pl.ds(pl.multiple_of(height * z, 16), height), :].astype(f32)
        for dz in (1, 3, 2):
            got(zrecv.at[dz - 1], rs.at[2 + dz])
            total = total + zrecv[dz - 1].astype(f32)
        return total

    def rows_x_first():
        for dx in (1, 3, 2):
            x_ = around(x, dx)
            block = r.ggua.at[pl.ds(4 * lax.rem(x_, 2), 4), lax.div(x_, 2)]
            send(block, r.xgua.at[dx - 1], r.s_ggua.at[dx - 1], r.r_ggua.at[dx - 1], along_x(dx))

    def rows_z_second():
        total = r.ggua[pl.ds(4 * xl, 4), xh].astype(f32)
        for dx in (1, 3, 2):
            got(r.xgua.at[dx - 1], r.r_ggua.at[dx - 1])
            total = total + r.xgua[dx - 1].astype(f32)
        r.sgua[...] = total.astype(bf16)
        for dz in (1, 3, 2):
            zz = around(z, dz)
            send(r.sgua.at[zz], r.zgua.at[dz - 1], r.s_ggua.at[2 + dz], r.r_ggua.at[2 + dz], place(xh, xl, y, zz, k))

    def rows_z_total():
        total = r.sgua[z].astype(f32)
        for dz in (1, 3, 2):
            got(r.zgua.at[dz - 1], r.r_ggua.at[2 + dz])
            total = total + r.zgua[dz - 1].astype(f32)
        return total

    def cross_sent(zrecv, xrecv, ss):
        for i in range(6):
            sent(zrecv.at[0, 0], ss.at[i])
        for i in range(3):
            sent(xrecv.at[0], ss.at[6 + i])

    gqa_piece, gqb_piece, ggub_piece = rows_at(r.gqa, 128), rows_at(r.gqb, 128), rows_at(r.ggub, 128)
    go_piece = rows_at(r.go, 32)

    def weight_gradient(left, right, out, first=0):
        def one(i, carry):
            cols = pl.ds(pl.multiple_of(256 * i, 256), 256)
            taken = pl.ds(pl.multiple_of(first + 256 * i, 256), 256)
            out[:, cols] = dot_tn(left(), right(taken)).astype(bf16)
            return carry

        lax.fori_loop(0, out.shape[1] // 256, one, 0)

    def middle_back(half):
        rows = rows_of(half)
        dn2 = reduce_third(1, r.pb, r.cb, r.rb, half)
        h1 = r.h1[rows, :]
        r2 = inverse_rms(h1)
        weighted = dn2 * g2
        back = r2 * weighted - h1 * (r2 * r2 * r2) * jnp.mean(weighted * h1, axis=-1, keepdims=True)
        dh1 = r.dyt[rows, :].astype(f32) + back
        r.dh1[rows, :] = dh1
        dg2 = jnp.sum(dn2 * h1 * r2, axis=0, keepdims=True)
        for i in range(8):
            r.dg[8 + i : 9 + i, :] += dg2[:, 128 * i : 128 * (i + 1)]
        r.x_all[y, k, rows, :] = dh1.astype(bf16)
        gather_start(r.x_all.at[y, k], r.x_all, r.s_dob, r.r_dob, half)

    ggua = dot_tn(r.n2_all[...].reshape(D, D), r.dgu_all[:, :, :, 0:256].reshape(D, 256))
    r.ggua[...] = ggua.astype(bf16).reshape(8, 2, 64, 256)
    rows_x_first()
    weight_gradient(
        lambda: r.n2_all[...].reshape(D, D),
        lambda cols: r.dgu_all[:, :, :, cols].reshape(D, 256),
        r.ggub,
        256,
    )
    cross_z(ggub_piece, r.zgub, r.s_ggub, r.r_ggub)
    reduce_near(1, r.pb, r.rb, 1)
    middle_back(0)
    weight_gradient(
        lambda: r.hid_all[...].reshape(D, 384),
        lambda cols: r.dy_all[:, :, :, cols].reshape(D, 256),
        r.gd,
    )
    cross_x_first(r.gd, 48, r.xd, r.s_gd, r.r_gd)
    middle_back(1)

    def direct_spread(total, hold, final, ss, rs):
        hold[...] = total.astype(bf16)

        def one(i, carry):
            there = place(lax.rem(xh + lax.div(i, 4), 2), xl, lax.rem(y + i, 4), z, xh)

            @pl.when((i > 0) | (k != xh))
            def _():
                send(hold, final.at[t], ss.at[i], rs.at[t], there)

            return carry

        lax.fori_loop(0, 8, one, 0)

        @pl.when(k == xh)
        def _():
            final[t] = hold[...]

    def direct_spread_sent(hold, ss):
        def one(i, carry):
            @pl.when((i > 0) | (k != xh))
            def _():
                sent(hold, ss.at[i])

            return carry

        lax.fori_loop(0, 8, one, 0)

    def direct_spread_got(final, rs):
        def one(i, carry):
            @pl.when((i != t) | (k != xh))
            def _():
                got(final.at[i], rs.at[i])

            return carry

        lax.fori_loop(0, 8, one, 0)

    other_half = place(1 - xh, xl, y, z, k)

    def rows_exchange(total, hold, ss, rs):
        hold[xh] = total.astype(bf16)
        send(hold.at[xh], hold.at[xh], ss.at[8], rs.at[8], other_half)

    def rows_spread(hold, final, ss, rs):
        for which in range(2):
            h = xh if which == 0 else 1 - xh
            if which == 1:
                got(hold.at[h], rs.at[8])
            for i in (2, 1, 3):
                send(hold.at[h], final.at[t], ss.at[4 * which + i], rs.at[t], place(xh, xl, around(y, i), z, h))

            @pl.when(k != h)
            def _():
                send(hold.at[h], final.at[t], ss.at[4 * which], rs.at[t], partner)

            @pl.when(k == h)
            def _():
                final[t] = hold[h]

    def rows_spread_sent(hold, ss):
        sent(hold.at[0], ss.at[8])
        for which in range(2):
            h = xh if which == 0 else 1 - xh
            for i in range(1, 4):
                sent(hold.at[0], ss.at[4 * which + i])

            @pl.when(k != h)
            def _():
                sent(hold.at[0], ss.at[4 * which])

    def rows_spread_got(final, rs):
        def one(i, carry):
            @pl.when(i != t)
            def _():
                got(final.at[i], rs.at[i])

            return carry

        lax.fori_loop(0, 8, one, 0)

    def block_exchange(total, hold, ss, rs):
        column_half(hold, xh)[...] = total.astype(bf16)
        send(column_half(hold, xh), column_half(hold, xh), ss.at[8], rs.at[8], other_half)

    def block_along_y(hold, held, ss, rs):
        got(column_half(hold, 1 - xh), rs.at[8])
        for i in (1, 3, 2):
            send(hold, held.at[i - 1], ss.at[i], rs.at[i], place(xh, xl, around(y, i), z, k))

    def block_target(i):
        slice_ = 2 * around(y, 4 - i) + k
        mine = (part == slice_) & (k == xl)
        return mine, place(xh, lax.div(slice_, 4), y, lax.rem(slice_, 4), xl)

    def block_deliver(hold, held, final, height, ss, rs):
        rows = pl.ds(pl.multiple_of(height * z, 16), height)
        for i in (0, 1, 3, 2):
            block = hold
            if i > 0:
                got(held.at[i - 1], rs.at[i])
                block = held.at[i - 1]
            mine, there = block_target(i)

            @pl.when(jnp.logical_not(mine))
            def _():
                send(block, final.at[rows], ss.at[4 + i], rs.at[4 + z], there)

            @pl.when(mine)
            def _():
                final[rows, :] = block[...]

    def block_sent(hold, ss):
        sent(column_half(hold, 0), ss.at[8])
        for i in range(4):
            if i > 0:
                sent(hold, ss.at[i])
            mine, there = block_target(i)

            @pl.when(jnp.logical_not(mine))
            def _():
                sent(hold, ss.at[4 + i])

    def block_got(final, height, rs):
        def one(i, carry):
            @pl.when(jnp.logical_not((xl == k) & (z == i) & (lax.rem(part, 2) == k)))
            def _():
                got(final.at[pl.ds(pl.multiple_of(height * i, 16), height)], rs.at[4 + i])

            return carry

        lax.fori_loop(0, 4, one, 0)

    def key_back(s, mine):
        span = slice(s * 128, (s + 1) * 128)
        rows = pl.ds(pl.multiple_of(512 * (xh if mine else 1 - xh), 512), 512)
        cos, sin = (r.cos_t, r.sin_t) if mine else (r.cos_o, r.sin_o)
        raw = r.qkraw[:, span, 256:384] if mine else r.kraw_o[:, span, :]
        du = unrotated(r.dkv[s, rows, 0:HEAD], cos[:, span, :].reshape(512, HEAD), sin[:, span, :].reshape(512, HEAD))
        back, gain_grad = norm_back(raw.reshape(512, HEAD), gk, du)
        out, first = (r.dqkv, 256) if mine else (r.dkv_o, 0)
        out[:, span, first : first + HEAD] = back.astype(bf16).reshape(4, 128, HEAD)
        out[:, span, first + HEAD : first + 2 * HEAD] = r.dkv[s, rows, HEAD : 2 * HEAD].astype(bf16).reshape(4, 128, HEAD)
        r.dg[17:18, :] += gain_grad

    def norm_back(value, gain, grad):
        inverse = inverse_rms(value)
        w = grad * gain
        back = inverse * w - value * (inverse * inverse * inverse) * jnp.mean(w * value, axis=-1, keepdims=True)
        return back, jnp.sum(grad * value * inverse, axis=0, keepdims=True)

    def attend_back(half, s):
        rows = rows_of(half)
        do_s = dot_nt(r.wo[...], r.x_all[:, s, rows, :].reshape(256, D)).astype(bf16)
        prod = do_s.astype(f32) * r.o_t[s, :, lanes(half)]
        r.do_t[s, :, lanes(half)] = do_s
        ok = allowed(s, half)
        keys, values = r.kv[s, :, 0:HEAD], r.kv[s, :, HEAD : 2 * HEAD]
        mine = pl.ds(s * 128 + 64 * half, 64)
        cos = r.cos_t[:, mine, :].reshape(256, HEAD)
        sin = r.sin_t[:, mine, :].reshape(256, HEAD)
        for h in range(2):
            head = slice(h * HEAD, (h + 1) * HEAD)
            q = r.q_s[s, half, :, head]
            do = r.do_t[s, head, lanes(half)]
            delta = jnp.sum(prod[head], axis=0, keepdims=True)
            scores = dot_nt(keys, q) * SCALE
            p = jnp.where(ok, jnp.exp(scores - r.lse[s, h, :, lanes(half)]), 0.0)
            ds = (p * (dot(values, do) - delta)).astype(bf16)
            dv = dot_nt(p.astype(bf16), do)
            dk = dot(ds, q) * SCALE
            if half == 0 and h == 0:
                r.dkv[s, :, HEAD : 2 * HEAD] = dv
                r.dkv[s, :, 0:HEAD] = dk
            else:
                r.dkv[s, :, HEAD : 2 * HEAD] += dv
                r.dkv[s, :, 0:HEAD] += dk
            dq = (dot_tn(keys, ds) * SCALE).T
            raw = r.qkraw[:, mine, head].reshape(256, HEAD)
            back, gain_grad = norm_back(raw, gq, unrotated(dq, cos, sin))
            r.dqkv[:, mine, head] = back.astype(bf16).reshape(4, 64, HEAD)
            r.dg[16:17, :] += gain_grad

    def gather_rest(half):
        gather_forward(r.x_all, r.s_dob, r.r_dob, 2, half)
        gather_own(r.x_all, r.r_dob, half)
        for d in (1, 3, 2):
            gather_pair(r.x_all, r.r_dob, d, half)

    for half in range(2):
        reduce_end(0, r.pa, half)

    def down_partial(i, carry):
        hid = r.hid_all[i].reshape(256, 384)
        r.pa[i] = dot(hid, r.wd[...]).astype(bf16).reshape(2, 128, D)
        return carry

    near_forward(r.x_all, r.s_dob, r.r_dob, 0)
    lax.fori_loop(0, 4, down_partial, 0)
    for d in (2, 1, 3, 0):
        reduce_first(2, r.pa, r.ca, d)
    def out_gradient(half, s):
        return lambda cols: dot(r.ob_t[s, :, lanes(half)], r.x_all[:, s, rows_of(half), cols].reshape(256, 256))

    def out_gradients(half):
        def one(i, carry):
            cols = pl.ds(pl.multiple_of(256 * i, 256), 256)
            total = out_gradient(half, 0)(cols) + out_gradient(half, 1)(cols)
            if half == 0:
                r.go_sum[:, cols] = total
            else:
                r.go[:, cols] = (r.go_sum[:, cols] + total).astype(bf16)
            return carry

        lax.fori_loop(0, 4, one, 0)

    gather_rest(0)
    attend_back(0, 0)
    near_forward(r.x_all, r.s_dob, r.r_dob, 1)
    rows_z_second()
    cross_x(ggub_piece, r.zgub, r.sgub, r.xgub, row_half, r.s_ggub, r.r_ggub)
    attend_back(0, 1)
    reduce_far(2, r.pa, r.ca, r.ra)
    out_gradients(0)
    gather_rest(1)
    out_gradients(1)
    cross_z_second(r.gd, 48, r.xd, r.sd, r.zd, r.s_gd, r.r_gd)
    cross_z(go_piece, r.zo, r.s_go, r.r_go)
    gu_total = jnp.concatenate([rows_z_total(), cross_total(r.sgub, r.xgub, row_half, r.r_ggub)], axis=1)
    rows_exchange(gu_total, r.hgu, r.s_fgu, r.r_fgu)
    for s in range(2):
        attend_back(1, s)
        key_back(s, False)
        block = pl.ds(128 * s, 128)
        send(r.dkv_o.at[:, block], r.dkv_recv.at[:, block], r.s_dkv.at[s], r.r_dkv.at[s], along_x(2))
        if s == 0:
            reduce_near(2, r.pa, r.ra)
    rows_spread(r.hgu, r.fgu, r.s_fgu, r.r_fgu)

    for s in range(2):
        key_back(s, True)

    def weighed(grad, weight):
        prod = grad * weight[...].reshape(D, 256).astype(f32)
        return prod[:, 0:128] + prod[:, 128:256]

    grad = dot_tn(r.n1_all[...].reshape(D, D), r.dqkv[:, :, 0:256].reshape(D, 256))
    r.gqa[...] = grad.astype(bf16)
    cross_z(gqa_piece, r.zqa, r.s_gqa, r.r_gqa)
    wdot = weighed(grad, r.wqq)
    grad = dot_tn(r.n1_all[...].reshape(D, D), r.dqkv[:, :, 256:512].reshape(D, 256))
    grad = grad + dot_tn(r.n1o_all[...].reshape(D, D), r.dkv_o[...].reshape(D, 256))
    r.gqb[...] = grad.astype(bf16)
    cross_z(gqb_piece, r.zqb, r.s_gqb, r.r_gqb)
    wdot = wdot + weighed(grad, r.wkv)
    dg1 = jnp.sum(wdot.T, axis=0, keepdims=True) / g1
    for i in range(8):
        r.dg[i : i + 1, :] = dg1[:, 128 * i : 128 * (i + 1)]
    for i in range(1, 8):
        there = place(xh, xl, around(y, i // 2), z, lax.rem(k + i, 2))
        send(r.dg, r.dg_r1.at[i], r.s_dg1.at[i], r.r_dg1.at[i], there)

    block_exchange(cross_z_total(48, r.sd, r.zd, r.r_gd), r.hd, r.s_fd, r.r_fd)
    cross_x(go_piece, r.zo, r.so, r.xo, column_half, r.s_go, r.r_go)
    r.out_tok[...] = (r.h1[...] + reduce_third(2, r.pa, r.ca, r.ra)).astype(bf16)
    cross_x(gqa_piece, r.zqa, r.sqa, r.xqa, row_half, r.s_gqa, r.r_gqa)
    block_along_y(r.hd, r.yd, r.s_fd, r.r_fd)
    for half in range(2):
        reduce_end(1, r.pb, half)

    for s in range(2):
        got(r.dkv_recv.at[:, pl.ds(128 * s, 128)], r.r_dkv.at[s])
    for d in (2, 1, 3, 0):
        yy = around(y, d)
        dkv = (r.dqkv[yy, :, 256:512].astype(f32) + r.dkv_recv[yy].astype(f32)).astype(bf16)
        dn1 = dot_nt(r.dqkv[yy, :, 0:256], r.wqq[...].reshape(D, 256)) + dot_nt(dkv, r.wkv[...].reshape(D, 256))
        r.pb[yy] = dn1.astype(bf16).reshape(2, 128, D)
        reduce_first(3, r.pb, r.cb, d)
    block_exchange(cross_total(r.so, r.xo, column_half, r.r_go), r.ho, r.s_fo, r.r_fo)
    reduce_far(3, r.pb, r.cb, r.rb)
    rows_exchange(cross_total(r.sqa, r.xqa, row_half, r.r_gqa), r.hqa, r.s_fqa, r.r_fqa)
    total = r.dg[...]
    for i in range(1, 8):
        got(r.dg_r1.at[i], r.r_dg1.at[i])
        total = total + r.dg_r1[i]
    r.dg_s[0] = total
    for dz in range(1, 4):
        send(r.dg_s.at[0], r.dg_r2.at[dz - 1], r.s_dg2.at[dz - 1], r.r_dg2.at[dz - 1], place(xh, xl, y, around(z, dz), k))
    cross_x(gqb_piece, r.zqb, r.sqb, r.xqb, row_half, r.s_gqb, r.r_gqb)
    block_along_y(r.ho, r.yo, r.s_fo, r.r_fo)
    reduce_near(3, r.pb, r.rb)
    rows_spread(r.hqa, r.fqa, r.s_fqa, r.r_fqa)
    block_deliver(r.hd, r.yd, r.fd, 48, r.s_fd, r.r_fd)
    direct_spread(cross_total(r.sqb, r.xqb, row_half, r.r_gqb), r.hqb, r.fqb, r.s_fqb, r.r_fqb)
    for dz in range(1, 4):
        got(r.dg_r2.at[dz - 1], r.r_dg2.at[dz - 1])
        total = total + r.dg_r2[dz - 1]
    r.dg_s[1] = total
    for dx in range(1, 4):
        send(r.dg_s.at[1], r.dg_r2.at[2 + dx], r.s_dg2.at[2 + dx], r.r_dg2.at[2 + dx], along_x(dx))

    block_deliver(r.ho, r.yo, r.fo, 32, r.s_fo, r.r_fo)

    dn1 = reduce_third(3, r.pb, r.cb, r.rb)
    rows = r.tok[...].astype(f32)
    back, unused = norm_back(rows, g1, dn1)
    r.dtok[...] = (r.dh1[...] + back).astype(bf16)

    block_got(r.fd, 48, r.r_fd)
    r.g_dn[...] = r.fd[...]
    rows_spread_got(r.fgu, r.r_fgu)
    for i in range(8):
        r.g_gu[:, 384 * i : 384 * (i + 1)] = r.fgu[i, :, 0:384]
        r.g_gu[:, 3072 + 384 * i : 3072 + 384 * (i + 1)] = r.fgu[i, :, 384:768]
    block_got(r.fo, 32, r.r_fo)
    r.g_out[...] = r.fo[...]
    for dx in range(1, 4):
        got(r.dg_r2.at[2 + dx], r.r_dg2.at[2 + dx])
        total = total + r.dg_r2[2 + dx]
    r.g_gain[...] = total
    rows_spread_got(r.fqa, r.r_fqa)
    direct_spread_got(r.fqb, r.r_fqb)
    for i in range(8):
        r.g_qkv[:, 256 * i : 256 * (i + 1)] = r.fqa[i]
        r.g_qkv[:, 2048 + 128 * i : 2048 + 128 * (i + 1)] = r.fqb[i, :, 0:128]
        r.g_qkv[:, 3072 + 128 * i : 3072 + 128 * (i + 1)] = r.fqb[i, :, 128:256]

    gather_end(r.dy_all, r.s_dy)
    for half in range(2):
        gather_end(r.n2_all, r.s_n2, half)
        gather_end(r.x_all, r.s_dob, half)
    sent(r.pos_in, r.s_pos.at[0])
    for whole, ss in ((r.gain_recv, r.s_gain), (r.wqq, r.s_wqq), (r.wkv, r.s_wkv), (r.wgu, r.s_wgu)):
        rows_sent(whole, ss)
    for i in range(4):
        here = (xl == k) & (z == i) & (to_core == k)

        @pl.when(is_source & jnp.logical_not(here))
        def _():
            sent(r.wo_own.at[pl.ds(32 * i, 32)], r.s_wo.at[i])
            sent(r.wd_own.at[pl.ds(48 * i, 48)], r.s_wd.at[i])

    loop_sent(wo_rows(part), r.s_wo2, 1, 8)
    loop_sent(wd_rows(part), r.s_wd2, 1, 8)
    gather_end(r.xo_all, r.s_xo)
    sent(r.tok, r.s_xo.at[8])
    reduce_end(2, r.pa)
    reduce_end(3, r.pb)
    for s in range(2):
        sent(r.dkv_o.at[:, pl.ds(128 * s, 128)], r.s_dkv.at[s])
    cross_sent(r.zqa, r.xqa, r.s_gqa)
    cross_sent(r.zqb, r.xqb, r.s_gqb)
    cross_sent(r.zgub, r.xgub, r.s_ggub)
    for i in range(3):
        sent(r.xgua.at[0], r.s_ggua.at[i])
        sent(r.zgua.at[0], r.s_ggua.at[3 + i])
    cross_sent(r.zo, r.xo, r.s_go)
    for i in range(3):
        sent(r.xd.at[0], r.s_gd.at[i])
        sent(r.zd.at[0], r.s_gd.at[3 + i])
    for hold, ss in ((r.hqa, r.s_fqa), (r.hgu, r.s_fgu)):
        rows_spread_sent(hold, ss)
    direct_spread_sent(r.hqb, r.s_fqb)
    block_sent(r.ho, r.s_fo)
    block_sent(r.hd, r.s_fd)
    loop_sent(r.dg, r.s_dg1, 1, 8)
    loop_sent(r.dg_s.at[0], r.s_dg2, 0, 6)


def layer(*args):
    vmem = pl.BlockSpec(memory_space=pltpu.VMEM)
    hbm = pl.BlockSpec(memory_space=pl.ANY)
    specs = [hbm if far else vmem for far in INPUTS.values()]
    return pl.pallas_call(
        layer_kernel,
        out_shape=[jax.ShapeDtypeStruct(shape, kind) for shape, kind in OUTPUTS.values()],
        in_specs=specs,
        out_specs=[vmem] * len(OUTPUTS),
        scratch_shapes=[pltpu.VMEM(shape, kind) for shape, kind in BUFFERS.values()]
        + [pltpu.SemaphoreType.DMA((count,)) for count in SEMAPHORES.values()],
        compiler_params=pltpu.CompilerParams(
            collective_id=0, has_side_effects=True, vmem_limit_bytes=62 << 20
        ),
        name="layer",
    )(*args)


RATES = (0.03, 0.3, 0.03, 0.03)
SHAPES = ((64, 4096), (128, D), (64, 6144), (192, D))
CHUNK_ROWS = (16, 64, 16, 64)


def adam_update(weight, moment, square, grad, rate, decay):
    moment_new = beta_first * moment + (1.0 - beta_first) * grad
    square_new = beta_second * square + (1.0 - beta_second) * grad * grad
    fix_first = 1.0 - beta_first**STEP
    fix_second = 1.0 - beta_second**STEP
    step = moment_new / fix_first / (jnp.sqrt(square_new / fix_second) + adam_eps)
    return (weight - rate * (step + decay * weight), moment_new, square_new)


def adam_kernel(*refs):
    ins, outs, rest = refs[:18], refs[18:32], refs[32:]
    held, made, load_sem, store_sem = rest[:16], rest[16:28], rest[28], rest[29]
    tokens = [pltpu.make_async_copy(ins[16 + i], outs[12 + i], store_sem.at[i]) for i in range(2)]
    for one in tokens:
        one.start()
    chunks = [(i, first) for i in (2, 0, 3, 1) for first in range(0, SHAPES[i][0], CHUNK_ROWS[i])]
    loads = []
    for n, (i, first) in enumerate(chunks):
        rows = pl.ds(first, CHUNK_ROWS[i])
        four = [
            pltpu.make_async_copy(ins[4 * i + a].at[rows], held[4 * i + a].at[rows], load_sem.at[4 * n + a])
            for a in range(4)
        ]
        for one in four:
            one.start()
        loads.append(four)
    stores = []
    for n, (i, first) in enumerate(chunks):
        rows = pl.ds(first, CHUNK_ROWS[i])
        for one in loads[n]:
            one.wait()
        weight, moment, square, grad = [held[4 * i + a][rows, :] for a in range(4)]
        new = adam_update(weight, moment, square, grad.astype(f32), RATES[i], decay_rate)
        for a in range(3):
            made[3 * i + a][rows, :] = new[a]
            one = pltpu.make_async_copy(
                made[3 * i + a].at[rows], outs[3 * i + a].at[rows], store_sem.at[2 + 3 * n + a]
            )
            one.start()
            stores.append(one)
    for one in tokens + stores:
        one.wait()


def adam(groups, tokens):
    hbm = pl.BlockSpec(memory_space=pl.ANY)
    counts = sum(shape[0] // rows for shape, rows in zip(SHAPES, CHUNK_ROWS))
    results = [jax.ShapeDtypeStruct(shape, f32) for shape in SHAPES for a in range(3)]
    results += [jax.ShapeDtypeStruct((128, D), bf16)] * 2
    held = [pltpu.VMEM(shape, kind) for shape in SHAPES for kind in (f32, f32, f32, bf16)]
    made = [pltpu.VMEM(shape, f32) for shape in SHAPES for a in range(3)]
    return pl.pallas_call(
        adam_kernel,
        out_shape=results,
        in_specs=[hbm] * 18,
        out_specs=[hbm] * 14,
        scratch_shapes=held
        + made
        + [pltpu.SemaphoreType.DMA((4 * counts,)), pltpu.SemaphoreType.DMA((2 + 3 * counts,))],
        compiler_params=pltpu.CompilerParams(vmem_limit_bytes=48 << 20),
        name="adam",
    )(*[array for group in groups for array in group], *tokens)


def on_device(
    tokens, d_out, block_ids,
    w_qkv, w_out, w_gate_up, w_down, gains,
    moment_qkv, moment_out, moment_gate_up, moment_down, moment_gains,
    square_qkv, square_out, square_gate_up, square_down, square_gains,
):
    f = lax.axis_index("fsdp")
    starts = block_ids[0].astype(f32) * BLOCK
    spots = starts[:, None] + jnp.arange(BLOCK, dtype=f32)[None, :]
    mine = lax.dynamic_slice(spots, (8 * lax.div(lax.axis_index("ctx"), 4), 0), (8, BLOCK))
    mine = mine.reshape(4, 2, BLOCK).transpose(1, 0, 2).reshape(1, 512)
    positions = jnp.concatenate([spots.reshape(1, D), jnp.tile(mine, (7, 2))], axis=0)
    gain_rows = lax.dynamic_update_slice(
        jnp.zeros((24 * 128,), f32), gains.astype(bf16).astype(f32), (f * 144,)
    ).reshape(24, 128)
    half = rope_base ** (-(np.arange(64, dtype=np.float32) * np.float32(2.0 / HEAD)))
    table = np.zeros((8, 128), np.float32)
    table[0] = np.concatenate([half, half])
    table[1] = np.concatenate([-np.ones(64), np.ones(64)])
    out_tok, dtok, g_qkv, g_out, g_gu, g_dn, g_gain = layer(
        tokens[0], d_out[0], positions, gain_rows, jnp.asarray(table), w_qkv, w_out, w_gate_up, w_down
    )
    grad_gains = lax.dynamic_slice(g_gain.reshape(24 * 128), (f * 144,), (144,))
    groups = (
        (w_qkv, moment_qkv, square_qkv, g_qkv),
        (w_out, moment_out, square_out, g_out),
        (w_gate_up, moment_gate_up, square_gate_up, g_gu),
        (w_down, moment_down, square_down, g_dn),
    )
    *updates, out_tokens, d_tokens = adam(groups, (out_tok, dtok))
    updates += adam_update(gains, moment_gains, square_gains, grad_gains, 0.5, 0.0)
    return (out_tokens[None], d_tokens[None], *updates[0::3], *updates[1::3], *updates[2::3])


def solution(mesh):
    rows, flat = P("fsdp", None), P("fsdp")
    tokens = P("fsdp", "ctx", None)
    state = (rows, rows, rows, rows, flat)
    return jax.shard_map(
        on_device,
        mesh=mesh,
        in_specs=(tokens, tokens, rows) + state * 3,
        out_specs=(tokens, tokens) + state * 3,
        check_vma=False,
    )
```

```python
import math
import types

import jax
import jax.numpy as jnp
import numpy as np
from jax import lax
from jax.experimental import pallas as pl
from jax.experimental.pallas import tpu as pltpu
from jax.sharding import PartitionSpec as P

D = 1024
HEAD = 128
STEP = 10
BLOCK = 64
norm_eps = 1e-06
rope_base = 1000000.0
beta_first = 0.9
beta_second = 0.95
adam_eps = 1e-08
decay_rate = 0.1
SCALE = 1.0 / math.sqrt(HEAD)

f32 = jnp.float32
bf16 = jnp.bfloat16
MESH = pl.DeviceIdType.MESH

INPUTS = dict(
    tok=False, dyt=False, pos_in=False, gain_in=False, freq=False, wqkv_f=True, wo_f=False, wgu_f=True, wd_f=False
)
OUTPUTS = dict(
    out_tok=((128, D), bf16),
    dtok=((128, D), bf16),
    g_qkv=((64, 4096), bf16),
    g_out=((128, D), bf16),
    g_gu=((64, 6144), bf16),
    g_dn=((192, D), bf16),
    g_gain=((24, 128), f32),
)
BUFFERS = dict(
    x_all=((4, 2, 128, D), bf16),
    dy_all=((4, 2, 128, D), bf16),
    n2_all=((4, 2, 128, D), bf16),
    n1_all=((4, 256, D), bf16),
    xo_all=((4, 2, 128, D), bf16),
    n1o_all=((4, 256, D), bf16),
    cos_o=((4, 256, HEAD), f32),
    sin_o=((4, 256, HEAD), f32),
    kraw_o=((4, 256, HEAD), f32),
    wq_f=((2, 64, 512), f32),
    wgu_fs=((2, 64, 768), f32),
    wqq_send=((2, 64, 256), bf16),
    wkv_send=((2, 64, 256), bf16),
    wgu_send=((2, 64, 768), bf16),
    wo_own=((128, D), bf16),
    wd_own=((192, D), bf16),
    wqq=((16, 64, 256), bf16),
    wkv=((16, 64, 256), bf16),
    wgu=((16, 64, 768), bf16),
    wo=((256, D), bf16),
    wd=((384, D), bf16),
    gain_recv=((16, 24, 128), f32),
    pos=((2, 8, D), f32),
    posk=((2, D, 1), f32),
    cos_t=((4, 256, HEAD), f32),
    sin_t=((4, 256, HEAD), f32),
    qkraw=((4, 256, 384), f32),
    q_s=((2, 2, 256, 256), bf16),
    kv=((2, D, 256), bf16),
    o_t=((2, 256, 512), f32),
    ob_t=((2, 256, 512), bf16),
    lse=((2, 2, 1, 512), f32),
    pa=((4, 2, 128, D), bf16),
    pb=((4, 2, 128, D), bf16),
    ca=((4, 128, D), bf16),
    cb=((4, 128, D), bf16),
    ra=((3, 128, D), bf16),
    rb=((3, 128, D), bf16),
    h1=((128, D), f32),
    dh1=((128, D), f32),
    hid_all=((4, 2, 128, 384), bf16),
    dgu_all=((4, 2, 128, 768), bf16),
    do_t=((2, 256, 512), bf16),
    delta=((2, 2, 1, 512), f32),
    dkv=((2, D, 256), f32),
    dkv_o=((4, 256, 256), bf16),
    dkv_recv=((4, 256, 256), bf16),
    go_sum=((256, D), f32),
    dqkv=((4, 256, 512), bf16),
    gqa=((D, 256), bf16),
    gqb=((D, 256), bf16),
    ggua=((8, 2, 64, 256), bf16),
    ggub=((D, 512), bf16),
    go=((256, D), bf16),
    gd=((384, D), bf16),
    zqa=((3, 2, 128, 256), bf16),
    zqb=((3, 2, 128, 256), bf16),
    zgua=((3, 64, 256), bf16),
    zgub=((3, 2, 128, 512), bf16),
    zo=((3, 2, 32, D), bf16),
    zd=((3, 48, 512), bf16),
    sqa=((2, 128, 256), bf16),
    sqb=((2, 128, 256), bf16),
    sgua=((4, 64, 256), bf16),
    sgub=((2, 128, 512), bf16),
    so=((2, 32, D), bf16),
    sd=((192, 512), bf16),
    xqa=((3, 64, 256), bf16),
    xqb=((3, 64, 256), bf16),
    xgua=((3, 4, 64, 256), bf16),
    xgub=((3, 64, 512), bf16),
    xo=((3, 32, 512), bf16),
    xd=((3, 192, 512), bf16),
    hqa=((2, 64, 256), bf16),
    hqb=((64, 256), bf16),
    hgu=((2, 64, 768), bf16),
    ho=((32, D), bf16),
    hd=((48, D), bf16),
    yo=((3, 32, D), bf16),
    yd=((3, 48, D), bf16),
    fqa=((8, 64, 256), bf16),
    fqb=((8, 64, 256), bf16),
    fgu=((8, 64, 768), bf16),
    fo=((128, D), bf16),
    fd=((192, D), bf16),
    dg=((24, 128), f32),
    dg_r1=((8, 24, 128), f32),
    dg_s=((2, 24, 128), f32),
    dg_r2=((6, 24, 128), f32),
)
SEMAPHORES = dict(
    ld=16,
    s_x=8, r_x=8,
    s_dy=8, r_dy=8,
    s_n2=16, r_n2=16,
    s_dob=16, r_dob=16,
    s_pos=1, r_pos=1,
    s_gain=12, r_gain=12,
    s_wqq=12, r_wqq=12,
    s_wkv=12, r_wkv=12,
    s_wgu=12, r_wgu=12,
    s_wo=4, r_wo=1, s_wd=4, r_wd=1,
    s_wo2=8, r_wo2=8, s_wd2=8, r_wd2=8,
    s_xo=9, r_xo=9,
    s_c=32, r_c=32,
    s_r=48, r_r=48,
    s_dkv=2, r_dkv=2,
    s_gqa=9, r_gqa=9,
    s_gqb=9, r_gqb=9,
    s_ggua=6, r_ggua=6,
    s_ggub=9, r_ggub=9,
    s_go=9, r_go=9,
    s_gd=6, r_gd=6,
    s_fqa=9, r_fqa=9,
    s_fqb=8, r_fqb=8,
    s_fgu=9, r_fgu=9,
    s_fo=9, r_fo=9,
    s_fd=9, r_fd=9,
    s_dg1=8, r_dg1=8,
    s_dg2=6, r_dg2=6,
)


def dot(a, b):
    return jnp.dot(a, b, preferred_element_type=f32)


def dot_nt(a, b):
    return lax.dot_general(a, b, (((1,), (1,)), ((), ())), preferred_element_type=f32)


def dot_tn(a, b):
    return lax.dot_general(a, b, (((0,), (0,)), ((), ())), preferred_element_type=f32)


def to_row(g, first, count):
    return jnp.concatenate([g[first + i : first + i + 1, :] for i in range(count)], axis=1)


def layer_kernel(*refs):
    names = [*INPUTS, *OUTPUTS, *BUFFERS, *SEMAPHORES]
    r = types.SimpleNamespace(**dict(zip(names, refs, strict=True)))

    c = lax.axis_index("ctx")
    f = lax.axis_index("fsdp")
    xh, y = lax.div(c, 4), lax.rem(c, 4)
    xl, z, k = lax.div(f, 8), lax.rem(lax.div(f, 2), 4), lax.rem(f, 2)
    x = 2 * xh + xl
    part = 4 * xl + z
    t = 2 * y + k
    other = 1 - k

    def place(xh_, xl_, y_, z_, k_):
        return (xh_ * 4 + y_, xl_ * 8 + z_ * 2 + k_)

    partner = place(xh, xl, y, z, other)

    def around(value, step):
        return lax.rem(value + step, 4)

    def copy(src, dst, ss, rs, device):
        return pltpu.make_async_remote_copy(
            src_ref=src, dst_ref=dst, send_sem=ss, recv_sem=rs,
            device_id=device, device_id_type=MESH,
        )

    def send(src, dst, ss, rs, device):
        copy(src, dst, ss, rs, device).start()

    def got(ref, rs):
        copy(ref, ref, rs, rs, partner).wait_recv()

    def sent(ref, ss):
        copy(ref, ref, ss, ss, partner).wait_send()

    loads = []

    def load(src, dst):
        one = pltpu.make_async_copy(src, dst, r.ld.at[len(loads)])
        one.start()
        loads.append(one)

    for i in range(2):
        ti = 2 * y + i
        load(r.wqkv_f.at[:, pl.ds(pl.multiple_of(256 * ti, 256), 256)], r.wq_f.at[i, :, pl.ds(0, 256)])
        load(r.wqkv_f.at[:, pl.ds(pl.multiple_of(2048 + 128 * ti, 128), 128)], r.wq_f.at[i, :, pl.ds(256, 128)])
        load(r.wqkv_f.at[:, pl.ds(pl.multiple_of(3072 + 128 * ti, 128), 128)], r.wq_f.at[i, :, pl.ds(384, 128)])
    for i in range(2):
        ti = 2 * y + i
        load(r.wgu_f.at[:, pl.ds(pl.multiple_of(384 * ti, 128), 384)], r.wgu_fs.at[i, :, pl.ds(0, 384)])
        load(r.wgu_f.at[:, pl.ds(pl.multiple_of(3072 + 384 * ti, 128), 384)], r.wgu_fs.at[i, :, pl.ds(384, 384)])

    barrier = pltpu.get_barrier_semaphore()

    def greet(device):
        pl.semaphore_signal(barrier, inc=1, device_id=device, device_id_type=MESH)

    def greet_plane(i, carry):
        greet(place(xh, lax.rem(xl + lax.div(i, 8), 2), y, around(z, lax.rem(lax.div(i, 2), 4)), lax.rem(k + i, 2)))
        return carry

    def along_x(d):
        x_ = around(x, d)
        return place(lax.div(x_, 2), lax.rem(x_, 2), y, z, k)

    for i in range(1, 8):
        greet(place(xh, xl, around(y, i // 2), z, lax.rem(k + i, 2)))
    for i in range(8):
        greet(place(1 - xh, xl, around(y, i // 2), z, lax.rem(k + i, 2)))
    lax.fori_loop(1, 16, greet_plane, 0)
    for d in range(1, 4):
        greet(along_x(d))

    for one in loads:
        one.wait()
    r.wqq_send[...] = r.wq_f[:, :, 0:256].astype(bf16)
    r.wkv_send[...] = r.wq_f[:, :, 256:512].astype(bf16)
    r.wgu_send[...] = r.wgu_fs[...].astype(bf16)
    r.wo_own[...] = r.wo_f[...].astype(bf16)
    r.wd_own[...] = r.wd_f[...].astype(bf16)
    r.wqq[f] = r.wqq_send[k]
    r.wkv[f] = r.wkv_send[k]
    r.wgu[f] = r.wgu_send[k]
    r.gain_recv[f] = r.gain_in[...]
    r.x_all[y, k] = r.tok[...]
    r.dy_all[y, k] = r.dyt[...]
    r.pos[k] = r.pos_in[...]
    r.dg[...] = jnp.zeros((24, 128), f32)
    pl.semaphore_wait(barrier, 33)

    def rows_of(half):
        return pl.ds(0, 128) if half is None else pl.ds(64 * half, 64)

    def far_part(half, which):
        size = 64 if half is None else 32
        return pl.ds((0 if half is None else 64 * half) + size * which, size)

    def gather_start(src, whole, ss, rs, half=None):
        rows, o = rows_of(half), 8 * (half or 0)
        for d in (1, 3):
            send(src.at[rows], whole.at[y, k, rows], ss.at[o + d - 1], rs.at[o + d - 1], place(xh, xl, around(y, d), z, k))
        send(src.at[rows], whole.at[y, k, rows], ss.at[o + 3], rs.at[o + 3], partner)

    def gather_forward(whole, ss, rs, d, half=None):
        rows, o = rows_of(half), 8 * (half or 0)
        block = whole.at[around(y, 4 - d), k, rows]
        if d == 2:
            for which in range(2):
                got(whole.at[around(y, 2), k, far_part(half, which)], rs.at[o + (1, 7)[which]])
        else:
            got(block, rs.at[o + d - 1])
            which = 0 if d == 1 else 1
            part_of = whole.at[around(y, 4 - d), k, far_part(half, which)]
            i = o + (1, 7)[which]
            send(part_of, part_of, ss.at[i], rs.at[i], place(xh, xl, around(y, d), z, k))
        send(block, block, ss.at[o + 3 + d], rs.at[o + 3 + d], partner)

    def gather_own(whole, rs, half=None):
        got(whole.at[y, other, rows_of(half)], rs.at[8 * (half or 0) + 3])

    def gather_pair(whole, rs, d, half=None):
        got(whole.at[around(y, 4 - d), other, rows_of(half)], rs.at[8 * (half or 0) + 3 + d])

    def gather_end(whole, ss, half=None):
        o = 8 * (half or 0)
        for i in (0, 2, 3, 4, 5, 6):
            sent(whole.at[y, k, rows_of(half)], ss.at[o + i])
        for i in (1, 7):
            sent(whole.at[y, k, far_part(half, 0)], ss.at[o + i])

    def chip_slots(whole, l_, zz):
        return whole.at[pl.ds(8 * l_ + 2 * zz, 2)]

    def z_send(src_of, whole, ss, rs):
        for i in range(1, 8):
            core = lax.rem(k + i, 2)
            send(src_of(core), whole.at[f], ss.at[i], rs.at[i], place(xh, xl, y, around(z, i // 2), core))

    def z_got(whole, rs, dz):
        for dk in range(2):
            if dz + dk > 0:
                got(whole.at[8 * xl + 2 * around(z, 4 - dz) + lax.rem(k + dk, 2)], rs.at[2 * dz + dk])

    def beside(dz):
        return along_x(1 if dz < 2 else 3)

    def x_send(whole, ss, rs, dz):
        block = chip_slots(whole, xl, around(z, 4 - dz))
        send(block, block, ss.at[8 + dz], rs.at[8 + dz], beside(dz))

    def x_got(whole, rs, dz):
        got(chip_slots(whole, 1 - xl, around(z, 4 - dz)), rs.at[8 + dz])

    def rows_sent(whole, ss):
        for i in range(1, 8):
            sent(whole.at[f], ss.at[i])
        for dz in range(4):
            sent(chip_slots(whole, xl, around(z, 4 - dz)), ss.at[8 + dz])

    def loop_sent(ref, ss, first, last):
        def one(i, carry):
            sent(ref, ss.at[i])
            return carry

        lax.fori_loop(first, last, one, 0)

    gather_start(r.tok, r.x_all, r.s_x, r.r_x)
    send(r.tok, r.xo_all.at[y, k], r.s_xo.at[8], r.r_xo.at[8], along_x(2))
    z_send(lambda k_: r.gain_in, r.gain_recv, r.s_gain, r.r_gain)
    z_send(lambda k_: r.wkv_send.at[k_], r.wkv, r.s_wkv, r.r_wkv)
    send(r.pos_in, r.pos.at[k], r.s_pos.at[0], r.r_pos.at[0], partner)
    z_send(lambda k_: r.wqq_send.at[k_], r.wqq, r.s_wqq, r.r_wqq)

    is_source = lax.div(part, 2) == y
    to_core = lax.rem(part, 2)
    for i in range(4):
        piece = 4 * k + i
        here = (xl == k) & (z == i) & (to_core == k)

        @pl.when(is_source & jnp.logical_not(here))
        def _():
            there = place(xh, k, y, i, to_core)
            send(r.wo_own.at[pl.ds(32 * i, 32)], r.wo.at[pl.ds(pl.multiple_of(32 * piece, 32), 32)], r.s_wo.at[i], r.r_wo.at[0], there)
            send(r.wd_own.at[pl.ds(48 * i, 48)], r.wd.at[pl.ds(pl.multiple_of(48 * piece, 16), 48)], r.s_wd.at[i], r.r_wd.at[0], there)

        @pl.when(is_source & here)
        def _():
            r.wo[pl.ds(pl.multiple_of(32 * piece, 32), 32), :] = r.wo_own[32 * i : 32 * i + 32, :]
            r.wd[pl.ds(pl.multiple_of(48 * piece, 16), 48), :] = r.wd_own[48 * i : 48 * i + 48, :]

    def wo_rows(q):
        return r.wo.at[pl.ds(pl.multiple_of(32 * q, 32), 32)]

    def wd_rows(q):
        return r.wd.at[pl.ds(pl.multiple_of(48 * q, 16), 48)]

    def pass_on(whole, ss, rs, dz):
        z_got(whole, rs, dz)
        x_send(whole, ss, rs, dz)

    pass_on(r.gain_recv, r.s_gain, r.r_gain, 0)
    pass_on(r.wkv, r.s_wkv, r.r_wkv, 0)

    got(r.pos.at[other], r.r_pos.at[0])
    steps = lax.broadcasted_iota(jnp.int32, (BLOCK, 1), 0).astype(f32)
    for s in range(2):
        for b in range(16):
            r.posk[s, b * BLOCK : (b + 1) * BLOCK, :] = r.pos[s, 0:1, b * BLOCK : b * BLOCK + 1] + steps
    freq = r.freq[0:1, :]
    sign = r.freq[1:2, :]

    def tables(i, carry):
        hh, yy = lax.rem(xh + lax.div(i, 4), 2), lax.rem(i, 4)
        for s in range(2):
            rows = r.posk[s, pl.ds(pl.multiple_of(512 * hh + 128 * yy, 128), 128), :]
            angle = rows * freq
            cos, sin = jnp.cos(angle), jnp.sin(angle) * sign

            @pl.when(i < 4)
            def _():
                r.cos_t[yy, s * 128 : (s + 1) * 128, :] = cos
                r.sin_t[yy, s * 128 : (s + 1) * 128, :] = sin

            @pl.when(i >= 4)
            def _():
                r.cos_o[yy, s * 128 : (s + 1) * 128, :] = cos
                r.sin_o[yy, s * 128 : (s + 1) * 128, :] = sin

        return carry

    lax.fori_loop(0, 2, tables, 0)

    for dz in (1, 3):
        pass_on(r.gain_recv, r.s_gain, r.r_gain, dz)
        pass_on(r.wkv, r.s_wkv, r.r_wkv, dz)
    for d in (1, 3):
        gather_forward(r.x_all, r.s_x, r.r_x, d)
    got(r.xo_all.at[y, k], r.r_xo.at[8])
    gather_start(r.xo_all.at[y, k], r.xo_all, r.s_xo, r.r_xo)
    gather_start(r.dyt, r.dy_all, r.s_dy, r.r_dy)
    pass_on(r.gain_recv, r.s_gain, r.r_gain, 2)
    pass_on(r.wkv, r.s_wkv, r.r_wkv, 2)
    lax.fori_loop(2, 4, tables, 0)
    own_piece = (2 * y + k == part) & (xl == k)

    def start_rest():
        for dz in (0, 1, 3, 2):
            pass_on(r.wqq, r.s_wqq, r.r_wqq, dz)

        @pl.when(jnp.logical_not(own_piece))
        def _():
            got(wo_rows(part), r.r_wo.at[0])
            got(wd_rows(part), r.r_wd.at[0])

        for dz in range(1, 4):
            there = place(xh, xl, y, around(z, dz), k)
            send(wo_rows(part), wo_rows(part), r.s_wo2.at[dz], r.r_wo2.at[dz], there)
        z_send(lambda k_: r.wgu_send.at[k_], r.wgu, r.s_wgu, r.r_wgu)
        for dz in range(1, 4):
            there = place(xh, xl, y, around(z, dz), k)
            send(wd_rows(part), wd_rows(part), r.s_wd2.at[dz], r.r_wd2.at[dz], there)

    def piece_of(l_, dz):
        return 4 * l_ + around(z, 4 - dz)

    for dz in range(4):
        x_got(r.gain_recv, r.r_gain, dz)
    gains = jnp.sum(r.gain_recv[...], axis=0)
    g1 = to_row(gains, 0, 8)
    g2 = to_row(gains, 8, 8)
    gq = gains[16:17, :]
    gk = gains[17:18, :]

    def rotated(u, cos, sin):
        return u * cos + pltpu.roll(u, 64, 1) * sin

    def unrotated(u, cos, sin):
        return u * cos - pltpu.roll(u, 64, 1) * sin

    def inverse_rms(u):
        return lax.rsqrt(jnp.mean(u * u, axis=-1, keepdims=True) + norm_eps)

    def project_keys(d, x_all, n1_all, raw_at, cos, sin, hh):
        yy = around(y, 4 - d)
        rows = x_all[yy].reshape(256, D).astype(f32)
        n1 = (rows * inverse_rms(rows) * g1).astype(bf16)
        n1_all[yy] = n1
        kv = dot(n1, r.wkv[...].reshape(D, 256))
        raw = kv[:, 0:HEAD]
        raw_at(yy)[...] = raw
        local = pl.ds(pl.multiple_of(512 * hh + 128 * yy, 128), 128)
        key = rotated(raw * inverse_rms(raw) * gk, cos[yy], sin[yy]).astype(bf16)
        value = kv[:, HEAD:].astype(bf16)
        for s in range(2):
            r.kv[s, local, 0:HEAD] = key[s * 128 : (s + 1) * 128]
            r.kv[s, local, HEAD : 2 * HEAD] = value[s * 128 : (s + 1) * 128]

    def project_mine(d):
        project_keys(d, r.x_all, r.n1_all, lambda yy: r.qkraw.at[yy, :, pl.ds(256, HEAD)], r.cos_t, r.sin_t, xh)

    def project_others(d):
        project_keys(d, r.xo_all, r.n1o_all, lambda yy: r.kraw_o.at[yy], r.cos_o, r.sin_o, 1 - xh)

    def project_queries(yy, carry):
        qs = dot(r.n1_all[yy], r.wqq[...].reshape(D, 256))
        r.qkraw[yy, :, 0:256] = qs
        for h in range(2):
            raw = qs[:, h * HEAD : (h + 1) * HEAD]
            query = rotated(raw * inverse_rms(raw) * gq, r.cos_t[yy], r.sin_t[yy]).astype(bf16)
            for s in range(2):
                for half in range(2):
                    first = s * 128 + half * 64
                    rows = pl.ds(pl.multiple_of(64 * yy, 64), 64)
                    r.q_s[s, half, rows, h * HEAD : (h + 1) * HEAD] = query[first : first + 64]
        return carry

    gather_own(r.x_all, r.r_x)
    for dz in range(4):
        x_got(r.wkv, r.r_wkv, dz)
    project_mine(0)
    gather_pair(r.x_all, r.r_x, 1)
    project_mine(1)
    gather_forward(r.x_all, r.s_x, r.r_x, 2)
    gather_pair(r.x_all, r.r_x, 3)
    project_mine(3)
    start_rest()
    gather_pair(r.x_all, r.r_x, 2)
    project_mine(2)
    for d in (1, 3):
        gather_forward(r.xo_all, r.s_xo, r.r_xo, d)
    lax.fori_loop(4, 8, tables, 0)
    for dz in range(4):
        if dz > 0:
            got(wo_rows(piece_of(xl, dz)), r.r_wo2.at[dz])
        block = wo_rows(piece_of(xl, dz))
        send(block, block, r.s_wo2.at[4 + dz], r.r_wo2.at[4 + dz], beside(dz))
    for dz in range(4):
        x_got(r.wqq, r.r_wqq, dz)
    lax.fori_loop(0, 4, project_queries, 0)
    gather_own(r.xo_all, r.r_xo)
    project_others(0)
    gather_forward(r.xo_all, r.s_xo, r.r_xo, 2)
    gather_pair(r.xo_all, r.r_xo, 1)
    project_others(1)
    gather_pair(r.xo_all, r.r_xo, 3)
    project_others(3)
    gather_pair(r.xo_all, r.r_xo, 2)
    project_others(2)
    gather_end(r.x_all, r.s_x)

    def rest_forward():
        for dz in range(4):
            pass_on(r.wgu, r.s_wgu, r.r_wgu, dz)
        for dz in range(4):
            if dz > 0:
                got(wd_rows(piece_of(xl, dz)), r.r_wd2.at[dz])
            block = wd_rows(piece_of(xl, dz))
            send(block, block, r.s_wd2.at[4 + dz], r.r_wd2.at[4 + dz], beside(dz))

    def lanes(half):
        return pl.ds(pl.multiple_of(256 * half, 256), 256)

    def allowed(s, half):
        return r.posk[s] <= r.pos[s, 1:2, lanes(half)]

    def attend(s, half):
        ok = allowed(s, half)
        for h in range(2):
            q = r.q_s[s, half, :, h * HEAD : (h + 1) * HEAD]
            scores = jnp.where(ok, dot_nt(r.kv[s, :, 0:HEAD], q) * SCALE, -1e30)
            top = jnp.max(scores, axis=0, keepdims=True)
            p = jnp.exp(scores - top)
            total = jnp.sum(p, axis=0, keepdims=True)
            o = dot_tn(r.kv[s, :, HEAD : 2 * HEAD], p.astype(bf16)) / total
            r.o_t[s, h * HEAD : (h + 1) * HEAD, lanes(half)] = o
            r.ob_t[s, h * HEAD : (h + 1) * HEAD, lanes(half)] = o.astype(bf16)
            r.lse[s, h, :, lanes(half)] = top + jnp.log(total)

    def reduce_first(use, p, cc, d, half=None):
        yy, rows, i = around(y, d), rows_of(half), 8 * use + 4 * (half or 0) + d
        send(p.at[yy, other, rows], cc.at[yy, rows], r.s_c.at[i], r.r_c.at[i], partner)

    def both_cores(use, p, cc, d, half):
        yy, rows, i = around(y, d), rows_of(half), 8 * use + 4 * (half or 0) + d
        got(cc.at[yy, rows], r.r_c.at[i])
        return p[yy, k, rows, :].astype(f32) + cc[yy, rows, :].astype(f32)

    def reduce_far(use, p, cc, rr, half=None):
        rows, o = rows_of(half), 12 * use + 6 * (half or 0)
        yy = around(y, 2)
        p[yy, k, rows, :] = both_cores(use, p, cc, 2, half).astype(bf16)
        for which in range(2):
            rest = far_part(half, which)
            there = place(xh, xl, around(y, 1 + 2 * which), z, k)
            send(p.at[yy, k, rest], rr.at[2, rest], r.s_r.at[o + which], r.r_r.at[o + which], there)
        for which in range(2):
            yy = around(y, 1 + 2 * which)
            p[yy, k, rows, :] = both_cores(use, p, cc, 1 + 2 * which, half).astype(bf16)
            early, i = far_part(half, 1 - which), o + 2 + which
            send(p.at[yy, k, early], rr.at[which, early], r.s_r.at[i], r.r_r.at[i], place(xh, xl, yy, z, k))

    def reduce_near(use, p, rr, half=None):
        o = 12 * use + 6 * (half or 0)
        for which in range(2):
            yy = around(y, 1 + 2 * which)
            late, i = far_part(half, which), o + 4 + which
            got(rr.at[2, late], r.r_r.at[o + which])
            p[yy, k, late, :] = (p[yy, k, late, :].astype(f32) + rr[2, late, :].astype(f32)).astype(bf16)
            send(p.at[yy, k, late], rr.at[which, late], r.s_r.at[i], r.r_r.at[i], place(xh, xl, yy, z, k))

    def reduce_third(use, p, cc, rr, half=None):
        rows, o = rows_of(half), 12 * use + 6 * (half or 0)
        total = both_cores(use, p, cc, 0, half)
        for which in range(2):
            got(rr.at[which, far_part(half, 1 - which)], r.r_r.at[o + 2 + which])
            got(rr.at[which, far_part(half, which)], r.r_r.at[o + 4 + which])
            total = total + rr[which, rows, :].astype(f32)
        return total

    def reduce_end(use, p, half=None):
        for d in range(4):
            sent(p.at[y, other, rows_of(half)], r.s_c.at[8 * use + 4 * (half or 0) + d])
        for i in range(6):
            sent(p.at[y, k, far_part(half, 0)], r.s_r.at[12 * use + 6 * (half or 0) + i])

    def out_partial(half):
        for s in range(2):
            o = r.ob_t[s, :, lanes(half)]
            r.pa[:, s, rows_of(half), :] = dot_tn(o, r.wo[...]).astype(bf16).reshape(4, 64, D)
        for d in (2, 1, 3, 0):
            reduce_first(0, r.pa, r.ca, d, half)

    for d in (1, 3):
        gather_forward(r.dy_all, r.s_dy, r.r_dy, d)
    attend(0, 0)
    attend(1, 0)
    for dz in range(4):
        got(wo_rows(piece_of(1 - xl, dz)), r.r_wo2.at[4 + dz])
    out_partial(0)
    rest_forward()
    attend(0, 1)
    reduce_far(0, r.pa, r.ca, r.ra, 0)
    gather_forward(r.dy_all, r.s_dy, r.r_dy, 2)
    attend(1, 1)
    out_partial(1)
    reduce_near(0, r.pa, r.ra, 0)
    reduce_far(0, r.pa, r.ca, r.ra, 1)

    def middle(half):
        rows = rows_of(half)
        h1 = r.tok[rows, :].astype(f32) + reduce_third(0, r.pa, r.ca, r.ra, half)
        r.h1[rows, :] = h1
        r.n2_all[y, k, rows, :] = (h1 * inverse_rms(h1) * g2).astype(bf16)
        gather_start(r.n2_all.at[y, k], r.n2_all, r.s_n2, r.r_n2, half)

    middle(0)
    reduce_near(0, r.pa, r.ra, 1)
    middle(1)

    gather_own(r.dy_all, r.r_dy)
    for d in (1, 3, 2):
        gather_pair(r.dy_all, r.r_dy, d)
    for dz in range(4):
        x_got(r.wgu, r.r_wgu, dz)
        got(wd_rows(piece_of(1 - xl, dz)), r.r_wd2.at[4 + dz])

    def two_blocks(whole, ds, half):
        blocks = [whole[around(y, d), :, rows_of(half), :].reshape(128, whole.shape[-1]) for d in ds]
        return jnp.concatenate(blocks, axis=0)

    def put_blocks(whole, ds, half, cols, value):
        for i, d in enumerate(ds):
            block = value[128 * i : 128 * (i + 1)].reshape(2, 64, value.shape[-1])
            whole[around(y, d), :, rows_of(half), cols] = block

    def feed(ds, half):
        n2 = two_blocks(r.n2_all, ds, half)
        ab = dot(n2, r.wgu[...].reshape(D, 768))
        a, b = ab[:, :384], ab[:, 384:]
        sig = jax.nn.sigmoid(a)
        silu = a * sig
        put_blocks(r.hid_all, ds, half, slice(None), (silu * b).astype(bf16))
        dhid = dot_nt(two_blocks(r.dy_all, ds, half), r.wd[...])
        da = (dhid * b * sig * (1.0 + a * (1.0 - sig))).astype(bf16)
        db = (dhid * silu).astype(bf16)
        put_blocks(r.dgu_all, ds, half, slice(0, 384), da)
        put_blocks(r.dgu_all, ds, half, slice(384, 768), db)
        dn2 = dot_nt(jnp.concatenate([da, db], axis=1), r.wgu[...].reshape(D, 768))
        put_blocks(r.pb, ds, half, slice(None), dn2.astype(bf16))
        for d in ds:
            reduce_first(1, r.pb, r.cb, d, half)

    def near_forward(whole, ss, rs, half):
        for d in (1, 3):
            gather_forward(whole, ss, rs, d, half)

    near_forward(r.n2_all, r.s_n2, r.r_n2, 0)
    for half in range(2):
        gather_own(r.n2_all, r.r_n2, half)
        gather_pair(r.n2_all, r.r_n2, 1, half)
        feed((0, 3), half)
        if half == 1:
            reduce_near(1, r.pb, r.rb, 0)
        gather_forward(r.n2_all, r.s_n2, r.r_n2, 2, half)
        if half == 0:
            near_forward(r.n2_all, r.s_n2, r.r_n2, 1)
        gather_pair(r.n2_all, r.r_n2, 3, half)
        gather_pair(r.n2_all, r.r_n2, 2, half)
        feed((2, 1), half)
        reduce_far(1, r.pb, r.cb, r.rb, half)

    def rows_at(whole, height):
        return lambda l_, z_: whole.at[pl.ds(pl.multiple_of(height * (4 * l_ + z_), 16), height)]

    def cross_z(piece, dst, ss, rs):
        for dz in (1, 3, 2):
            zz = around(z, dz)
            for l_ in range(2):
                i = 2 * (dz - 1) + l_
                send(piece(l_, zz), dst.at[dz - 1, l_], ss.at[i], rs.at[i], place(xh, xl, y, zz, k))

    def row_half(ref, h_):
        return ref.at[pl.ds(pl.multiple_of(64 * h_, 64), 64)]

    def column_half(ref, h_):
        return ref.at[:, pl.ds(pl.multiple_of(512 * h_, 512), 512)]

    def cross_x(piece, zrecv, sums, xrecv, half_of, ss, rs):
        for l_ in range(2):
            total = piece(l_, z)[...].astype(f32)
            for dz in range(1, 4):
                got(zrecv.at[dz - 1, l_], rs.at[2 * (dz - 1) + l_])
                total = total + zrecv[dz - 1, l_].astype(f32)
            sums[l_] = total.astype(bf16)
        for dx in (1, 3, 2):
            x_ = around(x, dx)
            block = half_of(sums.at[lax.rem(x_, 2)], lax.div(x_, 2))
            send(block, xrecv.at[dx - 1], ss.at[5 + dx], rs.at[5 + dx], along_x(dx))

    def cross_total(sums, xrecv, half_of, rs):
        total = half_of(sums.at[xl], xh)[...].astype(f32)
        for dx in (1, 3, 2):
            got(xrecv.at[dx - 1], rs.at[5 + dx])
            total = total + xrecv[dx - 1].astype(f32)
        return total

    def cross_x_first(whole, height, xrecv, ss, rs):
        for dx in (1, 3, 2):
            x_ = around(x, dx)
            rows = pl.ds(pl.multiple_of(4 * height * lax.rem(x_, 2), 16), 4 * height)
            block = column_half(whole.at[rows], lax.div(x_, 2))
            send(block, xrecv.at[dx - 1], ss.at[dx - 1], rs.at[dx - 1], along_x(dx))

    def cross_z_second(whole, height, xrecv, sums, zrecv, ss, rs):
        rows = pl.ds(pl.multiple_of(4 * height * xl, 16), 4 * height)
        total = column_half(whole.at[rows], xh)[...].astype(f32)
        for dx in (1, 3, 2):
            got(xrecv.at[dx - 1], rs.at[dx - 1])
            total = total + xrecv[dx - 1].astype(f32)
        sums[...] = total.astype(bf16)
        for dz in (1, 3, 2):
            zz = around(z, dz)
            block = sums.at[pl.ds(pl.multiple_of(height * zz, 16), height)]
            send(block, zrecv.at[dz - 1], ss.at[2 + dz], rs.at[2 + dz], place(xh, xl, y, zz, k))

    def cross_z_total(height, sums, zrecv, rs):
        total = sums[pl.ds(pl.multiple_of(height * z, 16), height), :].astype(f32)
        for dz in (1, 3, 2):
            got(zrecv.at[dz - 1], rs.at[2 + dz])
            total = total + zrecv[dz - 1].astype(f32)
        return total

    def rows_x_first():
        for dx in (1, 3, 2):
            x_ = around(x, dx)
            block = r.ggua.at[pl.ds(4 * lax.rem(x_, 2), 4), lax.div(x_, 2)]
            send(block, r.xgua.at[dx - 1], r.s_ggua.at[dx - 1], r.r_ggua.at[dx - 1], along_x(dx))

    def rows_z_second():
        total = r.ggua[pl.ds(4 * xl, 4), xh].astype(f32)
        for dx in (1, 3, 2):
            got(r.xgua.at[dx - 1], r.r_ggua.at[dx - 1])
            total = total + r.xgua[dx - 1].astype(f32)
        r.sgua[...] = total.astype(bf16)
        for dz in (1, 3, 2):
            zz = around(z, dz)
            send(r.sgua.at[zz], r.zgua.at[dz - 1], r.s_ggua.at[2 + dz], r.r_ggua.at[2 + dz], place(xh, xl, y, zz, k))

    def rows_z_total():
        total = r.sgua[z].astype(f32)
        for dz in (1, 3, 2):
            got(r.zgua.at[dz - 1], r.r_ggua.at[2 + dz])
            total = total + r.zgua[dz - 1].astype(f32)
        return total

    def cross_sent(zrecv, xrecv, ss):
        for i in range(6):
            sent(zrecv.at[0, 0], ss.at[i])
        for i in range(3):
            sent(xrecv.at[0], ss.at[6 + i])

    gqa_piece, gqb_piece, ggub_piece = rows_at(r.gqa, 128), rows_at(r.gqb, 128), rows_at(r.ggub, 128)
    go_piece = rows_at(r.go, 32)

    def weight_gradient(left, right, out, first=0):
        def one(i, carry):
            cols = pl.ds(pl.multiple_of(256 * i, 256), 256)
            taken = pl.ds(pl.multiple_of(first + 256 * i, 256), 256)
            out[:, cols] = dot_tn(left(), right(taken)).astype(bf16)
            return carry

        lax.fori_loop(0, out.shape[1] // 256, one, 0)

    def middle_back(half):
        rows = rows_of(half)
        dn2 = reduce_third(1, r.pb, r.cb, r.rb, half)
        h1 = r.h1[rows, :]
        r2 = inverse_rms(h1)
        weighted = dn2 * g2
        back = r2 * weighted - h1 * (r2 * r2 * r2) * jnp.mean(weighted * h1, axis=-1, keepdims=True)
        dh1 = r.dyt[rows, :].astype(f32) + back
        r.dh1[rows, :] = dh1
        dg2 = jnp.sum(dn2 * h1 * r2, axis=0, keepdims=True)
        for i in range(8):
            r.dg[8 + i : 9 + i, :] += dg2[:, 128 * i : 128 * (i + 1)]
        r.x_all[y, k, rows, :] = dh1.astype(bf16)
        gather_start(r.x_all.at[y, k], r.x_all, r.s_dob, r.r_dob, half)

    ggua = dot_tn(r.n2_all[...].reshape(D, D), r.dgu_all[:, :, :, 0:256].reshape(D, 256))
    r.ggua[...] = ggua.astype(bf16).reshape(8, 2, 64, 256)
    rows_x_first()
    weight_gradient(
        lambda: r.n2_all[...].reshape(D, D),
        lambda cols: r.dgu_all[:, :, :, cols].reshape(D, 256),
        r.ggub,
        256,
    )
    cross_z(ggub_piece, r.zgub, r.s_ggub, r.r_ggub)
    reduce_near(1, r.pb, r.rb, 1)
    middle_back(0)
    weight_gradient(
        lambda: r.hid_all[...].reshape(D, 384),
        lambda cols: r.dy_all[:, :, :, cols].reshape(D, 256),
        r.gd,
    )
    cross_x_first(r.gd, 48, r.xd, r.s_gd, r.r_gd)
    middle_back(1)

    def direct_spread(total, hold, final, ss, rs):
        hold[...] = total.astype(bf16)

        def one(i, carry):
            there = place(lax.rem(xh + lax.div(i, 4), 2), xl, lax.rem(y + i, 4), z, xh)

            @pl.when((i > 0) | (k != xh))
            def _():
                send(hold, final.at[t], ss.at[i], rs.at[t], there)

            return carry

        lax.fori_loop(0, 8, one, 0)

        @pl.when(k == xh)
        def _():
            final[t] = hold[...]

    def direct_spread_sent(hold, ss):
        def one(i, carry):
            @pl.when((i > 0) | (k != xh))
            def _():
                sent(hold, ss.at[i])

            return carry

        lax.fori_loop(0, 8, one, 0)

    def direct_spread_got(final, rs):
        def one(i, carry):
            @pl.when((i != t) | (k != xh))
            def _():
                got(final.at[i], rs.at[i])

            return carry

        lax.fori_loop(0, 8, one, 0)

    other_half = place(1 - xh, xl, y, z, k)

    def rows_exchange(total, hold, ss, rs):
        hold[xh] = total.astype(bf16)
        send(hold.at[xh], hold.at[xh], ss.at[8], rs.at[8], other_half)

    def rows_spread(hold, final, ss, rs):
        for which in range(2):
            h = xh if which == 0 else 1 - xh
            if which == 1:
                got(hold.at[h], rs.at[8])
            for i in (2, 1, 3):
                send(hold.at[h], final.at[t], ss.at[4 * which + i], rs.at[t], place(xh, xl, around(y, i), z, h))

            @pl.when(k != h)
            def _():
                send(hold.at[h], final.at[t], ss.at[4 * which], rs.at[t], partner)

            @pl.when(k == h)
            def _():
                final[t] = hold[h]

    def rows_spread_sent(hold, ss):
        sent(hold.at[0], ss.at[8])
        for which in range(2):
            h = xh if which == 0 else 1 - xh
            for i in range(1, 4):
                sent(hold.at[0], ss.at[4 * which + i])

            @pl.when(k != h)
            def _():
                sent(hold.at[0], ss.at[4 * which])

    def rows_spread_got(final, rs):
        def one(i, carry):
            @pl.when(i != t)
            def _():
                got(final.at[i], rs.at[i])

            return carry

        lax.fori_loop(0, 8, one, 0)

    def block_exchange(total, hold, ss, rs):
        column_half(hold, xh)[...] = total.astype(bf16)
        send(column_half(hold, xh), column_half(hold, xh), ss.at[8], rs.at[8], other_half)

    def block_along_y(hold, held, ss, rs):
        got(column_half(hold, 1 - xh), rs.at[8])
        for i in (1, 3, 2):
            send(hold, held.at[i - 1], ss.at[i], rs.at[i], place(xh, xl, around(y, i), z, k))

    def block_target(i):
        slice_ = 2 * around(y, 4 - i) + k
        mine = (part == slice_) & (k == xl)
        return mine, place(xh, lax.div(slice_, 4), y, lax.rem(slice_, 4), xl)

    def block_deliver(hold, held, final, height, ss, rs):
        rows = pl.ds(pl.multiple_of(height * z, 16), height)
        for i in (0, 1, 3, 2):
            block = hold
            if i > 0:
                got(held.at[i - 1], rs.at[i])
                block = held.at[i - 1]
            mine, there = block_target(i)

            @pl.when(jnp.logical_not(mine))
            def _():
                send(block, final.at[rows], ss.at[4 + i], rs.at[4 + z], there)

            @pl.when(mine)
            def _():
                final[rows, :] = block[...]

    def block_sent(hold, ss):
        sent(column_half(hold, 0), ss.at[8])
        for i in range(4):
            if i > 0:
                sent(hold, ss.at[i])
            mine, there = block_target(i)

            @pl.when(jnp.logical_not(mine))
            def _():
                sent(hold, ss.at[4 + i])

    def block_got(final, height, rs):
        def one(i, carry):
            @pl.when(jnp.logical_not((xl == k) & (z == i) & (lax.rem(part, 2) == k)))
            def _():
                got(final.at[pl.ds(pl.multiple_of(height * i, 16), height)], rs.at[4 + i])

            return carry

        lax.fori_loop(0, 4, one, 0)

    def key_back(s, mine):
        span = slice(s * 128, (s + 1) * 128)
        rows = pl.ds(pl.multiple_of(512 * (xh if mine else 1 - xh), 512), 512)
        cos, sin = (r.cos_t, r.sin_t) if mine else (r.cos_o, r.sin_o)
        raw = r.qkraw[:, span, 256:384] if mine else r.kraw_o[:, span, :]
        du = unrotated(r.dkv[s, rows, 0:HEAD], cos[:, span, :].reshape(512, HEAD), sin[:, span, :].reshape(512, HEAD))
        back, gain_grad = norm_back(raw.reshape(512, HEAD), gk, du)
        out, first = (r.dqkv, 256) if mine else (r.dkv_o, 0)
        out[:, span, first : first + HEAD] = back.astype(bf16).reshape(4, 128, HEAD)
        out[:, span, first + HEAD : first + 2 * HEAD] = r.dkv[s, rows, HEAD : 2 * HEAD].astype(bf16).reshape(4, 128, HEAD)
        r.dg[17:18, :] += gain_grad

    def norm_back(value, gain, grad):
        inverse = inverse_rms(value)
        w = grad * gain
        back = inverse * w - value * (inverse * inverse * inverse) * jnp.mean(w * value, axis=-1, keepdims=True)
        return back, jnp.sum(grad * value * inverse, axis=0, keepdims=True)

    def attend_back(half, s):
        rows = rows_of(half)
        do_s = dot_nt(r.wo[...], r.x_all[:, s, rows, :].reshape(256, D)).astype(bf16)
        prod = do_s.astype(f32) * r.o_t[s, :, lanes(half)]
        r.do_t[s, :, lanes(half)] = do_s
        ok = allowed(s, half)
        keys, values = r.kv[s, :, 0:HEAD], r.kv[s, :, HEAD : 2 * HEAD]
        mine = pl.ds(s * 128 + 64 * half, 64)
        cos = r.cos_t[:, mine, :].reshape(256, HEAD)
        sin = r.sin_t[:, mine, :].reshape(256, HEAD)
        for h in range(2):
            head = slice(h * HEAD, (h + 1) * HEAD)
            q = r.q_s[s, half, :, head]
            do = r.do_t[s, head, lanes(half)]
            delta = jnp.sum(prod[head], axis=0, keepdims=True)
            scores = dot_nt(keys, q) * SCALE
            p = jnp.where(ok, jnp.exp(scores - r.lse[s, h, :, lanes(half)]), 0.0)
            ds = (p * (dot(values, do) - delta)).astype(bf16)
            dv = dot_nt(p.astype(bf16), do)
            dk = dot(ds, q) * SCALE
            if half == 0 and h == 0:
                r.dkv[s, :, HEAD : 2 * HEAD] = dv
                r.dkv[s, :, 0:HEAD] = dk
            else:
                r.dkv[s, :, HEAD : 2 * HEAD] += dv
                r.dkv[s, :, 0:HEAD] += dk
            dq = (dot_tn(keys, ds) * SCALE).T
            raw = r.qkraw[:, mine, head].reshape(256, HEAD)
            back, gain_grad = norm_back(raw, gq, unrotated(dq, cos, sin))
            r.dqkv[:, mine, head] = back.astype(bf16).reshape(4, 64, HEAD)
            r.dg[16:17, :] += gain_grad

    def gather_rest(half):
        gather_forward(r.x_all, r.s_dob, r.r_dob, 2, half)
        gather_own(r.x_all, r.r_dob, half)
        for d in (1, 3, 2):
            gather_pair(r.x_all, r.r_dob, d, half)

    for half in range(2):
        reduce_end(0, r.pa, half)

    def down_partial(i, carry):
        hid = r.hid_all[i].reshape(256, 384)
        r.pa[i] = dot(hid, r.wd[...]).astype(bf16).reshape(2, 128, D)
        return carry

    near_forward(r.x_all, r.s_dob, r.r_dob, 0)
    lax.fori_loop(0, 4, down_partial, 0)
    for d in (2, 1, 3, 0):
        reduce_first(2, r.pa, r.ca, d)
    def out_gradient(half, s):
        return lambda cols: dot(r.ob_t[s, :, lanes(half)], r.x_all[:, s, rows_of(half), cols].reshape(256, 256))

    def out_gradients(half):
        def one(i, carry):
            cols = pl.ds(pl.multiple_of(256 * i, 256), 256)
            total = out_gradient(half, 0)(cols) + out_gradient(half, 1)(cols)
            if half == 0:
                r.go_sum[:, cols] = total
            else:
                r.go[:, cols] = (r.go_sum[:, cols] + total).astype(bf16)
            return carry

        lax.fori_loop(0, 4, one, 0)

    gather_rest(0)
    attend_back(0, 0)
    near_forward(r.x_all, r.s_dob, r.r_dob, 1)
    rows_z_second()
    cross_x(ggub_piece, r.zgub, r.sgub, r.xgub, row_half, r.s_ggub, r.r_ggub)
    attend_back(0, 1)
    reduce_far(2, r.pa, r.ca, r.ra)
    out_gradients(0)
    gather_rest(1)
    out_gradients(1)
    cross_z_second(r.gd, 48, r.xd, r.sd, r.zd, r.s_gd, r.r_gd)
    cross_z(go_piece, r.zo, r.s_go, r.r_go)
    gu_total = jnp.concatenate([rows_z_total(), cross_total(r.sgub, r.xgub, row_half, r.r_ggub)], axis=1)
    rows_exchange(gu_total, r.hgu, r.s_fgu, r.r_fgu)
    for s in range(2):
        attend_back(1, s)
        key_back(s, False)
        block = pl.ds(128 * s, 128)
        send(r.dkv_o.at[:, block], r.dkv_recv.at[:, block], r.s_dkv.at[s], r.r_dkv.at[s], along_x(2))
        if s == 0:
            reduce_near(2, r.pa, r.ra)
    rows_spread(r.hgu, r.fgu, r.s_fgu, r.r_fgu)

    for s in range(2):
        key_back(s, True)

    def weighed(grad, weight):
        prod = grad * weight[...].reshape(D, 256).astype(f32)
        return prod[:, 0:128] + prod[:, 128:256]

    grad = dot_tn(r.n1_all[...].reshape(D, D), r.dqkv[:, :, 0:256].reshape(D, 256))
    r.gqa[...] = grad.astype(bf16)
    cross_z(gqa_piece, r.zqa, r.s_gqa, r.r_gqa)
    wdot = weighed(grad, r.wqq)
    grad = dot_tn(r.n1_all[...].reshape(D, D), r.dqkv[:, :, 256:512].reshape(D, 256))
    grad = grad + dot_tn(r.n1o_all[...].reshape(D, D), r.dkv_o[...].reshape(D, 256))
    r.gqb[...] = grad.astype(bf16)
    cross_z(gqb_piece, r.zqb, r.s_gqb, r.r_gqb)
    wdot = wdot + weighed(grad, r.wkv)
    dg1 = jnp.sum(wdot.T, axis=0, keepdims=True) / g1
    for i in range(8):
        r.dg[i : i + 1, :] = dg1[:, 128 * i : 128 * (i + 1)]
    for i in range(1, 8):
        there = place(xh, xl, around(y, i // 2), z, lax.rem(k + i, 2))
        send(r.dg, r.dg_r1.at[i], r.s_dg1.at[i], r.r_dg1.at[i], there)

    block_exchange(cross_z_total(48, r.sd, r.zd, r.r_gd), r.hd, r.s_fd, r.r_fd)
    cross_x(go_piece, r.zo, r.so, r.xo, column_half, r.s_go, r.r_go)
    r.out_tok[...] = (r.h1[...] + reduce_third(2, r.pa, r.ca, r.ra)).astype(bf16)
    cross_x(gqa_piece, r.zqa, r.sqa, r.xqa, row_half, r.s_gqa, r.r_gqa)
    block_along_y(r.hd, r.yd, r.s_fd, r.r_fd)
    for half in range(2):
        reduce_end(1, r.pb, half)

    for s in range(2):
        got(r.dkv_recv.at[:, pl.ds(128 * s, 128)], r.r_dkv.at[s])
    for d in (2, 1, 3, 0):
        yy = around(y, d)
        dkv = (r.dqkv[yy, :, 256:512].astype(f32) + r.dkv_recv[yy].astype(f32)).astype(bf16)
        dn1 = dot_nt(r.dqkv[yy, :, 0:256], r.wqq[...].reshape(D, 256)) + dot_nt(dkv, r.wkv[...].reshape(D, 256))
        r.pb[yy] = dn1.astype(bf16).reshape(2, 128, D)
        reduce_first(3, r.pb, r.cb, d)
    block_exchange(cross_total(r.so, r.xo, column_half, r.r_go), r.ho, r.s_fo, r.r_fo)
    reduce_far(3, r.pb, r.cb, r.rb)
    rows_exchange(cross_total(r.sqa, r.xqa, row_half, r.r_gqa), r.hqa, r.s_fqa, r.r_fqa)
    total = r.dg[...]
    for i in range(1, 8):
        got(r.dg_r1.at[i], r.r_dg1.at[i])
        total = total + r.dg_r1[i]
    r.dg_s[0] = total
    for dz in range(1, 4):
        send(r.dg_s.at[0], r.dg_r2.at[dz - 1], r.s_dg2.at[dz - 1], r.r_dg2.at[dz - 1], place(xh, xl, y, around(z, dz), k))
    cross_x(gqb_piece, r.zqb, r.sqb, r.xqb, row_half, r.s_gqb, r.r_gqb)
    block_along_y(r.ho, r.yo, r.s_fo, r.r_fo)
    reduce_near(3, r.pb, r.rb)
    rows_spread(r.hqa, r.fqa, r.s_fqa, r.r_fqa)
    block_deliver(r.hd, r.yd, r.fd, 48, r.s_fd, r.r_fd)
    direct_spread(cross_total(r.sqb, r.xqb, row_half, r.r_gqb), r.hqb, r.fqb, r.s_fqb, r.r_fqb)
    for dz in range(1, 4):
        got(r.dg_r2.at[dz - 1], r.r_dg2.at[dz - 1])
        total = total + r.dg_r2[dz - 1]
    r.dg_s[1] = total
    for dx in range(1, 4):
        send(r.dg_s.at[1], r.dg_r2.at[2 + dx], r.s_dg2.at[2 + dx], r.r_dg2.at[2 + dx], along_x(dx))

    block_deliver(r.ho, r.yo, r.fo, 32, r.s_fo, r.r_fo)

    dn1 = reduce_third(3, r.pb, r.cb, r.rb)
    rows = r.tok[...].astype(f32)
    back, unused = norm_back(rows, g1, dn1)
    r.dtok[...] = (r.dh1[...] + back).astype(bf16)

    block_got(r.fd, 48, r.r_fd)
    r.g_dn[...] = r.fd[...]
    rows_spread_got(r.fgu, r.r_fgu)
    for i in range(8):
        r.g_gu[:, 384 * i : 384 * (i + 1)] = r.fgu[i, :, 0:384]
        r.g_gu[:, 3072 + 384 * i : 3072 + 384 * (i + 1)] = r.fgu[i, :, 384:768]
    block_got(r.fo, 32, r.r_fo)
    r.g_out[...] = r.fo[...]
    for dx in range(1, 4):
        got(r.dg_r2.at[2 + dx], r.r_dg2.at[2 + dx])
        total = total + r.dg_r2[2 + dx]
    r.g_gain[...] = total
    rows_spread_got(r.fqa, r.r_fqa)
    direct_spread_got(r.fqb, r.r_fqb)
    for i in range(8):
        r.g_qkv[:, 256 * i : 256 * (i + 1)] = r.fqa[i]
        r.g_qkv[:, 2048 + 128 * i : 2048 + 128 * (i + 1)] = r.fqb[i, :, 0:128]
        r.g_qkv[:, 3072 + 128 * i : 3072 + 128 * (i + 1)] = r.fqb[i, :, 128:256]

    gather_end(r.dy_all, r.s_dy)
    for half in range(2):
        gather_end(r.n2_all, r.s_n2, half)
        gather_end(r.x_all, r.s_dob, half)
    sent(r.pos_in, r.s_pos.at[0])
    for whole, ss in ((r.gain_recv, r.s_gain), (r.wqq, r.s_wqq), (r.wkv, r.s_wkv), (r.wgu, r.s_wgu)):
        rows_sent(whole, ss)
    for i in range(4):
        here = (xl == k) & (z == i) & (to_core == k)

        @pl.when(is_source & jnp.logical_not(here))
        def _():
            sent(r.wo_own.at[pl.ds(32 * i, 32)], r.s_wo.at[i])
            sent(r.wd_own.at[pl.ds(48 * i, 48)], r.s_wd.at[i])

    loop_sent(wo_rows(part), r.s_wo2, 1, 8)
    loop_sent(wd_rows(part), r.s_wd2, 1, 8)
    gather_end(r.xo_all, r.s_xo)
    sent(r.tok, r.s_xo.at[8])
    reduce_end(2, r.pa)
    reduce_end(3, r.pb)
    for s in range(2):
        sent(r.dkv_o.at[:, pl.ds(128 * s, 128)], r.s_dkv.at[s])
    cross_sent(r.zqa, r.xqa, r.s_gqa)
    cross_sent(r.zqb, r.xqb, r.s_gqb)
    cross_sent(r.zgub, r.xgub, r.s_ggub)
    for i in range(3):
        sent(r.xgua.at[0], r.s_ggua.at[i])
        sent(r.zgua.at[0], r.s_ggua.at[3 + i])
    cross_sent(r.zo, r.xo, r.s_go)
    for i in range(3):
        sent(r.xd.at[0], r.s_gd.at[i])
        sent(r.zd.at[0], r.s_gd.at[3 + i])
    for hold, ss in ((r.hqa, r.s_fqa), (r.hgu, r.s_fgu)):
        rows_spread_sent(hold, ss)
    direct_spread_sent(r.hqb, r.s_fqb)
    block_sent(r.ho, r.s_fo)
    block_sent(r.hd, r.s_fd)
    loop_sent(r.dg, r.s_dg1, 1, 8)
    loop_sent(r.dg_s.at[0], r.s_dg2, 0, 6)


def layer(*args):
    vmem = pl.BlockSpec(memory_space=pltpu.VMEM)
    hbm = pl.BlockSpec(memory_space=pl.ANY)
    specs = [hbm if far else vmem for far in INPUTS.values()]
    return pl.pallas_call(
        layer_kernel,
        out_shape=[jax.ShapeDtypeStruct(shape, kind) for shape, kind in OUTPUTS.values()],
        in_specs=specs,
        out_specs=[vmem] * len(OUTPUTS),
        scratch_shapes=[pltpu.VMEM(shape, kind) for shape, kind in BUFFERS.values()]
        + [pltpu.SemaphoreType.DMA((count,)) for count in SEMAPHORES.values()],
        compiler_params=pltpu.CompilerParams(
            collective_id=0, has_side_effects=True, vmem_limit_bytes=62 << 20
        ),
        name="layer",
    )(*args)


def adam_update(weight, moment, square, grad, rate, decay):
    moment_new = beta_first * moment + (1.0 - beta_first) * grad
    square_new = beta_second * square + (1.0 - beta_second) * grad * grad
    fix_first = 1.0 - beta_first**STEP
    fix_second = 1.0 - beta_second**STEP
    step = moment_new / fix_first / (jnp.sqrt(square_new / fix_second) + adam_eps)
    return (weight - rate * (step + decay * weight), moment_new, square_new)


def on_device(
    tokens, d_out, block_ids,
    w_qkv, w_out, w_gate_up, w_down, gains,
    moment_qkv, moment_out, moment_gate_up, moment_down, moment_gains,
    square_qkv, square_out, square_gate_up, square_down, square_gains,
):
    f = lax.axis_index("fsdp")
    starts = block_ids[0].astype(f32) * BLOCK
    spots = starts[:, None] + jnp.arange(BLOCK, dtype=f32)[None, :]
    mine = lax.dynamic_slice(spots, (8 * lax.div(lax.axis_index("ctx"), 4), 0), (8, BLOCK))
    mine = mine.reshape(4, 2, BLOCK).transpose(1, 0, 2).reshape(1, 512)
    positions = jnp.concatenate([spots.reshape(1, D), jnp.tile(mine, (7, 2))], axis=0)
    gain_rows = lax.dynamic_update_slice(
        jnp.zeros((24 * 128,), f32), gains.astype(bf16).astype(f32), (f * 144,)
    ).reshape(24, 128)
    half = rope_base ** (-(np.arange(64, dtype=np.float32) * np.float32(2.0 / HEAD)))
    table = np.zeros((8, 128), np.float32)
    table[0] = np.concatenate([half, half])
    table[1] = np.concatenate([-np.ones(64), np.ones(64)])
    out_tok, dtok, g_qkv, g_out, g_gu, g_dn, g_gain = layer(
        tokens[0], d_out[0], positions, gain_rows, jnp.asarray(table), w_qkv, w_out, w_gate_up, w_down
    )
    grad_gains = lax.dynamic_slice(g_gain.reshape(24 * 128), (f * 144,), (144,))
    grads = (g_qkv, g_out, g_gu, g_dn, grad_gains)
    masters = (w_qkv, w_out, w_gate_up, w_down, gains)
    moments = (moment_qkv, moment_out, moment_gate_up, moment_down, moment_gains)
    squares = (square_qkv, square_out, square_gate_up, square_down, square_gains)
    rates = (0.03, 0.3, 0.03, 0.03, 0.5)
    decays = (decay_rate, decay_rate, decay_rate, decay_rate, 0.0)
    updates = [
        adam_update(masters[i], moments[i], squares[i], grads[i].astype(f32), rates[i], decays[i])
        for i in range(5)
    ]
    return (
        out_tok[None],
        dtok[None],
        *(u[0] for u in updates),
        *(u[1] for u in updates),
        *(u[2] for u in updates),
    )


def solution(mesh):
    rows, flat = P("fsdp", None), P("fsdp")
    tokens = P("fsdp", "ctx", None)
    state = (rows, rows, rows, rows, flat)
    return jax.shard_map(
        on_device,
        mesh=mesh,
        in_specs=(tokens, tokens, rows) + state * 3,
        out_specs=(tokens, tokens) + state * 3,
        check_vma=False,
    )
```

```python
import math
import types

import jax
import jax.numpy as jnp
import numpy as np
from jax import lax
from jax.experimental import pallas as pl
from jax.experimental.pallas import tpu as pltpu
from jax.sharding import PartitionSpec as P

D = 1024
HEAD = 128
STEP = 10
BLOCK = 64
norm_eps = 1e-06
rope_base = 1000000.0
beta_first = 0.9
beta_second = 0.95
adam_eps = 1e-08
decay_rate = 0.1
SCALE = 1.0 / math.sqrt(HEAD)

f32 = jnp.float32
bf16 = jnp.bfloat16
MESH = pl.DeviceIdType.MESH

INPUTS = dict(
    tok=False, dyt=False, ids=False, gain_in=False, freq=False, wqkv_f=True, wo_f=False, wgu_f=True, wd_f=False
)
OUTPUTS = dict(
    out_tok=((128, D), bf16),
    dtok=((128, D), bf16),
    g_qkv=((64, 4096), bf16),
    g_out=((128, D), bf16),
    g_gu=((64, 6144), bf16),
    g_dn=((192, D), bf16),
    g_gain=((24, 128), f32),
)
BUFFERS = dict(
    x_all=((4, 2, 128, D), bf16),
    dy_all=((4, 2, 128, D), bf16),
    n2_all=((4, 2, 128, D), bf16),
    n1_all=((4, 256, D), bf16),
    xo_all=((4, 2, 128, D), bf16),
    n1o_all=((4, 256, D), bf16),
    cos_o=((4, 256, HEAD), f32),
    sin_o=((4, 256, HEAD), f32),
    kraw_o=((4, 256, HEAD), f32),
    wq_f=((2, 64, 512), f32),
    wgu_fs=((2, 64, 768), f32),
    wqq_send=((2, 64, 256), bf16),
    wkv_send=((2, 64, 256), bf16),
    wgu_send=((2, 64, 768), bf16),
    wo_own=((128, D), bf16),
    wd_own=((192, D), bf16),
    wqq=((16, 64, 256), bf16),
    wkv=((16, 64, 256), bf16),
    wgu=((16, 64, 768), bf16),
    wo=((256, D), bf16),
    wd=((384, D), bf16),
    gain_recv=((16, 24, 128), f32),
    pos=((2, 8, D), f32),
    pos_own=((8, D), f32),
    posk=((2, D, 1), f32),
    cos_t=((4, 256, HEAD), f32),
    sin_t=((4, 256, HEAD), f32),
    qkraw=((4, 256, 384), f32),
    q_s=((2, 2, 256, 256), bf16),
    kv=((2, D, 256), bf16),
    o_t=((2, 256, 512), f32),
    ob_t=((2, 256, 512), bf16),
    lse=((2, 2, 1, 512), f32),
    pa=((4, 2, 128, D), bf16),
    pb=((4, 2, 128, D), bf16),
    ca=((4, 128, D), bf16),
    cb=((4, 128, D), bf16),
    ra=((3, 128, D), bf16),
    rb=((3, 128, D), bf16),
    h1=((128, D), f32),
    dh1=((128, D), f32),
    hid_all=((4, 2, 128, 384), bf16),
    dgu_all=((4, 2, 128, 768), bf16),
    do_t=((2, 256, 512), bf16),
    delta=((2, 2, 1, 512), f32),
    dkv=((2, D, 256), f32),
    dkv_o=((4, 256, 256), bf16),
    dkv_recv=((4, 256, 256), bf16),
    go_sum=((256, D), f32),
    dqkv=((4, 256, 512), bf16),
    gqa=((D, 256), bf16),
    gqb=((D, 256), bf16),
    ggua=((8, 2, 64, 256), bf16),
    ggub=((D, 512), bf16),
    go=((256, D), bf16),
    gd=((384, D), bf16),
    zqa=((3, 2, 128, 256), bf16),
    zqb=((3, 2, 128, 256), bf16),
    zgua=((3, 64, 256), bf16),
    zgub=((3, 2, 128, 512), bf16),
    zo=((3, 2, 32, D), bf16),
    zd=((3, 48, 512), bf16),
    sqa=((2, 128, 256), bf16),
    sqb=((2, 128, 256), bf16),
    sgua=((4, 64, 256), bf16),
    sgub=((2, 128, 512), bf16),
    so=((2, 32, D), bf16),
    sd=((192, 512), bf16),
    xqa=((3, 64, 256), bf16),
    xqb=((3, 64, 256), bf16),
    xgua=((3, 4, 64, 256), bf16),
    xgub=((3, 64, 512), bf16),
    xo=((3, 32, 512), bf16),
    xd=((3, 192, 512), bf16),
    hqa=((2, 64, 256), bf16),
    hqb=((64, 256), bf16),
    hgu=((2, 64, 768), bf16),
    ho=((32, D), bf16),
    hd=((48, D), bf16),
    yo=((3, 32, D), bf16),
    yd=((3, 48, D), bf16),
    fqa=((8, 64, 256), bf16),
    fqb=((8, 64, 256), bf16),
    fgu=((8, 64, 768), bf16),
    fo=((128, D), bf16),
    fd=((192, D), bf16),
    dg=((24, 128), f32),
    dg_r1=((8, 24, 128), f32),
    dg_s=((2, 24, 128), f32),
    dg_r2=((6, 24, 128), f32),
)
SEMAPHORES = dict(
    ld=16,
    s_x=8, r_x=8,
    s_dy=8, r_dy=8,
    s_n2=16, r_n2=16,
    s_dob=16, r_dob=16,
    s_pos=1, r_pos=1,
    s_gain=12, r_gain=12,
    s_wqq=12, r_wqq=12,
    s_wkv=12, r_wkv=12,
    s_wgu=12, r_wgu=12,
    s_wo=4, r_wo=1, s_wd=4, r_wd=1,
    s_wo2=8, r_wo2=8, s_wd2=8, r_wd2=8,
    s_xo=9, r_xo=9,
    s_c=32, r_c=32,
    s_r=48, r_r=48,
    s_dkv=2, r_dkv=2,
    s_gqa=9, r_gqa=9,
    s_gqb=9, r_gqb=9,
    s_ggua=6, r_ggua=6,
    s_ggub=9, r_ggub=9,
    s_go=9, r_go=9,
    s_gd=6, r_gd=6,
    s_fqa=9, r_fqa=9,
    s_fqb=8, r_fqb=8,
    s_fgu=9, r_fgu=9,
    s_fo=9, r_fo=9,
    s_fd=9, r_fd=9,
    s_dg1=8, r_dg1=8,
    s_dg2=6, r_dg2=6,
)


def dot(a, b):
    return jnp.dot(a, b, preferred_element_type=f32)


def dot_nt(a, b):
    return lax.dot_general(a, b, (((1,), (1,)), ((), ())), preferred_element_type=f32)


def dot_tn(a, b):
    return lax.dot_general(a, b, (((0,), (0,)), ((), ())), preferred_element_type=f32)


def to_row(g, first, count):
    return jnp.concatenate([g[first + i : first + i + 1, :] for i in range(count)], axis=1)


def layer_kernel(*refs):
    names = [*INPUTS, *OUTPUTS, *BUFFERS, *SEMAPHORES]
    r = types.SimpleNamespace(**dict(zip(names, refs, strict=True)))

    c = lax.axis_index("ctx")
    f = lax.axis_index("fsdp")
    xh, y = lax.div(c, 4), lax.rem(c, 4)
    xl, z, k = lax.div(f, 8), lax.rem(lax.div(f, 2), 4), lax.rem(f, 2)
    x = 2 * xh + xl
    part = 4 * xl + z
    t = 2 * y + k
    other = 1 - k

    def place(xh_, xl_, y_, z_, k_):
        return (xh_ * 4 + y_, xl_ * 8 + z_ * 2 + k_)

    partner = place(xh, xl, y, z, other)

    def around(value, step):
        return lax.rem(value + step, 4)

    def copy(src, dst, ss, rs, device):
        return pltpu.make_async_remote_copy(
            src_ref=src, dst_ref=dst, send_sem=ss, recv_sem=rs,
            device_id=device, device_id_type=MESH,
        )

    def send(src, dst, ss, rs, device):
        copy(src, dst, ss, rs, device).start()

    def got(ref, rs):
        copy(ref, ref, rs, rs, partner).wait_recv()

    def sent(ref, ss):
        copy(ref, ref, ss, ss, partner).wait_send()

    loads = []

    def load(src, dst):
        one = pltpu.make_async_copy(src, dst, r.ld.at[len(loads)])
        one.start()
        loads.append(one)

    for i in range(2):
        ti = 2 * y + i
        load(r.wqkv_f.at[:, pl.ds(pl.multiple_of(256 * ti, 256), 256)], r.wq_f.at[i, :, pl.ds(0, 256)])
        load(r.wqkv_f.at[:, pl.ds(pl.multiple_of(2048 + 128 * ti, 128), 128)], r.wq_f.at[i, :, pl.ds(256, 128)])
        load(r.wqkv_f.at[:, pl.ds(pl.multiple_of(3072 + 128 * ti, 128), 128)], r.wq_f.at[i, :, pl.ds(384, 128)])
    for i in range(2):
        ti = 2 * y + i
        load(r.wgu_f.at[:, pl.ds(pl.multiple_of(384 * ti, 128), 384)], r.wgu_fs.at[i, :, pl.ds(0, 384)])
        load(r.wgu_f.at[:, pl.ds(pl.multiple_of(3072 + 384 * ti, 128), 384)], r.wgu_fs.at[i, :, pl.ds(384, 384)])

    barrier = pltpu.get_barrier_semaphore()

    def greet(device):
        pl.semaphore_signal(barrier, inc=1, device_id=device, device_id_type=MESH)

    def greet_plane(i, carry):
        greet(place(xh, lax.rem(xl + lax.div(i, 8), 2), y, around(z, lax.rem(lax.div(i, 2), 4)), lax.rem(k + i, 2)))
        return carry

    def along_x(d):
        x_ = around(x, d)
        return place(lax.div(x_, 2), lax.rem(x_, 2), y, z, k)

    for i in range(1, 8):
        greet(place(xh, xl, around(y, i // 2), z, lax.rem(k + i, 2)))
    for i in range(8):
        greet(place(1 - xh, xl, around(y, i // 2), z, lax.rem(k + i, 2)))
    lax.fori_loop(1, 16, greet_plane, 0)
    for d in range(1, 4):
        greet(along_x(d))

    for one in loads:
        one.wait()
    r.wqq_send[...] = r.wq_f[:, :, 0:256].astype(bf16)
    r.wkv_send[...] = r.wq_f[:, :, 256:512].astype(bf16)
    r.wgu_send[...] = r.wgu_fs[...].astype(bf16)
    r.wo_own[...] = r.wo_f[...].astype(bf16)
    r.wd_own[...] = r.wd_f[...].astype(bf16)
    r.wqq[f] = r.wqq_send[k]
    r.wkv[f] = r.wkv_send[k]
    r.wgu[f] = r.wgu_send[k]
    r.gain_recv[f] = r.gain_in[...]
    r.x_all[y, k] = r.tok[...]
    r.dy_all[y, k] = r.dyt[...]
    starts = r.ids[...].astype(f32) * BLOCK
    lane = lax.broadcasted_iota(jnp.int32, (1, D), 1)
    first = jnp.zeros((1, D), f32)
    for b in range(16):
        first = jnp.where(lax.div(lane, BLOCK) == b, starts[:, b : b + 1], first)
    inside = lax.rem(lane, BLOCK).astype(f32)
    r.pos_own[...] = jnp.zeros((8, D), f32)
    r.pos_own[0:1, :] = first + inside
    first = jnp.zeros((1, D), f32)
    for b in range(8):
        spot = 2 * (b % 4) + b // 4
        start = jnp.where(xh == 0, starts[:, spot : spot + 1], starts[:, spot + 8 : spot + 9])
        first = jnp.where(lax.div(lane, BLOCK) == b, start, first)
    r.pos_own[1:2, :] = first + inside
    r.pos[k] = r.pos_own[...]
    r.dg[...] = jnp.zeros((24, 128), f32)
    pl.semaphore_wait(barrier, 33)

    def rows_of(half):
        return pl.ds(0, 128) if half is None else pl.ds(64 * half, 64)

    def far_part(half, which):
        size = 64 if half is None else 32
        return pl.ds((0 if half is None else 64 * half) + size * which, size)

    def gather_start(src, whole, ss, rs, half=None):
        rows, o = rows_of(half), 8 * (half or 0)
        for d in (1, 3):
            send(src.at[rows], whole.at[y, k, rows], ss.at[o + d - 1], rs.at[o + d - 1], place(xh, xl, around(y, d), z, k))
        send(src.at[rows], whole.at[y, k, rows], ss.at[o + 3], rs.at[o + 3], partner)

    def gather_forward(whole, ss, rs, d, half=None):
        rows, o = rows_of(half), 8 * (half or 0)
        block = whole.at[around(y, 4 - d), k, rows]
        if d == 2:
            for which in range(2):
                got(whole.at[around(y, 2), k, far_part(half, which)], rs.at[o + (1, 7)[which]])
        else:
            got(block, rs.at[o + d - 1])
            which = 0 if d == 1 else 1
            part_of = whole.at[around(y, 4 - d), k, far_part(half, which)]
            i = o + (1, 7)[which]
            send(part_of, part_of, ss.at[i], rs.at[i], place(xh, xl, around(y, d), z, k))
        send(block, block, ss.at[o + 3 + d], rs.at[o + 3 + d], partner)

    def gather_own(whole, rs, half=None):
        got(whole.at[y, other, rows_of(half)], rs.at[8 * (half or 0) + 3])

    def gather_pair(whole, rs, d, half=None):
        got(whole.at[around(y, 4 - d), other, rows_of(half)], rs.at[8 * (half or 0) + 3 + d])

    def gather_end(whole, ss, half=None):
        o = 8 * (half or 0)
        for i in (0, 2, 3, 4, 5, 6):
            sent(whole.at[y, k, rows_of(half)], ss.at[o + i])
        for i in (1, 7):
            sent(whole.at[y, k, far_part(half, 0)], ss.at[o + i])

    def chip_slots(whole, l_, zz):
        return whole.at[pl.ds(8 * l_ + 2 * zz, 2)]

    def z_send(src_of, whole, ss, rs):
        for i in range(1, 8):
            core = lax.rem(k + i, 2)
            send(src_of(core), whole.at[f], ss.at[i], rs.at[i], place(xh, xl, y, around(z, i // 2), core))

    def z_got(whole, rs, dz):
        for dk in range(2):
            if dz + dk > 0:
                got(whole.at[8 * xl + 2 * around(z, 4 - dz) + lax.rem(k + dk, 2)], rs.at[2 * dz + dk])

    def beside(dz):
        return along_x(1 if dz < 2 else 3)

    def x_send(whole, ss, rs, dz):
        block = chip_slots(whole, xl, around(z, 4 - dz))
        send(block, block, ss.at[8 + dz], rs.at[8 + dz], beside(dz))

    def x_got(whole, rs, dz):
        got(chip_slots(whole, 1 - xl, around(z, 4 - dz)), rs.at[8 + dz])

    def rows_sent(whole, ss):
        for i in range(1, 8):
            sent(whole.at[f], ss.at[i])
        for dz in range(4):
            sent(chip_slots(whole, xl, around(z, 4 - dz)), ss.at[8 + dz])

    def loop_sent(ref, ss, first, last):
        def one(i, carry):
            sent(ref, ss.at[i])
            return carry

        lax.fori_loop(first, last, one, 0)

    gather_start(r.tok, r.x_all, r.s_x, r.r_x)
    send(r.tok, r.xo_all.at[y, k], r.s_xo.at[8], r.r_xo.at[8], along_x(2))
    z_send(lambda k_: r.gain_in, r.gain_recv, r.s_gain, r.r_gain)
    z_send(lambda k_: r.wkv_send.at[k_], r.wkv, r.s_wkv, r.r_wkv)
    send(r.pos_own, r.pos.at[k], r.s_pos.at[0], r.r_pos.at[0], partner)
    z_send(lambda k_: r.wqq_send.at[k_], r.wqq, r.s_wqq, r.r_wqq)

    is_source = lax.div(part, 2) == y
    to_core = lax.rem(part, 2)
    for i in range(4):
        piece = 4 * k + i
        here = (xl == k) & (z == i) & (to_core == k)

        @pl.when(is_source & jnp.logical_not(here))
        def _():
            there = place(xh, k, y, i, to_core)
            send(r.wo_own.at[pl.ds(32 * i, 32)], r.wo.at[pl.ds(pl.multiple_of(32 * piece, 32), 32)], r.s_wo.at[i], r.r_wo.at[0], there)
            send(r.wd_own.at[pl.ds(48 * i, 48)], r.wd.at[pl.ds(pl.multiple_of(48 * piece, 16), 48)], r.s_wd.at[i], r.r_wd.at[0], there)

        @pl.when(is_source & here)
        def _():
            r.wo[pl.ds(pl.multiple_of(32 * piece, 32), 32), :] = r.wo_own[32 * i : 32 * i + 32, :]
            r.wd[pl.ds(pl.multiple_of(48 * piece, 16), 48), :] = r.wd_own[48 * i : 48 * i + 48, :]

    def wo_rows(q):
        return r.wo.at[pl.ds(pl.multiple_of(32 * q, 32), 32)]

    def wd_rows(q):
        return r.wd.at[pl.ds(pl.multiple_of(48 * q, 16), 48)]

    def pass_on(whole, ss, rs, dz):
        z_got(whole, rs, dz)
        x_send(whole, ss, rs, dz)

    pass_on(r.gain_recv, r.s_gain, r.r_gain, 0)
    pass_on(r.wkv, r.s_wkv, r.r_wkv, 0)

    got(r.pos.at[other], r.r_pos.at[0])
    steps = lax.broadcasted_iota(jnp.int32, (BLOCK, 1), 0).astype(f32)
    for s in range(2):
        for b in range(16):
            r.posk[s, b * BLOCK : (b + 1) * BLOCK, :] = r.pos[s, 0:1, b * BLOCK : b * BLOCK + 1] + steps
    freq = r.freq[0:1, :]
    sign = r.freq[1:2, :]

    def tables(i, carry):
        hh, yy = lax.rem(xh + lax.div(i, 4), 2), lax.rem(i, 4)
        for s in range(2):
            rows = r.posk[s, pl.ds(pl.multiple_of(512 * hh + 128 * yy, 128), 128), :]
            angle = rows * freq
            cos, sin = jnp.cos(angle), jnp.sin(angle) * sign

            @pl.when(i < 4)
            def _():
                r.cos_t[yy, s * 128 : (s + 1) * 128, :] = cos
                r.sin_t[yy, s * 128 : (s + 1) * 128, :] = sin

            @pl.when(i >= 4)
            def _():
                r.cos_o[yy, s * 128 : (s + 1) * 128, :] = cos
                r.sin_o[yy, s * 128 : (s + 1) * 128, :] = sin

        return carry

    lax.fori_loop(0, 2, tables, 0)

    for dz in (1, 3):
        pass_on(r.gain_recv, r.s_gain, r.r_gain, dz)
        pass_on(r.wkv, r.s_wkv, r.r_wkv, dz)
    for d in (1, 3):
        gather_forward(r.x_all, r.s_x, r.r_x, d)
    got(r.xo_all.at[y, k], r.r_xo.at[8])
    gather_start(r.xo_all.at[y, k], r.xo_all, r.s_xo, r.r_xo)
    gather_start(r.dyt, r.dy_all, r.s_dy, r.r_dy)
    pass_on(r.gain_recv, r.s_gain, r.r_gain, 2)
    pass_on(r.wkv, r.s_wkv, r.r_wkv, 2)
    lax.fori_loop(2, 4, tables, 0)
    own_piece = (2 * y + k == part) & (xl == k)

    def start_rest():
        for dz in (0, 1, 3, 2):
            pass_on(r.wqq, r.s_wqq, r.r_wqq, dz)

        @pl.when(jnp.logical_not(own_piece))
        def _():
            got(wo_rows(part), r.r_wo.at[0])
            got(wd_rows(part), r.r_wd.at[0])

        for dz in range(1, 4):
            there = place(xh, xl, y, around(z, dz), k)
            send(wo_rows(part), wo_rows(part), r.s_wo2.at[dz], r.r_wo2.at[dz], there)
        z_send(lambda k_: r.wgu_send.at[k_], r.wgu, r.s_wgu, r.r_wgu)
        for dz in range(1, 4):
            there = place(xh, xl, y, around(z, dz), k)
            send(wd_rows(part), wd_rows(part), r.s_wd2.at[dz], r.r_wd2.at[dz], there)

    def piece_of(l_, dz):
        return 4 * l_ + around(z, 4 - dz)

    for dz in range(4):
        x_got(r.gain_recv, r.r_gain, dz)
    gains = jnp.sum(r.gain_recv[...], axis=0)
    g1 = to_row(gains, 0, 8)
    g2 = to_row(gains, 8, 8)
    gq = gains[16:17, :]
    gk = gains[17:18, :]

    def rotated(u, cos, sin):
        return u * cos + pltpu.roll(u, 64, 1) * sin

    def unrotated(u, cos, sin):
        return u * cos - pltpu.roll(u, 64, 1) * sin

    def inverse_rms(u):
        return lax.rsqrt(jnp.mean(u * u, axis=-1, keepdims=True) + norm_eps)

    def project_keys(d, x_all, n1_all, raw_at, cos, sin, hh):
        yy = around(y, 4 - d)
        rows = x_all[yy].reshape(256, D).astype(f32)
        n1 = (rows * inverse_rms(rows) * g1).astype(bf16)
        n1_all[yy] = n1
        kv = dot(n1, r.wkv[...].reshape(D, 256))
        raw = kv[:, 0:HEAD]
        raw_at(yy)[...] = raw
        local = pl.ds(pl.multiple_of(512 * hh + 128 * yy, 128), 128)
        key = rotated(raw * inverse_rms(raw) * gk, cos[yy], sin[yy]).astype(bf16)
        value = kv[:, HEAD:].astype(bf16)
        for s in range(2):
            r.kv[s, local, 0:HEAD] = key[s * 128 : (s + 1) * 128]
            r.kv[s, local, HEAD : 2 * HEAD] = value[s * 128 : (s + 1) * 128]

    def project_mine(d):
        project_keys(d, r.x_all, r.n1_all, lambda yy: r.qkraw.at[yy, :, pl.ds(256, HEAD)], r.cos_t, r.sin_t, xh)

    def project_others(d):
        project_keys(d, r.xo_all, r.n1o_all, lambda yy: r.kraw_o.at[yy], r.cos_o, r.sin_o, 1 - xh)

    def project_queries(yy, carry):
        qs = dot(r.n1_all[yy], r.wqq[...].reshape(D, 256))
        r.qkraw[yy, :, 0:256] = qs
        for h in range(2):
            raw = qs[:, h * HEAD : (h + 1) * HEAD]
            query = rotated(raw * inverse_rms(raw) * gq, r.cos_t[yy], r.sin_t[yy]).astype(bf16)
            for s in range(2):
                for half in range(2):
                    first = s * 128 + half * 64
                    rows = pl.ds(pl.multiple_of(64 * yy, 64), 64)
                    r.q_s[s, half, rows, h * HEAD : (h + 1) * HEAD] = query[first : first + 64]
        return carry

    gather_own(r.x_all, r.r_x)
    for dz in range(4):
        x_got(r.wkv, r.r_wkv, dz)
    project_mine(0)
    gather_pair(r.x_all, r.r_x, 1)
    project_mine(1)
    gather_forward(r.x_all, r.s_x, r.r_x, 2)
    gather_pair(r.x_all, r.r_x, 3)
    project_mine(3)
    start_rest()
    gather_pair(r.x_all, r.r_x, 2)
    project_mine(2)
    for d in (1, 3):
        gather_forward(r.xo_all, r.s_xo, r.r_xo, d)
    lax.fori_loop(4, 8, tables, 0)
    for dz in range(4):
        if dz > 0:
            got(wo_rows(piece_of(xl, dz)), r.r_wo2.at[dz])
        block = wo_rows(piece_of(xl, dz))
        send(block, block, r.s_wo2.at[4 + dz], r.r_wo2.at[4 + dz], beside(dz))
    for dz in range(4):
        x_got(r.wqq, r.r_wqq, dz)
    lax.fori_loop(0, 4, project_queries, 0)
    gather_own(r.xo_all, r.r_xo)
    project_others(0)
    gather_forward(r.xo_all, r.s_xo, r.r_xo, 2)
    gather_pair(r.xo_all, r.r_xo, 1)
    project_others(1)
    gather_pair(r.xo_all, r.r_xo, 3)
    project_others(3)
    gather_pair(r.xo_all, r.r_xo, 2)
    project_others(2)
    gather_end(r.x_all, r.s_x)

    def rest_forward():
        for dz in range(4):
            pass_on(r.wgu, r.s_wgu, r.r_wgu, dz)
        for dz in range(4):
            if dz > 0:
                got(wd_rows(piece_of(xl, dz)), r.r_wd2.at[dz])
            block = wd_rows(piece_of(xl, dz))
            send(block, block, r.s_wd2.at[4 + dz], r.r_wd2.at[4 + dz], beside(dz))

    def lanes(half):
        return pl.ds(pl.multiple_of(256 * half, 256), 256)

    def allowed(s, half):
        return r.posk[s] <= r.pos[s, 1:2, lanes(half)]

    def attend(s, half):
        ok = allowed(s, half)
        for h in range(2):
            q = r.q_s[s, half, :, h * HEAD : (h + 1) * HEAD]
            scores = jnp.where(ok, dot_nt(r.kv[s, :, 0:HEAD], q) * SCALE, -1e30)
            top = jnp.max(scores, axis=0, keepdims=True)
            p = jnp.exp(scores - top)
            total = jnp.sum(p, axis=0, keepdims=True)
            o = dot_tn(r.kv[s, :, HEAD : 2 * HEAD], p.astype(bf16)) / total
            r.o_t[s, h * HEAD : (h + 1) * HEAD, lanes(half)] = o
            r.ob_t[s, h * HEAD : (h + 1) * HEAD, lanes(half)] = o.astype(bf16)
            r.lse[s, h, :, lanes(half)] = top + jnp.log(total)

    def reduce_first(use, p, cc, d, half=None):
        yy, rows, i = around(y, d), rows_of(half), 8 * use + 4 * (half or 0) + d
        send(p.at[yy, other, rows], cc.at[yy, rows], r.s_c.at[i], r.r_c.at[i], partner)

    def both_cores(use, p, cc, d, half):
        yy, rows, i = around(y, d), rows_of(half), 8 * use + 4 * (half or 0) + d
        got(cc.at[yy, rows], r.r_c.at[i])
        return p[yy, k, rows, :].astype(f32) + cc[yy, rows, :].astype(f32)

    def reduce_far(use, p, cc, rr, half=None):
        rows, o = rows_of(half), 12 * use + 6 * (half or 0)
        yy = around(y, 2)
        p[yy, k, rows, :] = both_cores(use, p, cc, 2, half).astype(bf16)
        for which in range(2):
            rest = far_part(half, which)
            there = place(xh, xl, around(y, 1 + 2 * which), z, k)
            send(p.at[yy, k, rest], rr.at[2, rest], r.s_r.at[o + which], r.r_r.at[o + which], there)
        for which in range(2):
            yy = around(y, 1 + 2 * which)
            p[yy, k, rows, :] = both_cores(use, p, cc, 1 + 2 * which, half).astype(bf16)
            early, i = far_part(half, 1 - which), o + 2 + which
            send(p.at[yy, k, early], rr.at[which, early], r.s_r.at[i], r.r_r.at[i], place(xh, xl, yy, z, k))

    def reduce_near(use, p, rr, half=None):
        o = 12 * use + 6 * (half or 0)
        for which in range(2):
            yy = around(y, 1 + 2 * which)
            late, i = far_part(half, which), o + 4 + which
            got(rr.at[2, late], r.r_r.at[o + which])
            p[yy, k, late, :] = (p[yy, k, late, :].astype(f32) + rr[2, late, :].astype(f32)).astype(bf16)
            send(p.at[yy, k, late], rr.at[which, late], r.s_r.at[i], r.r_r.at[i], place(xh, xl, yy, z, k))

    def reduce_third(use, p, cc, rr, half=None):
        rows, o = rows_of(half), 12 * use + 6 * (half or 0)
        total = both_cores(use, p, cc, 0, half)
        for which in range(2):
            got(rr.at[which, far_part(half, 1 - which)], r.r_r.at[o + 2 + which])
            got(rr.at[which, far_part(half, which)], r.r_r.at[o + 4 + which])
            total = total + rr[which, rows, :].astype(f32)
        return total

    def reduce_end(use, p, half=None):
        for d in range(4):
            sent(p.at[y, other, rows_of(half)], r.s_c.at[8 * use + 4 * (half or 0) + d])
        for i in range(6):
            sent(p.at[y, k, far_part(half, 0)], r.s_r.at[12 * use + 6 * (half or 0) + i])

    def out_partial(half):
        for s in (other, k):
            o = r.ob_t[s, :, lanes(half)]
            r.pa[:, s, rows_of(half), :] = dot_tn(o, r.wo[...]).astype(bf16).reshape(4, 64, D)
            if s is other:
                for d in (2, 1, 3, 0):
                    reduce_first(0, r.pa, r.ca, d, half)

    for d in (1, 3):
        gather_forward(r.dy_all, r.s_dy, r.r_dy, d)
    attend(0, 0)
    attend(1, 0)
    for dz in range(4):
        got(wo_rows(piece_of(1 - xl, dz)), r.r_wo2.at[4 + dz])
    out_partial(0)
    rest_forward()
    attend(0, 1)
    reduce_far(0, r.pa, r.ca, r.ra, 0)
    gather_forward(r.dy_all, r.s_dy, r.r_dy, 2)
    attend(1, 1)
    out_partial(1)
    reduce_near(0, r.pa, r.ra, 0)
    reduce_far(0, r.pa, r.ca, r.ra, 1)

    def middle(half):
        rows = rows_of(half)
        h1 = r.tok[rows, :].astype(f32) + reduce_third(0, r.pa, r.ca, r.ra, half)
        r.h1[rows, :] = h1
        r.n2_all[y, k, rows, :] = (h1 * inverse_rms(h1) * g2).astype(bf16)
        gather_start(r.n2_all.at[y, k], r.n2_all, r.s_n2, r.r_n2, half)

    middle(0)
    reduce_near(0, r.pa, r.ra, 1)
    middle(1)

    gather_own(r.dy_all, r.r_dy)
    for d in (1, 3, 2):
        gather_pair(r.dy_all, r.r_dy, d)
    for dz in range(4):
        x_got(r.wgu, r.r_wgu, dz)
        got(wd_rows(piece_of(1 - xl, dz)), r.r_wd2.at[4 + dz])

    def two_blocks(whole, ds, half):
        blocks = [whole[around(y, d), :, rows_of(half), :].reshape(128, whole.shape[-1]) for d in ds]
        return jnp.concatenate(blocks, axis=0)

    def put_blocks(whole, ds, half, cols, value):
        for i, d in enumerate(ds):
            block = value[128 * i : 128 * (i + 1)].reshape(2, 64, value.shape[-1])
            whole[around(y, d), :, rows_of(half), cols] = block

    def feed(ds, half):
        n2 = two_blocks(r.n2_all, ds, half)
        ab = dot(n2, r.wgu[...].reshape(D, 768))
        a, b = ab[:, :384], ab[:, 384:]
        sig = jax.nn.sigmoid(a)
        silu = a * sig
        put_blocks(r.hid_all, ds, half, slice(None), (silu * b).astype(bf16))
        dhid = dot_nt(two_blocks(r.dy_all, ds, half), r.wd[...])
        da = (dhid * b * sig * (1.0 + a * (1.0 - sig))).astype(bf16)
        db = (dhid * silu).astype(bf16)
        put_blocks(r.dgu_all, ds, half, slice(0, 384), da)
        put_blocks(r.dgu_all, ds, half, slice(384, 768), db)
        dn2 = dot_nt(jnp.concatenate([da, db], axis=1), r.wgu[...].reshape(D, 768))
        put_blocks(r.pb, ds, half, slice(None), dn2.astype(bf16))
        for d in ds:
            reduce_first(1, r.pb, r.cb, d, half)

    def near_forward(whole, ss, rs, half):
        for d in (1, 3):
            gather_forward(whole, ss, rs, d, half)

    near_forward(r.n2_all, r.s_n2, r.r_n2, 0)
    for half in range(2):
        gather_own(r.n2_all, r.r_n2, half)
        gather_pair(r.n2_all, r.r_n2, 1, half)
        feed((0, 3), half)
        if half == 1:
            reduce_near(1, r.pb, r.rb, 0)
        gather_forward(r.n2_all, r.s_n2, r.r_n2, 2, half)
        if half == 0:
            near_forward(r.n2_all, r.s_n2, r.r_n2, 1)
        gather_pair(r.n2_all, r.r_n2, 3, half)
        gather_pair(r.n2_all, r.r_n2, 2, half)
        feed((2, 1), half)
        reduce_far(1, r.pb, r.cb, r.rb, half)

    def rows_at(whole, height):
        return lambda l_, z_: whole.at[pl.ds(pl.multiple_of(height * (4 * l_ + z_), 16), height)]

    def cross_z(piece, dst, ss, rs):
        for dz in (1, 3, 2):
            zz = around(z, dz)
            for l_ in range(2):
                i = 2 * (dz - 1) + l_
                send(piece(l_, zz), dst.at[dz - 1, l_], ss.at[i], rs.at[i], place(xh, xl, y, zz, k))

    def row_half(ref, h_):
        return ref.at[pl.ds(pl.multiple_of(64 * h_, 64), 64)]

    def column_half(ref, h_):
        return ref.at[:, pl.ds(pl.multiple_of(512 * h_, 512), 512)]

    def cross_x(piece, zrecv, sums, xrecv, half_of, ss, rs):
        for l_ in range(2):
            total = piece(l_, z)[...].astype(f32)
            for dz in range(1, 4):
                got(zrecv.at[dz - 1, l_], rs.at[2 * (dz - 1) + l_])
                total = total + zrecv[dz - 1, l_].astype(f32)
            sums[l_] = total.astype(bf16)
        for dx in (1, 3, 2):
            x_ = around(x, dx)
            block = half_of(sums.at[lax.rem(x_, 2)], lax.div(x_, 2))
            send(block, xrecv.at[dx - 1], ss.at[5 + dx], rs.at[5 + dx], along_x(dx))

    def cross_total(sums, xrecv, half_of, rs):
        total = half_of(sums.at[xl], xh)[...].astype(f32)
        for dx in (1, 3, 2):
            got(xrecv.at[dx - 1], rs.at[5 + dx])
            total = total + xrecv[dx - 1].astype(f32)
        return total

    def cross_x_first(whole, height, xrecv, ss, rs):
        for dx in (1, 3, 2):
            x_ = around(x, dx)
            rows = pl.ds(pl.multiple_of(4 * height * lax.rem(x_, 2), 16), 4 * height)
            block = column_half(whole.at[rows], lax.div(x_, 2))
            send(block, xrecv.at[dx - 1], ss.at[dx - 1], rs.at[dx - 1], along_x(dx))

    def cross_z_second(whole, height, xrecv, sums, zrecv, ss, rs):
        rows = pl.ds(pl.multiple_of(4 * height * xl, 16), 4 * height)
        total = column_half(whole.at[rows], xh)[...].astype(f32)
        for dx in (1, 3, 2):
            got(xrecv.at[dx - 1], rs.at[dx - 1])
            total = total + xrecv[dx - 1].astype(f32)
        sums[...] = total.astype(bf16)
        for dz in (1, 3, 2):
            zz = around(z, dz)
            block = sums.at[pl.ds(pl.multiple_of(height * zz, 16), height)]
            send(block, zrecv.at[dz - 1], ss.at[2 + dz], rs.at[2 + dz], place(xh, xl, y, zz, k))

    def cross_z_total(height, sums, zrecv, rs):
        total = sums[pl.ds(pl.multiple_of(height * z, 16), height), :].astype(f32)
        for dz in (1, 3, 2):
            got(zrecv.at[dz - 1], rs.at[2 + dz])
            total = total + zrecv[dz - 1].astype(f32)
        return total

    def rows_x_first():
        for dx in (1, 3, 2):
            x_ = around(x, dx)
            block = r.ggua.at[pl.ds(4 * lax.rem(x_, 2), 4), lax.div(x_, 2)]
            send(block, r.xgua.at[dx - 1], r.s_ggua.at[dx - 1], r.r_ggua.at[dx - 1], along_x(dx))

    def rows_z_second():
        total = r.ggua[pl.ds(4 * xl, 4), xh].astype(f32)
        for dx in (1, 3, 2):
            got(r.xgua.at[dx - 1], r.r_ggua.at[dx - 1])
            total = total + r.xgua[dx - 1].astype(f32)
        r.sgua[...] = total.astype(bf16)
        for dz in (1, 3, 2):
            zz = around(z, dz)
            send(r.sgua.at[zz], r.zgua.at[dz - 1], r.s_ggua.at[2 + dz], r.r_ggua.at[2 + dz], place(xh, xl, y, zz, k))

    def rows_z_total():
        total = r.sgua[z].astype(f32)
        for dz in (1, 3, 2):
            got(r.zgua.at[dz - 1], r.r_ggua.at[2 + dz])
            total = total + r.zgua[dz - 1].astype(f32)
        return total

    def cross_sent(zrecv, xrecv, ss):
        for i in range(6):
            sent(zrecv.at[0, 0], ss.at[i])
        for i in range(3):
            sent(xrecv.at[0], ss.at[6 + i])

    gqa_piece, gqb_piece, ggub_piece = rows_at(r.gqa, 128), rows_at(r.gqb, 128), rows_at(r.ggub, 128)
    go_piece = rows_at(r.go, 32)

    def weight_gradient(left, right, out, first=0):
        def one(i, carry):
            cols = pl.ds(pl.multiple_of(256 * i, 256), 256)
            taken = pl.ds(pl.multiple_of(first + 256 * i, 256), 256)
            out[:, cols] = dot_tn(left(), right(taken)).astype(bf16)
            return carry

        lax.fori_loop(0, out.shape[1] // 256, one, 0)

    def middle_back(half):
        rows = rows_of(half)
        dn2 = reduce_third(1, r.pb, r.cb, r.rb, half)
        h1 = r.h1[rows, :]
        r2 = inverse_rms(h1)
        weighted = dn2 * g2
        back = r2 * weighted - h1 * (r2 * r2 * r2) * jnp.mean(weighted * h1, axis=-1, keepdims=True)
        dh1 = r.dyt[rows, :].astype(f32) + back
        r.dh1[rows, :] = dh1
        dg2 = jnp.sum(dn2 * h1 * r2, axis=0, keepdims=True)
        for i in range(8):
            r.dg[8 + i : 9 + i, :] += dg2[:, 128 * i : 128 * (i + 1)]
        r.x_all[y, k, rows, :] = dh1.astype(bf16)
        gather_start(r.x_all.at[y, k], r.x_all, r.s_dob, r.r_dob, half)

    ggua = dot_tn(r.n2_all[...].reshape(D, D), r.dgu_all[:, :, :, 0:256].reshape(D, 256))
    r.ggua[...] = ggua.astype(bf16).reshape(8, 2, 64, 256)
    rows_x_first()
    weight_gradient(
        lambda: r.n2_all[...].reshape(D, D),
        lambda cols: r.dgu_all[:, :, :, cols].reshape(D, 256),
        r.ggub,
        256,
    )
    cross_z(ggub_piece, r.zgub, r.s_ggub, r.r_ggub)
    reduce_near(1, r.pb, r.rb, 1)
    middle_back(0)
    weight_gradient(
        lambda: r.hid_all[...].reshape(D, 384),
        lambda cols: r.dy_all[:, :, :, cols].reshape(D, 256),
        r.gd,
    )
    cross_x_first(r.gd, 48, r.xd, r.s_gd, r.r_gd)
    middle_back(1)

    def direct_spread(total, hold, final, ss, rs):
        hold[...] = total.astype(bf16)

        def one(i, carry):
            there = place(lax.rem(xh + lax.div(i, 4), 2), xl, lax.rem(y + i, 4), z, xh)

            @pl.when((i > 0) | (k != xh))
            def _():
                send(hold, final.at[t], ss.at[i], rs.at[t], there)

            return carry

        lax.fori_loop(0, 8, one, 0)

        @pl.when(k == xh)
        def _():
            final[t] = hold[...]

    def direct_spread_sent(hold, ss):
        def one(i, carry):
            @pl.when((i > 0) | (k != xh))
            def _():
                sent(hold, ss.at[i])

            return carry

        lax.fori_loop(0, 8, one, 0)

    def direct_spread_got(final, rs):
        def one(i, carry):
            @pl.when((i != t) | (k != xh))
            def _():
                got(final.at[i], rs.at[i])

            return carry

        lax.fori_loop(0, 8, one, 0)

    other_half = place(1 - xh, xl, y, z, k)

    def rows_exchange(total, hold, ss, rs):
        hold[xh] = total.astype(bf16)
        send(hold.at[xh], hold.at[xh], ss.at[8], rs.at[8], other_half)

    def rows_spread(hold, final, ss, rs):
        for which in range(2):
            h = xh if which == 0 else 1 - xh
            if which == 1:
                got(hold.at[h], rs.at[8])
            for i in (2, 1, 3):
                send(hold.at[h], final.at[t], ss.at[4 * which + i], rs.at[t], place(xh, xl, around(y, i), z, h))

            @pl.when(k != h)
            def _():
                send(hold.at[h], final.at[t], ss.at[4 * which], rs.at[t], partner)

            @pl.when(k == h)
            def _():
                final[t] = hold[h]

    def rows_spread_sent(hold, ss):
        sent(hold.at[0], ss.at[8])
        for which in range(2):
            h = xh if which == 0 else 1 - xh
            for i in range(1, 4):
                sent(hold.at[0], ss.at[4 * which + i])

            @pl.when(k != h)
            def _():
                sent(hold.at[0], ss.at[4 * which])

    def rows_spread_got(final, rs):
        def one(i, carry):
            @pl.when(i != t)
            def _():
                got(final.at[i], rs.at[i])

            return carry

        lax.fori_loop(0, 8, one, 0)

    def block_exchange(total, hold, ss, rs):
        column_half(hold, xh)[...] = total.astype(bf16)
        send(column_half(hold, xh), column_half(hold, xh), ss.at[8], rs.at[8], other_half)

    def block_along_y(hold, held, ss, rs):
        got(column_half(hold, 1 - xh), rs.at[8])
        for i in (1, 3, 2):
            send(hold, held.at[i - 1], ss.at[i], rs.at[i], place(xh, xl, around(y, i), z, k))

    def block_target(i):
        slice_ = 2 * around(y, 4 - i) + k
        mine = (part == slice_) & (k == xl)
        return mine, place(xh, lax.div(slice_, 4), y, lax.rem(slice_, 4), xl)

    def block_deliver(hold, held, final, height, ss, rs):
        rows = pl.ds(pl.multiple_of(height * z, 16), height)
        for i in (0, 1, 3, 2):
            block = hold
            if i > 0:
                got(held.at[i - 1], rs.at[i])
                block = held.at[i - 1]
            mine, there = block_target(i)

            @pl.when(jnp.logical_not(mine))
            def _():
                send(block, final.at[rows], ss.at[4 + i], rs.at[4 + z], there)

            @pl.when(mine)
            def _():
                final[rows, :] = block[...]

    def block_sent(hold, ss):
        sent(column_half(hold, 0), ss.at[8])
        for i in range(4):
            if i > 0:
                sent(hold, ss.at[i])
            mine, there = block_target(i)

            @pl.when(jnp.logical_not(mine))
            def _():
                sent(hold, ss.at[4 + i])

    def block_got(final, height, rs):
        def one(i, carry):
            @pl.when(jnp.logical_not((xl == k) & (z == i) & (lax.rem(part, 2) == k)))
            def _():
                got(final.at[pl.ds(pl.multiple_of(height * i, 16), height)], rs.at[4 + i])

            return carry

        lax.fori_loop(0, 4, one, 0)

    def key_back(s, mine):
        span = pl.ds(pl.multiple_of(s * 128, 128), 128)
        rows = pl.ds(pl.multiple_of(512 * (xh if mine else 1 - xh), 512), 512)
        cos, sin = (r.cos_t, r.sin_t) if mine else (r.cos_o, r.sin_o)
        raw = r.qkraw[:, span, 256:384] if mine else r.kraw_o[:, span, :]
        du = unrotated(r.dkv[s, rows, 0:HEAD], cos[:, span, :].reshape(512, HEAD), sin[:, span, :].reshape(512, HEAD))
        back, gain_grad = norm_back(raw.reshape(512, HEAD), gk, du)
        out, first = (r.dqkv, 256) if mine else (r.dkv_o, 0)
        out[:, span, first : first + HEAD] = back.astype(bf16).reshape(4, 128, HEAD)
        out[:, span, first + HEAD : first + 2 * HEAD] = r.dkv[s, rows, HEAD : 2 * HEAD].astype(bf16).reshape(4, 128, HEAD)
        r.dg[17:18, :] += gain_grad

    def norm_back(value, gain, grad):
        inverse = inverse_rms(value)
        w = grad * gain
        back = inverse * w - value * (inverse * inverse * inverse) * jnp.mean(w * value, axis=-1, keepdims=True)
        return back, jnp.sum(grad * value * inverse, axis=0, keepdims=True)

    def attend_back(half, s):
        rows = rows_of(half)
        do_s = dot_nt(r.wo[...], r.x_all[:, s, rows, :].reshape(256, D)).astype(bf16)
        prod = do_s.astype(f32) * r.o_t[s, :, lanes(half)]
        r.do_t[s, :, lanes(half)] = do_s
        ok = allowed(s, half)
        keys, values = r.kv[s, :, 0:HEAD], r.kv[s, :, HEAD : 2 * HEAD]
        mine = pl.ds(pl.multiple_of(s * 128 + 64 * half, 64), 64)
        cos = r.cos_t[:, mine, :].reshape(256, HEAD)
        sin = r.sin_t[:, mine, :].reshape(256, HEAD)
        for h in range(2):
            head = slice(h * HEAD, (h + 1) * HEAD)
            q = r.q_s[s, half, :, head]
            do = r.do_t[s, head, lanes(half)]
            delta = jnp.sum(prod[head], axis=0, keepdims=True)
            scores = dot_nt(keys, q) * SCALE
            p = jnp.where(ok, jnp.exp(scores - r.lse[s, h, :, lanes(half)]), 0.0)
            ds = (p * (dot(values, do) - delta)).astype(bf16)
            dv = dot_nt(p.astype(bf16), do)
            dk = dot(ds, q) * SCALE
            if half == 0 and h == 0:
                r.dkv[s, :, HEAD : 2 * HEAD] = dv
                r.dkv[s, :, 0:HEAD] = dk
            else:
                r.dkv[s, :, HEAD : 2 * HEAD] += dv
                r.dkv[s, :, 0:HEAD] += dk
            dq = (dot_tn(keys, ds) * SCALE).T
            raw = r.qkraw[:, mine, head].reshape(256, HEAD)
            back, gain_grad = norm_back(raw, gq, unrotated(dq, cos, sin))
            r.dqkv[:, mine, head] = back.astype(bf16).reshape(4, 64, HEAD)
            r.dg[16:17, :] += gain_grad

    def gather_rest(half):
        gather_own(r.x_all, r.r_dob, half)
        for d in (1, 3, 2):
            gather_pair(r.x_all, r.r_dob, d, half)

    for half in range(2):
        reduce_end(0, r.pa, half)

    def down_partial(i, carry):
        hid = r.hid_all[i].reshape(256, 384)
        r.pa[i] = dot(hid, r.wd[...]).astype(bf16).reshape(2, 128, D)
        return carry

    near_forward(r.x_all, r.s_dob, r.r_dob, 0)
    lax.fori_loop(0, 4, down_partial, 0)
    for d in (2, 1, 3, 0):
        reduce_first(2, r.pa, r.ca, d)
    def out_gradient(half, s):
        return lambda cols: dot(r.ob_t[s, :, lanes(half)], r.x_all[:, s, rows_of(half), cols].reshape(256, 256))

    def out_gradients(half):
        def one(i, carry):
            cols = pl.ds(pl.multiple_of(256 * i, 256), 256)
            total = out_gradient(half, 0)(cols) + out_gradient(half, 1)(cols)
            if half == 0:
                r.go_sum[:, cols] = total
            else:
                r.go[:, cols] = (r.go_sum[:, cols] + total).astype(bf16)
            return carry

        lax.fori_loop(0, 4, one, 0)

    gather_forward(r.x_all, r.s_dob, r.r_dob, 2, 0)
    attend_back(0, k)
    near_forward(r.x_all, r.s_dob, r.r_dob, 1)
    rows_z_second()
    cross_x(ggub_piece, r.zgub, r.sgub, r.xgub, row_half, r.s_ggub, r.r_ggub)
    gather_rest(0)
    attend_back(0, other)
    reduce_far(2, r.pa, r.ca, r.ra)
    out_gradients(0)
    gather_forward(r.x_all, r.s_dob, r.r_dob, 2, 1)
    gather_rest(1)
    out_gradients(1)
    cross_z_second(r.gd, 48, r.xd, r.sd, r.zd, r.s_gd, r.r_gd)
    cross_z(go_piece, r.zo, r.s_go, r.r_go)
    gu_total = jnp.concatenate([rows_z_total(), cross_total(r.sgub, r.xgub, row_half, r.r_ggub)], axis=1)
    rows_exchange(gu_total, r.hgu, r.s_fgu, r.r_fgu)
    for i, s in enumerate((k, other)):
        attend_back(1, s)
        key_back(s, False)
        block = pl.ds(pl.multiple_of(128 * s, 128), 128)
        send(r.dkv_o.at[:, block], r.dkv_recv.at[:, block], r.s_dkv.at[i], r.r_dkv.at[i], along_x(2))
        if i == 0:
            reduce_near(2, r.pa, r.ra)
    rows_spread(r.hgu, r.fgu, r.s_fgu, r.r_fgu)

    for s in range(2):
        key_back(s, True)

    def weighed(grad, weight):
        prod = grad * weight[...].reshape(D, 256).astype(f32)
        return prod[:, 0:128] + prod[:, 128:256]

    grad = dot_tn(r.n1_all[...].reshape(D, D), r.dqkv[:, :, 0:256].reshape(D, 256))
    r.gqa[...] = grad.astype(bf16)
    cross_z(gqa_piece, r.zqa, r.s_gqa, r.r_gqa)
    wdot = weighed(grad, r.wqq)
    grad = dot_tn(r.n1_all[...].reshape(D, D), r.dqkv[:, :, 256:512].reshape(D, 256))
    grad = grad + dot_tn(r.n1o_all[...].reshape(D, D), r.dkv_o[...].reshape(D, 256))
    r.gqb[...] = grad.astype(bf16)
    cross_z(gqb_piece, r.zqb, r.s_gqb, r.r_gqb)
    wdot = wdot + weighed(grad, r.wkv)
    dg1 = jnp.sum(wdot.T, axis=0, keepdims=True) / g1
    for i in range(8):
        r.dg[i : i + 1, :] = dg1[:, 128 * i : 128 * (i + 1)]
    for i in range(1, 8):
        there = place(xh, xl, around(y, i // 2), z, lax.rem(k + i, 2))
        send(r.dg, r.dg_r1.at[i], r.s_dg1.at[i], r.r_dg1.at[i], there)

    block_exchange(cross_z_total(48, r.sd, r.zd, r.r_gd), r.hd, r.s_fd, r.r_fd)
    cross_x(go_piece, r.zo, r.so, r.xo, column_half, r.s_go, r.r_go)
    r.out_tok[...] = (r.h1[...] + reduce_third(2, r.pa, r.ca, r.ra)).astype(bf16)
    block_along_y(r.hd, r.yd, r.s_fd, r.r_fd)
    for half in range(2):
        reduce_end(1, r.pb, half)

    for i, s in enumerate((k, other)):
        got(r.dkv_recv.at[:, pl.ds(pl.multiple_of(128 * s, 128), 128)], r.r_dkv.at[i])
    block_exchange(cross_total(r.so, r.xo, column_half, r.r_go), r.ho, r.s_fo, r.r_fo)
    for d in (2, 1, 3, 0):
        yy = around(y, d)
        dkv = (r.dqkv[yy, :, 256:512].astype(f32) + r.dkv_recv[yy].astype(f32)).astype(bf16)
        dn1 = dot_nt(r.dqkv[yy, :, 0:256], r.wqq[...].reshape(D, 256)) + dot_nt(dkv, r.wkv[...].reshape(D, 256))
        r.pb[yy] = dn1.astype(bf16).reshape(2, 128, D)
        for half in range(2):
            reduce_first(3, r.pb, r.cb, d, half)
    for half in range(2):
        reduce_far(3, r.pb, r.cb, r.rb, half)
    cross_x(gqa_piece, r.zqa, r.sqa, r.xqa, row_half, r.s_gqa, r.r_gqa)
    total = r.dg[...]
    for i in range(1, 8):
        got(r.dg_r1.at[i], r.r_dg1.at[i])
        total = total + r.dg_r1[i]
    r.dg_s[0] = total
    for dz in range(1, 4):
        send(r.dg_s.at[0], r.dg_r2.at[dz - 1], r.s_dg2.at[dz - 1], r.r_dg2.at[dz - 1], place(xh, xl, y, around(z, dz), k))
    block_along_y(r.ho, r.yo, r.s_fo, r.r_fo)
    cross_x(gqb_piece, r.zqb, r.sqb, r.xqb, row_half, r.s_gqb, r.r_gqb)
    block_deliver(r.hd, r.yd, r.fd, 48, r.s_fd, r.r_fd)
    reduce_near(3, r.pb, r.rb, 0)
    rows_exchange(cross_total(r.sqa, r.xqa, row_half, r.r_gqa), r.hqa, r.s_fqa, r.r_fqa)
    for dz in range(1, 4):
        got(r.dg_r2.at[dz - 1], r.r_dg2.at[dz - 1])
        total = total + r.dg_r2[dz - 1]
    r.dg_s[1] = total
    for dx in range(1, 4):
        send(r.dg_s.at[1], r.dg_r2.at[2 + dx], r.s_dg2.at[2 + dx], r.r_dg2.at[2 + dx], along_x(dx))
    reduce_near(3, r.pb, r.rb, 1)
    rows_spread(r.hqa, r.fqa, r.s_fqa, r.r_fqa)
    direct_spread(cross_total(r.sqb, r.xqb, row_half, r.r_gqb), r.hqb, r.fqb, r.s_fqb, r.r_fqb)


    block_deliver(r.ho, r.yo, r.fo, 32, r.s_fo, r.r_fo)

    for half in range(2):
        span = rows_of(half)
        rows = r.tok[span, :].astype(f32)
        back, unused = norm_back(rows, g1, reduce_third(3, r.pb, r.cb, r.rb, half))
        r.dtok[span, :] = (r.dh1[span, :] + back).astype(bf16)

    block_got(r.fd, 48, r.r_fd)
    r.g_dn[...] = r.fd[...]
    rows_spread_got(r.fgu, r.r_fgu)
    for i in range(8):
        r.g_gu[:, 384 * i : 384 * (i + 1)] = r.fgu[i, :, 0:384]
        r.g_gu[:, 3072 + 384 * i : 3072 + 384 * (i + 1)] = r.fgu[i, :, 384:768]
    block_got(r.fo, 32, r.r_fo)
    r.g_out[...] = r.fo[...]
    for dx in range(1, 4):
        got(r.dg_r2.at[2 + dx], r.r_dg2.at[2 + dx])
        total = total + r.dg_r2[2 + dx]
    r.g_gain[...] = total
    rows_spread_got(r.fqa, r.r_fqa)
    direct_spread_got(r.fqb, r.r_fqb)
    for i in range(8):
        r.g_qkv[:, 256 * i : 256 * (i + 1)] = r.fqa[i]
        r.g_qkv[:, 2048 + 128 * i : 2048 + 128 * (i + 1)] = r.fqb[i, :, 0:128]
        r.g_qkv[:, 3072 + 128 * i : 3072 + 128 * (i + 1)] = r.fqb[i, :, 128:256]

    gather_end(r.dy_all, r.s_dy)
    for half in range(2):
        gather_end(r.n2_all, r.s_n2, half)
        gather_end(r.x_all, r.s_dob, half)
    sent(r.pos_own, r.s_pos.at[0])
    for whole, ss in ((r.gain_recv, r.s_gain), (r.wqq, r.s_wqq), (r.wkv, r.s_wkv), (r.wgu, r.s_wgu)):
        rows_sent(whole, ss)
    for i in range(4):
        here = (xl == k) & (z == i) & (to_core == k)

        @pl.when(is_source & jnp.logical_not(here))
        def _():
            sent(r.wo_own.at[pl.ds(32 * i, 32)], r.s_wo.at[i])
            sent(r.wd_own.at[pl.ds(48 * i, 48)], r.s_wd.at[i])

    loop_sent(wo_rows(part), r.s_wo2, 1, 8)
    loop_sent(wd_rows(part), r.s_wd2, 1, 8)
    gather_end(r.xo_all, r.s_xo)
    sent(r.tok, r.s_xo.at[8])
    reduce_end(2, r.pa)
    for half in range(2):
        reduce_end(3, r.pb, half)
    for s in range(2):
        sent(r.dkv_o.at[:, pl.ds(128 * s, 128)], r.s_dkv.at[s])
    cross_sent(r.zqa, r.xqa, r.s_gqa)
    cross_sent(r.zqb, r.xqb, r.s_gqb)
    cross_sent(r.zgub, r.xgub, r.s_ggub)
    for i in range(3):
        sent(r.xgua.at[0], r.s_ggua.at[i])
        sent(r.zgua.at[0], r.s_ggua.at[3 + i])
    cross_sent(r.zo, r.xo, r.s_go)
    for i in range(3):
        sent(r.xd.at[0], r.s_gd.at[i])
        sent(r.zd.at[0], r.s_gd.at[3 + i])
    for hold, ss in ((r.hqa, r.s_fqa), (r.hgu, r.s_fgu)):
        rows_spread_sent(hold, ss)
    direct_spread_sent(r.hqb, r.s_fqb)
    block_sent(r.ho, r.s_fo)
    block_sent(r.hd, r.s_fd)
    loop_sent(r.dg, r.s_dg1, 1, 8)
    loop_sent(r.dg_s.at[0], r.s_dg2, 0, 6)


def layer(*args):
    vmem = pl.BlockSpec(memory_space=pltpu.VMEM)
    hbm = pl.BlockSpec(memory_space=pl.ANY)
    specs = [hbm if far else vmem for far in INPUTS.values()]
    return pl.pallas_call(
        layer_kernel,
        out_shape=[jax.ShapeDtypeStruct(shape, kind) for shape, kind in OUTPUTS.values()],
        in_specs=specs,
        out_specs=[vmem] * len(OUTPUTS),
        scratch_shapes=[pltpu.VMEM(shape, kind) for shape, kind in BUFFERS.values()]
        + [pltpu.SemaphoreType.DMA((count,)) for count in SEMAPHORES.values()],
        compiler_params=pltpu.CompilerParams(
            collective_id=0, has_side_effects=True, vmem_limit_bytes=62 << 20
        ),
        name="layer",
    )(*args)


def adam_update(weight, moment, square, grad, rate, decay):
    moment_new = beta_first * moment + (1.0 - beta_first) * grad
    square_new = beta_second * square + (1.0 - beta_second) * grad * grad
    fix_first = 1.0 - beta_first**STEP
    fix_second = 1.0 - beta_second**STEP
    step = moment_new / fix_first / (jnp.sqrt(square_new / fix_second) + adam_eps)
    return (weight - rate * (step + decay * weight), moment_new, square_new)


def on_device(
    tokens, d_out, block_ids,
    w_qkv, w_out, w_gate_up, w_down, gains,
    moment_qkv, moment_out, moment_gate_up, moment_down, moment_gains,
    square_qkv, square_out, square_gate_up, square_down, square_gains,
):
    f = lax.axis_index("fsdp")
    gain_rows = lax.dynamic_update_slice(
        jnp.zeros((24 * 128,), f32), gains.astype(bf16).astype(f32), (f * 144,)
    ).reshape(24, 128)
    half = rope_base ** (-(np.arange(64, dtype=np.float32) * np.float32(2.0 / HEAD)))
    table = np.zeros((8, 128), np.float32)
    table[0] = np.concatenate([half, half])
    table[1] = np.concatenate([-np.ones(64), np.ones(64)])
    out_tok, dtok, g_qkv, g_out, g_gu, g_dn, g_gain = layer(
        tokens[0], d_out[0], block_ids, gain_rows, jnp.asarray(table), w_qkv, w_out, w_gate_up, w_down
    )
    grad_gains = lax.dynamic_slice(g_gain.reshape(24 * 128), (f * 144,), (144,))
    grads = (g_qkv, g_out, g_gu, g_dn, grad_gains)
    masters = (w_qkv, w_out, w_gate_up, w_down, gains)
    moments = (moment_qkv, moment_out, moment_gate_up, moment_down, moment_gains)
    squares = (square_qkv, square_out, square_gate_up, square_down, square_gains)
    rates = (0.03, 0.3, 0.03, 0.03, 0.5)
    decays = (decay_rate, decay_rate, decay_rate, decay_rate, 0.0)
    updates = [
        adam_update(masters[i], moments[i], squares[i], grads[i].astype(f32), rates[i], decays[i])
        for i in range(5)
    ]
    return (
        out_tok[None],
        dtok[None],
        *(u[0] for u in updates),
        *(u[1] for u in updates),
        *(u[2] for u in updates),
    )


def solution(mesh):
    rows, flat = P("fsdp", None), P("fsdp")
    tokens = P("fsdp", "ctx", None)
    state = (rows, rows, rows, rows, flat)
    return jax.shard_map(
        on_device,
        mesh=mesh,
        in_specs=(tokens, tokens, rows) + state * 3,
        out_specs=(tokens, tokens) + state * 3,
        check_vma=False,
    )
```

```python
import math
import types

import jax
import jax.numpy as jnp
import numpy as np
from jax import lax
from jax.experimental import pallas as pl
from jax.experimental.pallas import tpu as pltpu
from jax.sharding import PartitionSpec as P

D = 1024
HEAD = 128
STEP = 10
BLOCK = 64
norm_eps = 1e-06
rope_base = 1000000.0
beta_first = 0.9
beta_second = 0.95
adam_eps = 1e-08
decay_rate = 0.1
SCALE = 1.0 / math.sqrt(HEAD)
LOG2E = 1.0 / math.log(2.0)

f32 = jnp.float32
bf16 = jnp.bfloat16
MESH = pl.DeviceIdType.MESH

INPUTS = dict(
    tok=False, dyt=False, ids=False, gain_in=False, freq=False, wqkv_f=True, wo_f=False, wgu_f=True, wd_f=False
)
OUTPUTS = dict(
    out_tok=((128, D), bf16),
    dtok=((128, D), bf16),
    g_qkv=((64, 4096), bf16),
    g_out=((128, D), bf16),
    g_gu=((64, 6144), bf16),
    g_dn=((192, D), bf16),
    g_gain=((24, 128), f32),
)
BUFFERS = dict(
    x_all=((4, 2, 128, D), bf16),
    dy_all=((4, 2, 128, D), bf16),
    n2_all=((4, 2, 128, D), bf16),
    n1_all=((4, 256, D), bf16),
    xo_all=((4, 2, 128, D), bf16),
    n1o_all=((4, 256, D), bf16),
    cos_o=((4, 256, HEAD), f32),
    sin_o=((4, 256, HEAD), f32),
    kraw_o=((4, 256, HEAD), f32),
    wq_f=((2, 64, 512), f32),
    wgu_fs=((2, 64, 768), f32),
    wqq_send=((2, 64, 256), bf16),
    wkv_send=((2, 64, 256), bf16),
    wgu_send=((2, 64, 768), bf16),
    wo_own=((128, D), bf16),
    wd_own=((192, D), bf16),
    wqq=((16, 64, 256), bf16),
    wkv=((16, 64, 256), bf16),
    wgu=((16, 64, 768), bf16),
    wo=((256, D), bf16),
    wd=((384, D), bf16),
    gain_recv=((16, 24, 128), f32),
    pos=((2, 8, D), f32),
    pos_own=((8, D), f32),
    posk=((2, D, 1), f32),
    cos_t=((4, 256, HEAD), f32),
    sin_t=((4, 256, HEAD), f32),
    qkraw=((4, 256, 384), f32),
    q_s=((2, 2, 256, 256), bf16),
    kv=((2, D, 256), bf16),
    o_t=((2, 256, 512), f32),
    ob_t=((2, 256, 512), bf16),
    lse=((2, 2, 1, 512), f32),
    pa=((4, 2, 128, D), bf16),
    pb=((4, 2, 128, D), bf16),
    ca=((4, 128, D), bf16),
    cb=((4, 128, D), bf16),
    ra=((3, 128, D), bf16),
    rb=((3, 128, D), bf16),
    h1=((128, D), f32),
    dh1=((128, D), f32),
    hid_all=((4, 2, 128, 384), bf16),
    dgu_all=((4, 2, 128, 768), bf16),
    do_t=((2, 256, 512), bf16),
    delta=((2, 2, 1, 512), f32),
    dkv=((2, D, 256), f32),
    dkv_o=((4, 256, 256), bf16),
    dkv_recv=((4, 256, 256), bf16),
    go_sum=((256, D), f32),
    dqkv=((4, 256, 512), bf16),
    gqa=((D, 256), bf16),
    gqb=((D, 256), bf16),
    ggua=((8, 2, 64, 256), bf16),
    ggub=((D, 512), bf16),
    go=((256, D), bf16),
    gd=((384, D), bf16),
    zqa=((3, 2, 128, 256), bf16),
    zqb=((3, 2, 128, 256), bf16),
    zgua=((3, 64, 256), bf16),
    zgub=((3, 2, 128, 512), bf16),
    zo=((3, 2, 32, D), bf16),
    zd=((3, 48, 512), bf16),
    sqa=((2, 128, 256), bf16),
    sqb=((2, 128, 256), bf16),
    sgua=((4, 64, 256), bf16),
    sgub=((2, 128, 512), bf16),
    so=((2, 32, D), bf16),
    sd=((192, 512), bf16),
    xqa=((3, 64, 256), bf16),
    xqb=((3, 64, 256), bf16),
    xgua=((3, 4, 64, 256), bf16),
    xgub=((3, 64, 512), bf16),
    xo=((3, 32, 512), bf16),
    xd=((3, 192, 512), bf16),
    hqa=((2, 64, 256), bf16),
    hqb=((64, 256), bf16),
    hgu=((2, 64, 768), bf16),
    ho=((32, D), bf16),
    hd=((48, D), bf16),
    yo=((3, 32, D), bf16),
    yd=((3, 48, D), bf16),
    fqa=((8, 64, 256), bf16),
    fqb=((8, 64, 256), bf16),
    fgu=((8, 64, 768), bf16),
    fo=((128, D), bf16),
    fd=((192, D), bf16),
    dg=((24, 128), f32),
    dg_r1=((8, 24, 128), f32),
    dg_s=((2, 24, 128), f32),
    dg_r2=((6, 24, 128), f32),
)
SEMAPHORES = dict(
    ld=16,
    s_x=8, r_x=8,
    s_dy=8, r_dy=8,
    s_n2=16, r_n2=16,
    s_dob=16, r_dob=16,
    s_pos=1, r_pos=1,
    s_gain=12, r_gain=12,
    s_wqq=12, r_wqq=12,
    s_wkv=12, r_wkv=12,
    s_wgu=12, r_wgu=12,
    s_wo=4, r_wo=1, s_wd=4, r_wd=1,
    s_wo2=8, r_wo2=8, s_wd2=8, r_wd2=8,
    s_xo=9, r_xo=9,
    s_c=32, r_c=32,
    s_r=48, r_r=48,
    s_dkv=2, r_dkv=2,
    s_gqa=9, r_gqa=9,
    s_gqb=9, r_gqb=9,
    s_ggua=6, r_ggua=6,
    s_ggub=9, r_ggub=9,
    s_go=9, r_go=9,
    s_gd=6, r_gd=6,
    s_fqa=9, r_fqa=9,
    s_fqb=8, r_fqb=8,
    s_fgu=9, r_fgu=9,
    s_fo=9, r_fo=9,
    s_fd=9, r_fd=9,
    s_dg1=8, r_dg1=8,
    s_dg2=6, r_dg2=6,
)


def dot(a, b):
    return jnp.dot(a, b, preferred_element_type=f32)


def dot_nt(a, b):
    return lax.dot_general(a, b, (((1,), (1,)), ((), ())), preferred_element_type=f32)


def dot_tn(a, b):
    return lax.dot_general(a, b, (((0,), (0,)), ((), ())), preferred_element_type=f32)


def to_row(g, first, count):
    return jnp.concatenate([g[first + i : first + i + 1, :] for i in range(count)], axis=1)


def layer_kernel(*refs):
    names = [*INPUTS, *OUTPUTS, *BUFFERS, *SEMAPHORES]
    r = types.SimpleNamespace(**dict(zip(names, refs, strict=True)))

    c = lax.axis_index("ctx")
    f = lax.axis_index("fsdp")
    xh, y = lax.div(c, 4), lax.rem(c, 4)
    xl, z, k = lax.div(f, 8), lax.rem(lax.div(f, 2), 4), lax.rem(f, 2)
    x = 2 * xh + xl
    part = 4 * xl + z
    t = 2 * y + k
    other = 1 - k

    def place(xh_, xl_, y_, z_, k_):
        return (xh_ * 4 + y_, xl_ * 8 + z_ * 2 + k_)

    partner = place(xh, xl, y, z, other)

    def around(value, step):
        return lax.rem(value + step, 4)

    def copy(src, dst, ss, rs, device):
        return pltpu.make_async_remote_copy(
            src_ref=src, dst_ref=dst, send_sem=ss, recv_sem=rs,
            device_id=device, device_id_type=MESH,
        )

    def send(src, dst, ss, rs, device):
        copy(src, dst, ss, rs, device).start()

    def got(ref, rs):
        copy(ref, ref, rs, rs, partner).wait_recv()

    def sent(ref, ss):
        copy(ref, ref, ss, ss, partner).wait_send()

    loads = []

    def load(src, dst):
        one = pltpu.make_async_copy(src, dst, r.ld.at[len(loads)])
        one.start()
        loads.append(one)

    for i in range(2):
        ti = 2 * y + i
        load(r.wqkv_f.at[:, pl.ds(pl.multiple_of(256 * ti, 256), 256)], r.wq_f.at[i, :, pl.ds(0, 256)])
        load(r.wqkv_f.at[:, pl.ds(pl.multiple_of(2048 + 128 * ti, 128), 128)], r.wq_f.at[i, :, pl.ds(256, 128)])
        load(r.wqkv_f.at[:, pl.ds(pl.multiple_of(3072 + 128 * ti, 128), 128)], r.wq_f.at[i, :, pl.ds(384, 128)])
    for i in range(2):
        ti = 2 * y + i
        load(r.wgu_f.at[:, pl.ds(pl.multiple_of(384 * ti, 128), 384)], r.wgu_fs.at[i, :, pl.ds(0, 384)])
        load(r.wgu_f.at[:, pl.ds(pl.multiple_of(3072 + 384 * ti, 128), 384)], r.wgu_fs.at[i, :, pl.ds(384, 384)])

    barrier = pltpu.get_barrier_semaphore()

    def greet(device):
        pl.semaphore_signal(barrier, inc=1, device_id=device, device_id_type=MESH)

    def greet_plane(i, carry):
        greet(place(xh, lax.rem(xl + lax.div(i, 8), 2), y, around(z, lax.rem(lax.div(i, 2), 4)), lax.rem(k + i, 2)))
        return carry

    def along_x(d):
        x_ = around(x, d)
        return place(lax.div(x_, 2), lax.rem(x_, 2), y, z, k)

    for i in range(1, 8):
        greet(place(xh, xl, around(y, i // 2), z, lax.rem(k + i, 2)))
    for i in range(8):
        greet(place(1 - xh, xl, around(y, i // 2), z, lax.rem(k + i, 2)))
    lax.fori_loop(1, 16, greet_plane, 0)
    for d in range(1, 4):
        greet(along_x(d))

    for one in loads:
        one.wait()
    r.wqq_send[...] = r.wq_f[:, :, 0:256].astype(bf16)
    r.wkv_send[...] = r.wq_f[:, :, 256:512].astype(bf16)
    r.wgu_send[...] = r.wgu_fs[...].astype(bf16)
    r.wo_own[...] = r.wo_f[...].astype(bf16)
    r.wd_own[...] = r.wd_f[...].astype(bf16)
    r.wqq[f] = r.wqq_send[k]
    r.wkv[f] = r.wkv_send[k]
    r.wgu[f] = r.wgu_send[k]
    r.gain_recv[f] = r.gain_in[...]
    r.x_all[y, k] = r.tok[...]
    r.dy_all[y, k] = r.dyt[...]
    starts = r.ids[...].astype(f32) * BLOCK
    lane = lax.broadcasted_iota(jnp.int32, (1, D), 1)
    first = jnp.zeros((1, D), f32)
    for b in range(16):
        first = jnp.where(lax.div(lane, BLOCK) == b, starts[:, b : b + 1], first)
    inside = lax.rem(lane, BLOCK).astype(f32)
    r.pos_own[...] = jnp.zeros((8, D), f32)
    r.pos_own[0:1, :] = first + inside
    first = jnp.zeros((1, D), f32)
    for b in range(8):
        spot = 2 * (b % 4) + b // 4
        start = jnp.where(xh == 0, starts[:, spot : spot + 1], starts[:, spot + 8 : spot + 9])
        first = jnp.where(lax.div(lane, BLOCK) == b, start, first)
    r.pos_own[1:2, :] = first + inside
    r.pos[k] = r.pos_own[...]
    r.dg[...] = jnp.zeros((24, 128), f32)
    pl.semaphore_wait(barrier, 33)

    def rows_of(half):
        return pl.ds(0, 128) if half is None else pl.ds(64 * half, 64)

    def far_part(half, which):
        size = 64 if half is None else 32
        return pl.ds((0 if half is None else 64 * half) + size * which, size)

    def gather_start(src, whole, ss, rs, half=None):
        rows, o = rows_of(half), 8 * (half or 0)
        for d in (1, 3):
            send(src.at[rows], whole.at[y, k, rows], ss.at[o + d - 1], rs.at[o + d - 1], place(xh, xl, around(y, d), z, k))
        send(src.at[rows], whole.at[y, k, rows], ss.at[o + 3], rs.at[o + 3], partner)

    def gather_forward(whole, ss, rs, d, half=None):
        rows, o = rows_of(half), 8 * (half or 0)
        block = whole.at[around(y, 4 - d), k, rows]
        if d == 2:
            for which in range(2):
                got(whole.at[around(y, 2), k, far_part(half, which)], rs.at[o + (1, 7)[which]])
        else:
            got(block, rs.at[o + d - 1])
            which = 0 if d == 1 else 1
            part_of = whole.at[around(y, 4 - d), k, far_part(half, which)]
            i = o + (1, 7)[which]
            send(part_of, part_of, ss.at[i], rs.at[i], place(xh, xl, around(y, d), z, k))
        send(block, block, ss.at[o + 3 + d], rs.at[o + 3 + d], partner)

    def gather_own(whole, rs, half=None):
        got(whole.at[y, other, rows_of(half)], rs.at[8 * (half or 0) + 3])

    def gather_pair(whole, rs, d, half=None):
        got(whole.at[around(y, 4 - d), other, rows_of(half)], rs.at[8 * (half or 0) + 3 + d])

    def gather_end(whole, ss, half=None):
        o = 8 * (half or 0)
        for i in (0, 2, 3, 4, 5, 6):
            sent(whole.at[y, k, rows_of(half)], ss.at[o + i])
        for i in (1, 7):
            sent(whole.at[y, k, far_part(half, 0)], ss.at[o + i])

    def chip_slots(whole, l_, zz):
        return whole.at[pl.ds(8 * l_ + 2 * zz, 2)]

    def z_send(src_of, whole, ss, rs):
        for i in range(1, 8):
            core = lax.rem(k + i, 2)
            send(src_of(core), whole.at[f], ss.at[i], rs.at[i], place(xh, xl, y, around(z, i // 2), core))

    def z_got(whole, rs, dz):
        for dk in range(2):
            if dz + dk > 0:
                got(whole.at[8 * xl + 2 * around(z, 4 - dz) + lax.rem(k + dk, 2)], rs.at[2 * dz + dk])

    def beside(dz):
        return along_x(1 if dz < 2 else 3)

    def x_send(whole, ss, rs, dz):
        block = chip_slots(whole, xl, around(z, 4 - dz))
        send(block, block, ss.at[8 + dz], rs.at[8 + dz], beside(dz))

    def x_got(whole, rs, dz):
        got(chip_slots(whole, 1 - xl, around(z, 4 - dz)), rs.at[8 + dz])

    def rows_sent(whole, ss):
        for i in range(1, 8):
            sent(whole.at[f], ss.at[i])
        for dz in range(4):
            sent(chip_slots(whole, xl, around(z, 4 - dz)), ss.at[8 + dz])

    def loop_sent(ref, ss, first, last):
        def one(i, carry):
            sent(ref, ss.at[i])
            return carry

        lax.fori_loop(first, last, one, 0)

    gather_start(r.tok, r.x_all, r.s_x, r.r_x)
    send(r.tok, r.xo_all.at[y, k], r.s_xo.at[8], r.r_xo.at[8], along_x(2))
    z_send(lambda k_: r.gain_in, r.gain_recv, r.s_gain, r.r_gain)
    z_send(lambda k_: r.wkv_send.at[k_], r.wkv, r.s_wkv, r.r_wkv)
    send(r.pos_own, r.pos.at[k], r.s_pos.at[0], r.r_pos.at[0], partner)
    z_send(lambda k_: r.wqq_send.at[k_], r.wqq, r.s_wqq, r.r_wqq)

    is_source = lax.div(part, 2) == y
    to_core = lax.rem(part, 2)
    for i in range(4):
        piece = 4 * k + i
        here = (xl == k) & (z == i) & (to_core == k)

        @pl.when(is_source & jnp.logical_not(here))
        def _():
            there = place(xh, k, y, i, to_core)
            send(r.wo_own.at[pl.ds(32 * i, 32)], r.wo.at[pl.ds(pl.multiple_of(32 * piece, 32), 32)], r.s_wo.at[i], r.r_wo.at[0], there)
            send(r.wd_own.at[pl.ds(48 * i, 48)], r.wd.at[pl.ds(pl.multiple_of(48 * piece, 16), 48)], r.s_wd.at[i], r.r_wd.at[0], there)

        @pl.when(is_source & here)
        def _():
            r.wo[pl.ds(pl.multiple_of(32 * piece, 32), 32), :] = r.wo_own[32 * i : 32 * i + 32, :]
            r.wd[pl.ds(pl.multiple_of(48 * piece, 16), 48), :] = r.wd_own[48 * i : 48 * i + 48, :]

    def wo_rows(q):
        return r.wo.at[pl.ds(pl.multiple_of(32 * q, 32), 32)]

    def wd_rows(q):
        return r.wd.at[pl.ds(pl.multiple_of(48 * q, 16), 48)]

    def pass_on(whole, ss, rs, dz):
        z_got(whole, rs, dz)
        x_send(whole, ss, rs, dz)

    pass_on(r.gain_recv, r.s_gain, r.r_gain, 0)
    pass_on(r.wkv, r.s_wkv, r.r_wkv, 0)

    got(r.pos.at[other], r.r_pos.at[0])
    steps = lax.broadcasted_iota(jnp.int32, (BLOCK, 1), 0).astype(f32)
    for s in range(2):
        for b in range(16):
            r.posk[s, b * BLOCK : (b + 1) * BLOCK, :] = r.pos[s, 0:1, b * BLOCK : b * BLOCK + 1] + steps
    freq = r.freq[0:1, :]
    sign = r.freq[1:2, :]

    def tables(i, carry):
        hh, yy = lax.rem(xh + lax.div(i, 4), 2), lax.rem(i, 4)
        for s in range(2):
            rows = r.posk[s, pl.ds(pl.multiple_of(512 * hh + 128 * yy, 128), 128), :]
            angle = rows * freq
            cos, sin = jnp.cos(angle), jnp.sin(angle) * sign

            @pl.when(i < 4)
            def _():
                r.cos_t[yy, s * 128 : (s + 1) * 128, :] = cos
                r.sin_t[yy, s * 128 : (s + 1) * 128, :] = sin

            @pl.when(i >= 4)
            def _():
                r.cos_o[yy, s * 128 : (s + 1) * 128, :] = cos
                r.sin_o[yy, s * 128 : (s + 1) * 128, :] = sin

        return carry

    lax.fori_loop(0, 2, tables, 0)

    for dz in (1, 3):
        pass_on(r.gain_recv, r.s_gain, r.r_gain, dz)
        pass_on(r.wkv, r.s_wkv, r.r_wkv, dz)
    for d in (1, 3):
        gather_forward(r.x_all, r.s_x, r.r_x, d)
    got(r.xo_all.at[y, k], r.r_xo.at[8])
    gather_start(r.xo_all.at[y, k], r.xo_all, r.s_xo, r.r_xo)
    gather_start(r.dyt, r.dy_all, r.s_dy, r.r_dy)
    pass_on(r.gain_recv, r.s_gain, r.r_gain, 2)
    pass_on(r.wkv, r.s_wkv, r.r_wkv, 2)
    lax.fori_loop(2, 4, tables, 0)
    own_piece = (2 * y + k == part) & (xl == k)

    def start_rest():
        for dz in (0, 1, 3, 2):
            pass_on(r.wqq, r.s_wqq, r.r_wqq, dz)

        @pl.when(jnp.logical_not(own_piece))
        def _():
            got(wo_rows(part), r.r_wo.at[0])
            got(wd_rows(part), r.r_wd.at[0])

        for dz in range(1, 4):
            there = place(xh, xl, y, around(z, dz), k)
            send(wo_rows(part), wo_rows(part), r.s_wo2.at[dz], r.r_wo2.at[dz], there)
        z_send(lambda k_: r.wgu_send.at[k_], r.wgu, r.s_wgu, r.r_wgu)
        for dz in range(1, 4):
            there = place(xh, xl, y, around(z, dz), k)
            send(wd_rows(part), wd_rows(part), r.s_wd2.at[dz], r.r_wd2.at[dz], there)

    def piece_of(l_, dz):
        return 4 * l_ + around(z, 4 - dz)

    for dz in range(4):
        x_got(r.gain_recv, r.r_gain, dz)
    gains = jnp.sum(r.gain_recv[...], axis=0)
    g1 = to_row(gains, 0, 8)
    g2 = to_row(gains, 8, 8)
    gq = gains[16:17, :]
    gk = gains[17:18, :]

    def rotated(u, cos, sin):
        return u * cos + pltpu.roll(u, 64, 1) * sin

    def unrotated(u, cos, sin):
        return u * cos - pltpu.roll(u, 64, 1) * sin

    def inverse_rms(u):
        return lax.rsqrt(jnp.mean(u * u, axis=-1, keepdims=True) + norm_eps)

    def project_keys(d, x_all, n1_all, raw_at, cos, sin, hh):
        yy = around(y, 4 - d)
        rows = x_all[yy].reshape(256, D).astype(f32)
        n1 = (rows * inverse_rms(rows) * g1).astype(bf16)
        n1_all[yy] = n1
        kv = dot(n1, r.wkv[...].reshape(D, 256))
        raw = kv[:, 0:HEAD]
        raw_at(yy)[...] = raw
        local = pl.ds(pl.multiple_of(512 * hh + 128 * yy, 128), 128)
        key = rotated(raw * inverse_rms(raw) * gk, cos[yy], sin[yy]).astype(bf16)
        value = kv[:, HEAD:].astype(bf16)
        for s in range(2):
            r.kv[s, local, 0:HEAD] = key[s * 128 : (s + 1) * 128]
            r.kv[s, local, HEAD : 2 * HEAD] = value[s * 128 : (s + 1) * 128]

    def project_mine(d):
        project_keys(d, r.x_all, r.n1_all, lambda yy: r.qkraw.at[yy, :, pl.ds(256, HEAD)], r.cos_t, r.sin_t, xh)

    def project_others(d):
        project_keys(d, r.xo_all, r.n1o_all, lambda yy: r.kraw_o.at[yy], r.cos_o, r.sin_o, 1 - xh)

    def project_queries(yy, carry):
        qs = dot(r.n1_all[yy], r.wqq[...].reshape(D, 256))
        r.qkraw[yy, :, 0:256] = qs
        for h in range(2):
            raw = qs[:, h * HEAD : (h + 1) * HEAD]
            query = rotated(raw * inverse_rms(raw) * gq, r.cos_t[yy], r.sin_t[yy]).astype(bf16)
            for s in range(2):
                for half in range(2):
                    first = s * 128 + half * 64
                    rows = pl.ds(pl.multiple_of(64 * yy, 64), 64)
                    r.q_s[s, half, rows, h * HEAD : (h + 1) * HEAD] = query[first : first + 64]
        return carry

    gather_own(r.x_all, r.r_x)
    for dz in range(4):
        x_got(r.wkv, r.r_wkv, dz)
    project_mine(0)
    gather_pair(r.x_all, r.r_x, 1)
    project_mine(1)
    gather_forward(r.x_all, r.s_x, r.r_x, 2)
    gather_pair(r.x_all, r.r_x, 3)
    project_mine(3)
    start_rest()
    gather_pair(r.x_all, r.r_x, 2)
    project_mine(2)
    for d in (1, 3):
        gather_forward(r.xo_all, r.s_xo, r.r_xo, d)
    lax.fori_loop(4, 8, tables, 0)
    for dz in range(4):
        if dz > 0:
            got(wo_rows(piece_of(xl, dz)), r.r_wo2.at[dz])
        block = wo_rows(piece_of(xl, dz))
        send(block, block, r.s_wo2.at[4 + dz], r.r_wo2.at[4 + dz], beside(dz))
    for dz in range(4):
        x_got(r.wqq, r.r_wqq, dz)
    lax.fori_loop(0, 4, project_queries, 0)
    gather_own(r.xo_all, r.r_xo)
    project_others(0)
    gather_forward(r.xo_all, r.s_xo, r.r_xo, 2)
    gather_pair(r.xo_all, r.r_xo, 1)
    project_others(1)
    gather_pair(r.xo_all, r.r_xo, 3)
    project_others(3)
    gather_pair(r.xo_all, r.r_xo, 2)
    project_others(2)
    gather_end(r.x_all, r.s_x)

    def rest_forward():
        for dz in range(4):
            pass_on(r.wgu, r.s_wgu, r.r_wgu, dz)
        for dz in range(4):
            if dz > 0:
                got(wd_rows(piece_of(xl, dz)), r.r_wd2.at[dz])
            block = wd_rows(piece_of(xl, dz))
            send(block, block, r.s_wd2.at[4 + dz], r.r_wd2.at[4 + dz], beside(dz))

    def lanes(half):
        return pl.ds(pl.multiple_of(256 * half, 256), 256)

    def allowed(s, half):
        return r.posk[s] <= r.pos[s, 1:2, lanes(half)]

    def attend(s, half):
        ok = allowed(s, half)
        for h in range(2):
            q = r.q_s[s, half, :, h * HEAD : (h + 1) * HEAD]
            scores = jnp.where(ok, dot_nt(r.kv[s, :, 0:HEAD], q) * (SCALE * LOG2E), -1e30)
            top = jnp.max(scores, axis=0, keepdims=True)
            p = jnp.exp2(scores - top)
            total = jnp.sum(p, axis=0, keepdims=True)
            o = dot_tn(r.kv[s, :, HEAD : 2 * HEAD], p.astype(bf16)) / total
            r.o_t[s, h * HEAD : (h + 1) * HEAD, lanes(half)] = o
            r.ob_t[s, h * HEAD : (h + 1) * HEAD, lanes(half)] = o.astype(bf16)
            r.lse[s, h, :, lanes(half)] = top + jnp.log(total) * LOG2E

    def reduce_first(use, p, cc, d, half=None):
        yy, rows, i = around(y, d), rows_of(half), 8 * use + 4 * (half or 0) + d
        send(p.at[yy, other, rows], cc.at[yy, rows], r.s_c.at[i], r.r_c.at[i], partner)

    def both_cores(use, p, cc, d, half):
        yy, rows, i = around(y, d), rows_of(half), 8 * use + 4 * (half or 0) + d
        got(cc.at[yy, rows], r.r_c.at[i])
        return p[yy, k, rows, :].astype(f32) + cc[yy, rows, :].astype(f32)

    def reduce_far(use, p, cc, rr, half=None):
        rows, o = rows_of(half), 12 * use + 6 * (half or 0)
        yy = around(y, 2)
        p[yy, k, rows, :] = both_cores(use, p, cc, 2, half).astype(bf16)
        for which in range(2):
            rest = far_part(half, which)
            there = place(xh, xl, around(y, 1 + 2 * which), z, k)
            send(p.at[yy, k, rest], rr.at[2, rest], r.s_r.at[o + which], r.r_r.at[o + which], there)
        for which in range(2):
            yy = around(y, 1 + 2 * which)
            p[yy, k, rows, :] = both_cores(use, p, cc, 1 + 2 * which, half).astype(bf16)
            early, i = far_part(half, 1 - which), o + 2 + which
            send(p.at[yy, k, early], rr.at[which, early], r.s_r.at[i], r.r_r.at[i], place(xh, xl, yy, z, k))

    def reduce_near(use, p, rr, half=None):
        o = 12 * use + 6 * (half or 0)
        for which in range(2):
            yy = around(y, 1 + 2 * which)
            late, i = far_part(half, which), o + 4 + which
            got(rr.at[2, late], r.r_r.at[o + which])
            p[yy, k, late, :] = (p[yy, k, late, :].astype(f32) + rr[2, late, :].astype(f32)).astype(bf16)
            send(p.at[yy, k, late], rr.at[which, late], r.s_r.at[i], r.r_r.at[i], place(xh, xl, yy, z, k))

    def reduce_third(use, p, cc, rr, half=None):
        rows, o = rows_of(half), 12 * use + 6 * (half or 0)
        total = both_cores(use, p, cc, 0, half)
        for which in range(2):
            got(rr.at[which, far_part(half, 1 - which)], r.r_r.at[o + 2 + which])
            got(rr.at[which, far_part(half, which)], r.r_r.at[o + 4 + which])
            total = total + rr[which, rows, :].astype(f32)
        return total

    def reduce_end(use, p, half=None):
        for d in range(4):
            sent(p.at[y, other, rows_of(half)], r.s_c.at[8 * use + 4 * (half or 0) + d])
        for i in range(6):
            sent(p.at[y, k, far_part(half, 0)], r.s_r.at[12 * use + 6 * (half or 0) + i])

    def out_partial(half):
        for s in (other, k):
            o = r.ob_t[s, :, lanes(half)]
            r.pa[:, s, rows_of(half), :] = dot_tn(o, r.wo[...]).astype(bf16).reshape(4, 64, D)
            if s is other:
                for d in (2, 1, 3, 0):
                    reduce_first(0, r.pa, r.ca, d, half)

    for d in (1, 3):
        gather_forward(r.dy_all, r.s_dy, r.r_dy, d)
    attend(0, 0)
    attend(1, 0)
    for dz in range(4):
        got(wo_rows(piece_of(1 - xl, dz)), r.r_wo2.at[4 + dz])
    out_partial(0)
    rest_forward()
    attend(0, 1)
    reduce_far(0, r.pa, r.ca, r.ra, 0)
    gather_forward(r.dy_all, r.s_dy, r.r_dy, 2)
    attend(1, 1)
    out_partial(1)
    reduce_near(0, r.pa, r.ra, 0)
    reduce_far(0, r.pa, r.ca, r.ra, 1)

    def middle(half):
        rows = rows_of(half)
        h1 = r.tok[rows, :].astype(f32) + reduce_third(0, r.pa, r.ca, r.ra, half)
        r.h1[rows, :] = h1
        r.n2_all[y, k, rows, :] = (h1 * inverse_rms(h1) * g2).astype(bf16)
        gather_start(r.n2_all.at[y, k], r.n2_all, r.s_n2, r.r_n2, half)

    middle(0)
    reduce_near(0, r.pa, r.ra, 1)
    middle(1)

    gather_own(r.dy_all, r.r_dy)
    for d in (1, 3, 2):
        gather_pair(r.dy_all, r.r_dy, d)
    for dz in range(4):
        x_got(r.wgu, r.r_wgu, dz)
        got(wd_rows(piece_of(1 - xl, dz)), r.r_wd2.at[4 + dz])

    def two_blocks(whole, ds, half):
        blocks = [whole[around(y, d), :, rows_of(half), :].reshape(128, whole.shape[-1]) for d in ds]
        return jnp.concatenate(blocks, axis=0)

    def put_blocks(whole, ds, half, cols, value):
        for i, d in enumerate(ds):
            block = value[128 * i : 128 * (i + 1)].reshape(2, 64, value.shape[-1])
            whole[around(y, d), :, rows_of(half), cols] = block

    def feed(ds, half):
        n2 = two_blocks(r.n2_all, ds, half)
        ab = dot(n2, r.wgu[...].reshape(D, 768))
        a, b = ab[:, :384], ab[:, 384:]
        sig = jax.nn.sigmoid(a)
        silu = a * sig
        put_blocks(r.hid_all, ds, half, slice(None), (silu * b).astype(bf16))
        dhid = dot_nt(two_blocks(r.dy_all, ds, half), r.wd[...])
        da = (dhid * b * sig * (1.0 + a * (1.0 - sig))).astype(bf16)
        db = (dhid * silu).astype(bf16)
        put_blocks(r.dgu_all, ds, half, slice(0, 384), da)
        put_blocks(r.dgu_all, ds, half, slice(384, 768), db)
        dn2 = dot_nt(jnp.concatenate([da, db], axis=1), r.wgu[...].reshape(D, 768))
        put_blocks(r.pb, ds, half, slice(None), dn2.astype(bf16))
        for d in ds:
            reduce_first(1, r.pb, r.cb, d, half)

    def near_forward(whole, ss, rs, half):
        for d in (1, 3):
            gather_forward(whole, ss, rs, d, half)

    near_forward(r.n2_all, r.s_n2, r.r_n2, 0)
    for half in range(2):
        gather_own(r.n2_all, r.r_n2, half)
        gather_pair(r.n2_all, r.r_n2, 1, half)
        feed((0, 3), half)
        if half == 1:
            reduce_near(1, r.pb, r.rb, 0)
        gather_forward(r.n2_all, r.s_n2, r.r_n2, 2, half)
        if half == 0:
            near_forward(r.n2_all, r.s_n2, r.r_n2, 1)
        gather_pair(r.n2_all, r.r_n2, 3, half)
        gather_pair(r.n2_all, r.r_n2, 2, half)
        feed((2, 1), half)
        reduce_far(1, r.pb, r.cb, r.rb, half)

    def rows_at(whole, height):
        return lambda l_, z_: whole.at[pl.ds(pl.multiple_of(height * (4 * l_ + z_), 16), height)]

    def cross_z(piece, dst, ss, rs):
        for dz in (1, 3, 2):
            zz = around(z, dz)
            for l_ in range(2):
                i = 2 * (dz - 1) + l_
                send(piece(l_, zz), dst.at[dz - 1, l_], ss.at[i], rs.at[i], place(xh, xl, y, zz, k))

    def row_half(ref, h_):
        return ref.at[pl.ds(pl.multiple_of(64 * h_, 64), 64)]

    def column_half(ref, h_):
        return ref.at[:, pl.ds(pl.multiple_of(512 * h_, 512), 512)]

    def cross_x(piece, zrecv, sums, xrecv, half_of, ss, rs):
        for l_ in range(2):
            total = piece(l_, z)[...].astype(f32)
            for dz in range(1, 4):
                got(zrecv.at[dz - 1, l_], rs.at[2 * (dz - 1) + l_])
                total = total + zrecv[dz - 1, l_].astype(f32)
            sums[l_] = total.astype(bf16)
        for dx in (1, 3, 2):
            x_ = around(x, dx)
            block = half_of(sums.at[lax.rem(x_, 2)], lax.div(x_, 2))
            send(block, xrecv.at[dx - 1], ss.at[5 + dx], rs.at[5 + dx], along_x(dx))

    def cross_total(sums, xrecv, half_of, rs):
        total = half_of(sums.at[xl], xh)[...].astype(f32)
        for dx in (1, 3, 2):
            got(xrecv.at[dx - 1], rs.at[5 + dx])
            total = total + xrecv[dx - 1].astype(f32)
        return total

    def cross_x_first(whole, height, xrecv, ss, rs):
        for dx in (1, 3, 2):
            x_ = around(x, dx)
            rows = pl.ds(pl.multiple_of(4 * height * lax.rem(x_, 2), 16), 4 * height)
            block = column_half(whole.at[rows], lax.div(x_, 2))
            send(block, xrecv.at[dx - 1], ss.at[dx - 1], rs.at[dx - 1], along_x(dx))

    def cross_z_second(whole, height, xrecv, sums, zrecv, ss, rs):
        rows = pl.ds(pl.multiple_of(4 * height * xl, 16), 4 * height)
        total = column_half(whole.at[rows], xh)[...].astype(f32)
        for dx in (1, 3, 2):
            got(xrecv.at[dx - 1], rs.at[dx - 1])
            total = total + xrecv[dx - 1].astype(f32)
        sums[...] = total.astype(bf16)
        for dz in (1, 3, 2):
            zz = around(z, dz)
            block = sums.at[pl.ds(pl.multiple_of(height * zz, 16), height)]
            send(block, zrecv.at[dz - 1], ss.at[2 + dz], rs.at[2 + dz], place(xh, xl, y, zz, k))

    def cross_z_total(height, sums, zrecv, rs):
        total = sums[pl.ds(pl.multiple_of(height * z, 16), height), :].astype(f32)
        for dz in (1, 3, 2):
            got(zrecv.at[dz - 1], rs.at[2 + dz])
            total = total + zrecv[dz - 1].astype(f32)
        return total

    def rows_x_first():
        for dx in (1, 3, 2):
            x_ = around(x, dx)
            block = r.ggua.at[pl.ds(4 * lax.rem(x_, 2), 4), lax.div(x_, 2)]
            send(block, r.xgua.at[dx - 1], r.s_ggua.at[dx - 1], r.r_ggua.at[dx - 1], along_x(dx))

    def rows_z_second():
        total = r.ggua[pl.ds(4 * xl, 4), xh].astype(f32)
        for dx in (1, 3, 2):
            got(r.xgua.at[dx - 1], r.r_ggua.at[dx - 1])
            total = total + r.xgua[dx - 1].astype(f32)
        r.sgua[...] = total.astype(bf16)
        for dz in (1, 3, 2):
            zz = around(z, dz)
            send(r.sgua.at[zz], r.zgua.at[dz - 1], r.s_ggua.at[2 + dz], r.r_ggua.at[2 + dz], place(xh, xl, y, zz, k))

    def rows_z_total():
        total = r.sgua[z].astype(f32)
        for dz in (1, 3, 2):
            got(r.zgua.at[dz - 1], r.r_ggua.at[2 + dz])
            total = total + r.zgua[dz - 1].astype(f32)
        return total

    def cross_sent(zrecv, xrecv, ss):
        for i in range(6):
            sent(zrecv.at[0, 0], ss.at[i])
        for i in range(3):
            sent(xrecv.at[0], ss.at[6 + i])

    gqa_piece, gqb_piece, ggub_piece = rows_at(r.gqa, 128), rows_at(r.gqb, 128), rows_at(r.ggub, 128)
    go_piece = rows_at(r.go, 32)

    def weight_gradient(left, right, out, first=0):
        def one(i, carry):
            cols = pl.ds(pl.multiple_of(256 * i, 256), 256)
            taken = pl.ds(pl.multiple_of(first + 256 * i, 256), 256)
            out[:, cols] = dot_tn(left(), right(taken)).astype(bf16)
            return carry

        lax.fori_loop(0, out.shape[1] // 256, one, 0)

    def middle_back(half):
        rows = rows_of(half)
        dn2 = reduce_third(1, r.pb, r.cb, r.rb, half)
        h1 = r.h1[rows, :]
        r2 = inverse_rms(h1)
        weighted = dn2 * g2
        back = r2 * weighted - h1 * (r2 * r2 * r2) * jnp.mean(weighted * h1, axis=-1, keepdims=True)
        dh1 = r.dyt[rows, :].astype(f32) + back
        r.dh1[rows, :] = dh1
        dg2 = jnp.sum(dn2 * h1 * r2, axis=0, keepdims=True)
        for i in range(8):
            r.dg[8 + i : 9 + i, :] += dg2[:, 128 * i : 128 * (i + 1)]
        r.x_all[y, k, rows, :] = dh1.astype(bf16)
        gather_start(r.x_all.at[y, k], r.x_all, r.s_dob, r.r_dob, half)

    ggua = dot_tn(r.n2_all[...].reshape(D, D), r.dgu_all[:, :, :, 0:256].reshape(D, 256))
    r.ggua[...] = ggua.astype(bf16).reshape(8, 2, 64, 256)
    rows_x_first()
    weight_gradient(
        lambda: r.n2_all[...].reshape(D, D),
        lambda cols: r.dgu_all[:, :, :, cols].reshape(D, 256),
        r.ggub,
        256,
    )
    cross_z(ggub_piece, r.zgub, r.s_ggub, r.r_ggub)
    reduce_near(1, r.pb, r.rb, 1)
    middle_back(0)
    weight_gradient(
        lambda: r.hid_all[...].reshape(D, 384),
        lambda cols: r.dy_all[:, :, :, cols].reshape(D, 256),
        r.gd,
    )
    cross_x_first(r.gd, 48, r.xd, r.s_gd, r.r_gd)
    middle_back(1)

    def direct_spread(total, hold, final, ss, rs):
        hold[...] = total.astype(bf16)

        def one(i, carry):
            there = place(lax.rem(xh + lax.div(i, 4), 2), xl, lax.rem(y + i, 4), z, xh)

            @pl.when((i > 0) | (k != xh))
            def _():
                send(hold, final.at[t], ss.at[i], rs.at[t], there)

            return carry

        lax.fori_loop(0, 8, one, 0)

        @pl.when(k == xh)
        def _():
            final[t] = hold[...]

    def direct_spread_sent(hold, ss):
        def one(i, carry):
            @pl.when((i > 0) | (k != xh))
            def _():
                sent(hold, ss.at[i])

            return carry

        lax.fori_loop(0, 8, one, 0)

    def direct_spread_got(final, rs):
        def one(i, carry):
            @pl.when((i != t) | (k != xh))
            def _():
                got(final.at[i], rs.at[i])

            return carry

        lax.fori_loop(0, 8, one, 0)

    other_half = place(1 - xh, xl, y, z, k)

    def rows_exchange(total, hold, ss, rs):
        hold[xh] = total.astype(bf16)
        send(hold.at[xh], hold.at[xh], ss.at[8], rs.at[8], other_half)

    def rows_spread(hold, final, ss, rs):
        for which in range(2):
            h = xh if which == 0 else 1 - xh
            if which == 1:
                got(hold.at[h], rs.at[8])
            for i in (2, 1, 3):
                send(hold.at[h], final.at[t], ss.at[4 * which + i], rs.at[t], place(xh, xl, around(y, i), z, h))

            @pl.when(k != h)
            def _():
                send(hold.at[h], final.at[t], ss.at[4 * which], rs.at[t], partner)

            @pl.when(k == h)
            def _():
                final[t] = hold[h]

    def rows_spread_sent(hold, ss):
        sent(hold.at[0], ss.at[8])
        for which in range(2):
            h = xh if which == 0 else 1 - xh
            for i in range(1, 4):
                sent(hold.at[0], ss.at[4 * which + i])

            @pl.when(k != h)
            def _():
                sent(hold.at[0], ss.at[4 * which])

    def rows_spread_got(final, rs):
        def one(i, carry):
            @pl.when(i != t)
            def _():
                got(final.at[i], rs.at[i])

            return carry

        lax.fori_loop(0, 8, one, 0)

    def block_exchange(total, hold, ss, rs):
        column_half(hold, xh)[...] = total.astype(bf16)
        send(column_half(hold, xh), column_half(hold, xh), ss.at[8], rs.at[8], other_half)

    def block_along_y(hold, held, ss, rs):
        got(column_half(hold, 1 - xh), rs.at[8])
        for i in (1, 3, 2):
            send(hold, held.at[i - 1], ss.at[i], rs.at[i], place(xh, xl, around(y, i), z, k))

    def block_target(i):
        slice_ = 2 * around(y, 4 - i) + k
        mine = (part == slice_) & (k == xl)
        return mine, place(xh, lax.div(slice_, 4), y, lax.rem(slice_, 4), xl)

    def block_deliver(hold, held, final, height, ss, rs):
        rows = pl.ds(pl.multiple_of(height * z, 16), height)
        for i in (0, 1, 3, 2):
            block = hold
            if i > 0:
                got(held.at[i - 1], rs.at[i])
                block = held.at[i - 1]
            mine, there = block_target(i)

            @pl.when(jnp.logical_not(mine))
            def _():
                send(block, final.at[rows], ss.at[4 + i], rs.at[4 + z], there)

            @pl.when(mine)
            def _():
                final[rows, :] = block[...]

    def block_sent(hold, ss):
        sent(column_half(hold, 0), ss.at[8])
        for i in range(4):
            if i > 0:
                sent(hold, ss.at[i])
            mine, there = block_target(i)

            @pl.when(jnp.logical_not(mine))
            def _():
                sent(hold, ss.at[4 + i])

    def block_got(final, height, rs):
        def one(i, carry):
            @pl.when(jnp.logical_not((xl == k) & (z == i) & (lax.rem(part, 2) == k)))
            def _():
                got(final.at[pl.ds(pl.multiple_of(height * i, 16), height)], rs.at[4 + i])

            return carry

        lax.fori_loop(0, 4, one, 0)

    def key_back(s, mine):
        span = pl.ds(pl.multiple_of(s * 128, 128), 128)
        rows = pl.ds(pl.multiple_of(512 * (xh if mine else 1 - xh), 512), 512)
        cos, sin = (r.cos_t, r.sin_t) if mine else (r.cos_o, r.sin_o)
        raw = r.qkraw[:, span, 256:384] if mine else r.kraw_o[:, span, :]
        du = unrotated(r.dkv[s, rows, 0:HEAD] * SCALE, cos[:, span, :].reshape(512, HEAD), sin[:, span, :].reshape(512, HEAD))
        back, gain_grad = norm_back(raw.reshape(512, HEAD), gk, du)
        out, first = (r.dqkv, 256) if mine else (r.dkv_o, 0)
        out[:, span, first : first + HEAD] = back.astype(bf16).reshape(4, 128, HEAD)
        out[:, span, first + HEAD : first + 2 * HEAD] = r.dkv[s, rows, HEAD : 2 * HEAD].astype(bf16).reshape(4, 128, HEAD)
        r.dg[17:18, :] += gain_grad

    def norm_back(value, gain, grad):
        inverse = inverse_rms(value)
        w = grad * gain
        back = inverse * w - value * (inverse * inverse * inverse) * jnp.mean(w * value, axis=-1, keepdims=True)
        return back, jnp.sum(grad * value * inverse, axis=0, keepdims=True)

    def attend_back(half, s):
        rows = rows_of(half)
        do_s = dot_nt(r.wo[...], r.x_all[:, s, rows, :].reshape(256, D)).astype(bf16)
        prod = do_s.astype(f32) * r.o_t[s, :, lanes(half)]
        r.do_t[s, :, lanes(half)] = do_s
        ok = allowed(s, half)
        keys, values = r.kv[s, :, 0:HEAD], r.kv[s, :, HEAD : 2 * HEAD]
        mine = pl.ds(pl.multiple_of(s * 128 + 64 * half, 64), 64)
        cos = r.cos_t[:, mine, :].reshape(256, HEAD)
        sin = r.sin_t[:, mine, :].reshape(256, HEAD)
        for h in range(2):
            head = slice(h * HEAD, (h + 1) * HEAD)
            q = r.q_s[s, half, :, head]
            do = r.do_t[s, head, lanes(half)]
            delta = jnp.sum(prod[head], axis=0, keepdims=True)
            scores = dot_nt(keys, q) * (SCALE * LOG2E)
            p = jnp.where(ok, jnp.exp2(scores - r.lse[s, h, :, lanes(half)]), 0.0)
            ds = (p * (dot(values, do) - delta)).astype(bf16)
            dv = dot_nt(p.astype(bf16), do)
            dk = dot(ds, q)
            if half == 0 and h == 0:
                r.dkv[s, :, HEAD : 2 * HEAD] = dv
                r.dkv[s, :, 0:HEAD] = dk
            else:
                r.dkv[s, :, HEAD : 2 * HEAD] += dv
                r.dkv[s, :, 0:HEAD] += dk
            dq = (dot_tn(keys, ds) * SCALE).T
            raw = r.qkraw[:, mine, head].reshape(256, HEAD)
            back, gain_grad = norm_back(raw, gq, unrotated(dq, cos, sin))
            r.dqkv[:, mine, head] = back.astype(bf16).reshape(4, 64, HEAD)
            r.dg[16:17, :] += gain_grad

    def gather_rest(half):
        gather_own(r.x_all, r.r_dob, half)
        for d in (1, 3, 2):
            gather_pair(r.x_all, r.r_dob, d, half)

    for half in range(2):
        reduce_end(0, r.pa, half)

    def down_partial(i, carry):
        hid = r.hid_all[i].reshape(256, 384)
        r.pa[i] = dot(hid, r.wd[...]).astype(bf16).reshape(2, 128, D)
        return carry

    near_forward(r.x_all, r.s_dob, r.r_dob, 0)
    lax.fori_loop(0, 4, down_partial, 0)
    for d in (2, 1, 3, 0):
        reduce_first(2, r.pa, r.ca, d)
    def out_gradient(half, s):
        return lambda cols: dot(r.ob_t[s, :, lanes(half)], r.x_all[:, s, rows_of(half), cols].reshape(256, 256))

    def out_gradients(half):
        def one(i, carry):
            cols = pl.ds(pl.multiple_of(256 * i, 256), 256)
            total = out_gradient(half, 0)(cols) + out_gradient(half, 1)(cols)
            if half == 0:
                r.go_sum[:, cols] = total
            else:
                r.go[:, cols] = (r.go_sum[:, cols] + total).astype(bf16)
            return carry

        lax.fori_loop(0, 4, one, 0)

    gather_forward(r.x_all, r.s_dob, r.r_dob, 2, 0)
    attend_back(0, k)
    near_forward(r.x_all, r.s_dob, r.r_dob, 1)
    rows_z_second()
    cross_x(ggub_piece, r.zgub, r.sgub, r.xgub, row_half, r.s_ggub, r.r_ggub)
    gather_rest(0)
    attend_back(0, other)
    reduce_far(2, r.pa, r.ca, r.ra)
    out_gradients(0)
    gather_forward(r.x_all, r.s_dob, r.r_dob, 2, 1)
    gather_rest(1)
    out_gradients(1)
    cross_z_second(r.gd, 48, r.xd, r.sd, r.zd, r.s_gd, r.r_gd)
    cross_z(go_piece, r.zo, r.s_go, r.r_go)
    gu_total = jnp.concatenate([rows_z_total(), cross_total(r.sgub, r.xgub, row_half, r.r_ggub)], axis=1)
    rows_exchange(gu_total, r.hgu, r.s_fgu, r.r_fgu)
    for i, s in enumerate((k, other)):
        attend_back(1, s)
        key_back(s, False)
        block = pl.ds(pl.multiple_of(128 * s, 128), 128)
        send(r.dkv_o.at[:, block], r.dkv_recv.at[:, block], r.s_dkv.at[i], r.r_dkv.at[i], along_x(2))
        if i == 0:
            reduce_near(2, r.pa, r.ra)
    rows_spread(r.hgu, r.fgu, r.s_fgu, r.r_fgu)

    for s in range(2):
        key_back(s, True)

    def weighed(grad, weight):
        prod = grad * weight[...].reshape(D, 256).astype(f32)
        return prod[:, 0:128] + prod[:, 128:256]

    grad = dot_tn(r.n1_all[...].reshape(D, D), r.dqkv[:, :, 0:256].reshape(D, 256))
    r.gqa[...] = grad.astype(bf16)
    cross_z(gqa_piece, r.zqa, r.s_gqa, r.r_gqa)
    wdot = weighed(grad, r.wqq)
    grad = dot_tn(r.n1_all[...].reshape(D, D), r.dqkv[:, :, 256:512].reshape(D, 256))
    grad = grad + dot_tn(r.n1o_all[...].reshape(D, D), r.dkv_o[...].reshape(D, 256))
    r.gqb[...] = grad.astype(bf16)
    cross_z(gqb_piece, r.zqb, r.s_gqb, r.r_gqb)
    wdot = wdot + weighed(grad, r.wkv)
    dg1 = jnp.sum(wdot.T, axis=0, keepdims=True) / g1
    for i in range(8):
        r.dg[i : i + 1, :] = dg1[:, 128 * i : 128 * (i + 1)]
    for i in range(1, 8):
        there = place(xh, xl, around(y, i // 2), z, lax.rem(k + i, 2))
        send(r.dg, r.dg_r1.at[i], r.s_dg1.at[i], r.r_dg1.at[i], there)

    block_exchange(cross_z_total(48, r.sd, r.zd, r.r_gd), r.hd, r.s_fd, r.r_fd)
    cross_x(go_piece, r.zo, r.so, r.xo, column_half, r.s_go, r.r_go)
    r.out_tok[...] = (r.h1[...] + reduce_third(2, r.pa, r.ca, r.ra)).astype(bf16)
    block_along_y(r.hd, r.yd, r.s_fd, r.r_fd)
    for half in range(2):
        reduce_end(1, r.pb, half)

    for i, s in enumerate((k, other)):
        got(r.dkv_recv.at[:, pl.ds(pl.multiple_of(128 * s, 128), 128)], r.r_dkv.at[i])
    block_exchange(cross_total(r.so, r.xo, column_half, r.r_go), r.ho, r.s_fo, r.r_fo)
    for d in (2, 1, 3, 0):
        yy = around(y, d)
        dkv = (r.dqkv[yy, :, 256:512].astype(f32) + r.dkv_recv[yy].astype(f32)).astype(bf16)
        dn1 = dot_nt(r.dqkv[yy, :, 0:256], r.wqq[...].reshape(D, 256)) + dot_nt(dkv, r.wkv[...].reshape(D, 256))
        r.pb[yy] = dn1.astype(bf16).reshape(2, 128, D)
        for half in range(2):
            reduce_first(3, r.pb, r.cb, d, half)
    for half in range(2):
        reduce_far(3, r.pb, r.cb, r.rb, half)
    cross_x(gqa_piece, r.zqa, r.sqa, r.xqa, row_half, r.s_gqa, r.r_gqa)
    total = r.dg[...]
    for i in range(1, 8):
        got(r.dg_r1.at[i], r.r_dg1.at[i])
        total = total + r.dg_r1[i]
    r.dg_s[0] = total
    for dz in range(1, 4):
        send(r.dg_s.at[0], r.dg_r2.at[dz - 1], r.s_dg2.at[dz - 1], r.r_dg2.at[dz - 1], place(xh, xl, y, around(z, dz), k))
    block_along_y(r.ho, r.yo, r.s_fo, r.r_fo)
    cross_x(gqb_piece, r.zqb, r.sqb, r.xqb, row_half, r.s_gqb, r.r_gqb)
    block_deliver(r.hd, r.yd, r.fd, 48, r.s_fd, r.r_fd)
    reduce_near(3, r.pb, r.rb, 0)
    rows_exchange(cross_total(r.sqa, r.xqa, row_half, r.r_gqa), r.hqa, r.s_fqa, r.r_fqa)
    for dz in range(1, 4):
        got(r.dg_r2.at[dz - 1], r.r_dg2.at[dz - 1])
        total = total + r.dg_r2[dz - 1]
    r.dg_s[1] = total
    for dx in range(1, 4):
        send(r.dg_s.at[1], r.dg_r2.at[2 + dx], r.s_dg2.at[2 + dx], r.r_dg2.at[2 + dx], along_x(dx))
    reduce_near(3, r.pb, r.rb, 1)
    rows_spread(r.hqa, r.fqa, r.s_fqa, r.r_fqa)
    direct_spread(cross_total(r.sqb, r.xqb, row_half, r.r_gqb), r.hqb, r.fqb, r.s_fqb, r.r_fqb)


    block_deliver(r.ho, r.yo, r.fo, 32, r.s_fo, r.r_fo)

    for half in range(2):
        span = rows_of(half)
        rows = r.tok[span, :].astype(f32)
        back, unused = norm_back(rows, g1, reduce_third(3, r.pb, r.cb, r.rb, half))
        r.dtok[span, :] = (r.dh1[span, :] + back).astype(bf16)

    block_got(r.fd, 48, r.r_fd)
    r.g_dn[...] = r.fd[...]
    rows_spread_got(r.fgu, r.r_fgu)
    for i in range(8):
        r.g_gu[:, 384 * i : 384 * (i + 1)] = r.fgu[i, :, 0:384]
        r.g_gu[:, 3072 + 384 * i : 3072 + 384 * (i + 1)] = r.fgu[i, :, 384:768]
    block_got(r.fo, 32, r.r_fo)
    r.g_out[...] = r.fo[...]
    for dx in range(1, 4):
        got(r.dg_r2.at[2 + dx], r.r_dg2.at[2 + dx])
        total = total + r.dg_r2[2 + dx]
    r.g_gain[...] = total
    rows_spread_got(r.fqa, r.r_fqa)
    direct_spread_got(r.fqb, r.r_fqb)
    for i in range(8):
        r.g_qkv[:, 256 * i : 256 * (i + 1)] = r.fqa[i]
        r.g_qkv[:, 2048 + 128 * i : 2048 + 128 * (i + 1)] = r.fqb[i, :, 0:128]
        r.g_qkv[:, 3072 + 128 * i : 3072 + 128 * (i + 1)] = r.fqb[i, :, 128:256]

    gather_end(r.dy_all, r.s_dy)
    for half in range(2):
        gather_end(r.n2_all, r.s_n2, half)
        gather_end(r.x_all, r.s_dob, half)
    sent(r.pos_own, r.s_pos.at[0])
    for whole, ss in ((r.gain_recv, r.s_gain), (r.wqq, r.s_wqq), (r.wkv, r.s_wkv), (r.wgu, r.s_wgu)):
        rows_sent(whole, ss)
    for i in range(4):
        here = (xl == k) & (z == i) & (to_core == k)

        @pl.when(is_source & jnp.logical_not(here))
        def _():
            sent(r.wo_own.at[pl.ds(32 * i, 32)], r.s_wo.at[i])
            sent(r.wd_own.at[pl.ds(48 * i, 48)], r.s_wd.at[i])

    loop_sent(wo_rows(part), r.s_wo2, 1, 8)
    loop_sent(wd_rows(part), r.s_wd2, 1, 8)
    gather_end(r.xo_all, r.s_xo)
    sent(r.tok, r.s_xo.at[8])
    reduce_end(2, r.pa)
    for half in range(2):
        reduce_end(3, r.pb, half)
    for s in range(2):
        sent(r.dkv_o.at[:, pl.ds(128 * s, 128)], r.s_dkv.at[s])
    cross_sent(r.zqa, r.xqa, r.s_gqa)
    cross_sent(r.zqb, r.xqb, r.s_gqb)
    cross_sent(r.zgub, r.xgub, r.s_ggub)
    for i in range(3):
        sent(r.xgua.at[0], r.s_ggua.at[i])
        sent(r.zgua.at[0], r.s_ggua.at[3 + i])
    cross_sent(r.zo, r.xo, r.s_go)
    for i in range(3):
        sent(r.xd.at[0], r.s_gd.at[i])
        sent(r.zd.at[0], r.s_gd.at[3 + i])
    for hold, ss in ((r.hqa, r.s_fqa), (r.hgu, r.s_fgu)):
        rows_spread_sent(hold, ss)
    direct_spread_sent(r.hqb, r.s_fqb)
    block_sent(r.ho, r.s_fo)
    block_sent(r.hd, r.s_fd)
    loop_sent(r.dg, r.s_dg1, 1, 8)
    loop_sent(r.dg_s.at[0], r.s_dg2, 0, 6)


def layer(*args):
    vmem = pl.BlockSpec(memory_space=pltpu.VMEM)
    hbm = pl.BlockSpec(memory_space=pl.ANY)
    specs = [hbm if far else vmem for far in INPUTS.values()]
    return pl.pallas_call(
        layer_kernel,
        out_shape=[jax.ShapeDtypeStruct(shape, kind) for shape, kind in OUTPUTS.values()],
        in_specs=specs,
        out_specs=[vmem] * len(OUTPUTS),
        scratch_shapes=[pltpu.VMEM(shape, kind) for shape, kind in BUFFERS.values()]
        + [pltpu.SemaphoreType.DMA((count,)) for count in SEMAPHORES.values()],
        compiler_params=pltpu.CompilerParams(
            collective_id=0, has_side_effects=True, vmem_limit_bytes=62 << 20
        ),
        name="layer",
    )(*args)


def adam_update(weight, moment, square, grad, rate, decay):
    moment_new = beta_first * moment + (1.0 - beta_first) * grad
    square_new = beta_second * square + (1.0 - beta_second) * grad * grad
    fix_first = 1.0 - beta_first**STEP
    fix_second = 1.0 - beta_second**STEP
    step = moment_new / fix_first / (jnp.sqrt(square_new / fix_second) + adam_eps)
    return (weight - rate * (step + decay * weight), moment_new, square_new)


def on_device(
    tokens, d_out, block_ids,
    w_qkv, w_out, w_gate_up, w_down, gains,
    moment_qkv, moment_out, moment_gate_up, moment_down, moment_gains,
    square_qkv, square_out, square_gate_up, square_down, square_gains,
):
    f = lax.axis_index("fsdp")
    gain_rows = lax.dynamic_update_slice(
        jnp.zeros((24 * 128,), f32), gains.astype(bf16).astype(f32), (f * 144,)
    ).reshape(24, 128)
    half = rope_base ** (-(np.arange(64, dtype=np.float32) * np.float32(2.0 / HEAD)))
    table = np.zeros((8, 128), np.float32)
    table[0] = np.concatenate([half, half])
    table[1] = np.concatenate([-np.ones(64), np.ones(64)])
    out_tok, dtok, g_qkv, g_out, g_gu, g_dn, g_gain = layer(
        tokens[0], d_out[0], block_ids, gain_rows, jnp.asarray(table), w_qkv, w_out, w_gate_up, w_down
    )
    grad_gains = lax.dynamic_slice(g_gain.reshape(24 * 128), (f * 144,), (144,))
    grads = (g_qkv, g_out, g_gu, g_dn, grad_gains)
    masters = (w_qkv, w_out, w_gate_up, w_down, gains)
    moments = (moment_qkv, moment_out, moment_gate_up, moment_down, moment_gains)
    squares = (square_qkv, square_out, square_gate_up, square_down, square_gains)
    rates = (0.03, 0.3, 0.03, 0.03, 0.5)
    decays = (decay_rate, decay_rate, decay_rate, decay_rate, 0.0)
    updates = [
        adam_update(masters[i], moments[i], squares[i], grads[i].astype(f32), rates[i], decays[i])
        for i in range(5)
    ]
    return (
        out_tok[None],
        dtok[None],
        *(u[0] for u in updates),
        *(u[1] for u in updates),
        *(u[2] for u in updates),
    )


def solution(mesh):
    rows, flat = P("fsdp", None), P("fsdp")
    tokens = P("fsdp", "ctx", None)
    state = (rows, rows, rows, rows, flat)
    return jax.shard_map(
        on_device,
        mesh=mesh,
        in_specs=(tokens, tokens, rows) + state * 3,
        out_specs=(tokens, tokens) + state * 3,
        check_vma=False,
    )
```
